32 devices in a mesh: dp: 8 (over z, core), mp: 4 (over y, x).
Axes of the slice: x: 2, y: 2, z: 4, core: 2. Of those that a mesh axis runs over, the one named last changes fastest.
Arguments:
- prefix_input: bfloat16 [6528, 2048], P('dp'), may hold values from -6 to 6
- action_input: bfloat16 [16, 50, 32], P('dp'), may hold values from -6 to 6
- valid_dims: int32 [16], P('dp'), may hold values from 0 to 18, as said below
- slot_item: int32 [16], P('dp'), may hold values from -1 to 7, as said below
- segments: int32 [8, 816], P('dp'), may hold values from 0 to 3, never falling along the last dimension, each value on 1 to 408 neighbouring positions
- pre_gain_attn: bfloat16 [2048], P('dp'), may hold values from 0.099609375 to 1.8984375
- pre_query: bfloat16 [2048, 2048], P('dp', 'mp'), may hold values from -0.125 to 0.125
- pre_key: bfloat16 [2048, 256], P('dp'), may hold values from -0.125 to 0.125
- pre_value: bfloat16 [2048, 256], P('dp'), may hold values from -0.125 to 0.125
- pre_output: bfloat16 [2048, 2048], P('mp', 'dp'), may hold values from -2 to 2
- pre_gain_ffn: bfloat16 [2048], P('dp'), may hold values from 0.099609375 to 1.8984375
- pre_gate: bfloat16 [2048, 16384], P('dp', 'mp'), may hold values from -0.125 to 0.125
- pre_up: bfloat16 [2048, 16384], P('dp', 'mp'), may hold values from -0.125 to 0.125
- pre_down: bfloat16 [16384, 2048], P('mp', 'dp'), may hold values from -0.046875 to 0.046875
- act_embed: bfloat16 [32, 1024], P(None, 'dp'), may hold values from -1.5 to 1.5
- act_gain_attn: bfloat16 [1024], P('dp'), may hold values from 0.099609375 to 1.8984375
- act_query: bfloat16 [1024, 2048], P('dp', 'mp'), may hold values from -0.1875 to 0.1875
- act_key: bfloat16 [1024, 256], P('dp'), may hold values from -0.1875 to 0.1875
- act_value: bfloat16 [1024, 256], P('dp'), may hold values from -0.1875 to 0.1875
- act_output: bfloat16 [2048, 1024], P('mp', 'dp'), may hold values from -2 to 2
- act_gain_ffn: bfloat16 [1024], P('dp'), may hold values from 0.099609375 to 1.8984375
- act_gate: bfloat16 [1024, 4096], P('dp', 'mp'), may hold values from -0.1875 to 0.1875
- act_up: bfloat16 [1024, 4096], P('dp', 'mp'), may hold values from -0.1875 to 0.1875
- act_down: bfloat16 [4096, 1024], P('mp', 'dp'), may hold values from -0.09375 to 0.09375
- prefix_cotangent: bfloat16 [6528, 2048], P('dp'), may hold values from -6 to 6
- action_cotangent: bfloat16 [16, 50, 1024], P('dp'), may hold values from -6 to 6
Outputs:
- prefix_output: bfloat16 [6528, 2048], P('dp')
- action_output: bfloat16 [16, 50, 1024], P('dp')
- prefix_grad: float32 [6528, 2048], P('dp')
- action_grad: float32 [16, 50, 32], P('dp')
- grad_pre_gain_attn: float32 [2048], P('dp')
- grad_pre_query: float32 [2048, 2048], P('dp', 'mp')
- grad_pre_key: float32 [2048, 256], P('dp')
- grad_pre_value: float32 [2048, 256], P('dp')
- grad_pre_output: float32 [2048, 2048], P('mp', 'dp')
- grad_pre_gain_ffn: float32 [2048], P('dp')
- grad_pre_gate: float32 [2048, 16384], P('dp', 'mp')
- grad_pre_up: float32 [2048, 16384], P('dp', 'mp')
- grad_pre_down: float32 [16384, 2048], P('mp', 'dp')
- grad_act_embed: float32 [32, 1024], P(None, 'dp')
- grad_act_gain_attn: float32 [1024], P('dp')
- grad_act_query: float32 [1024, 2048], P('dp', 'mp')
- grad_act_key: float32 [1024, 256], P('dp')
- grad_act_value: float32 [1024, 256], P('dp')
- grad_act_output: float32 [2048, 1024], P('mp', 'dp')
- grad_act_gain_ffn: float32 [1024], P('dp')
- grad_act_gate: float32 [1024, 4096], P('dp', 'mp')
- grad_act_up: float32 [1024, 4096], P('dp', 'mp')
- grad_act_down: float32 [4096, 1024], P('mp', 'dp')
The draws below stay inside these ranges and needn't reach their ends.
Inputs may be any that keep to these rules, and one draw needn't show every extreme that they name: `slot_item`: each of the 8 items stands in exactly one slot; -1 marks an empty slot; on each index of dp either all 2 slots are filled or none, and half of the indices are filled. `valid_dims`: 0 on empty slots, 7 or more on filled ones. `segments`: never falling along an item's prefix.
All inputs are finite; a program needn't handle non-finite values.
Results may differ from the reference program's by a relative error of at most 0.02.
Values may be sent and summed in bfloat16 or wider, within the bound.
A program may use at most 320 MiB of HBM per device.

```python
import math
import jax
import jax.numpy as jnp
import numpy as np
from jax import lax

DP = 2048
FP = 16384
DA = 1024
FA = 4096
H = 8
HD = 256
PRE = 816
ACT = 50
AIN = 32
CAP = 2
ITEMS = 8
SLOTS = 16


def slot_table(key):
    devices = SLOTS // CAP
    order = jax.random.permutation(jax.random.fold_in(key, 101), devices)
    items = jax.random.permutation(jax.random.fold_in(key, 102), ITEMS)
    slot = jnp.arange(SLOTS, dtype=jnp.int32)
    owner_rank = order[slot // CAP]
    filled = owner_rank < devices // 2
    place = jnp.minimum(owner_rank * CAP + slot % CAP, ITEMS - 1)
    return jnp.where(filled, items[place], -1).astype(jnp.int32)


def draw_slot_item(key, part):
    return slot_table(key)


def draw_valid_dims(key, part):
    table = slot_table(key)
    key = jax.random.fold_in(key, 7)
    counts = jax.random.randint(key, (SLOTS,), 7, 19)
    counts = jnp.where(table == 0, 18, counts)
    return jnp.where(table >= 0, counts, 0).astype(jnp.int32)


def level_of(own_key, shape, shards, smallest, top_value):
    def one(position, blocks):
        draws = jax.random.uniform(jax.random.fold_in(jax.random.fold_in(own_key, 6), position), (blocks,), jnp.float32, smallest / len(shards), top_value / len(shards))
        return jnp.repeat(jnp.exp(draws), shape[position] // blocks).reshape((-1,) + (1,) * (len(shape) - position - 1))

    loudness = one(*shards[0])
    for cut in shards[1:]:
        loudness = loudness * one(*cut)
    return loudness


def split_up(count, total, limit, slope):
    portions = [(1 << 20) // math.isqrt(standing ** slope) + 1 for standing in range(2, count + 1)]
    rest, holding = total - limit - (count - 1), [1] * (count - 1)
    while rest > 0:
        movable = [i for i in range(count - 1) if holding[i] < limit]
        pool, remaining = sum([portions[i] for i in movable]), rest
        for i in movable:
            more = min(limit - holding[i], max(1, remaining * portions[i] // pool), rest)
            holding[i] = holding[i] + more
            rest = rest - more
    return np.array([limit] + holding)


def ragged(key, count, total, reach, lean):
    if count == 2:
        one = jax.random.randint(key, (), max(1, total - reach), min(reach, total - 1) + 1)
        return jnp.stack([one, total - one])
    lengths = jnp.asarray(split_up(count, total, reach, lean), jnp.int32)
    couples = (count - 1) // 2
    donor, receiver = lengths[1:1 + 2 * couples:2], lengths[2:2 + 2 * couples:2]
    slack = jnp.minimum(donor - 1, reach - receiver)
    moved = jax.random.randint(jax.random.fold_in(key, 1), (couples,), 0, 1 << 20) % (slack + 1)
    lengths = lengths.at[1:1 + 2 * couples:2].set(donor - moved).at[2:2 + 2 * couples:2].set(receiver + moved)
    return lengths[jax.random.permutation(jax.random.fold_in(key, 2), count)]


def gaussian(key, shape, width, limit, shards=(), kind=jnp.bfloat16):
    level = level_of(key, shape, shards, -0.22, 0.18) if shards else 1.0
    values = jax.random.normal(key, shape, jnp.float32) * width * level
    return jnp.minimum(jnp.maximum(values, -limit), limit).astype(kind)


def setup_inputs(seed: int = 0) -> dict:
    streams_of = jax.random.split(jax.random.key(seed), 27)
    prefix_input = gaussian(streams_of[0], (ITEMS * PRE, DP), 1.0, 6.0, ((0, 8),))
    action_input = gaussian(streams_of[1], (SLOTS, ACT, AIN), 1.0, 6.0, ((0, 8),))
    valid_dims = draw_valid_dims(jax.random.fold_in(streams_of[26], 71), 0)
    slot_item = draw_slot_item(jax.random.fold_in(streams_of[26], 71), 0)
    segments = jax.vmap(lambda own: jnp.searchsorted(jnp.cumsum(ragged(own, 4, PRE, PRE // 2, 2)), jnp.arange(PRE), side="right"))(jax.random.split(streams_of[4], ITEMS)).reshape((ITEMS, PRE)).astype(jnp.int32)
    pre_gain_attn = jnp.clip(1.0 + 0.18 * jax.random.normal(streams_of[5], (DP,), jnp.float32), 0.099609375, 1.8984375).astype(jnp.bfloat16)
    pre_query = gaussian(streams_of[6], (DP, H * HD), DP ** -0.5, 0.125, ((0, 8), (1, 4)))
    pre_key = gaussian(streams_of[7], (DP, HD), DP ** -0.5, 0.125, ((0, 8),))
    pre_value = gaussian(streams_of[8], (DP, HD), DP ** -0.5, 0.125, ((0, 8),))
    pre_output = gaussian(streams_of[9], (H * HD, DP), (max(1, H * HD * 4 // PRE)) ** -0.5, 2.0, ((0, 4), (1, 8)))
    pre_gain_ffn = jnp.clip(1.0 + 0.18 * jax.random.normal(streams_of[10], (DP,), jnp.float32), 0.099609375, 1.8984375).astype(jnp.bfloat16)
    pre_gate = gaussian(streams_of[11], (DP, FP), DP ** -0.5, 0.125, ((0, 8), (1, 4)))
    pre_up = gaussian(streams_of[12], (DP, FP), DP ** -0.5, 0.125, ((0, 8), (1, 4)))
    pre_down = gaussian(streams_of[13], (FP, DP), FP ** -0.5, 0.046875, ((0, 4), (1, 8)))
    act_embed = gaussian(streams_of[14], (AIN, DA), 16 ** -0.5, 1.5, ((1, 8),))
    act_gain_attn = jnp.clip(1.0 + 0.18 * jax.random.normal(streams_of[15], (DA,), jnp.float32), 0.099609375, 1.8984375).astype(jnp.bfloat16)
    act_query = gaussian(streams_of[16], (DA, H * HD), DA ** -0.5, 0.1875, ((0, 8), (1, 4)))
    act_key = gaussian(streams_of[17], (DA, HD), DA ** -0.5, 0.1875, ((0, 8),))
    act_value = gaussian(streams_of[18], (DA, HD), DA ** -0.5, 0.1875, ((0, 8),))
    act_output = gaussian(streams_of[19], (H * HD, DA), (max(1, H * HD * 4 // (PRE + ACT))) ** -0.5, 2.0, ((0, 4), (1, 8)))
    act_gain_ffn = jnp.clip(1.0 + 0.18 * jax.random.normal(streams_of[20], (DA,), jnp.float32), 0.099609375, 1.8984375).astype(jnp.bfloat16)
    act_gate = gaussian(streams_of[21], (DA, FA), DA ** -0.5, 0.1875, ((0, 8), (1, 4)))
    act_up = gaussian(streams_of[22], (DA, FA), DA ** -0.5, 0.1875, ((0, 8), (1, 4)))
    act_down = gaussian(streams_of[23], (FA, DA), FA ** -0.5, 0.09375, ((0, 4), (1, 8)))
    prefix_cotangent = gaussian(streams_of[24], (ITEMS * PRE, DP), 1.0, 6.0, ((0, 8),))
    action_cotangent = gaussian(streams_of[25], (SLOTS, ACT, DA), 1.0, 6.0, ((0, 8),))
    return {"prefix_input": prefix_input, "action_input": action_input, "valid_dims": valid_dims, "slot_item": slot_item, "segments": segments, "pre_gain_attn": pre_gain_attn, "pre_query": pre_query, "pre_key": pre_key, "pre_value": pre_value, "pre_output": pre_output, "pre_gain_ffn": pre_gain_ffn, "pre_gate": pre_gate, "pre_up": pre_up, "pre_down": pre_down, "act_embed": act_embed, "act_gain_attn": act_gain_attn, "act_query": act_query, "act_key": act_key, "act_value": act_value, "act_output": act_output, "act_gain_ffn": act_gain_ffn, "act_gate": act_gate, "act_up": act_up, "act_down": act_down, "prefix_cotangent": prefix_cotangent, "action_cotangent": action_cotangent}


@jax.custom_vjp
def low(v):
    return lax.optimization_barrier(v.astype(jnp.bfloat16)).astype(jnp.float32)

@jax.custom_vjp
def low_back(v):
    return v

def low_keep(v):
    return (low(v), None)

def low_pass(kept, grad):
    return (grad,)

def back_keep(v):
    return (v, None)

def back_low(kept, grad):
    return (low(grad),)
low.defvjp(low_keep, low_pass)
low_back.defvjp(back_keep, back_low)
EPS = 1e-06
HIGH = lax.Precision.HIGHEST

def both_ways(value):
    return low(low_back(value))

def mat(left, right):
    return jnp.dot(left, right, precision=HIGH, preferred_element_type=jnp.float32)

def rms_gain(values, gain):
    return values * lax.rsqrt(lax.optimization_barrier(jnp.mean(values * values, axis=-1, keepdims=True)) + EPS) * gain

def attend(query, keys, values, allowed):
    scale = HD ** (-0.5)
    scores = low_back(jnp.einsum('lhd,md->hlm', query, keys, precision=HIGH) * scale)
    masked = jnp.where(allowed[None], scores, -1e+30)
    top = lax.optimization_barrier(jnp.max(masked, axis=-1, keepdims=True))
    expo = jnp.exp(masked - top)
    probs = low(expo / lax.optimization_barrier(jnp.sum(expo, axis=-1, keepdims=True)))
    return both_ways(jnp.einsum('hlm,md->lhd', probs, values, precision=HIGH))

def finish(resid, mixed, w_out, gain_ffn, w_gate, w_up, w_down):
    second = resid + low_back(mat(mixed, w_out))
    normed = low(rms_gain(second, gain_ffn))
    gate = low_back(mat(normed, w_gate))
    upward = low_back(mat(normed, w_up))
    hidden = low(jax.nn.gelu(gate, approximate=True) * upward)
    return second + low_back(mat(hidden, w_down))

def prefix_block(weights, resid, seg):
    gain_one, w_query, w_key, w_value, w_out, gain_two, w_gate, w_up, w_down = weights[:9]
    normed = low(rms_gain(resid, gain_one))
    query = both_ways(mat(normed, w_query)).reshape(PRE, H, HD)
    keys = both_ways(mat(normed, w_key))
    values = both_ways(mat(normed, w_value))
    allowed = seg[:, None] >= seg[None, :]
    mixed = attend(query, keys, values, allowed)
    result = finish(resid, mixed.reshape(PRE, H * HD), w_out, gain_two, w_gate, w_up, w_down)
    return (result, keys, values)

def action_block(weights, acts, dims, keys_in, values_in):
    w_embed, gain_one, w_query, w_key, w_value, w_out, gain_two, w_gate, w_up, w_down = weights[9:]
    resid = low_back(mat(acts * dims[None, :], w_embed))
    normed = low(rms_gain(resid, gain_one))
    query = both_ways(mat(normed, w_query)).reshape(ACT, H, HD)
    keys = jnp.concatenate([keys_in, both_ways(mat(normed, w_key))], axis=0)
    values = jnp.concatenate([values_in, both_ways(mat(normed, w_value))], axis=0)
    allowed = jnp.ones((ACT, PRE + ACT), dtype=bool)
    mixed = attend(query, keys, values, allowed)
    return finish(resid, mixed.reshape(ACT, H * HD), w_out, gain_two, w_gate, w_up, w_down)

def forward(prefix_x, action_x, weights, segments, slot_item, dims):
    items = prefix_x.reshape(ITEMS, PRE, DP)
    run_prefix = jax.checkpoint(lambda pair: prefix_block(weights, pair[0], pair[1]))
    out_pre, keys, values = lax.map(run_prefix, (items, segments))
    live = (slot_item >= 0).astype(jnp.float32)
    pick = jnp.maximum(slot_item, 0).astype(jnp.int32)
    keys_in = keys[pick] * live[:, None, None]
    values_in = values[pick] * live[:, None, None]
    run_action = jax.checkpoint(lambda group: action_block(weights, group[0], group[1], group[2], group[3]))
    out_act = lax.map(run_action, (action_x, dims, keys_in, values_in))
    return (out_pre.reshape(ITEMS * PRE, DP), out_act)

def reference(prefix_input, action_input, valid_dims, slot_item, segments, pre_gain_attn, pre_query, pre_key, pre_value, pre_output, pre_gain_ffn, pre_gate, pre_up, pre_down, act_embed, act_gain_attn, act_query, act_key, act_value, act_output, act_gain_ffn, act_gate, act_up, act_down, prefix_cotangent, action_cotangent):
    weights = tuple((w.astype(jnp.float32) for w in (pre_gain_attn, pre_query, pre_key, pre_value, pre_output, pre_gain_ffn, pre_gate, pre_up, pre_down, act_embed, act_gain_attn, act_query, act_key, act_value, act_output, act_gain_ffn, act_gate, act_up, act_down)))
    dims = (jnp.arange(AIN, dtype=jnp.int32)[None, :] < valid_dims[:, None]).astype(jnp.float32)
    live = (slot_item >= 0).astype(jnp.float32)

    def run(prefix_x, action_x, params):
        return forward(prefix_x, action_x, params, segments, slot_item, dims)
    (out_pre, out_act), pull = jax.vjp(run, prefix_input.astype(jnp.float32), action_input.astype(jnp.float32), weights)
    grad_x, grad_a, grad_w = pull((prefix_cotangent.astype(jnp.float32), action_cotangent.astype(jnp.float32) * live[:, None, None]))
    return (out_pre.astype(jnp.bfloat16), out_act.astype(jnp.bfloat16), grad_x, grad_a, grad_w[0], grad_w[1], grad_w[2], grad_w[3], grad_w[4], grad_w[5], grad_w[6], grad_w[7], grad_w[8], grad_w[9], grad_w[10], grad_w[11], grad_w[12], grad_w[13], grad_w[14], grad_w[15], grad_w[16], grad_w[17], grad_w[18])
```

```python
import functools

import jax
import jax.numpy as jnp
from jax import lax
from jax.experimental import pallas as pl
from jax.experimental.pallas import tpu as pltpu
from jax.sharding import PartitionSpec as P

HD = 256
EPS = 1e-06
BF = jnp.bfloat16
F32 = jnp.float32


def rms_gain(values, gain):
    return values * lax.rsqrt(jnp.mean(values * values, axis=-1, keepdims=True) + EPS) * gain


def norm_backward(values, gain, grad_out):
    unused, pull = jax.vjp(rms_gain, values, gain)
    return pull(grad_out)


def glu_value(gate, upward):
    return jax.nn.gelu(gate, approximate=True) * upward


def dot_plain(left, right):
    return jnp.dot(left, right, preferred_element_type=F32)


def dot_left(left, right):
    return lax.dot_general(left, right, (((0,), (0,)), ((), ())), preferred_element_type=F32)


def dot_right(left, right):
    return lax.dot_general(left, right, (((1,), (1,)), ((), ())), preferred_element_type=F32)


def round_up(value, step):
    return -(-value // step) * step


def swap_mp(block, step):
    size = lax.axis_size("mp")
    return lax.ppermute(block, "mp", [(i, i ^ step) for i in range(size)])


def swap_core(block):
    size = lax.axis_size("dp")
    return lax.ppermute(block, "dp", [(i, i ^ 1) for i in range(size)])


def send_dp(block, step):
    size = lax.axis_size("dp")
    return lax.ppermute(block, "dp", [(i, (i + step) % size) for i in range(size)])


def pair_sum(parts):
    size, me = lax.axis_size("dp"), lax.axis_index("dp")
    parts = parts.reshape((size // 2, 2) + parts.shape[1:])
    here = lax.rem(me, 2)
    kept = lax.dynamic_index_in_dim(parts, here, 1, False)
    got = swap_core(lax.dynamic_index_in_dim(parts, 1 - here, 1, False))
    return (kept.astype(F32) + got.astype(F32)).astype(BF)


def reduce_dp(parts):
    size, me = lax.axis_size("dp"), lax.axis_index("dp")
    half = size // 2
    both = pair_sum(parts)
    total = 0.0
    for s in range(half):
        chip = lax.rem(me // 2 + s, half)
        block = lax.dynamic_index_in_dim(both, chip, 0, False)
        total = total + (send_dp(block, 2 * s) if s else block).astype(F32)
    return total


def gather_mp(block, axis):
    size = lax.axis_size("mp")
    return jnp.concatenate([block] + [swap_mp(block, s) for s in range(1, size)], axis=axis)


def reduce_mp(matrix, axis):
    size = lax.axis_size("mp")
    parts = jnp.split(matrix, size, axis=axis)
    total = parts[0].astype(F32)
    for s in range(1, size):
        total = total + swap_mp(parts[s].astype(BF), s).astype(F32)
    return total


def pick_mp(blocks, place):
    at = lax.axis_index("mp") ^ place
    block = blocks[0]
    for s in range(1, len(blocks)):
        block = jnp.where(at == s, blocks[s], block)
    return block


def own_order(array):
    col = lax.axis_index("mp")
    return jnp.stack(
        [lax.dynamic_index_in_dim(array, col ^ s, 0, False) for s in range(array.shape[0])]
    )


def pack(prefix, action):
    wider = ((0, 0), (0, prefix.shape[1] - action.shape[1]))
    return jnp.concatenate([prefix, jnp.pad(action, wider)], axis=0)


def unpack(block, rows, width):
    return block[:rows], block[rows:, :width]


MESH = pl.DeviceIdType.MESH
HBM = pl.BlockSpec(memory_space=pl.ANY)


def peers(n, m):
    me, col = lax.axis_index("dp"), lax.axis_index("mp")
    column = [(lax.rem(me + s, n), col) for s in range(1, n)]
    return column + [(me, col ^ s) for s in range(1, m)]


def greet(devices):
    barrier = pltpu.get_barrier_semaphore()
    for device in devices:
        pl.semaphore_signal(barrier, inc=1, device_id=device, device_id_type=MESH)
    pl.semaphore_wait(barrier, len(devices))


def remote(src, dst, sent, arrived, device):
    return pltpu.make_async_remote_copy(
        src_ref=src,
        dst_ref=dst,
        send_sem=sent,
        recv_sem=arrived,
        device_id=device,
        device_id_type=MESH,
    )


def at(start, size):
    return pl.ds(pl.multiple_of(start * size, size), size)


class Line:
    def __init__(self, own, place, sems, row):
        self.n = lax.axis_size("dp")
        self.me, self.col = lax.axis_index("dp"), lax.axis_index("mp")
        self.own, self.place, self.row = own, place, row
        self.sent, self.arrived, self.local = sems
        self.chips = self.n // 2
        self.chip = self.me // 2

    def copy(self, way, k):
        step = (2, -2)[way]
        origin = lax.rem(self.me - step * (k - 1) + 2 * self.n, self.n)
        source = self.own if k == 1 else self.place(origin)
        target = (lax.rem(self.me + step + self.n, self.n), self.col)
        slot = way * self.chips + k
        return remote(
            source,
            self.place(origin),
            self.sent.at[self.row, slot],
            self.arrived.at[self.row, slot],
            target,
        )

    def across(self, way, k):
        step = (2, -2)[way]
        origin = lax.rem(self.me - step * k + 2 * self.n, self.n)
        source = self.own if k == 0 else self.place(origin)
        slot = (2 + way) * self.chips + k
        return remote(
            source,
            self.place(origin),
            self.sent.at[self.row, slot],
            self.arrived.at[self.row, slot],
            (self.me ^ 1, self.col),
        )

    def sends(self, way, k):
        beyond = self.chip < self.chips - 1 if way == 0 else self.chip > 0
        return beyond & self.receives(way, k - 1)

    def receives(self, way, k):
        if k == 0:
            return self.chip >= 0
        return self.chip >= k if way == 0 else self.chip < self.chips - k

    def start(self):
        self.keep = pltpu.make_async_copy(self.own, self.place(self.me), self.local.at[self.row])
        self.keep.start()
        for way in (0, 1):
            pl.when(self.sends(way, 1))(self.copy(way, 1).start)
        self.across(0, 0).start()

    def step(self, k):
        for way in (0, 1):

            @pl.when(self.receives(way, k))
            def _(way=way):
                self.copy(way, k).wait_recv()
                self.across(way, k).start()

            if k < self.chips - 1:
                pl.when(self.sends(way, k + 1))(self.copy(way, k + 1).start)

    def finish(self):
        self.keep.wait()
        self.across(0, 0).wait()
        for way in (0, 1):
            for k in range(1, self.chips):
                pl.when(self.sends(way, k))(self.copy(way, k).wait_send)
                pl.when(self.receives(way, k))(self.across(way, k).wait)


def line_sems(count, n):
    return [
        pltpu.SemaphoreType.DMA((count, 2 * n)),
        pltpu.SemaphoreType.DMA((count, 2 * n)),
        pltpu.SemaphoreType.DMA((count,)),
    ]


def gather_kernel(n, m, count, places, shares, *refs):
    sources, results = refs[:count], refs[count : 2 * count]
    sent, arrived, local, share_sent, share_arrived = refs[2 * count :]
    me, col = lax.axis_index("dp"), lax.axis_index("mp")
    greet(peers(n, m))
    lines = []
    for a in range(count):
        place = functools.partial(places[a], results[a])
        lines.append(Line(sources[a], place, (sent, arrived, local), a))
        lines[-1].start()
    for k in range(1, n // 2):
        for line in lines:
            line.step(k)
    for line in lines:
        line.finish()

    def passed(x, a, s):
        whole = results[a].at[col]
        return remote(
            whole, whole, share_sent.at[x, s], share_arrived.at[x, s], (me, col ^ s)
        )

    copies = [passed(x, a, s) for x, a in enumerate(shares) for s in range(1, m)]
    for c in copies:
        c.start()
    for c in copies:
        c.wait()


def gather_all(arrays, shapes, places, shares, collective_id):
    n, m = lax.axis_size("dp"), lax.axis_size("mp")
    count = len(arrays)
    return pl.pallas_call(
        functools.partial(gather_kernel, n, m, count, places, shares),
        out_shape=[jax.ShapeDtypeStruct(s, a.dtype) for s, a in zip(shapes, arrays)],
        in_specs=[HBM] * count,
        out_specs=[HBM] * count,
        scratch_shapes=line_sems(count, n)
        + [pltpu.SemaphoreType.DMA((max(len(shares), 1), m))] * 2,
        compiler_params=pltpu.CompilerParams(collective_id=collective_id, has_side_effects=True),
        name="gather_all",
    )(*arrays)


def by_rows(size):
    return lambda ref, i: ref.at[at(i, size)]


def by_columns(size):
    return lambda ref, i: ref.at[:, at(i, size)]


def by_lead(ref, i):
    return ref.at[i]


def by_share(size):
    return lambda ref, i: ref.at[lax.axis_index("mp"), at(i, size)]


def deal_kernel(n, m, kinds, lines_count, *refs):
    count = len(kinds)
    total = count + lines_count
    sources, results = refs[:total], refs[total : 2 * total]
    sems = refs[2 * total :]
    deal_sent, deal_arrived, local = sems[:3]
    x_sent, x_arrived, y_sent, y_arrived = sems[3:7]
    xy_sent, xy_arrived, yx_sent, yx_arrived = sems[7:11]
    all_sent, all_arrived = sems[11:13]
    line_sent, line_arrived, line_local = sems[13:16]
    me, col = lax.axis_index("dp"), lax.axis_index("mp")
    greet(peers(n, m))
    beside_x, beside_y = (me, col ^ 1), (me, col ^ 2)

    def source(t, i):
        ref = sources[t]
        if kinds[t] == 2:
            return ref.at[i]
        if kinds[t] == 0:
            return ref.at[:, at(i, ref.shape[1] // n)]
        return ref.at[at(i, ref.shape[0] // n)]

    def region(t, i, place, part=None):
        ref = results[t]
        if kinds[t] == 2:
            if part is None:
                return ref.at[place, i]
            few = ref.shape[2] // 2
            return ref.at[place, i, pl.ds(part * few, few)]
        if kinds[t] == 0:
            rows, width = ref.shape[0] // n, ref.shape[1] // m
            row = i * rows
            columns = pl.ds(place * width, width)
        else:
            rows, width = ref.shape[0] // m, ref.shape[1] // n
            row = place * rows
            columns = at(i, width)
        if part is None:
            return ref.at[pl.ds(pl.multiple_of(row, rows), rows), columns]
        few = rows // 2
        return ref.at[pl.ds(pl.multiple_of(row + part * few, few), few), columns]

    def origin(s):
        return lax.rem(me - s + n, n)

    def deal(t, s):
        target = lax.rem(me + s, n)
        return remote(
            source(t, target), region(t, me, 0), deal_sent.at[t, s], deal_arrived.at[t, s],
            (target, col),
        )

    def keep(t):
        return pltpu.make_async_copy(source(t, me), region(t, me, 0), local.at[t])

    def pass_x(t, s):
        i = origin(s)
        return remote(
            region(t, i, 0), region(t, i, 1), x_sent.at[t, s], x_arrived.at[t, s], beside_x
        )

    def pass_y(t, s):
        i = origin(s)
        return remote(
            region(t, i, 0), region(t, i, 2), y_sent.at[t, s], y_arrived.at[t, s], beside_y
        )

    def pass_xy(t, s):
        i = origin(s)
        return remote(
            region(t, i, 1, 0), region(t, i, 3, 0), xy_sent.at[t, s], xy_arrived.at[t, s], beside_y
        )

    def pass_yx(t, s):
        i = origin(s)
        return remote(
            region(t, i, 2, 1), region(t, i, 3, 1), yx_sent.at[t, s], yx_arrived.at[t, s], beside_x
        )

    def pass_all(t, s, k):
        i = origin(s)
        slot = s * m + k
        return remote(
            region(t, i, 0), region(t, i, k), all_sent.at[t, slot], all_arrived.at[t, slot],
            (me, col ^ k),
        )

    def hand_on(t, s):
        if m == 4:
            pass_x(t, s).start()
            pass_y(t, s).start()
        else:
            for k in range(1, m):
                pass_all(t, s, k).start()

    def each(first, body):
        lax.fori_loop(first, n, lambda s, c: (body(s), c)[1], 0)

    def begin(t):
        keep(t).start()
        each(1, lambda s: deal(t, s).start())

    def arrive(t):
        keep(t).wait()
        hand_on(t, 0)

        def body(s):
            deal(t, s).wait_recv()
            hand_on(t, s)

        each(1, body)

    def relay(t):
        if m != 4:
            return

        def body(s):
            pass_x(t, s).wait_recv()
            pass_xy(t, s).start()
            pass_y(t, s).wait_recv()
            pass_yx(t, s).start()

        each(0, body)

    def finish(t):
        each(1, lambda s: deal(t, s).wait_send())

        def body(s):
            if m != 4:
                for k in range(1, m):
                    pass_all(t, s, k).wait()
                return
            pass_x(t, s).wait_send()
            pass_y(t, s).wait_send()
            pass_xy(t, s).wait()
            pass_yx(t, s).wait()

        each(0, body)

    lines = []
    for a in range(lines_count):
        ref = results[count + a]
        place = functools.partial(by_rows(ref.shape[0] // n), ref)
        lines.append(Line(sources[count + a], place, (line_sent, line_arrived, line_local), a))
    begin(0)
    begin(1)
    for t in range(count):
        arrive(t)
        if t + 2 < count:
            begin(t + 2)
        if t + 2 == count - 1:
            for line in lines:
                line.start()
        if t:
            relay(t - 1)
    relay(count - 1)
    for k in range(1, n // 2):
        for line in lines:
            line.step(k)
    for line in lines:
        line.finish()
    for t in range(count):
        finish(t)


def deal_all(weights, kinds, arrays, collective_id):
    n, m = lax.axis_size("dp"), lax.axis_size("mp")
    count, total = len(weights), len(weights) + len(arrays)
    shapes = []
    for w, kind in zip(weights, kinds):
        r, c = w.shape[-2:]
        if kind == 2:
            shapes.append((m,) + w.shape)
        else:
            shapes.append((n * r, m * (c // n)) if kind == 0 else (m * (r // n), n * c))
    shapes += [(n * a.shape[0], a.shape[1]) for a in arrays]
    pair = [pltpu.SemaphoreType.DMA((count, n))] * 2
    return pl.pallas_call(
        functools.partial(deal_kernel, n, m, kinds, len(arrays)),
        out_shape=[jax.ShapeDtypeStruct(s, BF) for s in shapes],
        in_specs=[HBM] * total,
        out_specs=[HBM] * total,
        scratch_shapes=pair
        + [pltpu.SemaphoreType.DMA((count,))]
        + pair * 4
        + [pltpu.SemaphoreType.DMA((count, n * m if m != 4 else 1))] * 2
        + line_sems(max(len(arrays), 1), n),
        compiler_params=pltpu.CompilerParams(collective_id=collective_id, has_side_effects=True),
        name="deal_all",
    )(*weights, *arrays)


def return_kernel(n, kinds, *refs):
    count = len(kinds)
    sources, results = refs[:count], refs[count : 2 * count]
    sent, arrived, local = refs[2 * count :]
    me, col = lax.axis_index("dp"), lax.axis_index("mp")
    greet(peers(n, 1))

    def source(t, i):
        ref = sources[t]
        if kinds[t] == 0:
            return ref.at[at(i, ref.shape[0] // n)]
        if kinds[t] == 1:
            return ref.at[:, at(i, ref.shape[1] // n)]
        return ref if kinds[t] == 3 else ref.at[i // 2 if kinds[t] == 2 else i]

    def place(t):
        ref = results[t]
        if kinds[t] == 0:
            return ref.at[:, at(me, ref.shape[1] // n)]
        if kinds[t] == 1:
            return ref.at[at(me, ref.shape[0] // n)]
        return ref.at[me // 2] if kinds[t] == 2 else ref.at[me]

    def move(t, s):
        target = lax.rem(me + s, n)
        return remote(
            source(t, target), place(t), sent.at[t, s], arrived.at[t, s], (target, col)
        )

    def keep(t):
        return pltpu.make_async_copy(source(t, me), place(t), local.at[t])

    def each(t, do):
        if kinds[t] == 2:
            lax.fori_loop(1, n // 2, lambda s, c: (do(t, 2 * s), c)[1], 0)
        else:
            lax.fori_loop(1, n, lambda s, c: (do(t, s), c)[1], 0)

    for t in range(count):
        keep(t).start()
        each(t, lambda t, s: move(t, s).start())
    for t in range(count):
        keep(t).wait()
        each(t, lambda t, s: move(t, s).wait())


def return_all(arrays, kinds, collective_id):
    n = lax.axis_size("dp")
    count = len(arrays)
    shapes = []
    for a, kind in zip(arrays, kinds):
        if kind == 0:
            shapes.append((a.shape[0] // n, a.shape[1] * n))
        elif kind == 1:
            shapes.append((a.shape[0] * n, a.shape[1] // n))
        else:
            shapes.append((n,) + a.shape if kind == 3 else a.shape)
    return pl.pallas_call(
        functools.partial(return_kernel, n, kinds),
        out_shape=[jax.ShapeDtypeStruct(s, a.dtype) for s, a in zip(shapes, arrays)],
        in_specs=[HBM] * count,
        out_specs=[HBM] * count,
        scratch_shapes=[
            pltpu.SemaphoreType.DMA((count, n)),
            pltpu.SemaphoreType.DMA((count, n)),
            pltpu.SemaphoreType.DMA((count,)),
        ],
        compiler_params=pltpu.CompilerParams(collective_id=collective_id, has_side_effects=True),
        name="return_all",
    )(*arrays)


def local(
    prefix_input,
    action_input,
    valid_dims,
    slot_item,
    segments,
    pre_gain_attn,
    pre_query,
    pre_key,
    pre_value,
    pre_output,
    pre_gain_ffn,
    pre_gate,
    pre_up,
    pre_down,
    act_embed,
    act_gain_attn,
    act_query,
    act_key,
    act_value,
    act_output,
    act_gain_ffn,
    act_gate,
    act_up,
    act_down,
    prefix_cotangent,
    action_cotangent,
):
    n, m = lax.axis_size("dp"), lax.axis_size("mp")
    me, col = lax.axis_index("dp"), lax.axis_index("mp")
    length, wide = prefix_input.shape
    slot_count, steps, dims_count = action_input.shape
    narrow = action_cotangent.shape[2]
    rq = round_up(-(-length // m), 16)
    aq = round_up(-(-steps // m), 16)
    rows, acts = m * rq, m * aq
    heads = pre_query.shape[1] // HD
    scale = HD ** (-0.5)
    kvw = 2 * HD // m

    d_pre, d_act = pre_query.shape[0], act_query.shape[0]
    lanes = 128

    def pad_rows(array, count):
        return jnp.pad(array, ((0, count - array.shape[0]), (0, 0)))

    def lane_rows(array):
        flat = array.reshape(-1)
        count = round_up(-(-flat.shape[0] // lanes), 16)
        return jnp.pad(flat, (0, count * lanes - flat.shape[0])).reshape(count, lanes)

    smalls = [pre_gain_attn, pre_gain_ffn, act_gain_attn, act_gain_ffn, act_embed, action_input]
    small = jnp.concatenate([lane_rows(a) for a in smalls], axis=0)
    ints = jnp.pad(jnp.stack([slot_item, valid_dims]), ((0, 6), (0, lanes - slot_count)))
    cot_rows = lax.dynamic_slice_in_dim(
        jnp.pad(action_cotangent, ((0, 0), (0, acts - steps), (0, 0))), col * aq, aq, 1
    ).reshape(slot_count * aq, narrow)

    def share_of(key, value):
        return lax.dynamic_slice_in_dim(
            jnp.concatenate([key, value], axis=1), col * kvw, kvw, 1
        )

    split = heads * HD
    small, ints, w_q_pre, w_q_act, w_kv_pre, w_kv_act, w_out_pre, w_out_act, cot_all = gather_all(
        [
            small,
            ints,
            pre_query,
            act_query,
            share_of(pre_key, pre_value),
            share_of(act_key, act_value),
            pre_output,
            act_output,
            cot_rows,
        ],
        [
            (n * small.shape[0], lanes),
            (n * 8, lanes),
            (wide, split),
            (narrow, split),
            (m, wide, kvw),
            (m, narrow, kvw),
            (split, wide),
            (n, split, d_act),
            (n * slot_count * aq, narrow),
        ],
        [
            by_rows(small.shape[0]),
            by_rows(8),
            by_rows(d_pre),
            by_rows(d_act),
            by_share(d_pre),
            by_share(d_act),
            by_columns(d_pre),
            by_lead,
            by_rows(slot_count * aq),
        ],
        (4, 5),
        1,
    )
    small = small.reshape(n, -1, lanes)
    smalls_all, begin = [], 0
    for a in smalls:
        count = round_up(-(-a.size // lanes), 16)
        flat = small[:, begin : begin + count].reshape(n, -1)[:, : a.size]
        smalls_all.append(flat.reshape((n,) + a.shape))
        begin += count
    gain_pa, gain_pf, gain_aa, gain_af = [g.reshape(-1).astype(F32) for g in smalls_all[:4]]
    embed = smalls_all[4].transpose(1, 0, 2).reshape(dims_count, narrow)
    act_all = smalls_all[5].reshape(n * slot_count, steps, dims_count)
    ints = ints.reshape(n, 8, lanes)
    slot_all = ints[:, 0, :slot_count].reshape(-1)
    valid_all = ints[:, 1, :slot_count].reshape(-1)
    cot_all = cot_all.reshape(n * slot_count, aq, narrow)
    w_out_act = w_out_act.transpose(1, 0, 2).reshape(split, narrow)
    w_in_pre = jnp.concatenate([w_q_pre] + [w_kv_pre[k] for k in range(m)], axis=1)
    w_in_act = jnp.concatenate([w_q_act] + [w_kv_act[k] for k in range(m)], axis=1)
    twice = wide // narrow

    def by_block(array):
        padded = jnp.pad(array, ((0, rows - length), (0, 0)))
        return own_order(padded.reshape(m, rq, array.shape[1]))

    x_blocks = by_block(prefix_input)
    gz_pre = by_block(prefix_cotangent)[0]
    seg = jnp.pad(segments[0], (0, rows - length), constant_values=1 << 20)
    seg = own_order(seg.reshape(m, rq)).reshape(rows)
    act_place = own_order(jnp.arange(acts, dtype=jnp.int32).reshape(m, aq)).reshape(acts)
    last = 1 << 10
    seg_q = jnp.concatenate([jnp.minimum(seg, last), jnp.full((acts,), last, jnp.int32)])
    seg_k = jnp.concatenate([seg, jnp.where(act_place < steps, last, 1 << 20)])
    allowed = seg_q[:, None] >= seg_k[None, :]

    mine = (slot_all == me).astype(F32)
    valid = jnp.sum(mine * valid_all.astype(F32))
    dims_mask = (lax.broadcasted_iota(jnp.int32, (1, dims_count), 1).astype(F32) < valid).astype(BF)
    act_in = jnp.sum(mine[:, None, None] * act_all.astype(F32), axis=0).astype(BF) * dims_mask
    act_in = own_order(
        jnp.pad(act_in, ((0, acts - steps), (0, 0))).reshape(m, aq, dims_count)
    ).reshape(acts, dims_count)

    x_pre = x_blocks.reshape(rows, wide).astype(F32)
    h1_pre = rms_gain(x_pre, gain_pa).astype(BF)
    x_act = dot_plain(act_in, embed)
    h1_act = rms_gain(x_act, gain_aa).astype(BF)

    in_pre = dot_plain(h1_pre, w_in_pre).astype(BF)
    in_act = dot_plain(h1_act, w_in_act).astype(BF)
    into_all = jnp.concatenate([in_pre, in_act], axis=0)
    query, kv_part = into_all[:, : heads * HD], into_all[:, heads * HD :]

    def reorder(array, s):
        if s == 0:
            return array
        pieces = [array[(r ^ s) * rq : (r ^ s) * rq + rq] for r in range(m)]
        pieces += [array[rows + (r ^ s) * aq : rows + (r ^ s) * aq + aq] for r in range(m)]
        return jnp.concatenate(pieces, axis=0)

    keys, values = kv_part[:, :HD], kv_part[:, HD:]

    probs, mixed = [], []
    for h in range(heads):
        scores = dot_right(query[:, h * HD : (h + 1) * HD], keys) * scale
        masked = jnp.where(allowed, scores, -1e30)
        top = jnp.max(masked, axis=-1, keepdims=True)
        raised = jnp.exp(masked - top)
        p = (raised / jnp.sum(raised, axis=-1, keepdims=True)).astype(BF)
        probs.append(p)
        mixed.append(dot_plain(p, values).astype(BF))
    mixed = jnp.concatenate(mixed, axis=1)

    def blocks_of(pre, act):
        return jnp.concatenate(
            [
                pack(pre[s * rq : (s + 1) * rq], act[s * aq : (s + 1) * aq])
                for s in range(m)
            ],
            axis=0,
        )

    def rows_of(blocks):
        pairs = [unpack(b, rq, narrow) for b in jnp.split(blocks, m, axis=0)]
        return jnp.concatenate([p[0] for p in pairs] + []), jnp.concatenate([p[1] for p in pairs])

    y_pre = dot_plain(mixed[:rows], w_out_pre).astype(BF)
    y_act = dot_plain(mixed[rows:], w_out_act).astype(BF)
    y = reduce_mp(blocks_of(y_pre, y_act), 0)
    y_pre, y_act = unpack(y, rq, narrow)
    x2_pre = x_pre[:rq] + y_pre
    x2_act = x_act[:aq] + y_act
    h2 = pack(rms_gain(x2_pre, gain_pf).astype(BF), rms_gain(x2_act, gain_af).astype(BF))


    def items_of(blocks):
        pairs = [unpack(b, rq, narrow) for b in jnp.split(blocks, n, axis=0)]
        return jnp.concatenate([p[0] for p in pairs]), jnp.concatenate([p[1] for p in pairs])

    def by_item(pre, act):
        return jnp.stack(
            [
                pack(pre[s * rq : (s + 1) * rq], act[s * aq : (s + 1) * aq])
                for s in range(n)
            ]
        )

    few = act_gate.shape[1] // n

    def columns_first(array):
        return array.reshape(array.shape[0], n, -1).transpose(1, 0, 2)

    act_weights = jnp.concatenate(
        [
            columns_first(act_gate),
            columns_first(act_up),
            act_down.reshape(n, few, d_act).transpose(0, 2, 1),
        ],
        axis=1,
    )
    wg, wu, wd, act_weights, h2_all, gz_pre_all = deal_all(
        [pre_gate, pre_up, pre_down, act_weights], (0, 0, 1, 2), [h2, gz_pre], 2
    )

    def square(array):
        return array.transpose(1, 2, 0, 3).reshape(narrow, m * few)

    ag, au = square(act_weights[:, :, :d_act]), square(act_weights[:, :, d_act : 2 * d_act])
    ad = square(act_weights[:, :, 2 * d_act :]).T
    h2_pre, h2_act = items_of(h2_all)
    match = (lax.broadcasted_iota(jnp.int32, (n, 1), 0) == slot_all[None, :]).astype(BF)
    gz_act_all = dot_plain(match, cot_all.reshape(cot_all.shape[0], -1)).astype(BF)
    gz_act_all = gz_act_all.reshape(n * aq, narrow)
    gz_act = lax.dynamic_slice_in_dim(gz_act_all, me * aq, aq, 0)

    def forward(h2_rows, gate_w, up_w, down_w):
        gate = dot_plain(h2_rows, gate_w)
        upward = dot_plain(h2_rows, up_w)
        hidden = glu_value(gate, upward).astype(BF)
        return gate.astype(BF), upward.astype(BF), hidden, dot_plain(hidden, down_w).astype(BF)

    def backward(h2_rows, gate, upward, hidden, gate_w, up_w, down_w, gz):
        grad_hidden = dot_right(gz, down_w)
        unused, pull = jax.vjp(glu_value, gate.astype(F32), upward.astype(F32))
        dgate, dup = pull(grad_hidden)
        dgate, dup = dgate.astype(BF), dup.astype(BF)
        dh2 = (dot_right(dgate, gate_w) + dot_right(dup, up_w)).astype(BF)
        return (
            dh2,
            dot_left(h2_rows, dgate).astype(BF),
            dot_left(h2_rows, dup).astype(BF),
            dot_left(hidden, gz).astype(BF),
        )

    gate_p, up_p, hid_p, z_p = forward(h2_pre, wg, wu, wd)
    gate_a, up_a, hid_a, z_a = forward(h2_act, ag, au, ad)
    dh2_p, g_gate_p, g_up_p, g_down_p = backward(
        h2_pre, gate_p, up_p, hid_p, wg, wu, wd, gz_pre_all
    )
    dh2_a, g_gate_a, g_up_a, g_down_a = backward(
        h2_act, gate_a, up_a, hid_a, ag, au, ad, gz_act_all
    )
    z_pre, z_act = unpack(reduce_dp(by_item(z_p, z_a)), rq, narrow)
    dh2_pre, dh2_act = unpack(reduce_dp(by_item(dh2_p, dh2_a)), rq, narrow)

    def natural(blocks, count):
        return jnp.concatenate([pick_mp(blocks, place) for place in range(m)], axis=0)[:count]

    out_pre = (x2_pre + z_pre).astype(BF)
    out_act = (x2_act + z_act).astype(BF)
    prefix_output = natural([out_pre] + [swap_mp(out_pre, s) for s in range(1, m)], length)
    out_act = natural([out_act] + [swap_mp(out_act, s) for s in range(1, m)], acts)

    gx2n_pre, g_gain_pf = norm_backward(x2_pre, gain_pf, dh2_pre)
    gx2n_act, g_gain_af = norm_backward(x2_act, gain_af, dh2_act)
    gx2_pre = gz_pre.astype(F32) + gx2n_pre
    gx2_act = gz_act.astype(F32) + gx2n_act
    gy = gather_mp(pack(gx2_pre.astype(BF), gx2_act.astype(BF)), 0)
    gy_pre, gy_act = rows_of(gy)

    g_out_pre = dot_left(mixed[:rows], gy_pre).astype(BF)
    g_out_act = dot_left(mixed[rows:], gy_act).astype(BF)
    gmix = jnp.concatenate(
        [dot_right(gy_pre, w_out_pre).astype(BF), dot_right(gy_act, w_out_act).astype(BF)], axis=0
    )
    gq, gk, gv = [], 0.0, 0.0
    for h in range(heads):
        cut = slice(h * HD, (h + 1) * HD)
        gm = gmix[:, cut]
        pe = probs[h].astype(F32)
        gp = dot_right(gm, values)
        ds = (pe * (gp - jnp.sum(pe * gp, axis=-1, keepdims=True))).astype(BF)
        gq.append((dot_plain(ds, keys) * scale).astype(BF))
        gk = gk + dot_left(ds, query[:, cut]) * scale
        gv = gv + dot_left(probs[h], gm)
    gkv = jnp.concatenate([gk, gv], axis=1).astype(BF)

    def share(s):
        return lax.dynamic_slice_in_dim(gkv, (col ^ s) * kvw, kvw, 1)

    gkv_sum = share(0).astype(F32)
    for s in range(1, m):
        gkv_sum = gkv_sum + reorder(swap_mp(share(s), s), s).astype(F32)
    gin = jnp.concatenate(gq + [gkv], axis=1)
    gh1_pre = dot_right(gin[:rows], w_in_pre).astype(BF)
    gh1_act = dot_right(gin[rows:], w_in_act).astype(BF)
    gh1 = reduce_mp(blocks_of(gh1_pre, gh1_act), 0)
    gh1_pre, gh1_act = unpack(gh1, rq, narrow)
    gin = jnp.concatenate(gq + [gkv_sum.astype(BF)], axis=1)
    g_in_pre = dot_left(h1_pre, gin[:rows]).astype(BF)
    g_in_act = dot_left(h1_act, gin[rows:]).astype(BF)

    gxn_pre, g_gain_pa = norm_backward(x_pre[:rq], gain_pa, gh1_pre)
    gxn_act, g_gain_aa = norm_backward(x_act[:aq], gain_aa, gh1_act)
    grad_pre = (gx2_pre + gxn_pre).astype(BF)
    prefix_grad = natural(
        [grad_pre] + [swap_mp(grad_pre, s) for s in range(1, m)], length
    ).astype(F32)
    gxa = (gx2_act + gxn_act).astype(BF)
    g_embed = dot_left(act_in[:aq], gxa)
    act_grad = dot_right(gxa, embed)
    act_grad = natural([act_grad] + [swap_mp(act_grad, s) for s in range(1, m)], acts)

    def by_index(vector):
        return vector.reshape(n, -1, narrow // n).transpose(1, 0, 2).reshape(-1, narrow)

    tiny = jnp.concatenate(
        [
            by_index(g_gain_pa),
            by_index(g_gain_pf),
            by_index(g_gain_aa),
            by_index(g_gain_af),
            g_embed,
        ],
        axis=0,
    )
    tiny_rows = tiny.shape[0]
    tiny = columns_first(pad_rows(tiny, round_up(tiny_rows, 8)))
    tiny_sum = tiny
    for s in range(1, m):
        tiny_sum = tiny_sum + swap_mp(tiny, s)
    act_grad, out_act, tiny = return_all(
        [jnp.pad(act_grad, ((0, 0), (0, lanes - dims_count))), out_act, tiny_sum], (3, 3, 4), 4
    )
    mine_items = (slot_item[:, None] == lax.broadcasted_iota(jnp.int32, (1, n), 1)).astype(BF)
    action_output = dot_plain(mine_items, out_act[:, :steps].reshape(n, steps * narrow))
    action_output = action_output.astype(BF).reshape(slot_count, steps, narrow)
    own_mask = lax.broadcasted_iota(jnp.int32, (slot_count, dims_count), 1) < valid_dims[:, None]
    action_grad = jnp.sum(
        mine_items.astype(F32)[:, :, None, None] * act_grad[None, :, :steps, :dims_count], axis=1
    ) * own_mask.astype(F32)[:, None, :]
    tiny = jnp.sum(tiny, axis=0)
    grad_gain_pa = tiny[:twice].reshape(-1)
    grad_gain_pf = tiny[twice : 2 * twice].reshape(-1)
    rest = tiny[2 * twice : tiny_rows]

    def attn_block(item):
        left = lax.slice_in_dim(g_in_pre, item * d_pre, (item + 1) * d_pre, axis=0)
        out = lax.slice_in_dim(g_out_pre, item * d_pre, (item + 1) * d_pre, axis=1)
        left_a = lax.slice_in_dim(g_in_act, item * d_act, (item + 1) * d_act, axis=0)
        out_a = lax.slice_in_dim(g_out_act, item * d_act, (item + 1) * d_act, axis=1)
        top = jnp.concatenate([left] + jnp.split(out, out.shape[0] // d_pre, axis=0), axis=1)
        low = jnp.concatenate([left_a] + jnp.split(out_a, out_a.shape[0] // d_act, axis=0), axis=1)
        return jnp.concatenate([top, low], axis=0)

    act_back = jnp.concatenate(
        [
            g_gate_a.reshape(n, d_act, m * few),
            g_up_a.reshape(n, d_act, m * few),
            g_down_a.T.reshape(n, d_act, m * few),
        ],
        axis=1,
    )
    act_back = reduce_mp(act_back, 2).astype(BF)
    parts = pair_sum(jnp.stack([attn_block(i) for i in range(n)]))
    returned = return_all(
        [
            reduce_mp(g_down_p, 0).astype(BF),
            reduce_mp(g_gate_p, 1).astype(BF),
            reduce_mp(g_up_p, 1).astype(BF),
            act_back,
            parts,
        ],
        (1, 0, 0, 4, 2),
        3,
    )
    grad_down, grad_gate, grad_up, act_back = [g.astype(F32) for g in returned[:4]]
    grad_gate_a = act_back[:, :d_act].transpose(1, 0, 2).reshape(d_act, n * few)
    grad_up_a = act_back[:, d_act : 2 * d_act].transpose(1, 0, 2).reshape(d_act, n * few)
    grad_down_a = act_back[:, 2 * d_act :].transpose(0, 2, 1).reshape(n * few, d_act)
    total = jnp.sum(returned[4].astype(F32), axis=0)
    grad_query, grad_kv = total[:d_pre, :split], total[:d_pre, split : split + kvw]
    grad_out = jnp.concatenate(
        jnp.split(total[:d_pre, split + kvw :], split // d_pre, axis=1), axis=0
    )
    grad_query_a, grad_kv_a = total[d_pre:, :split], total[d_pre:, split : split + kvw]
    grad_out_a = jnp.concatenate(
        jnp.split(total[d_pre:, split + kvw :], split // d_act, axis=1), axis=0
    )
    both = jnp.concatenate([grad_kv, grad_kv_a], axis=0).astype(BF)
    both = [both] + [swap_mp(both, s) for s in range(1, m)]
    both = jnp.concatenate([pick_mp(both, place) for place in range(m)], axis=1).astype(F32)

    return (
        prefix_output,
        action_output,
        prefix_grad,
        action_grad,
        grad_gain_pa,
        grad_query,
        both[:d_pre, :HD],
        both[:d_pre, HD:],
        grad_out,
        grad_gain_pf,
        grad_gate,
        grad_up,
        grad_down,
        rest[2:],
        rest[0],
        grad_query_a,
        both[d_pre:, :HD],
        both[d_pre:, HD:],
        grad_out_a,
        rest[1],
        grad_gate_a,
        grad_up_a,
        grad_down_a,
    )


def solution(mesh):
    return jax.shard_map(
        local,
        mesh=mesh,
        in_specs=(
            P("dp", None),
            P("dp", None, None),
            P("dp"),
            P("dp"),
            P("dp", None),
            P("dp"),
            P("dp", "mp"),
            P("dp", None),
            P("dp", None),
            P("mp", "dp"),
            P("dp"),
            P("dp", "mp"),
            P("dp", "mp"),
            P("mp", "dp"),
            P(None, "dp"),
            P("dp"),
            P("dp", "mp"),
            P("dp", None),
            P("dp", None),
            P("mp", "dp"),
            P("dp"),
            P("dp", "mp"),
            P("dp", "mp"),
            P("mp", "dp"),
            P("dp", None),
            P("dp", None, None),
        ),
        out_specs=(
            P("dp", None),
            P("dp", None, None),
            P("dp", None),
            P("dp", None, None),
            P("dp"),
            P("dp", "mp"),
            P("dp", None),
            P("dp", None),
            P("mp", "dp"),
            P("dp"),
            P("dp", "mp"),
            P("dp", "mp"),
            P("mp", "dp"),
            P(None, "dp"),
            P("dp"),
            P("dp", "mp"),
            P("dp", None),
            P("dp", None),
            P("mp", "dp"),
            P("dp"),
            P("dp", "mp"),
            P("dp", "mp"),
            P("mp", "dp"),
        ),
        check_vma=False,
    )
```

```python
import functools

import jax
import jax.numpy as jnp
from jax import lax
from jax.experimental import pallas as pl
from jax.experimental.pallas import tpu as pltpu
from jax.sharding import PartitionSpec as P

HD = 256
EPS = 1e-06
BF = jnp.bfloat16
F32 = jnp.float32


def rms_gain(values, gain):
    return values * lax.rsqrt(jnp.mean(values * values, axis=-1, keepdims=True) + EPS) * gain


def norm_backward(values, gain, grad_out):
    unused, pull = jax.vjp(rms_gain, values, gain)
    return pull(grad_out)


def glu_value(gate, upward):
    return jax.nn.gelu(gate, approximate=True) * upward


def dot_plain(left, right):
    return jnp.dot(left, right, preferred_element_type=F32)


def dot_left(left, right):
    return lax.dot_general(left, right, (((0,), (0,)), ((), ())), preferred_element_type=F32)


def dot_right(left, right):
    return lax.dot_general(left, right, (((1,), (1,)), ((), ())), preferred_element_type=F32)


def round_up(value, step):
    return -(-value // step) * step


def swap_mp(block, step):
    size = lax.axis_size("mp")
    return lax.ppermute(block, "mp", [(i, i ^ step) for i in range(size)])


def swap_core(block):
    size = lax.axis_size("dp")
    return lax.ppermute(block, "dp", [(i, i ^ 1) for i in range(size)])


def send_dp(block, step):
    size = lax.axis_size("dp")
    return lax.ppermute(block, "dp", [(i, (i + step) % size) for i in range(size)])


def pair_sum(parts):
    half = parts.shape[0] // 2
    return add(parts[:half], swap_core(parts[half:]))


def gather_dp(block):
    half = lax.axis_size("dp") // 2
    same = jnp.stack([block] + [send_dp(block, -2 * s) for s in range(1, half)])
    return jnp.concatenate([same, swap_core(same)], axis=0)


def reduce_dp(parts):
    both = pair_sum(parts)
    total = both[0].astype(F32)
    for s in range(1, both.shape[0]):
        total = total + send_dp(both[s], 2 * s).astype(F32)
    return total


def gather_mp(block, axis):
    size = lax.axis_size("mp")
    return jnp.concatenate([block] + [swap_mp(block, s) for s in range(1, size)], axis=axis)


def reduce_mp(matrix, axis):
    size = lax.axis_size("mp")
    parts = jnp.split(matrix, size, axis=axis)
    total = parts[0].astype(F32)
    for s in range(1, size):
        total = total + swap_mp(parts[s].astype(BF), s).astype(F32)
    return total


def pick_mp(blocks, place):
    at = lax.axis_index("mp") ^ place
    block = blocks[0]
    for s in range(1, len(blocks)):
        block = jnp.where(at == s, blocks[s], block)
    return block


def own_order(array):
    col = lax.axis_index("mp")
    return jnp.stack(
        [lax.dynamic_index_in_dim(array, col ^ s, 0, False) for s in range(array.shape[0])]
    )


def pack(prefix, action):
    wider = ((0, 0), (0, prefix.shape[1] - action.shape[1]))
    return jnp.concatenate([prefix, jnp.pad(action, wider)], axis=0)


def unpack(block, rows, width):
    return block[:rows], block[rows:, :width]


MESH = pl.DeviceIdType.MESH
HBM = pl.BlockSpec(memory_space=pl.ANY)


def peers(n, m):
    me, col = lax.axis_index("dp"), lax.axis_index("mp")
    column = [(lax.rem(me + s, n), col) for s in range(1, n)]
    return column + [(me, col ^ s) for s in range(1, m)]


def greet(devices):
    barrier = pltpu.get_barrier_semaphore()
    for device in devices:
        pl.semaphore_signal(barrier, inc=1, device_id=device, device_id_type=MESH)
    pl.semaphore_wait(barrier, len(devices))


def remote(src, dst, sent, arrived, device):
    return pltpu.make_async_remote_copy(
        src_ref=src,
        dst_ref=dst,
        send_sem=sent,
        recv_sem=arrived,
        device_id=device,
        device_id_type=MESH,
    )


def at(start, size):
    return pl.ds(pl.multiple_of(start * size, size), size)


class Line:
    def __init__(self, own, place, sems, row, pass_on=None):
        self.n = lax.axis_size("dp")
        self.me, self.col = lax.axis_index("dp"), lax.axis_index("mp")
        self.own, self.place, self.row = own, place, row
        self.sent, self.arrived, self.local = sems
        self.chips = self.n // 2
        self.chip = self.me // 2
        self.pass_on = pass_on

    def copy(self, way, k):
        step = (2, -2)[way]
        origin = lax.rem(self.me - step * (k - 1) + 2 * self.n, self.n)
        source = self.own if k == 1 else self.place(origin, self.me)
        target = lax.rem(self.me + step + self.n, self.n)
        slot = way * self.chips + k
        return remote(
            source,
            self.place(origin, target),
            self.sent.at[self.row, slot],
            self.arrived.at[self.row, slot],
            (target, self.col),
        )

    def across(self, way, k):
        step = (2, -2)[way]
        origin = lax.rem(self.me - step * k + 2 * self.n, self.n)
        source = self.own if k == 0 else self.place(origin, self.me)
        slot = (2 + way) * self.chips + k
        target = self.me ^ 1
        return remote(
            source,
            self.place(origin, target),
            self.sent.at[self.row, slot],
            self.arrived.at[self.row, slot],
            (target, self.col),
        )

    def sends(self, way, k):
        beyond = self.chip < self.chips - 1 if way == 0 else self.chip > 0
        return beyond & self.receives(way, k - 1)

    def receives(self, way, k):
        if k == 0:
            return self.chip >= 0
        return self.chip >= k if way == 0 else self.chip < self.chips - k

    def start(self):
        self.keep = pltpu.make_async_copy(
            self.own, self.place(self.me, self.me), self.local.at[self.row]
        )
        self.keep.start()
        for way in (0, 1):
            pl.when(self.sends(way, 1))(self.copy(way, 1).start)
        self.across(0, 0).start()

    def step(self, k):
        for way in (0, 1):

            @pl.when(self.receives(way, k))
            def _(way=way):
                self.copy(way, k).wait_recv()
                self.across(way, k).start()

            if k < self.chips - 1:
                pl.when(self.sends(way, k + 1))(self.copy(way, k + 1).start)
        if self.pass_on is not None:
            self.hand_on(k)

    def crossed(self, way, k):
        self.across(way, k).wait_recv()
        if self.pass_on is not None:
            self.pass_on(lax.rem((self.me ^ 1) - (2, -2)[way] * k + 2 * self.n, self.n))

    def hand_on(self, k):
        if k == 1:
            self.keep.wait()
            self.pass_on(self.me)
            self.crossed(0, 0)
        for way in (0, 1):

            @pl.when(self.receives(way, k))
            def _(way=way):
                self.pass_on(lax.rem(self.me - (2, -2)[way] * k + 2 * self.n, self.n))

            if k > 1:
                pl.when(self.receives(way, k - 1))(functools.partial(self.crossed, way, k - 1))

    def finish(self):
        passing = self.pass_on is not None
        if passing:
            for way in (0, 1):
                k = self.chips - 1
                pl.when(self.receives(way, k))(functools.partial(self.crossed, way, k))
        else:
            self.keep.wait()
        last = self.across(0, 0)
        (last.wait_send if passing else last.wait)()
        for way in (0, 1):
            for k in range(1, self.chips):
                pl.when(self.sends(way, k))(self.copy(way, k).wait_send)
                last = self.across(way, k)
                pl.when(self.receives(way, k))(last.wait_send if passing else last.wait)


def line_sems(count, n):
    return [
        pltpu.SemaphoreType.DMA((count, 2 * n)),
        pltpu.SemaphoreType.DMA((count, 2 * n)),
        pltpu.SemaphoreType.DMA((count,)),
    ]


def gather_kernel(n, m, count, places, shares, *refs):
    sources, results = refs[:count], refs[count : 2 * count]
    sent, arrived, local, share_sent, share_arrived = refs[2 * count :]
    me, col = lax.axis_index("dp"), lax.axis_index("mp")
    greet(peers(n, m))

    def passed(a, i, k):
        block = places[a](results[a], i, me)
        slot = i * m + k
        x = shares.index(a)
        return remote(
            block, block, share_sent.at[x, slot], share_arrived.at[x, slot], (me, col ^ k)
        )

    def pass_on(a, i):
        for k in range(1, m):
            passed(a, i, k).start()

    lines = []
    for a in range(count):
        place = functools.partial(places[a], results[a])
        hook = functools.partial(pass_on, a) if a in shares else None
        lines.append(Line(sources[a], place, (sent, arrived, local), a, hook))
        lines[-1].start()
    for k in range(1, n // 2):
        for line in lines:
            line.step(k)
    for line in lines:
        line.finish()
    for a in shares:

        def body(i, carry, a=a):
            for k in range(1, m):
                passed(a, i, k).wait()
            return carry

        lax.fori_loop(0, n, body, 0)


def gather_all(arrays, shapes, places, shares, collective_id):
    n, m = lax.axis_size("dp"), lax.axis_size("mp")
    count = len(arrays)
    return pl.pallas_call(
        functools.partial(gather_kernel, n, m, count, places, shares),
        out_shape=[jax.ShapeDtypeStruct(s, a.dtype) for s, a in zip(shapes, arrays)],
        in_specs=[HBM] * count,
        out_specs=[HBM] * count,
        scratch_shapes=line_sems(count, n)
        + [pltpu.SemaphoreType.DMA((max(len(shares), 1), n * m))] * 2,
        compiler_params=pltpu.CompilerParams(collective_id=collective_id, has_side_effects=True),
        name="gather_all",
    )(*arrays)


def by_rows(size):
    return lambda ref, i, j: ref.at[at(i, size)]


def by_columns(size):
    return lambda ref, i, j: ref.at[:, at(i, size)]


def by_lead(ref, i, j):
    return ref.at[i]


def in_turn(ref, i, j):
    chips = lax.axis_size("dp") // 2
    chip = lax.rem(i // 2 - j // 2 + chips, chips)
    return ref.at[chip + chips * lax.rem(i + j, 2)]


def by_share(size):
    return lambda ref, i, j: ref.at[lax.axis_index("mp"), at(i, size)]


def deal_kernel(n, m, kinds, lines_count, *refs):
    count = len(kinds)
    total = count + lines_count
    sources, results = refs[:total], refs[total : 2 * total]
    sems = refs[2 * total :]
    deal_sent, deal_arrived, local = sems[:3]
    x_sent, x_arrived, y_sent, y_arrived = sems[3:7]
    xy_sent, xy_arrived, yx_sent, yx_arrived = sems[7:11]
    all_sent, all_arrived = sems[11:13]
    line_sent, line_arrived, line_local = sems[13:16]
    me, col = lax.axis_index("dp"), lax.axis_index("mp")
    greet(peers(n, m))
    beside_x, beside_y = (me, col ^ 1), (me, col ^ 2)

    def source(t, i):
        ref = sources[t]
        if kinds[t] == 2:
            return ref.at[i]
        if kinds[t] == 0:
            return ref.at[:, at(i, ref.shape[1] // n)]
        return ref.at[at(i, ref.shape[0] // n)]

    def region(t, i, place, part=None):
        ref = results[t]
        if kinds[t] == 2:
            if part is None:
                return ref.at[place, i]
            few = ref.shape[2] // 2
            return ref.at[place, i, pl.ds(part * few, few)]
        if kinds[t] == 0:
            rows, width = ref.shape[0] // n, ref.shape[1] // m
            row = i * rows
            columns = pl.ds(place * width, width)
        else:
            rows, width = ref.shape[0] // m, ref.shape[1] // n
            row = place * rows
            columns = at(i, width)
        if part is None:
            return ref.at[pl.ds(pl.multiple_of(row, rows), rows), columns]
        few = rows // 2
        return ref.at[pl.ds(pl.multiple_of(row + part * few, few), few), columns]

    def origin(s):
        return lax.rem(me - s + n, n)

    def deal(t, s):
        target = lax.rem(me + s, n)
        return remote(
            source(t, target), region(t, me, 0), deal_sent.at[t, s], deal_arrived.at[t, s],
            (target, col),
        )

    def keep(t):
        return pltpu.make_async_copy(source(t, me), region(t, me, 0), local.at[t])

    def pass_x(t, s):
        i = origin(s)
        return remote(
            region(t, i, 0), region(t, i, 1), x_sent.at[t, s], x_arrived.at[t, s], beside_x
        )

    def pass_y(t, s):
        i = origin(s)
        return remote(
            region(t, i, 0), region(t, i, 2), y_sent.at[t, s], y_arrived.at[t, s], beside_y
        )

    def pass_xy(t, s):
        i = origin(s)
        return remote(
            region(t, i, 1, 0), region(t, i, 3, 0), xy_sent.at[t, s], xy_arrived.at[t, s], beside_y
        )

    def pass_yx(t, s):
        i = origin(s)
        return remote(
            region(t, i, 2, 1), region(t, i, 3, 1), yx_sent.at[t, s], yx_arrived.at[t, s], beside_x
        )

    def pass_all(t, s, k):
        i = origin(s)
        slot = s * m + k
        return remote(
            region(t, i, 0), region(t, i, k), all_sent.at[t, slot], all_arrived.at[t, slot],
            (me, col ^ k),
        )

    def hand_on(t, s):
        if m == 4:
            pass_x(t, s).start()
            pass_y(t, s).start()
        else:
            for k in range(1, m):
                pass_all(t, s, k).start()

    def each(first, body):
        lax.fori_loop(first, n, lambda s, c: (body(s), c)[1], 0)

    def begin(t):
        keep(t).start()
        each(1, lambda s: deal(t, s).start())

    def arrive(t):
        keep(t).wait()
        hand_on(t, 0)

        def body(s):
            deal(t, s).wait_recv()
            hand_on(t, s)

        each(1, body)

    def relay(t):
        if m != 4:
            return

        def body(s):
            pass_x(t, s).wait_recv()
            pass_xy(t, s).start()
            pass_y(t, s).wait_recv()
            pass_yx(t, s).start()

        each(0, body)

    def finish(t):
        each(1, lambda s: deal(t, s).wait_send())

        def body(s):
            if m != 4:
                for k in range(1, m):
                    pass_all(t, s, k).wait()
                return
            pass_x(t, s).wait_send()
            pass_y(t, s).wait_send()
            pass_xy(t, s).wait()
            pass_yx(t, s).wait()

        each(0, body)

    lines = []
    for a in range(lines_count):
        ref = results[count + a]
        place = functools.partial(in_turn, ref)
        lines.append(Line(sources[count + a], place, (line_sent, line_arrived, line_local), a))
    begin(0)
    begin(1)
    for t in range(count):
        arrive(t)
        if t + 2 < count:
            begin(t + 2)
        if t + 2 == count - 1:
            for line in lines:
                line.start()
        if t:
            relay(t - 1)
    relay(count - 1)
    for k in range(1, n // 2):
        for line in lines:
            line.step(k)
    for line in lines:
        line.finish()
    for t in range(count):
        finish(t)


def deal_all(weights, kinds, arrays, collective_id):
    n, m = lax.axis_size("dp"), lax.axis_size("mp")
    count, total = len(weights), len(weights) + len(arrays)
    shapes = []
    for w, kind in zip(weights, kinds):
        r, c = w.shape[-2:]
        if kind == 2:
            shapes.append((m,) + w.shape)
        else:
            shapes.append((n * r, m * (c // n)) if kind == 0 else (m * (r // n), n * c))
    shapes += [(n,) + a.shape for a in arrays]
    pair = [pltpu.SemaphoreType.DMA((count, n))] * 2
    return pl.pallas_call(
        functools.partial(deal_kernel, n, m, kinds, len(arrays)),
        out_shape=[jax.ShapeDtypeStruct(s, BF) for s in shapes],
        in_specs=[HBM] * total,
        out_specs=[HBM] * total,
        scratch_shapes=pair
        + [pltpu.SemaphoreType.DMA((count,))]
        + pair * 4
        + [pltpu.SemaphoreType.DMA((count, n * m if m != 4 else 1))] * 2
        + line_sems(max(len(arrays), 1), n),
        compiler_params=pltpu.CompilerParams(collective_id=collective_id, has_side_effects=True),
        name="deal_all",
    )(*weights, *arrays)


ROWS = 0
COLUMNS = 1
CHIPS = 2
PARTS = 3
WHOLE = 4
SWAP_X = 5
SWAP_Y = 6
HALVES_0 = 10
HALVES_1 = 11
WORLD = 7
SPREAD = 8
EACH = 9

KEPT = (ROWS, COLUMNS, EACH, WORLD, SPREAD)


def exchange_kernel(n, m, kinds, jobs, *refs):
    count = len(kinds)
    takes, gives = sum(j.takes for j in jobs), sum(j.gives for j in jobs)
    sources, given = refs[:count], refs[count : count + takes]
    results, made = refs[count + takes : 2 * count + takes], refs[2 * count + takes :][:gives]
    sent, arrived, local = refs[2 * count + takes + gives :]
    me, col = lax.axis_index("dp"), lax.axis_index("mp")
    world = any(kind in (WORLD, SPREAD) for kind in kinds)
    over_dp = any(kind in (ROWS, COLUMNS, CHIPS, EACH) for kind in kinds)
    over_mp = any(kind in (PARTS, WHOLE, SWAP_X, SWAP_Y, HALVES_0, HALVES_1) for kind in kinds)
    if world:
        greet([(lax.rem(me + s, n), col ^ k) for s in range(n) for k in range(m) if s or k])
    else:
        greet(peers(n if over_dp else 1, m if over_mp else 1))

    def move(t, s, k=0):
        kind, src, dst = kinds[t], sources[t], results[t]
        target, slot = (lax.rem(me + s, n), col), s
        if kind == ROWS:
            src = src.at[at(target[0], src.shape[0] // n)]
            dst = dst.at[:, at(me, dst.shape[1] // n)]
        elif kind == COLUMNS:
            src = src.at[:, at(target[0], src.shape[1] // n)]
            dst = dst.at[at(me, dst.shape[0] // n)]
        elif kind == EACH:
            src, dst = src.at[target[0]], dst.at[me]
        elif kind == CHIPS:
            target = (lax.rem(me + 2 * s, n), col)
            src, dst = src.at[s], dst.at[s]
        elif kind == PARTS:
            target, slot, src, dst = (me, col ^ k), k, src.at[k], dst.at[k]
        elif kind == WHOLE:
            target, slot, dst = (me, col ^ k), k, dst.at[k]
        elif kind in (SWAP_X, SWAP_Y):
            target, slot = (me, col ^ k), 0
        elif kind in (HALVES_0, HALVES_1):
            target, slot, dst = (me, col ^ (1 + k // 2)), k, dst.at[k]
            axis = kind - HALVES_0
            width, deep = src.shape[axis] // m, src.shape[1 - axis] // 2
            block = pl.ds((1, 3, 2, 3)[k] * width, width)
            half = pl.ds(k // 2 * deep, deep)
            src = src.at[half, block] if axis else src.at[block, half]
        else:
            target, slot = (target[0], col ^ k), s * m + k
            src = src if kind == WORLD else src.at[target[0]]
            dst = dst.at[me, col]
        return remote(src, dst, sent.at[t, slot], arrived.at[t, slot], target)

    def keep(t):
        kind, src, dst = kinds[t], sources[t], results[t]
        if kind == ROWS:
            src, dst = src.at[at(me, src.shape[0] // n)], dst.at[:, at(me, dst.shape[1] // n)]
        elif kind == COLUMNS:
            src, dst = src.at[:, at(me, src.shape[1] // n)], dst.at[at(me, dst.shape[0] // n)]
        elif kind == EACH:
            src, dst = src.at[me], dst.at[me]
        elif kind in (WORLD, SPREAD):
            src, dst = src if kind == WORLD else src.at[me], dst.at[me, col]
        return pltpu.make_async_copy(src, dst, local.at[t])

    def each(t, do):
        kind = kinds[t]
        if kind in (ROWS, COLUMNS, EACH):
            lax.fori_loop(1, n, lambda s, c: (do(move(t, s)), c)[1], 0)
        elif kind == CHIPS:
            lax.fori_loop(1, n // 2, lambda s, c: (do(move(t, s)), c)[1], 0)
        elif kind in (PARTS, WHOLE):
            for k in range(1, m):
                do(move(t, 0, k))
        elif kind in (SWAP_X, SWAP_Y):
            do(move(t, 0, 1 if kind == SWAP_X else 2))
        elif kind in (HALVES_0, HALVES_1):
            for k in range(4):
                do(move(t, 0, k))
        else:
            for k in range(m):
                lax.fori_loop(0 if k else 1, n, lambda s, c, k=k: (do(move(t, s, k)), c)[1], 0)

    for t in range(count):
        if kinds[t] in KEPT:
            keep(t).start()
        each(t, lambda c: c.start())
    for job in jobs:
        job.run(given[: job.takes], made[: job.gives])
        given, made = given[job.takes :], made[job.gives :]
    for t in range(count):
        if kinds[t] in KEPT:
            keep(t).wait()
        each(t, lambda c: c.wait())


def exchange_all(flows, collective_id, jobs=()):
    n, m = lax.axis_size("dp"), lax.axis_size("mp")
    arrays, kinds = [f[0] for f in flows], tuple(f[1] for f in flows)
    count = len(flows)
    shapes = []
    for a, kind in flows:
        if kind == ROWS:
            shapes.append((a.shape[0] // n, a.shape[1] * n))
        elif kind == COLUMNS:
            shapes.append((a.shape[0] * n, a.shape[1] // n))
        elif kind == WHOLE:
            shapes.append((m,) + a.shape)
        elif kind == WORLD:
            shapes.append((n, m) + a.shape)
        elif kind == SPREAD:
            shapes.append((n, m) + a.shape[1:])
        elif kind == HALVES_0:
            shapes.append((4, a.shape[0] // m, a.shape[1] // 2))
        elif kind == HALVES_1:
            shapes.append((4, a.shape[0] // 2, a.shape[1] // m))
        else:
            shapes.append(a.shape)
    inputs = [a for job in jobs for a in job.arrays]
    outputs = [jax.ShapeDtypeStruct(s, BF) for job in jobs for s in job.shapes]
    return pl.pallas_call(
        functools.partial(exchange_kernel, n, m, kinds, [job.bare() for job in jobs]),
        out_shape=[jax.ShapeDtypeStruct(s, a.dtype) for s, a in zip(shapes, arrays)] + outputs,
        in_specs=[HBM] * (count + len(inputs)),
        out_specs=[HBM] * (count + len(outputs)),
        scratch_shapes=[
            pltpu.SemaphoreType.DMA((max(count, 1), n * m)),
            pltpu.SemaphoreType.DMA((max(count, 1), n * m)),
            pltpu.SemaphoreType.DMA((max(count, 1),)),
        ],
        compiler_params=pltpu.CompilerParams(
            collective_id=collective_id, has_side_effects=True, vmem_limit_bytes=56 << 20
        ),
        name="exchange",
    )(*arrays, *inputs)


class Job:
    def __init__(self, body, arrays, shapes):
        self.body, self.arrays, self.shapes = body, arrays, shapes
        self.takes, self.gives = len(arrays), len(shapes)

    def bare(self):
        job = Job(self.body, (), self.shapes)
        job.takes = self.takes
        return job

    def run(self, inputs, outputs):
        self.body(inputs, outputs)


def tile(size, most):
    return max(t for t in range(16, most + 1, 16) if size % t == 0)


def products_plain(inputs, outputs):
    a, b = inputs
    (rows, depth), width = a.shape, b.shape[1]
    bm, bn = tile(rows, 416), tile(width, 512)

    def body(a_ref, b_ref, o_ref):
        o_ref[...] = dot_plain(a_ref[...], b_ref[...]).astype(BF)

    pltpu.emit_pipeline(
        body,
        grid=(width // bn, rows // bm),
        in_specs=[
            pl.BlockSpec((bm, depth), lambda j, i: (i, 0)),
            pl.BlockSpec((depth, bn), lambda j, i: (0, j)),
        ],
        out_specs=[pl.BlockSpec((bm, bn), lambda j, i: (i, j))],
    )(a, b, outputs[0])


def products_right(inputs, outputs):
    pairs = len(inputs) // 2
    (rows, depth), width = inputs[0].shape, inputs[1].shape[0]
    bm, bn = tile(rows, 416), tile(width, 512)

    def body(*refs):
        total = dot_right(refs[0][...], refs[1][...])
        for p in range(1, pairs):
            total = total + dot_right(refs[2 * p][...], refs[2 * p + 1][...])
        refs[-1][...] = total.astype(BF)

    pltpu.emit_pipeline(
        body,
        grid=(width // bn, rows // bm),
        in_specs=[
            pl.BlockSpec((bm, depth), lambda j, i: (i, 0)),
            pl.BlockSpec((bn, depth), lambda j, i: (j, 0)),
        ]
        * pairs,
        out_specs=[pl.BlockSpec((bm, bn), lambda j, i: (i, j))],
    )(*inputs, outputs[0])


def products_left(inputs, outputs):
    a, rest = inputs[0], inputs[1:]
    (depth, rows), width = a.shape, rest[0].shape[1]
    bm, bn = tile(rows, 1024), tile(width, 512)
    count = len(rest)

    def body(a_ref, *refs):
        for p in range(count):
            refs[count + p][...] = dot_left(a_ref[...], refs[p][...]).astype(BF)

    pltpu.emit_pipeline(
        body,
        grid=(rows // bm, width // bn),
        in_specs=[pl.BlockSpec((depth, bm), lambda i, j: (0, i))]
        + [pl.BlockSpec((depth, bn), lambda i, j: (0, j))] * count,
        out_specs=[pl.BlockSpec((bm, bn), lambda i, j: (i, j))] * count,
    )(a, *rest, *outputs)


def hidden_forward(inputs, outputs):
    h, w_gate, w_up = inputs
    (rows, depth), width = h.shape, w_gate.shape[1]
    bm, bn = tile(rows, 416), tile(width, 512)

    def body(h_ref, gate_w, up_w, gate_ref, up_ref, hidden_ref):
        gate = dot_plain(h_ref[...], gate_w[...])
        upward = dot_plain(h_ref[...], up_w[...])
        gate_ref[...] = gate.astype(BF)
        up_ref[...] = upward.astype(BF)
        hidden_ref[...] = glu_value(gate, upward).astype(BF)

    block = pl.BlockSpec((bm, bn), lambda j, i: (i, j))
    pltpu.emit_pipeline(
        body,
        grid=(width // bn, rows // bm),
        in_specs=[pl.BlockSpec((bm, depth), lambda j, i: (i, 0))]
        + [pl.BlockSpec((depth, bn), lambda j, i: (0, j))] * 2,
        out_specs=[block] * 3,
    )(h, w_gate, w_up, *outputs)


def hidden_backward(inputs, outputs):
    gz, w_down, gate, upward = inputs
    (rows, depth), width = gz.shape, w_down.shape[0]
    bm, bn = tile(rows, 416), tile(width, 512)

    def body(gz_ref, down_w, gate_ref, up_ref, dgate_ref, dup_ref):
        grad = dot_right(gz_ref[...], down_w[...])
        unused, pull = jax.vjp(
            glu_value, gate_ref[...].astype(F32), up_ref[...].astype(F32)
        )
        dgate, dup = pull(grad)
        dgate_ref[...] = dgate.astype(BF)
        dup_ref[...] = dup.astype(BF)

    block = pl.BlockSpec((bm, bn), lambda j, i: (i, j))
    pltpu.emit_pipeline(
        body,
        grid=(width // bn, rows // bm),
        in_specs=[
            pl.BlockSpec((bm, depth), lambda j, i: (i, 0)),
            pl.BlockSpec((bn, depth), lambda j, i: (j, 0)),
            block,
            block,
        ],
        out_specs=[block] * 2,
    )(gz, w_down, gate, upward, *outputs)


class Halves:
    def __init__(self, whole, axis):
        self.whole, self.axis = whole, axis

    def first(self):
        return [(self.whole, HALVES_1 if self.axis else HALVES_0)]

    def take(self, got):
        top, low = jnp.split(self.whole, 2, axis=1 - self.axis)
        t, b = jnp.split(top, 4, axis=self.axis), jnp.split(low, 4, axis=self.axis)
        self.top, self.next_y = add(t[0], got[0]), add(t[2], got[1])
        self.low, self.next_x = add(b[0], got[2]), add(b[1], got[3])

    def second(self):
        return [(self.next_y, SWAP_Y), (self.next_x, SWAP_X)]

    def total(self, from_y, from_x):
        return jnp.concatenate(
            [add(self.top, from_y), add(self.low, from_x)], axis=1 - self.axis
        )


class Direct:
    def __init__(self, whole, axis):
        self.whole, self.axis = whole, axis

    def first(self):
        return []

    def take(self):
        self.sum = reduce_mp(self.whole, self.axis).astype(BF)

    def second(self):
        return []

    def total(self):
        return self.sum


def add(left, right):
    return (left.astype(F32) + right.astype(F32)).astype(BF)


def local(
    prefix_input,
    action_input,
    valid_dims,
    slot_item,
    segments,
    pre_gain_attn,
    pre_query,
    pre_key,
    pre_value,
    pre_output,
    pre_gain_ffn,
    pre_gate,
    pre_up,
    pre_down,
    act_embed,
    act_gain_attn,
    act_query,
    act_key,
    act_value,
    act_output,
    act_gain_ffn,
    act_gate,
    act_up,
    act_down,
    prefix_cotangent,
    action_cotangent,
):
    n, m = lax.axis_size("dp"), lax.axis_size("mp")
    me, col = lax.axis_index("dp"), lax.axis_index("mp")
    length, wide = prefix_input.shape
    slot_count, steps, dims_count = action_input.shape
    narrow = action_cotangent.shape[2]
    rq = round_up(-(-length // m), 16)
    aq = round_up(-(-steps // m), 16)
    rows, acts = m * rq, m * aq
    heads = pre_query.shape[1] // HD
    scale = HD ** (-0.5)
    kvw = 2 * HD // m

    d_pre, d_act = pre_query.shape[0], act_query.shape[0]
    lanes = 128

    def pad_rows(array, count):
        return jnp.pad(array, ((0, count - array.shape[0]), (0, 0)))

    def lane_rows(array):
        flat = array.reshape(-1)
        count = round_up(-(-flat.shape[0] // lanes), 16)
        return jnp.pad(flat, (0, count * lanes - flat.shape[0])).reshape(count, lanes)

    smalls = [pre_gain_attn, pre_gain_ffn, act_gain_attn, act_gain_ffn, act_embed, action_input]
    small = jnp.concatenate([lane_rows(a) for a in smalls], axis=0)
    ints = jnp.pad(jnp.stack([slot_item, valid_dims]), ((0, 6), (0, lanes - slot_count)))
    cot_rows = lax.dynamic_slice_in_dim(
        jnp.pad(action_cotangent, ((0, 0), (0, acts - steps), (0, 0))), col * aq, aq, 1
    ).reshape(slot_count * aq, narrow)

    def share_of(key, value):
        return lax.dynamic_slice_in_dim(
            jnp.concatenate([key, value], axis=1), col * kvw, kvw, 1
        )

    split = heads * HD
    small, ints, w_q_pre, w_q_act, w_kv_pre, w_kv_act, w_out_pre, w_out_act, cot_all = gather_all(
        [
            small,
            ints,
            pre_query,
            act_query,
            share_of(pre_key, pre_value),
            share_of(act_key, act_value),
            pre_output,
            act_output,
            cot_rows,
        ],
        [
            (n * small.shape[0], lanes),
            (n * 8, lanes),
            (wide, split),
            (narrow, split),
            (m, wide, kvw),
            (m, narrow, kvw),
            (split, wide),
            (n, split, d_act),
            (n * slot_count * aq, narrow),
        ],
        [
            by_rows(small.shape[0]),
            by_rows(8),
            by_rows(d_pre),
            by_rows(d_act),
            by_share(d_pre),
            by_share(d_act),
            by_columns(d_pre),
            by_lead,
            by_rows(slot_count * aq),
        ],
        (4, 5),
        1,
    )
    small = small.reshape(n, -1, lanes)
    smalls_all, begin = [], 0
    for a in smalls:
        count = round_up(-(-a.size // lanes), 16)
        flat = small[:, begin : begin + count].reshape(n, -1)[:, : a.size]
        smalls_all.append(flat.reshape((n,) + a.shape))
        begin += count
    gain_pa, gain_pf, gain_aa, gain_af = [g.reshape(-1).astype(F32) for g in smalls_all[:4]]
    embed = smalls_all[4].transpose(1, 0, 2).reshape(dims_count, narrow)
    act_all = smalls_all[5].reshape(n * slot_count, steps, dims_count)
    ints = ints.reshape(n, 8, lanes)
    slot_all = ints[:, 0, :slot_count].reshape(-1)
    valid_all = ints[:, 1, :slot_count].reshape(-1)
    cot_all = cot_all.reshape(n * slot_count, aq, narrow)
    w_out_act = w_out_act.transpose(1, 0, 2).reshape(split, narrow)
    w_in_pre = jnp.concatenate([w_q_pre] + [w_kv_pre[k] for k in range(m)], axis=1)
    w_in_act = jnp.concatenate([w_q_act] + [w_kv_act[k] for k in range(m)], axis=1)
    twice = wide // narrow

    def by_block(array):
        padded = jnp.pad(array, ((0, rows - length), (0, 0)))
        return own_order(padded.reshape(m, rq, array.shape[1]))

    x_blocks = by_block(prefix_input)
    gz_pre = by_block(prefix_cotangent)[0]
    seg = jnp.pad(segments[0], (0, rows - length), constant_values=1 << 20)
    seg = own_order(seg.reshape(m, rq)).reshape(rows)
    act_place = own_order(jnp.arange(acts, dtype=jnp.int32).reshape(m, aq)).reshape(acts)
    last = 1 << 10
    seg_q = jnp.concatenate([jnp.minimum(seg, last), jnp.full((acts,), last, jnp.int32)])
    seg_k = jnp.concatenate([seg, jnp.where(act_place < steps, last, 1 << 20)])
    allowed = seg_q[:, None] >= seg_k[None, :]

    mine = (slot_all == me).astype(F32)
    valid = jnp.sum(mine * valid_all.astype(F32))
    dims_mask = (lax.broadcasted_iota(jnp.int32, (1, dims_count), 1).astype(F32) < valid).astype(BF)
    act_in = jnp.sum(mine[:, None, None] * act_all.astype(F32), axis=0).astype(BF) * dims_mask
    act_in = own_order(
        jnp.pad(act_in, ((0, acts - steps), (0, 0))).reshape(m, aq, dims_count)
    ).reshape(acts, dims_count)

    gz_pre, embed = lax.optimization_barrier((gz_pre, embed))
    gz_pre_all = gather_dp(gz_pre).reshape(n * rq, wide)

    x_pre = x_blocks.reshape(rows, wide).astype(F32)
    h1_pre = rms_gain(x_pre, gain_pa).astype(BF)
    x_act = dot_plain(act_in, embed)
    h1_act = rms_gain(x_act, gain_aa).astype(BF)

    in_pre = dot_plain(h1_pre, w_in_pre).astype(BF)
    in_act = dot_plain(h1_act, w_in_act).astype(BF)
    into_all = jnp.concatenate([in_pre, in_act], axis=0)
    query, kv_part = into_all[:, : heads * HD], into_all[:, heads * HD :]

    def reorder(array, s):
        if s == 0:
            return array
        pieces = [array[(r ^ s) * rq : (r ^ s) * rq + rq] for r in range(m)]
        pieces += [array[rows + (r ^ s) * aq : rows + (r ^ s) * aq + aq] for r in range(m)]
        return jnp.concatenate(pieces, axis=0)

    keys, values = kv_part[:, :HD], kv_part[:, HD:]

    probs, mixed = [], []
    for h in range(heads):
        scores = dot_right(query[:, h * HD : (h + 1) * HD], keys) * scale
        masked = jnp.where(allowed, scores, -1e30)
        top = jnp.max(masked, axis=-1, keepdims=True)
        raised = jnp.exp(masked - top)
        p = (raised / jnp.sum(raised, axis=-1, keepdims=True)).astype(BF)
        probs.append(p)
        mixed.append(dot_plain(p, values).astype(BF))
    mixed = jnp.concatenate(mixed, axis=1)

    def blocks_of(pre, act):
        return jnp.stack(
            [pack(pre[s * rq : (s + 1) * rq], act[s * aq : (s + 1) * aq]) for s in range(m)]
        )

    def rows_of(blocks):
        pairs = [unpack(b, rq, narrow) for b in blocks]
        return jnp.concatenate([p[0] for p in pairs]), jnp.concatenate([p[1] for p in pairs])

    y_pre = dot_plain(mixed[:rows], w_out_pre).astype(BF)
    y_act = dot_plain(mixed[rows:], w_out_act).astype(BF)
    y = reduce_mp(blocks_of(y_pre, y_act), 0)[0]
    y_pre, y_act = unpack(y, rq, narrow)
    x2_pre = x_pre[:rq] + y_pre
    x2_act = x_act[:aq] + y_act
    h2 = pack(rms_gain(x2_pre, gain_pf).astype(BF), rms_gain(x2_act, gain_af).astype(BF))


    def items_of(blocks):
        pairs = [unpack(blocks[i], rq, narrow) for i in range(n)]
        return jnp.concatenate([p[0] for p in pairs]), jnp.concatenate([p[1] for p in pairs])

    def by_item(pre, act):
        return jnp.stack(
            [
                pack(pre[s * rq : (s + 1) * rq], act[s * aq : (s + 1) * aq])
                for s in range(n)
            ]
        )

    few = act_gate.shape[1] // n

    def columns_first(array):
        return array.reshape(array.shape[0], n, -1).transpose(1, 0, 2)

    act_weights = jnp.concatenate(
        [
            columns_first(act_gate),
            columns_first(act_up),
            act_down.reshape(n, few, d_act).transpose(0, 2, 1),
        ],
        axis=1,
    )
    wg, wu, wd, act_weights, h2_all = deal_all(
        [pre_gate, pre_up, pre_down, act_weights], (0, 0, 1, 2), [h2], 2
    )

    def square(array):
        return array.transpose(1, 2, 0, 3).reshape(narrow, m * few)

    ag, au = square(act_weights[:, :, :d_act]), square(act_weights[:, :, d_act : 2 * d_act])
    ad = square(act_weights[:, :, 2 * d_act :]).T
    h2_pre, h2_act = items_of(h2_all)
    half = n // 2
    turns = [lax.rem(me + 2 * k, n) for k in range(half)]
    turns = turns + [t ^ 1 for t in turns]
    match = (jnp.stack(turns)[:, None] == slot_all[None, :]).astype(BF)
    gz_act_all = dot_plain(match, cot_all.reshape(cot_all.shape[0], -1)).astype(BF)
    gz_act_all = gz_act_all.reshape(n * aq, narrow)
    gz_act = gz_act_all[:aq]

    summed = Halves if m == 4 else Direct

    def feed_forward(h2_rows, gate_w, up_w, down_w, gz):
        gate = dot_plain(h2_rows, gate_w)
        upward = dot_plain(h2_rows, up_w)
        hidden = glu_value(gate, upward).astype(BF)
        z = dot_plain(hidden, down_w).astype(BF)
        g_down = dot_left(hidden, gz).astype(BF)
        grad_hidden = dot_right(gz, down_w)
        unused, pull = jax.vjp(glu_value, gate, upward)
        dgate, dup = pull(grad_hidden)
        dgate, dup = dgate.astype(BF), dup.astype(BF)
        g_gate, g_up = dot_left(h2_rows, dgate).astype(BF), dot_left(h2_rows, dup).astype(BF)
        dh2 = (dot_right(dgate, gate_w) + dot_right(dup, up_w)).astype(BF)
        return z, dh2, g_gate, g_up, g_down

    z_a, dh2_a, g_gate_a, g_up_a, g_down_a = feed_forward(h2_act, ag, au, ad, gz_act_all)
    items, units = n * rq, wg.shape[1]
    gate = dot_plain(h2_pre, wg)
    upward = dot_plain(h2_pre, wu)
    hidden = glu_value(gate, upward).astype(BF)
    gate, upward = gate.astype(BF), upward.astype(BF)
    g_down = summed(dot_left(hidden, gz_pre_all).astype(BF), 0)
    z_parts = pair_sum(by_item(dot_plain(hidden, wd).astype(BF), z_a))
    *got, dgate, dup = exchange_all(
        [(z_parts, CHIPS)] + g_down.first(),
        7,
        [Job(hidden_backward, [gz_pre_all, wd, gate, upward], [(items, units)] * 2)],
    )
    z_sum = z_parts[0].astype(F32)
    for k in range(1, half):
        z_sum = z_sum + got[0][k].astype(F32)
    z_pre, z_act = unpack(z_sum, rq, narrow)
    g_down.take(*got[1:])
    *got, g_gate, g_up = exchange_all(
        g_down.second(),
        8,
        [Job(products_left, [h2_pre, dgate, dup], [(wide, units)] * 2)],
    )
    g_down = g_down.total(*got)
    g_gate, g_up = summed(g_gate, 1), summed(g_up, 1)
    grad_down, *got, dh2_p = exchange_all(
        [(g_down, COLUMNS)] + g_gate.first() + g_up.first(),
        9,
        [Job(products_right, [dgate, wg, dup, wu], [(items, wide)])],
    )
    g_gate.take(*got[: len(got) // 2])
    g_up.take(*got[len(got) // 2 :])
    dh2_parts = pair_sum(by_item(dh2_p, dh2_a))
    act_back = jnp.stack(
        [
            jnp.concatenate(
                [
                    g_gate_a[:, k * few : (k + 1) * few],
                    g_up_a[:, k * few : (k + 1) * few],
                    g_down_a[k * few : (k + 1) * few].T,
                ],
                axis=0,
            )
            for k in range(m)
        ]
    )
    got = exchange_all(
        [(dh2_parts, CHIPS), (act_back, PARTS)] + g_gate.second() + g_up.second(), 3
    )
    dh2 = dh2_parts[0].astype(F32)
    for k in range(1, half):
        dh2 = dh2 + got[0][k].astype(F32)
    dh2_pre, dh2_act = unpack(dh2, rq, narrow)
    act_sum = act_back[0].astype(F32)
    for k in range(1, m):
        act_sum = act_sum + got[1][k].astype(F32)
    act_sum = act_sum.astype(BF).reshape(3, n, d_act, few).transpose(1, 0, 2, 3)
    act_sum = act_sum.reshape(n, 3 * d_act, few)
    pairs = len(g_gate.second())
    g_gate = g_gate.total(*got[2 : 2 + pairs])
    g_up = g_up.total(*got[2 + pairs :])

    def natural(blocks, count):
        return jnp.concatenate([pick_mp(blocks, place) for place in range(m)], axis=0)[:count]

    out_pre = (x2_pre + z_pre).astype(BF)
    out_act = (x2_act + z_act).astype(BF)
    gx2n_pre, g_gain_pf = norm_backward(x2_pre, gain_pf, dh2_pre)
    gx2n_act, g_gain_af = norm_backward(x2_act, gain_af, dh2_act)
    gx2_pre = gz_pre.astype(F32) + gx2n_pre
    gx2_act = gz_act.astype(F32) + gx2n_act
    gy = pack(gx2_pre.astype(BF), gx2_act.astype(BF))
    got = exchange_all([(gy, WHOLE), (g_gate, ROWS)], 4)
    gy_pre, gy_act = rows_of([gy] + [got[0][k] for k in range(1, m)])
    grad_gate = got[1].astype(F32)

    g_out_pre = dot_left(mixed[:rows], gy_pre).astype(BF)
    g_out_act = dot_left(mixed[rows:], gy_act).astype(BF)
    gmix = jnp.concatenate(
        [dot_right(gy_pre, w_out_pre).astype(BF), dot_right(gy_act, w_out_act).astype(BF)], axis=0
    )
    gq, gk, gv = [], 0.0, 0.0
    for h in range(heads):
        cut = slice(h * HD, (h + 1) * HD)
        gm = gmix[:, cut]
        pe = probs[h].astype(F32)
        gp = dot_right(gm, values)
        ds = (pe * (gp - jnp.sum(pe * gp, axis=-1, keepdims=True))).astype(BF)
        gq.append((dot_plain(ds, keys) * scale).astype(BF))
        gk = gk + dot_left(ds, query[:, cut]) * scale
        gv = gv + dot_left(probs[h], gm)
    gkv = jnp.concatenate([gk, gv], axis=1).astype(BF)

    shares = [lax.dynamic_slice_in_dim(gkv, (col ^ k) * kvw, kvw, 1) for k in range(m)]
    gin = jnp.concatenate(gq + [gkv], axis=1)
    gh1_pre = dot_right(gin[:rows], w_in_pre).astype(BF)
    gh1_act = dot_right(gin[rows:], w_in_act).astype(BF)
    gh1_parts = blocks_of(gh1_pre, gh1_act)
    got = exchange_all(
        [(jnp.stack(shares), PARTS), (gh1_parts, PARTS), (g_up, ROWS)], 5
    )
    gkv_sum = shares[0].astype(F32)
    gh1 = gh1_parts[0].astype(F32)
    for k in range(1, m):
        gkv_sum = gkv_sum + reorder(got[0][k], k).astype(F32)
        gh1 = gh1 + got[1][k].astype(F32)
    grad_up = got[2].astype(F32)
    gh1_pre, gh1_act = unpack(gh1, rq, narrow)
    gin = jnp.concatenate(gq + [gkv_sum.astype(BF)], axis=1)
    g_in_pre = dot_left(h1_pre, gin[:rows]).astype(BF)
    g_in_act = dot_left(h1_act, gin[rows:]).astype(BF)

    gxn_pre, g_gain_pa = norm_backward(x_pre[:rq], gain_pa, gh1_pre)
    gxn_act, g_gain_aa = norm_backward(x_act[:aq], gain_aa, gh1_act)
    grad_pre = (gx2_pre + gxn_pre).astype(BF)
    gxa = (gx2_act + gxn_act).astype(BF)
    g_embed = dot_left(act_in[:aq], gxa)
    act_grad = dot_right(gxa, embed)
    def by_index(vector):
        return vector.reshape(n, -1, narrow // n).transpose(1, 0, 2).reshape(-1, narrow)

    tiny = jnp.concatenate(
        [
            by_index(g_gain_pa),
            by_index(g_gain_pf),
            by_index(g_gain_aa),
            by_index(g_gain_af),
            g_embed,
        ],
        axis=0,
    )
    tiny_rows = tiny.shape[0]
    tiny = columns_first(pad_rows(tiny, round_up(tiny_rows, 8)))

    def attn_block(item):
        left = lax.dynamic_slice_in_dim(g_in_pre, item * d_pre, d_pre, 0)
        out = lax.dynamic_slice_in_dim(g_out_pre, item * d_pre, d_pre, 1)
        left_a = lax.dynamic_slice_in_dim(g_in_act, item * d_act, d_act, 0)
        out_a = lax.dynamic_slice_in_dim(g_out_act, item * d_act, d_act, 1)
        top = jnp.concatenate([left] + jnp.split(out, out.shape[0] // d_pre, axis=0), axis=1)
        low = jnp.concatenate([left_a] + jnp.split(out_a, out_a.shape[0] // d_act, axis=0), axis=1)
        return jnp.concatenate([top, low], axis=0)

    parts = pair_sum(jnp.stack([attn_block(i) for i in turns]))
    got = exchange_all(
        [
            (act_sum, EACH),
            (parts, CHIPS),
            (grad_pre, WHOLE),
            (out_pre, WHOLE),
            (jnp.pad(act_grad, ((0, 0), (0, lanes - dims_count))), WORLD),
            (out_act, WORLD),
            (tiny, SPREAD),
        ],
        6,
    )
    grad_down = grad_down.astype(F32)
    act_back = got[0].astype(F32)
    grad_gate_a = act_back[:, :d_act].transpose(1, 0, 2).reshape(d_act, n * few)
    grad_up_a = act_back[:, d_act : 2 * d_act].transpose(1, 0, 2).reshape(d_act, n * few)
    grad_down_a = act_back[:, 2 * d_act :].transpose(0, 2, 1).reshape(n * few, d_act)
    total = parts[0].astype(F32)
    for k in range(1, half):
        total = total + got[1][k].astype(F32)
    prefix_grad = natural([grad_pre] + [got[2][k] for k in range(1, m)], length).astype(F32)
    prefix_output = natural([out_pre] + [got[3][k] for k in range(1, m)], length)
    act_grad = got[4].reshape(n, acts, lanes)[:, :steps, :dims_count]
    out_act = got[5].reshape(n, acts, narrow)[:, :steps]
    mine_items = (slot_item[:, None] == lax.broadcasted_iota(jnp.int32, (1, n), 1)).astype(BF)
    action_output = dot_plain(mine_items, out_act.reshape(n, steps * narrow))
    action_output = action_output.astype(BF).reshape(slot_count, steps, narrow)
    own_mask = lax.broadcasted_iota(jnp.int32, (slot_count, dims_count), 1) < valid_dims[:, None]
    action_grad = jnp.sum(
        mine_items.astype(F32)[:, :, None, None] * act_grad[None], axis=1
    ) * own_mask.astype(F32)[:, None, :]
    tiny = jnp.sum(got[6], axis=(0, 1))
    grad_gain_pa = tiny[:twice].reshape(-1)
    grad_gain_pf = tiny[twice : 2 * twice].reshape(-1)
    rest = tiny[2 * twice : tiny_rows]
    grad_query, grad_kv = total[:d_pre, :split], total[:d_pre, split : split + kvw]
    grad_out = jnp.concatenate(
        jnp.split(total[:d_pre, split + kvw :], split // d_pre, axis=1), axis=0
    )
    grad_query_a, grad_kv_a = total[d_pre:, :split], total[d_pre:, split : split + kvw]
    grad_out_a = jnp.concatenate(
        jnp.split(total[d_pre:, split + kvw :], split // d_act, axis=1), axis=0
    )
    both = jnp.concatenate([grad_kv, grad_kv_a], axis=0).astype(BF)
    both = [both] + [swap_mp(both, s) for s in range(1, m)]
    both = jnp.concatenate([pick_mp(both, place) for place in range(m)], axis=1).astype(F32)

    return (
        prefix_output,
        action_output,
        prefix_grad,
        action_grad,
        grad_gain_pa,
        grad_query,
        both[:d_pre, :HD],
        both[:d_pre, HD:],
        grad_out,
        grad_gain_pf,
        grad_gate,
        grad_up,
        grad_down,
        rest[2:],
        rest[0],
        grad_query_a,
        both[d_pre:, :HD],
        both[d_pre:, HD:],
        grad_out_a,
        rest[1],
        grad_gate_a,
        grad_up_a,
        grad_down_a,
    )


def solution(mesh):
    return jax.shard_map(
        local,
        mesh=mesh,
        in_specs=(
            P("dp", None),
            P("dp", None, None),
            P("dp"),
            P("dp"),
            P("dp", None),
            P("dp"),
            P("dp", "mp"),
            P("dp", None),
            P("dp", None),
            P("mp", "dp"),
            P("dp"),
            P("dp", "mp"),
            P("dp", "mp"),
            P("mp", "dp"),
            P(None, "dp"),
            P("dp"),
            P("dp", "mp"),
            P("dp", None),
            P("dp", None),
            P("mp", "dp"),
            P("dp"),
            P("dp", "mp"),
            P("dp", "mp"),
            P("mp", "dp"),
            P("dp", None),
            P("dp", None, None),
        ),
        out_specs=(
            P("dp", None),
            P("dp", None, None),
            P("dp", None),
            P("dp", None, None),
            P("dp"),
            P("dp", "mp"),
            P("dp", None),
            P("dp", None),
            P("mp", "dp"),
            P("dp"),
            P("dp", "mp"),
            P("dp", "mp"),
            P("mp", "dp"),
            P(None, "dp"),
            P("dp"),
            P("dp", "mp"),
            P("dp", None),
            P("dp", None),
            P("mp", "dp"),
            P("dp"),
            P("dp", "mp"),
            P("dp", "mp"),
            P("mp", "dp"),
        ),
        check_vma=False,
    )
```

```python
import functools

import jax
import jax.numpy as jnp
from jax import lax
from jax.experimental import pallas as pl
from jax.experimental.pallas import tpu as pltpu
from jax.sharding import PartitionSpec as P

HD = 256
EPS = 1e-06
BF = jnp.bfloat16
F32 = jnp.float32
MESH = pl.DeviceIdType.MESH
HBM = pl.BlockSpec(memory_space=pl.ANY)


def rms_gain(values, gain):
    return values * lax.rsqrt(jnp.mean(values * values, axis=-1, keepdims=True) + EPS) * gain


def norm_backward(values, gain, grad_out):
    unused, pull = jax.vjp(rms_gain, values, gain)
    return pull(grad_out)


def glu_value(gate, upward):
    return jax.nn.gelu(gate, approximate=True) * upward


def glu_backward(gate, upward, grad):
    unused, pull = jax.vjp(glu_value, gate, upward)
    return pull(grad)


def dot_plain(left, right):
    return jnp.dot(left, right, preferred_element_type=F32)


def dot_left(left, right):
    return lax.dot_general(left, right, (((0,), (0,)), ((), ())), preferred_element_type=F32)


def dot_right(left, right):
    return lax.dot_general(left, right, (((1,), (1,)), ((), ())), preferred_element_type=F32)


def round_up(value, step):
    return -(-value // step) * step


def add(left, right):
    return (left.astype(F32) + right.astype(F32)).astype(BF)


def greet(devices):
    barrier = pltpu.get_barrier_semaphore()
    for device in devices:
        pl.semaphore_signal(barrier, inc=1, device_id=device, device_id_type=MESH)
    pl.semaphore_wait(barrier, len(devices))


def at(start, size):
    return pl.ds(pl.multiple_of(start * size, size), size)


class Place:
    def __init__(self, n, m, sent, arrived, row):
        self.n, self.m = n, m
        self.me, self.col = lax.axis_index("dp"), lax.axis_index("mp")
        self.sent, self.arrived, self.row = sent, arrived, row

    def remote(self, src, dst, slot, device):
        return pltpu.make_async_remote_copy(
            src_ref=src,
            dst_ref=dst,
            send_sem=self.sent.at[self.row, slot],
            recv_sem=self.arrived.at[self.row, slot],
            device_id=device,
            device_id_type=MESH,
        )

    def keep(self, src, dst):
        def scoped(buffer):
            pltpu.sync_copy(src, buffer)
            pltpu.sync_copy(buffer, dst)

        pl.run_scoped(scoped, pltpu.VMEM(src.shape, src.dtype))

    def over_dp(self, s):
        return (lax.rem(self.me + s, self.n), self.col)

    def over_mp(self, k):
        return (self.me, self.col ^ k)


def loop(first, last, body):
    lax.fori_loop(first, last, lambda s, carry: (body(s), carry)[1], 0)


class Flow:
    reach = "dp"
    kept = False

    def result(self, shape, n, m):
        return shape

    def each(self, p, src, dst, do):
        pass

    def own(self, p, src, dst):
        return None

    def start(self, p, src, dst):
        self.each(p, src, dst, lambda c: c.start())
        if self.kept:
            p.keep(*self.own(p, src, dst))

    def relay(self, p, src, dst, k):
        return None

    def wait(self, p, src, dst):
        self.each(p, src, dst, lambda c: c.wait())


class Rows(Flow):
    kept = True

    def result(self, shape, n, m):
        return (shape[0] // n, shape[1] * n)

    def own(self, p, src, dst):
        return src.at[at(p.me, src.shape[0] // p.n)], dst.at[:, at(p.me, dst.shape[1] // p.n)]

    def each(self, p, src, dst, do):
        def body(s):
            target = p.over_dp(s)
            block = src.at[at(target[0], src.shape[0] // p.n)]
            do(p.remote(block, dst.at[:, at(p.me, dst.shape[1] // p.n)], s, target))

        loop(1, p.n, body)


class Columns(Flow):
    kept = True

    def result(self, shape, n, m):
        return (shape[0] * n, shape[1] // n)

    def own(self, p, src, dst):
        return src.at[:, at(p.me, src.shape[1] // p.n)], dst.at[at(p.me, dst.shape[0] // p.n)]

    def each(self, p, src, dst, do):
        def body(s):
            target = p.over_dp(s)
            block = src.at[:, at(target[0], src.shape[1] // p.n)]
            do(p.remote(block, dst.at[at(p.me, dst.shape[0] // p.n)], s, target))

        loop(1, p.n, body)


class Each(Flow):
    kept = True

    def own(self, p, src, dst):
        return src.at[p.me], dst.at[p.me]

    def each(self, p, src, dst, do):
        def body(s):
            target = p.over_dp(s)
            do(p.remote(src.at[target[0]], dst.at[p.me], s, target))

        loop(1, p.n, body)


class Chips(Flow):
    def each(self, p, src, dst, do):
        loop(1, p.n // 2, lambda s: do(p.remote(src.at[s], dst.at[s], s, p.over_dp(2 * s))))


class Core(Flow):
    def result(self, shape, n, m):
        return (shape[0] // 2, shape[1])

    def each(self, p, src, dst, do):
        half = src.shape[0] // 2
        do(p.remote(src.at[pl.ds(half, half)], dst, 0, (p.me ^ 1, p.col)))


class CoreRows(Flow):
    axis = 0

    def result(self, shape, n, m):
        return (shape[0] // 2, shape[1]) if self.axis == 0 else (shape[0], shape[1] // 2)

    def cut(self, ref, i, count):
        size = ref.shape[self.axis] // count
        return ref.at[at(i, size)] if self.axis == 0 else ref.at[:, at(i, size)]

    def each(self, p, src, dst, do):
        def body(c):
            block = self.cut(src, 2 * c + lax.rem(p.me + 1, 2), p.n)
            do(p.remote(block, self.cut(dst, c, p.n // 2), c, (p.me ^ 1, p.col)))

        loop(0, p.n // 2, body)


class CoreColumns(CoreRows):
    axis = 1


class ChipRows(CoreRows):
    def result(self, shape, n, m):
        if self.axis == 0:
            return (n // 2, shape[0] // (n // 2), shape[1])
        return (n // 2, shape[0], shape[1] // (n // 2))

    def each(self, p, src, dst, do):
        def body(s):
            target = p.over_dp(2 * s)
            do(p.remote(self.cut(src, target[0] // 2, p.n // 2), dst.at[s], s, target))

        loop(1, p.n // 2, body)


class ChipColumns(ChipRows):
    axis = 1


class Line(Flow):
    def __init__(self, place=None, result=None, share=False):
        self.place = place or Line.in_turn
        self.shape = result
        self.share = share
        self.reach = "both" if share else "dp"

    def in_turn(ref, i, j):
        chips = lax.axis_size("dp") // 2
        chip = lax.rem(i // 2 - j // 2 + chips, chips)
        return ref.at[chip + chips * lax.rem(i + j, 2)]

    def result(self, shape, n, m):
        return self.shape or (n,) + shape

    def origin(self, p, first, way, k):
        return lax.rem(first - (2, -2)[way] * k + 2 * p.n, p.n)

    def along(self, p, src, dst, way, k):
        i = self.origin(p, p.me, way, k - 1)
        target = lax.rem(p.me + (2, -2)[way] + p.n, p.n)
        source = src if k == 1 else self.place(dst, i, p.me)
        slot = way * p.n // 2 + k
        return p.remote(source, self.place(dst, i, target), slot, (target, p.col))

    def across(self, p, src, dst, way, k):
        i = self.origin(p, p.me, way, k)
        source = src if k == 0 else self.place(dst, i, p.me)
        slot = (2 + way) * p.n // 2 + k
        return p.remote(source, self.place(dst, i, p.me ^ 1), slot, (p.me ^ 1, p.col))

    def passed(self, p, dst, i, k, source=None):
        block = self.place(dst, i, p.me)
        source = block if source is None else source
        return p.remote(source, block, 2 * p.n + i * p.m + k, p.over_mp(k))

    def receives(self, p, way, k):
        chip = p.me // 2
        if k == 0:
            return chip >= 0
        return chip >= k if way == 0 else chip < p.n // 2 - k

    def sends(self, p, way, k):
        chip = p.me // 2
        beyond = chip < p.n // 2 - 1 if way == 0 else chip > 0
        return beyond & self.receives(p, way, k - 1)

    def start(self, p, src, dst):
        for way in (0, 1):
            pl.when(self.sends(p, way, 1))(self.along(p, src, dst, way, 1).start)
        self.across(p, src, dst, 0, 0).start()
        self.hand(p, dst, p.me, src)
        p.keep(src, self.place(dst, p.me, p.me))

    def hand(self, p, dst, i, source=None):
        if self.share:
            for k in range(1, p.m):
                self.passed(p, dst, i, k, source).start()

    def crossed(self, p, src, dst, way, k):
        self.across(p, src, dst, way, k).wait_recv()
        self.hand(p, dst, self.origin(p, p.me ^ 1, way, k))

    def relay(self, p, src, dst, k):
        if k == 1:
            self.crossed(p, src, dst, 0, 0)
        for way in (0, 1):

            @pl.when(self.receives(p, way, k))
            def _(way=way):
                self.along(p, src, dst, way, k).wait_recv()
                self.across(p, src, dst, way, k).start()
                self.hand(p, dst, self.origin(p, p.me, way, k))

            if k < p.n // 2 - 1:
                pl.when(self.sends(p, way, k + 1))(self.along(p, src, dst, way, k + 1).start)
            if k > 1:
                before = functools.partial(self.crossed, p, src, dst, way, k - 1)
                pl.when(self.receives(p, way, k - 1))(before)

    def wait(self, p, src, dst):
        last = p.n // 2 - 1
        for way in (0, 1):
            end = functools.partial(self.crossed, p, src, dst, way, last)
            pl.when(self.receives(p, way, last))(end)
        self.across(p, src, dst, 0, 0).wait_send()
        for way in (0, 1):
            for k in range(1, last + 1):
                pl.when(self.sends(p, way, k))(self.along(p, src, dst, way, k).wait_send)
                pl.when(self.receives(p, way, k))(self.across(p, src, dst, way, k).wait_send)
        if self.share:
            for k in range(1, p.m):
                loop(0, p.n, lambda i, k=k: self.passed(p, dst, i, k).wait())


class Pass(Flow):
    reach = "mp"
    kept = True
    parts = 8

    def __init__(self, axis):
        self.axis = axis

    def result(self, shape, n, m):
        return (shape[0], m * shape[1]) if self.axis else (m * shape[0], shape[1])

    def spot(self, p, src, dst, k, c=None):
        rows, width = src.shape
        first, count = (0, rows) if c is None else (c * (rows // self.parts), rows // self.parts)
        if self.axis:
            return dst.at[pl.ds(first, count), pl.ds(k * width, width)]
        return dst.at[pl.ds(k * rows + first, count)]

    def own(self, p, src, dst):
        return src, self.spot(p, src, dst, 0)

    def direct(self, p, src, dst, k, c):
        few = src.shape[0] // self.parts
        block = src.at[pl.ds(c * few, few)]
        slot = k * self.parts + c
        return p.remote(block, self.spot(p, src, dst, k, c), slot, p.over_mp(k))

    def turned(self, p, src, dst, c):
        via = 1 + c % 2
        source = self.spot(p, src, dst, via, c)
        slot = 3 * self.parts + c
        return p.remote(source, self.spot(p, src, dst, 3, c), slot, p.over_mp(3 - via))

    def each(self, p, src, dst, do):
        for c in range(self.parts):
            for k in range(1, 3 if p.m == 4 else p.m):
                do(self.direct(p, src, dst, k, c))

    def start(self, p, src, dst):
        self.each(p, src, dst, lambda c: c.start())

    def relay(self, p, src, dst, k):
        if p.m == 4:
            for c in range((k - 1) * self.parts // 2, k * self.parts // 2):
                self.direct(p, src, dst, 1 + c % 2, c).wait_recv()
                self.turned(p, src, dst, c).start()

    def wait(self, p, src, dst):
        p.keep(*self.own(p, src, dst))
        for c in range(self.parts):
            for k in range(1, 3 if p.m == 4 else p.m):
                copy = self.direct(p, src, dst, k, c)
                (copy.wait_send if p.m == 4 and k == 1 + c % 2 else copy.wait)()
            if p.m == 4:
                self.turned(p, src, dst, c).wait()


class Parts(Flow):
    reach = "mp"

    def result(self, shape, n, m):
        return shape if len(shape) == 3 else (m, shape[0] // m, shape[1])

    def each(self, p, src, dst, do):
        for k in range(1, p.m):
            target = p.over_mp(k)
            if len(src.shape) == 3:
                block = src.at[target[1]]
            else:
                block = src.at[at(target[1], src.shape[0] // p.m)]
            do(p.remote(block, dst.at[k], k, target))


class Swaps(Parts):
    def each(self, p, src, dst, do):
        for k in range(1, p.m):
            do(p.remote(src.at[k], dst.at[k], k, p.over_mp(k)))


class Whole(Flow):
    reach = "mp"
    kept = True

    def result(self, shape, n, m):
        return (m * shape[0], shape[1])

    def own(self, p, src, dst):
        return src, dst.at[at(p.col, src.shape[0])]

    def each(self, p, src, dst, do):
        for k in range(1, p.m):
            do(p.remote(src, dst.at[at(p.col, src.shape[0])], k, p.over_mp(k)))


class Swap(Flow):
    reach = "mp"

    def __init__(self, k):
        self.k = k

    def each(self, p, src, dst, do):
        do(p.remote(src, dst, 0, p.over_mp(self.k)))


class First(Flow):
    reach = "mp"

    def __init__(self, axis):
        self.axis = axis

    def result(self, shape, n, m):
        if self.axis:
            return (4, shape[0] // 2, shape[1] // m)
        return (4, shape[0] // m, shape[1] // 2)

    def each(self, p, src, dst, do):
        width, deep = src.shape[self.axis] // p.m, src.shape[1 - self.axis] // 2
        for k, part in enumerate((1, 3, 2, 3)):
            block, half = pl.ds(part * width, width), pl.ds(k // 2 * deep, deep)
            source = src.at[half, block] if self.axis else src.at[block, half]
            do(p.remote(source, dst.at[k], k, p.over_mp(1 + k // 2)))


class World(Flow):
    reach = "world"
    kept = True

    def result(self, shape, n, m):
        return (n, m) + shape

    def block(self, src, i):
        return src

    def own(self, p, src, dst):
        return self.block(src, p.me), dst.at[p.me, p.col]

    def each(self, p, src, dst, do):
        for k in range(p.m):

            def body(s, k=k):
                target = (lax.rem(p.me + s, p.n), p.col ^ k)
                copy = p.remote(
                    self.block(src, target[0]), dst.at[p.me, p.col], s * p.m + k, target
                )
                do(copy)

            loop(0 if k else 1, p.n, body)


class Spread(World):
    def result(self, shape, n, m):
        return (n, m) + shape[1:]

    def block(self, src, i):
        return src.at[i]


class Kernel:
    def __init__(self, collective_id):
        self.collective_id = collective_id
        self.inputs, self.outputs, self.flows, self.steps = [], [], [], []

    def operand(self, source):
        if isinstance(source, int):
            return ("out", source)
        self.inputs.append(source)
        return ("in", len(self.inputs) - 1)

    def shape_of(self, source):
        return self.outputs[source] if isinstance(source, int) else source

    def new_output(self, shape, dtype):
        self.outputs.append(jax.ShapeDtypeStruct(shape, dtype))
        return len(self.outputs) - 1

    def flow(self, kind, source, now=True, into=None):
        n, m = lax.axis_size("dp"), lax.axis_size("mp")
        like = self.shape_of(source)
        out = into
        if into is None:
            out = self.new_output(kind.result(like.shape, n, m), like.dtype)
        name = out if into is None else -1 - len(self.flows)
        self.flows.append((kind, self.operand(source), out, name))
        if now:
            self.go(name)
        return name

    def go(self, name):
        self.steps.append(("start", name))

    def relay(self, name, k):
        self.steps.append(("relay", name, k))

    def ready(self, name):
        self.steps.append(("wait", name))

    def job(self, body, sources, shapes, dtype=BF, into=None):
        outs = into or [self.new_output(s, dtype) for s in shapes]
        self.steps.append(("job", body, [self.operand(s) for s in sources], outs))
        return outs if len(outs) > 1 else outs[0]

    def call(self, name):
        n, m = lax.axis_size("dp"), lax.axis_size("mp")
        takes, gives = len(self.inputs), len(self.outputs)
        flows, steps = self.flows, self.steps
        count = max(len(flows), 1)
        rows = {flow[3]: row for row, flow in enumerate(flows)}
        reach = {flow[0].reach for flow in flows}
        slots = max(2 * n + n * m, 4 * Pass.parts, Pass.parts * m)

        def kernel(*refs):
            ins, outs = refs[:takes], refs[takes : takes + gives]
            sent, arrived = refs[takes + gives :]
            me, col = lax.axis_index("dp"), lax.axis_index("mp")
            if "world" in reach:
                greet([(lax.rem(me + s, n), col ^ k) for s in range(n) for k in range(m) if s or k])
            else:
                column = [(lax.rem(me + s, n), col) for s in range(1, n)]
                row = [(me, col ^ k) for k in range(1, m)]
                greet(
                    (column if reach & {"dp", "both"} else [])
                    + (row if reach & {"mp", "both"} else [])
                )

            def ref(operand):
                return (ins if operand[0] == "in" else outs)[operand[1]]

            def act(what, name, *rest):
                kind, source, out, unused = flows[rows[name]]
                place = Place(n, m, sent, arrived, rows[name])
                getattr(kind, what)(place, ref(source), outs[out], *rest)

            ended = set()
            for step in steps:
                if step[0] == "job":
                    step[1]([ref(s) for s in step[2]], [outs[o] for o in step[3]])
                else:
                    act(*step)
                    if step[0] == "wait":
                        ended.add(step[1])
            for flow in flows:
                if flow[3] not in ended:
                    act("wait", flow[3])

        return pl.pallas_call(
            kernel,
            out_shape=self.outputs,
            in_specs=[HBM] * takes,
            out_specs=[HBM] * gives,
            scratch_shapes=[
                pltpu.SemaphoreType.DMA((count, slots)),
                pltpu.SemaphoreType.DMA((count, slots)),
            ],
            compiler_params=pltpu.CompilerParams(
                collective_id=self.collective_id,
                has_side_effects=True,
                vmem_limit_bytes=56 << 20,
            ),
            name=name,
        )(*self.inputs)


def tile(size, most):
    return max(t for t in range(16, most + 1, 16) if size % t == 0)


def products_plain(inputs, outputs):
    a, b = inputs
    (rows, depth), width = a.shape, b.shape[1]
    bm, bn = tile(rows, 416), tile(width, 512)

    def body(a_ref, b_ref, o_ref):
        o_ref[...] = dot_plain(a_ref[...], b_ref[...]).astype(BF)

    pltpu.emit_pipeline(
        body,
        grid=(width // bn, rows // bm),
        in_specs=[
            pl.BlockSpec((bm, depth), lambda j, i: (i, 0)),
            pl.BlockSpec((depth, bn), lambda j, i: (0, j)),
        ],
        out_specs=[pl.BlockSpec((bm, bn), lambda j, i: (i, j))],
    )(a, b, outputs[0])


def products_right(inputs, outputs):
    pairs = len(inputs) // 2
    rows, width = inputs[0].shape[0], inputs[1].shape[0]
    bm, bn = tile(rows, 416), tile(width, 512)

    def body(*refs):
        total = dot_right(refs[0][...], refs[1][...])
        for p in range(1, pairs):
            total = total + dot_right(refs[2 * p][...], refs[2 * p + 1][...])
        refs[-1][...] = total.astype(BF)

    specs = []
    for p in range(pairs):
        depth = inputs[2 * p].shape[1]
        specs.append(pl.BlockSpec((bm, depth), lambda j, i: (i, 0)))
        specs.append(pl.BlockSpec((bn, depth), lambda j, i: (j, 0)))
    pltpu.emit_pipeline(
        body,
        grid=(width // bn, rows // bm),
        in_specs=specs,
        out_specs=[pl.BlockSpec((bm, bn), lambda j, i: (i, j))],
    )(*inputs, outputs[0])


def products_left(inputs, outputs):
    a, rest = inputs[0], inputs[1:]
    (depth, rows), width = a.shape, rest[0].shape[1]
    bm, bn = tile(rows, 1024), tile(width, 512)
    count = len(rest)

    def body(a_ref, *refs):
        for p in range(count):
            refs[count + p][...] = dot_left(a_ref[...], refs[p][...]).astype(BF)

    pltpu.emit_pipeline(
        body,
        grid=(rows // bm, width // bn),
        in_specs=[pl.BlockSpec((depth, bm), lambda i, j: (0, i))]
        + [pl.BlockSpec((depth, bn), lambda i, j: (0, j))] * count,
        out_specs=[pl.BlockSpec((bm, bn), lambda i, j: (i, j))] * count,
    )(a, *rest, *outputs)


def hidden_forward(part, parts, inputs, outputs):
    h, w_gate, w_up = inputs
    (rows, depth), width = h.shape, w_gate.shape[1] // parts
    cut = pl.ds(part * width, width)
    w_gate, w_up = w_gate.at[:, cut], w_up.at[:, cut]
    outputs = [o.at[:, cut] for o in outputs]
    bm, bn = tile(rows, 416), tile(width, 512)

    def body(h_ref, gate_w, up_w, gate_ref, up_ref, hidden_ref):
        gate = dot_plain(h_ref[...], gate_w[...])
        upward = dot_plain(h_ref[...], up_w[...])
        gate_ref[...] = gate.astype(BF)
        up_ref[...] = upward.astype(BF)
        hidden_ref[...] = glu_value(gate, upward).astype(BF)

    block = pl.BlockSpec((bm, bn), lambda j, i: (i, j))
    pltpu.emit_pipeline(
        body,
        grid=(width // bn, rows // bm),
        in_specs=[pl.BlockSpec((bm, depth), lambda j, i: (i, 0))]
        + [pl.BlockSpec((depth, bn), lambda j, i: (0, j))] * 2,
        out_specs=[block] * 3,
    )(h, w_gate, w_up, *outputs)


def hidden_backward(inputs, outputs):
    gz, w_down, gate, upward = inputs
    (rows, depth), width = gz.shape, w_down.shape[0]
    bm, bn = tile(rows, 416), tile(width, 512)

    def body(gz_ref, down_w, gate_ref, up_ref, dgate_ref, dup_ref):
        grad = dot_right(gz_ref[...], down_w[...])
        dgate, dup = glu_backward(gate_ref[...].astype(F32), up_ref[...].astype(F32), grad)
        dgate_ref[...] = dgate.astype(BF)
        dup_ref[...] = dup.astype(BF)

    block = pl.BlockSpec((bm, bn), lambda j, i: (i, j))
    pltpu.emit_pipeline(
        body,
        grid=(width // bn, rows // bm),
        in_specs=[
            pl.BlockSpec((bm, depth), lambda j, i: (i, 0)),
            pl.BlockSpec((bn, depth), lambda j, i: (j, 0)),
            block,
            block,
        ],
        out_specs=[block] * 2,
    )(gz, w_down, gate, upward, *outputs)


def attend_forward(inputs, outputs):
    query, keys, values, seg_q, seg_k = inputs
    probs, mixed = outputs
    total = query.shape[0]
    rows = tile(total, 448)

    def body(q_ref, k_ref, v_ref, sq_ref, sk_ref, p_ref, o_ref):
        allowed = sq_ref[:, :1] >= sk_ref[:1]
        scores = dot_right(q_ref[...], k_ref[...]) * HD ** (-0.5)
        scores = jnp.where(allowed, scores, -1e30)
        raised = jnp.exp(scores - jnp.max(scores, axis=-1, keepdims=True))
        p = (raised / jnp.sum(raised, axis=-1, keepdims=True)).astype(BF)
        p_ref[...] = p
        o_ref[...] = dot_plain(p, v_ref[...]).astype(BF)

    def rest(shape):
        return pl.BlockSpec(shape, lambda i: (0, 0))

    pltpu.emit_pipeline(
        body,
        grid=(total // rows,),
        in_specs=[
            pl.BlockSpec((rows, HD), lambda i: (i, 0)),
            rest(keys.shape),
            rest(values.shape),
            pl.BlockSpec((rows, seg_q.shape[1]), lambda i: (i, 0)),
            rest(seg_k.shape),
        ],
        out_specs=[
            pl.BlockSpec((rows, total), lambda i: (i, 0)),
            pl.BlockSpec((rows, HD), lambda i: (i, 0)),
        ],
    )(query, keys, values, seg_q, seg_k, probs, mixed)


def attend_backward(heads, inputs, outputs):
    probs, query = inputs[:heads], inputs[heads : 2 * heads]
    keys, values, grad = inputs[2 * heads :]
    grad_query, (both, shares) = outputs[:heads], outputs[heads:]
    total, scale = keys.shape[0], HD ** (-0.5)
    rows = tile(total, 448)
    width = shares.shape[2]

    def scoped(sums, rounded, parted):
        sums[...] = jnp.zeros_like(sums)

        def body(*refs):
            k_ref, v_ref, g_ref = refs[2 * heads : 2 * heads + 3]
            for h in range(heads):
                g = g_ref[:, h * HD : (h + 1) * HD]
                p, q = refs[h][...], refs[heads + h][...]
                wide_p = p.astype(F32)
                dp = dot_right(g, v_ref[...])
                ds = wide_p * (dp - jnp.sum(wide_p * dp, axis=-1, keepdims=True))
                ds = ds.astype(BF)
                refs[2 * heads + 3 + h][...] = (dot_plain(ds, k_ref[...]) * scale).astype(BF)
                sums[:, :HD] += dot_left(ds, q) * scale
                sums[:, HD:] += dot_left(p, g)

        def rest(ref):
            return pl.BlockSpec(ref.shape, lambda i: (0, 0))

        block = pl.BlockSpec((rows, HD), lambda i: (i, 0))
        pltpu.emit_pipeline(
            body,
            grid=(total // rows,),
            in_specs=[pl.BlockSpec((rows, total), lambda i: (i, 0))] * heads
            + [block] * heads
            + [rest(keys), rest(values), pl.BlockSpec((rows, heads * HD), lambda i: (i, 0))],
            out_specs=[block] * heads,
        )(*probs, *query, keys, values, grad, *grad_query)
        rounded[...] = sums[...].astype(BF)
        for k in range(shares.shape[0]):
            parted[k] = sums[:, k * width : (k + 1) * width].astype(BF)
        pltpu.sync_copy(rounded, both)
        pltpu.sync_copy(parted, shares)

    pl.run_scoped(
        scoped,
        pltpu.VMEM((total, 2 * HD), F32),
        pltpu.VMEM((total, 2 * HD), BF),
        pltpu.VMEM(shares.shape, BF),
    )


def rows_from(first, count, body):
    return lambda inputs, outputs: body([inputs[0].at[pl.ds(first, count)]] + inputs[1:], outputs)


class Halves:
    def __init__(self, whole, axis):
        self.whole, self.axis = whole, axis

    def take(self, got):
        top, low = jnp.split(self.whole, 2, axis=1 - self.axis)
        t, b = jnp.split(top, 4, axis=self.axis), jnp.split(low, 4, axis=self.axis)
        self.top, self.next_y = add(t[0], got[0]), add(t[2], got[1])
        self.low, self.next_x = add(b[0], got[2]), add(b[1], got[3])

    def second(self, kernel):
        self.from_y = kernel.flow(Swap(2), self.next_y)
        self.from_x = kernel.flow(Swap(1), self.next_x)

    def total(self, got):
        return jnp.concatenate(
            [add(self.top, got[self.from_y]), add(self.low, got[self.from_x])], axis=1 - self.axis
        )


class Direct:
    def __init__(self, whole, axis):
        parts = jnp.split(whole, lax.axis_size("mp"), axis=axis)
        total = parts[0].astype(F32)
        for k in range(1, len(parts)):
            pairs = [(i, i ^ k) for i in range(len(parts))]
            total = total + lax.ppermute(parts[k], "mp", pairs).astype(F32)
        self.sum = total.astype(BF)

    def take(self, got):
        return None

    def second(self, kernel):
        return None

    def total(self, got):
        return self.sum


def local(
    prefix_input,
    action_input,
    valid_dims,
    slot_item,
    segments,
    pre_gain_attn,
    pre_query,
    pre_key,
    pre_value,
    pre_output,
    pre_gain_ffn,
    pre_gate,
    pre_up,
    pre_down,
    act_embed,
    act_gain_attn,
    act_query,
    act_key,
    act_value,
    act_output,
    act_gain_ffn,
    act_gate,
    act_up,
    act_down,
    prefix_cotangent,
    action_cotangent,
):
    n, m = lax.axis_size("dp"), lax.axis_size("mp")
    me, col = lax.axis_index("dp"), lax.axis_index("mp")
    length, wide = prefix_input.shape
    slot_count, steps, dims_count = action_input.shape
    narrow = action_cotangent.shape[2]
    rq = round_up(-(-length // m), 16)
    aq = round_up(-(-steps // m), 16)
    rows, acts = m * rq, m * aq
    total_rows = rows + acts
    half = n // 2
    heads = pre_query.shape[1] // HD
    split = heads * HD
    scale = HD ** (-0.5)
    kvw = 2 * HD // m
    d_pre, d_act = pre_query.shape[0], act_query.shape[0]
    few = act_gate.shape[1] // n
    lanes = 128
    twice = wide // narrow
    turns = [lax.rem(me + 2 * k, n) for k in range(half)]
    turns = turns + [t ^ 1 for t in turns]

    def own(array, count):
        return lax.dynamic_slice_in_dim(array, col * count, count, 0)

    def pad_rows(array, count):
        return jnp.pad(array, ((0, count - array.shape[0]), (0, 0)))

    def lane_rows(array):
        flat = array.reshape(-1)
        count = round_up(-(-flat.shape[0] // lanes), 16)
        return jnp.pad(flat, (0, count * lanes - flat.shape[0])).reshape(count, lanes)

    def columns_first(array):
        return array.reshape(array.shape[0], n, -1).transpose(1, 0, 2)

    smalls = [pre_gain_attn, pre_gain_ffn, act_gain_attn, act_gain_ffn, act_embed, action_input]
    small = jnp.concatenate([lane_rows(a) for a in smalls], axis=0)
    ints = jnp.pad(jnp.stack([slot_item, valid_dims]), ((0, 6), (0, lanes - slot_count)))
    cot_rows = lax.dynamic_slice_in_dim(
        jnp.pad(action_cotangent, ((0, 0), (0, acts - steps), (0, 0))), col * aq, aq, 1
    ).reshape(slot_count * aq, narrow)

    def share_of(key, value):
        return own(jnp.concatenate([key, value], axis=1).T, kvw).T

    def by_rows(size):
        return lambda ref, i, j: ref.at[at(i, size)]

    def by_columns(size):
        return lambda ref, i, j: ref.at[:, at(i, size)]

    def by_share(size):
        return lambda ref, i, j: ref.at[lax.axis_index("mp"), at(i, size)]

    def by_lead(ref, i, j):
        return ref.at[i]

    kernel = Kernel(1)
    aligned = kvw % lanes == 0
    in_pre, in_act = (wide, split + 2 * HD), (narrow, split + 2 * HD)
    kv_pre, kv_act = share_of(pre_key, pre_value), share_of(act_key, act_value)

    def in_columns(size, share):
        def place(ref, i, j):
            start = split + lax.axis_index("mp") * kvw if share else 0
            columns = pl.ds(pl.multiple_of(start, lanes), kvw if share else split)
            return ref.at[at(i, size), columns]

        return place

    if aligned:
        w_in_pre = kernel.flow(Line(in_columns(d_pre, True), in_pre, True), kv_pre)
        w_in_act = kernel.flow(Line(in_columns(d_act, True), in_act, True), kv_act)
        lines = [w_in_pre, w_in_act]
    else:
        w_kv_pre = kernel.flow(Line(by_share(d_pre), (m, wide, kvw), True), kv_pre)
        w_kv_act = kernel.flow(Line(by_share(d_act), (m, narrow, kvw), True), kv_act)
        lines = [w_kv_pre, w_kv_act]
    small = kernel.flow(Line(by_lead, (n,) + small.shape), small)
    ints = kernel.flow(Line(by_lead, (n, 8, lanes)), ints)
    if aligned:
        w_q_pre = kernel.flow(Line(in_columns(d_pre, False)), pre_query, into=w_in_pre)
        w_q_act = kernel.flow(Line(in_columns(d_act, False)), act_query, into=w_in_act)
    else:
        w_q_pre = kernel.flow(Line(by_rows(d_pre), (wide, split)), pre_query)
        w_q_act = kernel.flow(Line(by_rows(d_act), (narrow, split)), act_query)
    w_out_pre = kernel.flow(Line(by_columns(d_pre), (split, wide)), pre_output)
    w_out_act = kernel.flow(Line(by_lead, (n, split, d_act)), act_output)
    cot_all = kernel.flow(Line(by_lead, (n, slot_count * aq, narrow)), cot_rows)
    lines += [small, ints, w_q_pre, w_q_act, w_out_pre, w_out_act, cot_all]
    for k in range(1, half):
        for out in lines:
            kernel.relay(out, k)
    got = kernel.call("gather")
    small, ints, cot_all = got[small], got[ints], got[cot_all]
    w_out_pre, w_out_act = got[w_out_pre], got[w_out_act]
    if aligned:
        w_in_pre, w_in_act = got[w_in_pre], got[w_in_act]
    else:
        w_in_pre = jnp.concatenate([got[w_q_pre]] + [got[w_kv_pre][k] for k in range(m)], axis=1)
        w_in_act = jnp.concatenate([got[w_q_act]] + [got[w_kv_act][k] for k in range(m)], axis=1)
    smalls_all, begin = [], 0
    for a in smalls:
        count = round_up(-(-a.size // lanes), 16)
        flat = small[:, begin : begin + count].reshape(n, -1)[:, : a.size]
        smalls_all.append(flat.reshape((n,) + a.shape))
        begin += count
    gain_pa, gain_pf, gain_aa, gain_af = [g.reshape(-1).astype(F32) for g in smalls_all[:4]]
    embed = smalls_all[4].transpose(1, 0, 2).reshape(dims_count, narrow)
    act_all = smalls_all[5].reshape(n * slot_count, steps, dims_count)
    slot_all = ints[:, 0, :slot_count].reshape(-1)
    valid_all = ints[:, 1, :slot_count].reshape(-1)
    w_out_act = w_out_act.transpose(1, 0, 2).reshape(split, narrow)

    mine = (slot_all == me).astype(F32)
    valid = jnp.sum(mine * valid_all.astype(F32))
    dims_mask = (lax.broadcasted_iota(jnp.int32, (1, dims_count), 1).astype(F32) < valid).astype(BF)
    act_in = jnp.sum(mine[:, None, None] * act_all.astype(F32), axis=0).astype(BF) * dims_mask
    act_in = pad_rows(act_in, acts)

    x_pre = pad_rows(prefix_input, rows).astype(F32)
    h1_pre = rms_gain(x_pre, gain_pa).astype(BF)
    x_act = dot_plain(act_in, embed)
    h1_act = rms_gain(x_act, gain_aa).astype(BF)
    into = jnp.concatenate(
        [dot_plain(h1_pre, w_in_pre).astype(BF), dot_plain(h1_act, w_in_act).astype(BF)], axis=0
    )
    query = [into[:, h * HD : (h + 1) * HD] for h in range(heads)]
    keys, values = into[:, split : split + HD], into[:, split + HD :]
    last, never = 1 << 10, 1 << 20
    seg = jnp.pad(segments[0], (0, rows - length), constant_values=never)
    seg_q = jnp.concatenate([jnp.minimum(seg, last), jnp.full((acts,), last, jnp.int32)])
    own_keys = jnp.where(jnp.arange(acts, dtype=jnp.int32) < steps, last, never)
    seg_k = jnp.concatenate([seg, own_keys])
    seg_q = jnp.broadcast_to(seg_q[:, None], (total_rows, lanes))
    seg_k = jnp.broadcast_to(seg_k[None, :], (8, total_rows))

    gz_pre = own(pad_rows(prefix_cotangent, rows), rq)
    even = few % lanes == 0 and d_act % lanes == 0
    if not even:
        act_weights = jnp.concatenate(
            [
                columns_first(act_gate),
                columns_first(act_up),
                act_down.reshape(n, few, d_act).transpose(0, 2, 1),
            ],
            axis=1,
        )

    def project(first, count):
        def body(inputs, outputs):
            pairs = len(inputs) - 1
            w_out = inputs[-1]
            width = w_out.shape[1]
            bm, bn = tile(count, 416), tile(width, 1024)

            def step(*refs):
                value = dot_plain(refs[0][...], refs[1][...])
                for h in range(1, pairs):
                    value = value + dot_plain(refs[2 * h][...], refs[2 * h + 1][...])
                refs[-1][...] = value.astype(BF)

            operands, specs = [], []
            for h in range(pairs):
                operands += [inputs[h].at[pl.ds(first, count)], w_out.at[pl.ds(h * HD, HD)]]
                specs += [
                    pl.BlockSpec((bm, HD), lambda j, i: (i, 0)),
                    pl.BlockSpec((HD, bn), lambda j, i: (0, j)),
                ]
            pltpu.emit_pipeline(
                step,
                grid=(width // bn, count // bm),
                in_specs=specs,
                out_specs=[pl.BlockSpec((bm, bn), lambda j, i: (i, j))],
            )(*operands, outputs[0])

        return body

    kernel = Kernel(2)
    gate_own = kernel.flow(Columns(), pre_gate)
    if even:
        act_own = [kernel.flow(Columns(), act_gate), kernel.flow(Columns(), act_up)]
        act_own.append(kernel.flow(Rows(), act_down))
    else:
        act_own = [kernel.flow(Each(), act_weights)]
    up_own = kernel.flow(Columns(), pre_up, now=False)
    probs, mixed = [], []
    for h in range(heads):
        p, o = kernel.job(
            attend_forward,
            [query[h], keys, values, seg_q, seg_k],
            [(total_rows, total_rows), (total_rows, HD)],
        )
        probs.append(p)
        mixed.append(o)
        if h == 0:
            kernel.go(up_own)
    y_pre = kernel.job(project(0, rows), mixed + [w_out_pre], [(rows, wide)])
    y_act = kernel.job(project(rows, acts), mixed + [w_out_act], [(acts, narrow)])
    y_pre_parts = kernel.flow(Parts(), y_pre)
    y_act_parts = kernel.flow(Parts(), y_act)
    kernel.ready(gate_own)
    w_gate = kernel.flow(Pass(1), gate_own)
    down_own = kernel.flow(Rows(), pre_down)
    kernel.relay(w_gate, 1)
    kernel.relay(w_gate, 2)
    got = kernel.call("attend")
    probs, mixed = [got[p] for p in probs], [got[o] for o in mixed]
    up_own, down_own, w_gate = got[up_own], got[down_own], got[w_gate]
    act_own = [got[a] for a in act_own]

    def summed(first, parts):
        value = first.astype(F32)
        for k in range(1, parts.shape[0]):
            value = value + parts[k].astype(F32)
        return value

    x2_pre = own(x_pre, rq) + summed(own(got[y_pre], rq), got[y_pre_parts])
    x2_act = own(x_act, aq) + summed(own(got[y_act], aq), got[y_act_parts])
    h2_pre = rms_gain(x2_pre, gain_pf).astype(BF)
    h2_act = rms_gain(x2_act, gain_af).astype(BF)

    kernel = Kernel(3)
    h2_pre = kernel.flow(Line(), h2_pre)
    h2_act = kernel.flow(Line(), h2_act)
    w_up = kernel.flow(Pass(1), up_own)
    if even:
        act_all_w = [kernel.flow(Pass(axis), a) for axis, a in zip((1, 1, 0), act_own)]
    else:
        act_all_w = [kernel.flow(Pass(0), act_own[0].reshape(n * 3 * d_act, few))]
    for k in range(1, half):
        kernel.relay(h2_pre, k)
        kernel.relay(h2_act, k)
        if k < 3:
            kernel.relay(w_up, k)
    for k in (1, 2):
        for a in act_all_w:
            kernel.relay(a, k)
    got = kernel.call("spread")
    h2_pre, h2_act = got[h2_pre].reshape(n * rq, wide), got[h2_act].reshape(n * aq, narrow)
    w_up = got[w_up]
    if even:
        act_gate_w, act_up_w, act_down_w = [got[a] for a in act_all_w]
    else:
        act_all_w = got[act_all_w[0]].reshape(m, n, 3, d_act, few).transpose(2, 1, 3, 0, 4)
        act_gate_w, act_up_w, act_down_w = act_all_w.reshape(3, narrow, m * few)
        act_down_w = act_down_w.T

    match = (jnp.stack(turns)[:, None] == slot_all[None, :]).astype(BF)
    cot_all = cot_all.reshape(n * slot_count, aq * narrow)
    gz_act_all = dot_plain(match, cot_all).astype(BF).reshape(n * aq, narrow)
    gz_act = gz_act_all[:aq]
    gate_a = dot_plain(h2_act, act_gate_w)
    up_a = dot_plain(h2_act, act_up_w)
    hid_a = glu_value(gate_a, up_a).astype(BF)
    z_a = dot_plain(hid_a, act_down_w).astype(BF)
    dgate_a, dup_a = glu_backward(gate_a, up_a, dot_right(gz_act_all, act_down_w))
    dgate_a, dup_a = dgate_a.astype(BF), dup_a.astype(BF)
    dh2_a = (dot_right(dgate_a, act_gate_w) + dot_right(dup_a, act_up_w)).astype(BF)
    act_back = [dot_left(h2_act, dgate_a), dot_left(h2_act, dup_a)]
    if even:
        g_down_a = dot_left(hid_a, gz_act_all).astype(BF).reshape(m, few, narrow)
    else:
        act_back.append(dot_left(gz_act_all, hid_a))
    act_back = [jnp.concatenate(act_back, axis=0).astype(BF)]
    act_back = [jnp.stack(jnp.split(a, m, axis=1)) for a in act_back]
    if even:
        act_back.append(g_down_a)

    items, units = h2_pre.shape[0], w_gate.shape[1]
    summing = Halves if m == 4 else Direct

    kernel = Kernel(4)
    gz_all = kernel.flow(Line(), gz_pre)
    w_down = kernel.flow(Pass(0), down_own)
    pieces = max(half - 1, m)
    relays = [(gz_all, k) for k in range(1, half)]
    turn = {pieces // 2: (w_down, 1), pieces - 1: (w_down, 2)}
    into = None
    for piece in range(pieces):
        into = kernel.job(
            functools.partial(hidden_forward, piece, pieces),
            [h2_pre, w_gate, w_up],
            [(items, units)] * 3,
            into=into,
        )
        if piece in turn:
            kernel.relay(*turn[piece])
        if piece < len(relays):
            kernel.relay(*relays[piece])
    got = kernel.call("hidden")
    gate, upward, hidden = [got[o] for o in into]
    w_down, gz_pre_all = got[w_down], got[gz_all].reshape(n * rq, wide)

    kernel = Kernel(5)
    g_down = kernel.job(products_left, [hidden, gz_pre_all], [(units, wide)])
    first = kernel.flow(First(0), g_down) if m == 4 else None
    z_p = kernel.job(products_plain, [hidden, w_down], [(items, wide)])
    z_p_core, z_a_core = kernel.flow(Core(), z_p), kernel.flow(Core(), z_a)
    dgate, dup = kernel.job(
        hidden_backward, [gz_pre_all, w_down, gate, upward], [(items, units)] * 2
    )
    got = kernel.call("hidden_grads")
    dgate, dup = got[dgate], got[dup]
    g_down = summing(got[g_down], 0)
    g_down.take(got[first] if m == 4 else None)

    def pair_sum(parts, other):
        return add(parts[: other.shape[0]], other).reshape(half, -1, other.shape[1])

    z_p = pair_sum(got[z_p], got[z_p_core])
    z_a = pair_sum(z_a, got[z_a_core])

    kernel = Kernel(6)
    z_p_parts, z_a_parts = kernel.flow(Chips(), z_p), kernel.flow(Chips(), z_a)
    g_down.second(kernel)
    g_gate = kernel.job(products_left, [h2_pre, dgate], [(wide, units)])
    first = kernel.flow(First(1), g_gate) if m == 4 else None
    g_up = kernel.job(products_left, [h2_pre, dup], [(wide, units)])
    got = kernel.call("in_grads")
    g_gate, g_up = summing(got[g_gate], 1), got[g_up]
    g_gate.take(got[first] if m == 4 else None)
    g_down = g_down.total(got)
    out_pre = (x2_pre + summed(z_p[0], got[z_p_parts])).astype(BF)
    out_act = (x2_act + summed(z_a[0], got[z_a_parts])).astype(BF)

    kernel = Kernel(7)
    first = kernel.flow(First(1), g_up) if m == 4 else None
    grad_down = kernel.flow(Columns(), g_down)
    out_act = kernel.flow(Line(), out_act)
    dh2_p = kernel.job(products_right, [dgate, w_gate, dup, w_up], [(items, wide)])
    dh2_p_core, dh2_a_core = kernel.flow(Core(), dh2_p), kernel.flow(Core(), dh2_a)
    for k in range(1, half):
        kernel.relay(out_act, k)
    got = kernel.call("row_grads")
    out_act = got[out_act].reshape(n * aq, narrow)
    g_up = summing(g_up, 1)
    g_up.take(got[first] if m == 4 else None)
    grad_down = got[grad_down].astype(F32)
    dh2_p = pair_sum(got[dh2_p], got[dh2_p_core])
    dh2_a = pair_sum(dh2_a, got[dh2_a_core])

    kernel = Kernel(8)
    dh2_p_parts, dh2_a_parts = kernel.flow(Chips(), dh2_p), kernel.flow(Chips(), dh2_a)
    g_gate.second(kernel)
    g_up.second(kernel)
    act_parts = [kernel.flow(Swaps(), a) for a in act_back]
    got = kernel.call("sum_rows")
    g_gate, g_up = g_gate.total(got), g_up.total(got)
    act_sum = [summed(a[0], got[b]).astype(BF) for a, b in zip(act_back, act_parts)]
    if not even:
        act_sum = jnp.concatenate(act_sum, axis=0).reshape(3, n, d_act, few)
        act_sum = [act_sum.transpose(1, 0, 2, 3).reshape(n, 3 * d_act, few)]
    gx2n_pre, g_gain_pf = norm_backward(x2_pre, gain_pf, summed(dh2_p[0], got[dh2_p_parts]))
    gx2n_act, g_gain_af = norm_backward(x2_act, gain_af, summed(dh2_a[0], got[dh2_a_parts]))
    gx2_pre = gz_pre.astype(F32) + gx2n_pre
    gx2_act = gz_act.astype(F32) + gx2n_act

    def both_rows(inputs, outputs):
        products_right(inputs[:2], [outputs[0].at[pl.ds(0, rows)]])
        products_right(inputs[2:], [outputs[0].at[pl.ds(rows, acts)]])

    def input_grads(first, count, inputs, outputs):
        w_in, operands = inputs[-1], []
        for h in range(heads):
            operands += [inputs[h].at[pl.ds(first, count)], w_in.at[:, pl.ds(h * HD, HD)]]
        operands += [inputs[heads].at[pl.ds(first, count)], w_in.at[:, pl.ds(split, 2 * HD)]]
        products_right(operands, outputs)

    def weight_grads(first, count, inputs, outputs):
        products_left([a if a.shape[0] == count else a.at[pl.ds(first, count)] for a in inputs], outputs)

    kernel = Kernel(9)
    gy_pre = kernel.flow(Whole(), gx2_pre.astype(BF))
    gy_act = kernel.flow(Whole(), gx2_act.astype(BF))
    grad_gate = kernel.flow(Rows(), g_gate)
    kernel.ready(gy_pre)
    kernel.ready(gy_act)
    grad_up = kernel.flow(Rows(), g_up)
    gmix = kernel.job(both_rows, [gy_pre, w_out_pre, gy_act, w_out_act], [(total_rows, split)])
    *gq, gkv, shares = kernel.job(
        functools.partial(attend_backward, heads),
        probs + query + [keys, values, gmix],
        [(total_rows, HD)] * heads + [(total_rows, 2 * HD), (m, total_rows, kvw)],
    )
    share_parts = kernel.flow(Parts(), shares)
    gh1_pre = kernel.job(
        functools.partial(input_grads, 0, rows), gq + [gkv, w_in_pre], [(rows, wide)]
    )
    gh1_pre_parts = kernel.flow(Parts(), gh1_pre)
    gh1_act = kernel.job(
        functools.partial(input_grads, rows, acts), gq + [gkv, w_in_act], [(acts, narrow)]
    )
    gh1_act_parts = kernel.flow(Parts(), gh1_act)
    if even:
        both = [kernel.flow(Rows(), act_sum[0][k * narrow : (k + 1) * narrow]) for k in (0, 1)]
        act_sum = both + [kernel.flow(Columns(), act_sum[1])]
    else:
        act_sum = [kernel.flow(Each(), act_sum[0])]
    out_act = kernel.flow(Whole(), out_act)
    g_out_pre, g_out_act, g_q_pre, g_q_act = [], [], [], []
    for h in range(heads):
        of_pre = functools.partial(weight_grads, 0, rows)
        of_act = functools.partial(weight_grads, rows, acts)
        g_out_pre.append(kernel.job(of_pre, [mixed[h], gy_pre], [(HD, wide)]))
        g_q_pre.append(kernel.job(of_pre, [h1_pre, gq[h]], [(wide, HD)]))
        g_out_act.append(kernel.job(of_act, [mixed[h], gy_act], [(HD, narrow)]))
        g_q_act.append(kernel.job(of_act, [h1_act, gq[h]], [(narrow, HD)]))
    got = kernel.call("heads")
    grad_gate, grad_up = got[grad_gate].astype(F32), got[grad_up].astype(F32)
    g_out_pre, g_out_act, g_q_pre, g_q_act = [
        [got[o] for o in group] for group in (g_out_pre, g_out_act, g_q_pre, g_q_act)
    ]
    shares, gh1_pre, gh1_act, out_act = got[shares], got[gh1_pre], got[gh1_act], got[out_act]
    gkv_sum = summed(lax.dynamic_index_in_dim(shares, col, 0, False), got[share_parts])
    gh1_pre = summed(own(gh1_pre, rq), got[gh1_pre_parts])
    gh1_act = summed(own(gh1_act, aq), got[gh1_act_parts])
    act_sum = [got[a].astype(F32) for a in act_sum]
    gkv_sum = gkv_sum.astype(BF)
    g_in_pre = g_q_pre + [dot_left(h1_pre, gkv_sum[:rows]).astype(BF)]
    g_in_act = g_q_act + [dot_left(h1_act, gkv_sum[rows:]).astype(BF)]
    gxn_pre, g_gain_pa = norm_backward(own(x_pre, rq), gain_pa, gh1_pre)
    gxn_act, g_gain_aa = norm_backward(own(x_act, aq), gain_aa, gh1_act)
    grad_pre = (gx2_pre + gxn_pre).astype(BF)
    gxa = (gx2_act + gxn_act).astype(BF)
    g_embed = dot_left(own(act_in, aq), gxa)
    act_grad = dot_right(gxa, embed).reshape(aq * dims_count // lanes, lanes)

    def attn_block(item):
        left = [lax.dynamic_slice_in_dim(g, item * d_pre, d_pre, 0) for g in g_in_pre]
        out = [lax.dynamic_slice_in_dim(g, item * d_pre, d_pre, 1) for g in g_out_pre]
        left_a = [lax.dynamic_slice_in_dim(g, item * d_act, d_act, 0) for g in g_in_act]
        out_a = [lax.dynamic_slice_in_dim(g, item * d_act, d_act, 1) for g in g_out_act]

        def aside(blocks, height):
            return [p for b in blocks for p in jnp.split(b, b.shape[0] // height, axis=0)]

        top = jnp.concatenate(left + aside(out, d_pre), axis=1)
        low = jnp.concatenate(left_a + aside(out_a, d_act), axis=1)
        return jnp.concatenate([top, low], axis=0)

    parts = jnp.stack([attn_block(i) for i in turns])
    swapped = lax.ppermute(parts[half:], "dp", [(i, i ^ 1) for i in range(n)])
    parts = add(parts[:half], swapped)

    def by_index(vector):
        return vector.reshape(n, -1, narrow // n).transpose(1, 0, 2).reshape(-1, narrow)

    tiny = [by_index(g) for g in (g_gain_pa, g_gain_pf, g_gain_aa, g_gain_af)] + [g_embed]
    tiny = jnp.concatenate(tiny, axis=0)
    tiny_rows = tiny.shape[0]
    tiny = columns_first(pad_rows(tiny, round_up(tiny_rows, 16)).astype(BF))

    kernel = Kernel(11)
    attn_parts = kernel.flow(Chips(), parts)
    prefix_grad = kernel.flow(Whole(), grad_pre)
    prefix_output = kernel.flow(Whole(), out_pre)
    act_grad = kernel.flow(World(), act_grad)
    tiny = kernel.flow(Spread(), tiny)
    got = kernel.call("finish")
    total = summed(parts[0], got[attn_parts])
    prefix_grad = got[prefix_grad][:length].astype(F32)
    prefix_output = got[prefix_output][:length]
    act_grad = got[act_grad].reshape(n, acts, dims_count)[:, :steps]
    tiny = jnp.sum(got[tiny].astype(F32), axis=(0, 1))
    mine_items = (slot_item[:, None] == lax.broadcasted_iota(jnp.int32, (1, n), 1)).astype(F32)
    mine_turns = (slot_item[:, None] == jnp.stack(turns)[None, :]).astype(F32)
    out_act = out_act.reshape(1, m, n, aq, narrow).astype(F32)
    action_output = jnp.sum(mine_turns[:, None, :, None, None] * out_act, axis=2)
    action_output = action_output.reshape(slot_count, acts, narrow)[:, :steps].astype(BF)
    own_mask = lax.broadcasted_iota(jnp.int32, (slot_count, dims_count), 1) < valid_dims[:, None]
    action_grad = jnp.sum(
        mine_items[:, :, None, None] * act_grad[None], axis=1
    ) * own_mask.astype(F32)[:, None, :]
    grad_gain_pa = tiny[:twice].reshape(-1)
    grad_gain_pf = tiny[twice : 2 * twice].reshape(-1)
    rest = tiny[2 * twice : tiny_rows]

    if even:
        grad_gate_a, grad_up_a, grad_down_a = act_sum
    else:
        act_sum = act_sum[0]
        grad_gate_a = act_sum[:, :d_act].transpose(1, 0, 2).reshape(d_act, n * few)
        grad_up_a = act_sum[:, d_act : 2 * d_act].transpose(1, 0, 2).reshape(d_act, n * few)
        grad_down_a = act_sum[:, 2 * d_act :].transpose(0, 2, 1).reshape(n * few, d_act)
    grad_query, grad_kv = total[:d_pre, :split], total[:d_pre, split : split + kvw]
    grad_out = jnp.concatenate(
        jnp.split(total[:d_pre, split + kvw :], split // d_pre, axis=1), axis=0
    )
    grad_query_a, grad_kv_a = total[d_pre:, :split], total[d_pre:, split : split + kvw]
    grad_out_a = jnp.concatenate(
        jnp.split(total[d_pre:, split + kvw :], split // d_act, axis=1), axis=0
    )
    both = jnp.concatenate([grad_kv, grad_kv_a], axis=0).astype(BF)
    both = lax.all_gather(both, "mp", axis=1, tiled=True).astype(F32)

    return (
        prefix_output,
        action_output,
        prefix_grad,
        action_grad,
        grad_gain_pa,
        grad_query,
        both[:d_pre, :HD],
        both[:d_pre, HD:],
        grad_out,
        grad_gain_pf,
        grad_gate,
        grad_up,
        grad_down,
        rest[2:],
        rest[0],
        grad_query_a,
        both[d_pre:, :HD],
        both[d_pre:, HD:],
        grad_out_a,
        rest[1],
        grad_gate_a,
        grad_up_a,
        grad_down_a,
    )


def solution(mesh):
    return jax.shard_map(
        local,
        mesh=mesh,
        in_specs=(
            P("dp", None),
            P("dp", None, None),
            P("dp"),
            P("dp"),
            P("dp", None),
            P("dp"),
            P("dp", "mp"),
            P("dp", None),
            P("dp", None),
            P("mp", "dp"),
            P("dp"),
            P("dp", "mp"),
            P("dp", "mp"),
            P("mp", "dp"),
            P(None, "dp"),
            P("dp"),
            P("dp", "mp"),
            P("dp", None),
            P("dp", None),
            P("mp", "dp"),
            P("dp"),
            P("dp", "mp"),
            P("dp", "mp"),
            P("mp", "dp"),
            P("dp", None),
            P("dp", None, None),
        ),
        out_specs=(
            P("dp", None),
            P("dp", None, None),
            P("dp", None),
            P("dp", None, None),
            P("dp"),
            P("dp", "mp"),
            P("dp", None),
            P("dp", None),
            P("mp", "dp"),
            P("dp"),
            P("dp", "mp"),
            P("dp", "mp"),
            P("mp", "dp"),
            P(None, "dp"),
            P("dp"),
            P("dp", "mp"),
            P("dp", None),
            P("dp", None),
            P("mp", "dp"),
            P("dp"),
            P("dp", "mp"),
            P("dp", "mp"),
            P("mp", "dp"),
        ),
        check_vma=False,
    )
```

```python
import functools

import jax
import jax.numpy as jnp
from jax import lax
from jax.experimental import pallas as pl
from jax.experimental.pallas import tpu as pltpu
from jax.sharding import PartitionSpec as P

HD = 256
EPS = 1e-06
BF = jnp.bfloat16
F32 = jnp.float32
MESH = pl.DeviceIdType.MESH
HBM = pl.BlockSpec(memory_space=pl.ANY)


def rms_gain(values, gain):
    return values * lax.rsqrt(jnp.mean(values * values, axis=-1, keepdims=True) + EPS) * gain


def norm_backward(values, gain, grad_out):
    unused, pull = jax.vjp(rms_gain, values, gain)
    return pull(grad_out)


def glu_value(gate, upward):
    return jax.nn.gelu(gate, approximate=True) * upward


def glu_backward(gate, upward, grad):
    unused, pull = jax.vjp(glu_value, gate, upward)
    return pull(grad)


def dot_plain(left, right):
    return jnp.dot(left, right, preferred_element_type=F32)


def dot_left(left, right):
    return lax.dot_general(left, right, (((0,), (0,)), ((), ())), preferred_element_type=F32)


def dot_right(left, right):
    return lax.dot_general(left, right, (((1,), (1,)), ((), ())), preferred_element_type=F32)


def round_up(value, step):
    return -(-value // step) * step


def add(left, right):
    return (left.astype(F32) + right.astype(F32)).astype(BF)


def greet(devices):
    barrier = pltpu.get_barrier_semaphore()
    for device in devices:
        pl.semaphore_signal(barrier, inc=1, device_id=device, device_id_type=MESH)
    pl.semaphore_wait(barrier, len(devices))


def at(start, size):
    return pl.ds(pl.multiple_of(start * size, size), size)


class Place:
    def __init__(self, n, m, sent, arrived, first):
        self.n, self.m = n, m
        self.me, self.col = lax.axis_index("dp"), lax.axis_index("mp")
        self.sent, self.arrived, self.first = sent, arrived, first

    def remote(self, src, dst, slot, device):
        return pltpu.make_async_remote_copy(
            src_ref=src,
            dst_ref=dst,
            send_sem=self.sent.at[self.first + slot],
            recv_sem=self.arrived.at[self.first + slot],
            device_id=device,
            device_id_type=MESH,
        )

    def keep(self, src, dst):
        def scoped(buffer):
            pltpu.sync_copy(src, buffer)
            pltpu.sync_copy(buffer, dst)

        pl.run_scoped(scoped, pltpu.VMEM(src.shape, src.dtype))

    def over_dp(self, s):
        return (lax.rem(self.me + s, self.n), self.col)

    def over_mp(self, k):
        return (self.me, self.col ^ k)


def loop(first, last, body):
    lax.fori_loop(first, last, lambda s, carry: (body(s), carry)[1], 0)


class Flow:
    reach = "dp"
    kept = False

    def slots(self, n, m):
        return max(n, m, 4)

    def result(self, shape, n, m):
        return shape

    def each(self, p, src, dst, do):
        pass

    def own(self, p, src, dst):
        return None

    def start(self, p, src, dst):
        self.each(p, src, dst, lambda c: c.start())
        if self.kept:
            p.keep(*self.own(p, src, dst))

    def relay(self, p, src, dst, k):
        return None

    def wait(self, p, src, dst):
        self.each(p, src, dst, lambda c: c.wait())


class Rows(Flow):
    kept = True

    def result(self, shape, n, m):
        return (shape[0] // n, shape[1] * n)

    def own(self, p, src, dst):
        return src.at[at(p.me, src.shape[0] // p.n)], dst.at[:, at(p.me, dst.shape[1] // p.n)]

    def each(self, p, src, dst, do):
        def body(s):
            target = p.over_dp(s)
            block = src.at[at(target[0], src.shape[0] // p.n)]
            do(p.remote(block, dst.at[:, at(p.me, dst.shape[1] // p.n)], s, target))

        loop(1, p.n, body)


class Columns(Flow):
    kept = True

    def result(self, shape, n, m):
        return (shape[0] * n, shape[1] // n)

    def own(self, p, src, dst):
        return src.at[:, at(p.me, src.shape[1] // p.n)], dst.at[at(p.me, dst.shape[0] // p.n)]

    def each(self, p, src, dst, do):
        def body(s):
            target = p.over_dp(s)
            block = src.at[:, at(target[0], src.shape[1] // p.n)]
            do(p.remote(block, dst.at[at(p.me, dst.shape[0] // p.n)], s, target))

        loop(1, p.n, body)


class Each(Flow):
    kept = True

    def own(self, p, src, dst):
        return src.at[p.me], dst.at[p.me]

    def each(self, p, src, dst, do):
        def body(s):
            target = p.over_dp(s)
            do(p.remote(src.at[target[0]], dst.at[p.me], s, target))

        loop(1, p.n, body)


class EachRows(Each):
    def result(self, shape, n, m):
        return (n, shape[0] // n, shape[1])

    def own(self, p, src, dst):
        return src.at[at(p.me, dst.shape[1])], dst.at[p.me]

    def each(self, p, src, dst, do):
        def body(s):
            target = p.over_dp(s)
            do(p.remote(src.at[at(target[0], dst.shape[1])], dst.at[p.me], s, target))

        loop(1, p.n, body)


class Chips(Flow):
    def each(self, p, src, dst, do):
        loop(1, p.n // 2, lambda s: do(p.remote(src.at[s], dst.at[s], s, p.over_dp(2 * s))))


class Core(Flow):
    def result(self, shape, n, m):
        return (shape[0] // 2, shape[1])

    def each(self, p, src, dst, do):
        half = src.shape[0] // 2
        do(p.remote(src.at[pl.ds(half, half)], dst, 0, (p.me ^ 1, p.col)))


class CoreRows(Flow):
    def result(self, shape, n, m):
        return (shape[0] // 2, shape[1])

    def cut(self, ref, i, count):
        return ref.at[at(i, ref.shape[0] // count)]

    def each(self, p, src, dst, do):
        def body(c):
            block = self.cut(src, 2 * c + lax.rem(p.me + 1, 2), p.n)
            do(p.remote(block, self.cut(dst, c, p.n // 2), c, (p.me ^ 1, p.col)))

        loop(0, p.n // 2, body)


class ChipRows(CoreRows):
    def result(self, shape, n, m):
        return (n // 2, shape[0] // (n // 2), shape[1])

    def each(self, p, src, dst, do):
        def body(s):
            target = p.over_dp(2 * s)
            do(p.remote(self.cut(src, target[0] // 2, p.n // 2), dst.at[s], s, target))

        loop(1, p.n // 2, body)


class Line(Flow):
    def __init__(self, place=None, result=None, share=False):
        self.place = place or Line.in_turn
        self.shape = result
        self.share = share
        self.reach = "both" if share else "dp"

    def slots(self, n, m):
        return 2 * n + (n * m if self.share else 0)

    def in_turn(ref, i, j):
        chips = lax.axis_size("dp") // 2
        chip = lax.rem(i // 2 - j // 2 + chips, chips)
        return ref.at[chip + chips * lax.rem(i + j, 2)]

    def result(self, shape, n, m):
        return self.shape or (n,) + shape

    def origin(self, p, first, way, k):
        return lax.rem(first - (2, -2)[way] * k + 2 * p.n, p.n)

    def along(self, p, src, dst, way, k):
        i = self.origin(p, p.me, way, k - 1)
        target = lax.rem(p.me + (2, -2)[way] + p.n, p.n)
        source = src if k == 1 else self.place(dst, i, p.me)
        slot = way * p.n // 2 + k
        return p.remote(source, self.place(dst, i, target), slot, (target, p.col))

    def across(self, p, src, dst, way, k):
        i = self.origin(p, p.me, way, k)
        source = src if k == 0 else self.place(dst, i, p.me)
        slot = (2 + way) * p.n // 2 + k
        return p.remote(source, self.place(dst, i, p.me ^ 1), slot, (p.me ^ 1, p.col))

    def passed(self, p, dst, i, k, source=None):
        block = self.place(dst, i, p.me)
        source = block if source is None else source
        return p.remote(source, block, 2 * p.n + i * p.m + k, p.over_mp(k))

    def receives(self, p, way, k):
        chip = p.me // 2
        if k == 0:
            return chip >= 0
        return chip >= k if way == 0 else chip < p.n // 2 - k

    def sends(self, p, way, k):
        chip = p.me // 2
        beyond = chip < p.n // 2 - 1 if way == 0 else chip > 0
        return beyond & self.receives(p, way, k - 1)

    def start(self, p, src, dst):
        for way in (0, 1):
            pl.when(self.sends(p, way, 1))(self.along(p, src, dst, way, 1).start)
        self.across(p, src, dst, 0, 0).start()
        self.hand(p, dst, p.me, src)
        p.keep(src, self.place(dst, p.me, p.me))

    def hand(self, p, dst, i, source=None):
        if self.share:
            for k in range(1, p.m):
                self.passed(p, dst, i, k, source).start()

    def crossed(self, p, src, dst, way, k):
        self.across(p, src, dst, way, k).wait_recv()
        self.hand(p, dst, self.origin(p, p.me ^ 1, way, k))

    def relay(self, p, src, dst, k):
        if k == 1:
            self.crossed(p, src, dst, 0, 0)
        for way in (0, 1):

            @pl.when(self.receives(p, way, k))
            def _(way=way):
                self.along(p, src, dst, way, k).wait_recv()
                self.across(p, src, dst, way, k).start()
                self.hand(p, dst, self.origin(p, p.me, way, k))

            if k < p.n // 2 - 1:
                pl.when(self.sends(p, way, k + 1))(self.along(p, src, dst, way, k + 1).start)
            if k > 1:
                before = functools.partial(self.crossed, p, src, dst, way, k - 1)
                pl.when(self.receives(p, way, k - 1))(before)

    def wait(self, p, src, dst):
        last = p.n // 2 - 1
        for way in (0, 1):
            end = functools.partial(self.crossed, p, src, dst, way, last)
            pl.when(self.receives(p, way, last))(end)
        self.across(p, src, dst, 0, 0).wait_send()
        for way in (0, 1):
            for k in range(1, last + 1):
                pl.when(self.sends(p, way, k))(self.along(p, src, dst, way, k).wait_send)
                pl.when(self.receives(p, way, k))(self.across(p, src, dst, way, k).wait_send)
        if self.share:
            for k in range(1, p.m):
                loop(0, p.n, lambda i, k=k: self.passed(p, dst, i, k).wait())


class Pass(Flow):
    reach = "mp"
    kept = True
    parts = 8

    def __init__(self, axis):
        self.axis = axis

    def slots(self, n, m):
        return max(4, m) * self.parts

    def result(self, shape, n, m):
        return (shape[0], m * shape[1]) if self.axis else (m * shape[0], shape[1])

    def spot(self, p, src, dst, k, c=None):
        rows, width = src.shape
        first, count = (0, rows) if c is None else (c * (rows // self.parts), rows // self.parts)
        if self.axis:
            return dst.at[pl.ds(first, count), pl.ds(k * width, width)]
        return dst.at[pl.ds(k * rows + first, count)]

    def own(self, p, src, dst):
        return src, self.spot(p, src, dst, 0)

    def direct(self, p, src, dst, k, c):
        few = src.shape[0] // self.parts
        block = src.at[pl.ds(c * few, few)]
        slot = k * self.parts + c
        return p.remote(block, self.spot(p, src, dst, k, c), slot, p.over_mp(k))

    def turned(self, p, src, dst, c):
        via = 1 + c % 2
        source = self.spot(p, src, dst, via, c)
        slot = 3 * self.parts + c
        return p.remote(source, self.spot(p, src, dst, 3, c), slot, p.over_mp(3 - via))

    def each(self, p, src, dst, do):
        for c in range(self.parts):
            for k in range(1, 3 if p.m == 4 else p.m):
                do(self.direct(p, src, dst, k, c))

    def start(self, p, src, dst):
        self.each(p, src, dst, lambda c: c.start())

    def relay(self, p, src, dst, k):
        if p.m == 4:
            for c in range((k - 1) * self.parts // 2, k * self.parts // 2):
                self.direct(p, src, dst, 1 + c % 2, c).wait_recv()
                self.turned(p, src, dst, c).start()

    def wait(self, p, src, dst):
        p.keep(*self.own(p, src, dst))
        for c in range(self.parts):
            for k in range(1, 3 if p.m == 4 else p.m):
                copy = self.direct(p, src, dst, k, c)
                (copy.wait_send if p.m == 4 and k == 1 + c % 2 else copy.wait)()
            if p.m == 4:
                self.turned(p, src, dst, c).wait()


class Parts(Flow):
    reach = "mp"

    def result(self, shape, n, m):
        return shape if len(shape) == 3 else (m, shape[0] // m, shape[1])

    def each(self, p, src, dst, do):
        for k in range(1, p.m):
            target = p.over_mp(k)
            if len(src.shape) == 3:
                block = src.at[target[1]]
            else:
                block = src.at[at(target[1], src.shape[0] // p.m)]
            do(p.remote(block, dst.at[k], k, target))


class Swaps(Parts):
    def each(self, p, src, dst, do):
        for k in range(1, p.m):
            do(p.remote(src.at[k], dst.at[k], k, p.over_mp(k)))


class Whole(Flow):
    reach = "mp"
    kept = True

    def result(self, shape, n, m):
        return (m * shape[0], shape[1])

    def own(self, p, src, dst):
        return src, dst.at[at(p.col, src.shape[0])]

    def each(self, p, src, dst, do):
        for k in range(1, p.m):
            do(p.remote(src, dst.at[at(p.col, src.shape[0])], k, p.over_mp(k)))


class Swap(Flow):
    reach = "mp"

    def __init__(self, k):
        self.k = k

    def each(self, p, src, dst, do):
        do(p.remote(src, dst, 0, p.over_mp(self.k)))


class First(Flow):
    reach = "mp"

    def __init__(self, axis):
        self.axis = axis

    def result(self, shape, n, m):
        if self.axis:
            return (4, shape[0] // 2, shape[1] // m)
        return (4, shape[0] // m, shape[1] // 2)

    def each(self, p, src, dst, do):
        width, deep = src.shape[self.axis] // p.m, src.shape[1 - self.axis] // 2
        for k, part in enumerate((1, 3, 2, 3)):
            block, half = pl.ds(part * width, width), pl.ds(k // 2 * deep, deep)
            source = src.at[half, block] if self.axis else src.at[block, half]
            do(p.remote(source, dst.at[k], k, p.over_mp(1 + k // 2)))


class World(Flow):
    reach = "world"
    kept = True

    def slots(self, n, m):
        return n * m

    def result(self, shape, n, m):
        return (n, m) + shape

    def block(self, src, i):
        return src

    def own(self, p, src, dst):
        return self.block(src, p.me), dst.at[p.me, p.col]

    def each(self, p, src, dst, do):
        for k in range(p.m):

            def body(s, k=k):
                target = (lax.rem(p.me + s, p.n), p.col ^ k)
                copy = p.remote(
                    self.block(src, target[0]), dst.at[p.me, p.col], s * p.m + k, target
                )
                do(copy)

            loop(0 if k else 1, p.n, body)


class Spread(World):
    def result(self, shape, n, m):
        return (n, m) + shape[1:]

    def block(self, src, i):
        return src.at[i]


class Kernel:
    def __init__(self, collective_id):
        self.collective_id = collective_id
        self.inputs, self.outputs, self.flows, self.steps = [], [], [], []

    def operand(self, source):
        if isinstance(source, int):
            return ("out", source)
        self.inputs.append(source)
        return ("in", len(self.inputs) - 1)

    def shape_of(self, source):
        return self.outputs[source] if isinstance(source, int) else source

    def new_output(self, shape, dtype):
        self.outputs.append(jax.ShapeDtypeStruct(shape, dtype))
        return len(self.outputs) - 1

    def flow(self, kind, source, now=True, into=None):
        n, m = lax.axis_size("dp"), lax.axis_size("mp")
        like = self.shape_of(source)
        out = into
        if into is None:
            out = self.new_output(kind.result(like.shape, n, m), like.dtype)
        name = out if into is None else -1 - len(self.flows)
        self.flows.append((kind, self.operand(source), out, name))
        if now:
            self.go(name)
        return name

    def go(self, name):
        self.steps.append(("start", name))

    def relay(self, name, k):
        self.steps.append(("relay", name, k))

    def ready(self, name):
        self.steps.append(("wait", name))

    def job(self, body, sources, shapes, dtype=BF, into=None):
        outs = into or [self.new_output(s, dtype) for s in shapes]
        self.steps.append(("job", body, [self.operand(s) for s in sources], outs))
        return outs if len(outs) > 1 else outs[0]

    def call(self, name):
        n, m = lax.axis_size("dp"), lax.axis_size("mp")
        takes, gives = len(self.inputs), len(self.outputs)
        flows, steps = self.flows, self.steps
        rows = {flow[3]: row for row, flow in enumerate(flows)}
        reach = {flow[0].reach for flow in flows}
        firsts = [0]
        for flow in flows:
            firsts.append(firsts[-1] + flow[0].slots(n, m))

        def kernel(*refs):
            ins, outs = refs[:takes], refs[takes : takes + gives]
            sent, arrived = refs[takes + gives :]
            me, col = lax.axis_index("dp"), lax.axis_index("mp")
            if "world" in reach:
                greet([(lax.rem(me + s, n), col ^ k) for s in range(n) for k in range(m) if s or k])
            else:
                column = [(lax.rem(me + s, n), col) for s in range(1, n)]
                row = [(me, col ^ k) for k in range(1, m)]
                greet(
                    (column if reach & {"dp", "both"} else [])
                    + (row if reach & {"mp", "both"} else [])
                )

            def ref(operand):
                return (ins if operand[0] == "in" else outs)[operand[1]]

            def act(what, name, *rest):
                kind, source, out, unused = flows[rows[name]]
                place = Place(n, m, sent, arrived, firsts[rows[name]])
                getattr(kind, what)(place, ref(source), outs[out], *rest)

            ended = set()
            for step in steps:
                if step[0] == "job":
                    step[1]([ref(s) for s in step[2]], [outs[o] for o in step[3]])
                else:
                    act(*step)
                    if step[0] == "wait":
                        ended.add(step[1])
            for flow in flows:
                if flow[3] not in ended:
                    act("wait", flow[3])

        return pl.pallas_call(
            kernel,
            out_shape=self.outputs,
            in_specs=[HBM] * takes,
            out_specs=[HBM] * gives,
            scratch_shapes=[
                pltpu.SemaphoreType.DMA((firsts[-1],)),
                pltpu.SemaphoreType.DMA((firsts[-1],)),
            ],
            compiler_params=pltpu.CompilerParams(
                collective_id=self.collective_id,
                has_side_effects=True,
                vmem_limit_bytes=56 << 20,
            ),
            name=name,
        )(*self.inputs)


def tile(size, most):
    return max(t for t in range(16, most + 1, 16) if size % t == 0)


def products_plain(inputs, outputs):
    a, b = inputs
    (rows, depth), width = a.shape, b.shape[1]
    bm, bn = tile(rows, 832), tile(width, 512)

    def body(a_ref, b_ref, o_ref):
        o_ref[...] = dot_plain(a_ref[...], b_ref[...]).astype(BF)

    pltpu.emit_pipeline(
        body,
        grid=(width // bn, rows // bm),
        in_specs=[
            pl.BlockSpec((bm, depth), lambda j, i: (i, 0)),
            pl.BlockSpec((depth, bn), lambda j, i: (0, j)),
        ],
        out_specs=[pl.BlockSpec((bm, bn), lambda j, i: (i, j))],
    )(a, b, outputs[0])


def products_right(inputs, outputs):
    pairs = len(inputs) // 2
    rows, width = inputs[0].shape[0], inputs[1].shape[0]
    bm, bn = tile(rows, 832), tile(width, 512)

    def body(*refs):
        total = dot_right(refs[0][...], refs[1][...])
        for p in range(1, pairs):
            total = total + dot_right(refs[2 * p][...], refs[2 * p + 1][...])
        refs[-1][...] = total.astype(BF)

    specs = []
    for p in range(pairs):
        depth = inputs[2 * p].shape[1]
        specs.append(pl.BlockSpec((bm, depth), lambda i, j: (i, 0)))
        specs.append(pl.BlockSpec((bn, depth), lambda i, j: (j, 0)))
    pltpu.emit_pipeline(
        body,
        grid=(rows // bm, width // bn),
        in_specs=specs,
        out_specs=[pl.BlockSpec((bm, bn), lambda i, j: (i, j))],
    )(*inputs, outputs[0])


def products_left(inputs, outputs):
    a, rest = inputs[0], inputs[1:]
    (depth, rows), width = a.shape, rest[0].shape[1]
    bm, bn = tile(rows, 1024), tile(width, 512)
    count = len(rest)

    def body(a_ref, *refs):
        for p in range(count):
            refs[count + p][...] = dot_left(a_ref[...], refs[p][...]).astype(BF)

    pltpu.emit_pipeline(
        body,
        grid=(rows // bm, width // bn),
        in_specs=[pl.BlockSpec((depth, bm), lambda i, j: (0, i))]
        + [pl.BlockSpec((depth, bn), lambda i, j: (0, j))] * count,
        out_specs=[pl.BlockSpec((bm, bn), lambda i, j: (i, j))] * count,
    )(a, *rest, *outputs)


def hidden_forward(part, parts, inputs, outputs):
    h, w_gate, w_up = inputs
    (rows, depth), width = h.shape, w_gate.shape[1] // parts
    cut = pl.ds(part * width, width)
    w_gate, w_up = w_gate.at[:, cut], w_up.at[:, cut]
    outputs = [o.at[:, cut] for o in outputs]
    bm, bn = tile(rows, 832), tile(width, 512)

    def body(h_ref, gate_w, up_w, gate_ref, up_ref, hidden_ref):
        gate = dot_plain(h_ref[...], gate_w[...])
        upward = dot_plain(h_ref[...], up_w[...])
        gate_ref[...] = gate.astype(BF)
        up_ref[...] = upward.astype(BF)
        hidden_ref[...] = glu_value(gate, upward).astype(BF)

    block = pl.BlockSpec((bm, bn), lambda j, i: (i, j))
    pltpu.emit_pipeline(
        body,
        grid=(width // bn, rows // bm),
        in_specs=[pl.BlockSpec((bm, depth), lambda j, i: (i, 0))]
        + [pl.BlockSpec((depth, bn), lambda j, i: (0, j))] * 2,
        out_specs=[block] * 3,
    )(h, w_gate, w_up, *outputs)


def hidden_backward(inputs, outputs):
    gz, w_down, gate, upward = inputs
    (rows, depth), width = gz.shape, w_down.shape[0]
    bm, bn = tile(rows, 832), tile(width, 512)

    def body(gz_ref, down_w, gate_ref, up_ref, dgate_ref, dup_ref):
        grad = dot_right(gz_ref[...], down_w[...])
        dgate, dup = glu_backward(gate_ref[...].astype(F32), up_ref[...].astype(F32), grad)
        dgate_ref[...] = dgate.astype(BF)
        dup_ref[...] = dup.astype(BF)

    block = pl.BlockSpec((bm, bn), lambda j, i: (i, j))
    pltpu.emit_pipeline(
        body,
        grid=(width // bn, rows // bm),
        in_specs=[
            pl.BlockSpec((bm, depth), lambda j, i: (i, 0)),
            pl.BlockSpec((bn, depth), lambda j, i: (j, 0)),
            block,
            block,
        ],
        out_specs=[block] * 2,
    )(gz, w_down, gate, upward, *outputs)


def attend_forward(inputs, outputs):
    query, keys, values, seg_q, seg_k = inputs
    probs, mixed = outputs
    total = query.shape[0]
    rows = tile(total, 448)

    def body(q_ref, k_ref, v_ref, sq_ref, sk_ref, p_ref, o_ref):
        allowed = sq_ref[:, :1] >= sk_ref[:1]
        scores = dot_right(q_ref[...], k_ref[...]) * HD ** (-0.5)
        scores = jnp.where(allowed, scores, -1e30)
        raised = jnp.exp(scores - jnp.max(scores, axis=-1, keepdims=True))
        p = (raised / jnp.sum(raised, axis=-1, keepdims=True)).astype(BF)
        p_ref[...] = p
        o_ref[...] = dot_plain(p, v_ref[...]).astype(BF)

    def rest(shape):
        return pl.BlockSpec(shape, lambda i: (0, 0))

    pltpu.emit_pipeline(
        body,
        grid=(total // rows,),
        in_specs=[
            pl.BlockSpec((rows, HD), lambda i: (i, 0)),
            rest(keys.shape),
            rest(values.shape),
            pl.BlockSpec((rows, seg_q.shape[1]), lambda i: (i, 0)),
            rest(seg_k.shape),
        ],
        out_specs=[
            pl.BlockSpec((rows, total), lambda i: (i, 0)),
            pl.BlockSpec((rows, HD), lambda i: (i, 0)),
        ],
    )(query, keys, values, seg_q, seg_k, probs, mixed)


def attend_backward(heads, inputs, outputs):
    probs, query = inputs[:heads], inputs[heads : 2 * heads]
    keys, values, grad = inputs[2 * heads :]
    grad_query, (both, shares) = outputs[:heads], outputs[heads:]
    total, scale = keys.shape[0], HD ** (-0.5)
    rows = tile(total, 448)
    width = shares.shape[2]

    def scoped(sums, rounded, parted):
        sums[...] = jnp.zeros_like(sums)

        def body(*refs):
            k_ref, v_ref, g_ref = refs[2 * heads : 2 * heads + 3]
            for h in range(heads):
                g = g_ref[:, h * HD : (h + 1) * HD]
                p, q = refs[h][...], refs[heads + h][...]
                wide_p = p.astype(F32)
                dp = dot_right(g, v_ref[...])
                ds = wide_p * (dp - jnp.sum(wide_p * dp, axis=-1, keepdims=True))
                ds = ds.astype(BF)
                refs[2 * heads + 3 + h][...] = (dot_plain(ds, k_ref[...]) * scale).astype(BF)
                sums[:, :HD] += dot_left(ds, q) * scale
                sums[:, HD:] += dot_left(p, g)

        def rest(ref):
            return pl.BlockSpec(ref.shape, lambda i: (0, 0))

        block = pl.BlockSpec((rows, HD), lambda i: (i, 0))
        pltpu.emit_pipeline(
            body,
            grid=(total // rows,),
            in_specs=[pl.BlockSpec((rows, total), lambda i: (i, 0))] * heads
            + [block] * heads
            + [rest(keys), rest(values), pl.BlockSpec((rows, heads * HD), lambda i: (i, 0))],
            out_specs=[block] * heads,
        )(*probs, *query, keys, values, grad, *grad_query)
        rounded[...] = sums[...].astype(BF)
        for k in range(shares.shape[0]):
            parted[k] = sums[:, k * width : (k + 1) * width].astype(BF)
        pltpu.sync_copy(rounded, both)
        pltpu.sync_copy(parted, shares)

    pl.run_scoped(
        scoped,
        pltpu.VMEM((total, 2 * HD), F32),
        pltpu.VMEM((total, 2 * HD), BF),
        pltpu.VMEM(shares.shape, BF),
    )


def rows_from(first, count, body):
    return lambda inputs, outputs: body([inputs[0].at[pl.ds(first, count)]] + inputs[1:], outputs)


class Halves:
    def __init__(self, whole, axis):
        self.whole, self.axis = whole, axis

    def take(self, got):
        top, low = jnp.split(self.whole, 2, axis=1 - self.axis)
        t, b = jnp.split(top, 4, axis=self.axis), jnp.split(low, 4, axis=self.axis)
        self.top, self.next_y = add(t[0], got[0]), add(t[2], got[1])
        self.low, self.next_x = add(b[0], got[2]), add(b[1], got[3])

    def second(self, kernel):
        self.from_y = kernel.flow(Swap(2), self.next_y)
        self.from_x = kernel.flow(Swap(1), self.next_x)

    def total(self, got):
        return jnp.concatenate(
            [add(self.top, got[self.from_y]), add(self.low, got[self.from_x])], axis=1 - self.axis
        )


class Direct:
    def __init__(self, whole, axis):
        parts = jnp.split(whole, lax.axis_size("mp"), axis=axis)
        total = parts[0].astype(F32)
        for k in range(1, len(parts)):
            pairs = [(i, i ^ k) for i in range(len(parts))]
            total = total + lax.ppermute(parts[k], "mp", pairs).astype(F32)
        self.sum = total.astype(BF)

    def take(self, got):
        return None

    def second(self, kernel):
        return None

    def total(self, got):
        return self.sum


def local(
    prefix_input,
    action_input,
    valid_dims,
    slot_item,
    segments,
    pre_gain_attn,
    pre_query,
    pre_key,
    pre_value,
    pre_output,
    pre_gain_ffn,
    pre_gate,
    pre_up,
    pre_down,
    act_embed,
    act_gain_attn,
    act_query,
    act_key,
    act_value,
    act_output,
    act_gain_ffn,
    act_gate,
    act_up,
    act_down,
    prefix_cotangent,
    action_cotangent,
):
    n, m = lax.axis_size("dp"), lax.axis_size("mp")
    me, col = lax.axis_index("dp"), lax.axis_index("mp")
    length, wide = prefix_input.shape
    slot_count, steps, dims_count = action_input.shape
    narrow = action_cotangent.shape[2]
    rq = round_up(-(-length // m), 16)
    aq = round_up(-(-steps // m), 16)
    rows, acts = m * rq, m * aq
    total_rows = rows + acts
    half = n // 2
    heads = pre_query.shape[1] // HD
    split = heads * HD
    scale = HD ** (-0.5)
    kvw = 2 * HD // m
    d_pre, d_act = pre_query.shape[0], act_query.shape[0]
    few = act_gate.shape[1] // n
    lanes = 128
    twice = wide // narrow
    turns = [lax.rem(me + 2 * k, n) for k in range(half)]
    turns = turns + [t ^ 1 for t in turns]

    def own(array, count):
        return lax.dynamic_slice_in_dim(array, col * count, count, 0)

    def pad_rows(array, count):
        return jnp.pad(array, ((0, count - array.shape[0]), (0, 0)))

    def lane_rows(array):
        flat = array.reshape(-1)
        count = round_up(-(-flat.shape[0] // lanes), 16)
        return jnp.pad(flat, (0, count * lanes - flat.shape[0])).reshape(count, lanes)

    def columns_first(array):
        return array.reshape(array.shape[0], n, -1).transpose(1, 0, 2)

    smalls = [pre_gain_attn, pre_gain_ffn, act_gain_attn, act_gain_ffn, act_embed, action_input]
    small = jnp.concatenate([lane_rows(a) for a in smalls], axis=0)
    ints = jnp.pad(jnp.stack([slot_item, valid_dims]), ((0, 6), (0, lanes - slot_count)))
    cot_rows = lax.dynamic_slice_in_dim(
        jnp.pad(action_cotangent, ((0, 0), (0, acts - steps), (0, 0))), col * aq, aq, 1
    ).reshape(slot_count * aq, narrow)

    def share_of(key, value):
        return own(jnp.concatenate([key, value], axis=1).T, kvw).T

    def by_rows(size):
        return lambda ref, i, j: ref.at[at(i, size)]

    def by_columns(size):
        return lambda ref, i, j: ref.at[:, at(i, size)]

    def by_share(size):
        return lambda ref, i, j: ref.at[lax.axis_index("mp"), at(i, size)]

    def by_lead(ref, i, j):
        return ref.at[i]

    kernel = Kernel(1)
    aligned = kvw % lanes == 0
    in_pre, in_act = (wide, split + 2 * HD), (narrow, split + 2 * HD)
    kv_pre, kv_act = share_of(pre_key, pre_value), share_of(act_key, act_value)

    def in_columns(size, share):
        def place(ref, i, j):
            start = split + lax.axis_index("mp") * kvw if share else 0
            columns = pl.ds(pl.multiple_of(start, lanes), kvw if share else split)
            return ref.at[at(i, size), columns]

        return place

    if aligned:
        w_in_pre = kernel.flow(Line(in_columns(d_pre, True), in_pre, True), kv_pre)
        w_in_act = kernel.flow(Line(in_columns(d_act, True), in_act, True), kv_act)
        lines = [w_in_pre, w_in_act]
    else:
        w_kv_pre = kernel.flow(Line(by_share(d_pre), (m, wide, kvw), True), kv_pre)
        w_kv_act = kernel.flow(Line(by_share(d_act), (m, narrow, kvw), True), kv_act)
        lines = [w_kv_pre, w_kv_act]
    small = kernel.flow(Line(by_lead, (n,) + small.shape), small)
    ints = kernel.flow(Line(by_lead, (n, 8, lanes)), ints)
    if aligned:
        w_q_pre = kernel.flow(Line(in_columns(d_pre, False)), pre_query, into=w_in_pre)
        w_q_act = kernel.flow(Line(in_columns(d_act, False)), act_query, into=w_in_act)
    else:
        w_q_pre = kernel.flow(Line(by_rows(d_pre), (wide, split)), pre_query)
        w_q_act = kernel.flow(Line(by_rows(d_act), (narrow, split)), act_query)
    w_out_pre = kernel.flow(Line(by_columns(d_pre), (split, wide)), pre_output)
    w_out_act = kernel.flow(Line(by_lead, (n, split, d_act)), act_output)
    cot_all = kernel.flow(Line(by_lead, (n, slot_count * aq, narrow)), cot_rows)
    lines += [small, ints, w_q_pre, w_q_act, w_out_pre, w_out_act, cot_all]
    for k in range(1, half):
        for out in lines:
            kernel.relay(out, k)
    got = kernel.call("gather")
    small, ints, cot_all = got[small], got[ints], got[cot_all]
    w_out_pre, w_out_act = got[w_out_pre], got[w_out_act]
    if aligned:
        w_in_pre, w_in_act = got[w_in_pre], got[w_in_act]
    else:
        w_in_pre = jnp.concatenate([got[w_q_pre]] + [got[w_kv_pre][k] for k in range(m)], axis=1)
        w_in_act = jnp.concatenate([got[w_q_act]] + [got[w_kv_act][k] for k in range(m)], axis=1)
    smalls_all, begin = [], 0
    for a in smalls:
        count = round_up(-(-a.size // lanes), 16)
        flat = small[:, begin : begin + count].reshape(n, -1)[:, : a.size]
        smalls_all.append(flat.reshape((n,) + a.shape))
        begin += count
    gain_pa, gain_pf, gain_aa, gain_af = [g.reshape(-1).astype(F32) for g in smalls_all[:4]]
    embed = smalls_all[4].transpose(1, 0, 2).reshape(dims_count, narrow)
    act_all = smalls_all[5].reshape(n * slot_count, steps, dims_count)
    slot_all = ints[:, 0, :slot_count].reshape(-1)
    valid_all = ints[:, 1, :slot_count].reshape(-1)
    w_out_act = w_out_act.transpose(1, 0, 2).reshape(split, narrow)

    mine = (slot_all == me).astype(F32)
    valid = jnp.sum(mine * valid_all.astype(F32))
    dims_mask = (lax.broadcasted_iota(jnp.int32, (1, dims_count), 1).astype(F32) < valid).astype(BF)
    act_in = jnp.sum(mine[:, None, None] * act_all.astype(F32), axis=0).astype(BF) * dims_mask
    act_in = pad_rows(act_in, acts)

    x_pre = pad_rows(prefix_input, rows).astype(F32)
    h1_pre = rms_gain(x_pre, gain_pa).astype(BF)
    x_act = dot_plain(act_in, embed)
    h1_act = rms_gain(x_act, gain_aa).astype(BF)
    into = jnp.concatenate(
        [dot_plain(h1_pre, w_in_pre).astype(BF), dot_plain(h1_act, w_in_act).astype(BF)], axis=0
    )
    query = [into[:, h * HD : (h + 1) * HD] for h in range(heads)]
    keys, values = into[:, split : split + HD], into[:, split + HD :]
    last, never = 1 << 10, 1 << 20
    seg = jnp.pad(segments[0], (0, rows - length), constant_values=never)
    seg_q = jnp.concatenate([jnp.minimum(seg, last), jnp.full((acts,), last, jnp.int32)])
    own_keys = jnp.where(jnp.arange(acts, dtype=jnp.int32) < steps, last, never)
    seg_k = jnp.concatenate([seg, own_keys])
    seg_q = jnp.broadcast_to(seg_q[:, None], (total_rows, lanes))
    seg_k = jnp.broadcast_to(seg_k[None, :], (8, total_rows))

    gz_pre = own(pad_rows(prefix_cotangent, rows), rq)
    even = few % lanes == 0 and d_act % lanes == 0
    if not even:
        act_weights = jnp.concatenate(
            [
                columns_first(act_gate),
                columns_first(act_up),
                act_down.reshape(n, few, d_act).transpose(0, 2, 1),
            ],
            axis=1,
        )

    def project(first, count):
        def body(inputs, outputs):
            pairs = len(inputs) - 1
            w_out = inputs[-1]
            width = w_out.shape[1]
            bm, bn = tile(count, 416), tile(width, 1024)

            def step(*refs):
                value = dot_plain(refs[0][...], refs[1][...])
                for h in range(1, pairs):
                    value = value + dot_plain(refs[2 * h][...], refs[2 * h + 1][...])
                refs[-1][...] = value.astype(BF)

            operands, specs = [], []
            for h in range(pairs):
                operands += [inputs[h].at[pl.ds(first, count)], w_out.at[pl.ds(h * HD, HD)]]
                specs += [
                    pl.BlockSpec((bm, HD), lambda j, i: (i, 0)),
                    pl.BlockSpec((HD, bn), lambda j, i: (0, j)),
                ]
            pltpu.emit_pipeline(
                step,
                grid=(width // bn, count // bm),
                in_specs=specs,
                out_specs=[pl.BlockSpec((bm, bn), lambda j, i: (i, j))],
            )(*operands, outputs[0])

        return body

    kernel = Kernel(2)
    gate_own = kernel.flow(Columns(), pre_gate)
    up_own = kernel.flow(Columns(), pre_up, now=False)
    probs, mixed = [], []
    for h in range(heads):
        p, o = kernel.job(
            attend_forward,
            [query[h], keys, values, seg_q, seg_k],
            [(total_rows, total_rows), (total_rows, HD)],
        )
        probs.append(p)
        mixed.append(o)
        if h == 0:
            kernel.go(up_own)
    y_pre = kernel.job(project(0, rows), mixed + [w_out_pre], [(rows, wide)])
    y_act = kernel.job(project(rows, acts), mixed + [w_out_act], [(acts, narrow)])
    y_pre_parts = kernel.flow(Parts(), y_pre)
    y_act_parts = kernel.flow(Parts(), y_act)
    kernel.ready(gate_own)
    w_gate = kernel.flow(Pass(1), gate_own)
    down_own = kernel.flow(Rows(), pre_down)
    kernel.relay(w_gate, 1)
    kernel.relay(w_gate, 2)
    got = kernel.call("attend")
    probs, mixed = [got[p] for p in probs], [got[o] for o in mixed]
    up_own, down_own, w_gate = got[up_own], got[down_own], got[w_gate]

    def summed(first, parts):
        value = first.astype(F32)
        for k in range(1, parts.shape[0]):
            value = value + parts[k].astype(F32)
        return value

    x2_pre = own(x_pre, rq) + summed(own(got[y_pre], rq), got[y_pre_parts])
    x2_act = own(x_act, aq) + summed(own(got[y_act], aq), got[y_act_parts])
    h2_pre = rms_gain(x2_pre, gain_pf).astype(BF)
    h2_act = rms_gain(x2_act, gain_af).astype(BF)

    kernel = Kernel(3)
    h2_pre = kernel.flow(Line(), h2_pre)
    h2_act = kernel.flow(Line(by_lead, (n, aq, narrow)), h2_act)
    w_up = kernel.flow(Pass(1), up_own)
    if even:
        act_own = [kernel.flow(Columns(), act_gate), kernel.flow(Columns(), act_up)]
        act_own.append(kernel.flow(Rows(), act_down))
    else:
        act_own = [kernel.flow(Each(), act_weights)]
    for k in range(1, half):
        kernel.relay(h2_pre, k)
        kernel.relay(h2_act, k)
        if k < 3:
            kernel.relay(w_up, k)
    got = kernel.call("spread")
    act_own = [got[a] for a in act_own]
    h2_pre, h2_act = got[h2_pre].reshape(n * rq, wide), got[h2_act].reshape(n * aq, narrow)
    w_up = got[w_up]
    items, units = h2_pre.shape[0], w_gate.shape[1]
    summing = Halves if m == 4 else Direct

    kernel = Kernel(4)
    gz_all = kernel.flow(Line(), gz_pre)
    w_down = kernel.flow(Pass(0), down_own)
    into = None
    for piece in range(2):
        into = kernel.job(
            functools.partial(hidden_forward, piece, 2),
            [h2_pre, w_gate, w_up],
            [(items, units)] * 3,
            into=into,
        )
        kernel.relay(gz_all, piece + 1)
    kernel.relay(w_down, 1)
    kernel.relay(w_down, 2)
    for k in range(3, half):
        kernel.relay(gz_all, k)
    got = kernel.call("hidden")
    gate, upward, hidden = [got[o] for o in into]
    w_down, gz_pre_all = got[w_down], got[gz_all].reshape(n * rq, wide)

    kernel = Kernel(5)
    if even:
        act_all_w = [kernel.flow(Pass(axis), a) for axis, a in zip((1, 1, 0), act_own)]
    else:
        act_all_w = [kernel.flow(Pass(0), act_own[0].reshape(n * 3 * d_act, few))]
    g_down = kernel.job(products_left, [hidden, gz_pre_all], [(units, wide)])
    first = kernel.flow(First(0), g_down) if m == 4 else None
    z_p = kernel.job(products_plain, [hidden, w_down], [(items, wide)])
    z_p_core = kernel.flow(Core(), z_p)
    for k in (1, 2):
        for a in act_all_w:
            kernel.relay(a, k)
    dgate, dup = kernel.job(
        hidden_backward, [gz_pre_all, w_down, gate, upward], [(items, units)] * 2
    )
    got = kernel.call("hidden_grads")
    dgate, dup = got[dgate], got[dup]
    g_down = summing(got[g_down], 0)
    g_down.take(got[first] if m == 4 else None)

    def pair_sum(parts, other):
        return add(parts[: other.shape[0]], other).reshape(half, -1, other.shape[1])

    z_p = pair_sum(got[z_p], got[z_p_core])
    if even:
        act_gate_w, act_up_w, act_down_w = [got[a] for a in act_all_w]
    else:
        act_all_w = got[act_all_w[0]].reshape(m, n, 3, d_act, few).transpose(2, 1, 3, 0, 4)
        act_gate_w, act_up_w, act_down_w = act_all_w.reshape(3, narrow, m * few)
        act_down_w = act_down_w.T

    match = (lax.broadcasted_iota(jnp.int32, (n, 1), 0) == slot_all[None, :]).astype(BF)
    cot_all = cot_all.reshape(n * slot_count, aq * narrow)
    gz_act_all = dot_plain(match, cot_all).astype(BF).reshape(n * aq, narrow)
    gz_act = lax.dynamic_slice_in_dim(gz_act_all, me * aq, aq, 0)
    gate_a = dot_plain(h2_act, act_gate_w)
    up_a = dot_plain(h2_act, act_up_w)
    hid_a = glu_value(gate_a, up_a).astype(BF)
    z_a = dot_plain(hid_a, act_down_w).astype(BF)
    dgate_a, dup_a = glu_backward(gate_a, up_a, dot_right(gz_act_all, act_down_w))
    dgate_a, dup_a = dgate_a.astype(BF), dup_a.astype(BF)
    dh2_a = (dot_right(dgate_a, act_gate_w) + dot_right(dup_a, act_up_w)).astype(BF)
    act_back = [dot_left(h2_act, dgate_a), dot_left(h2_act, dup_a)]
    if even:
        g_down_a = dot_left(hid_a, gz_act_all).astype(BF).reshape(m, few, narrow)
    else:
        act_back.append(dot_left(gz_act_all, hid_a))
    act_back = [jnp.concatenate(act_back, axis=0).astype(BF)]
    act_back = [jnp.stack(jnp.split(a, m, axis=1)) for a in act_back]
    if even:
        act_back.append(g_down_a)

    kernel = Kernel(6)
    z_p_parts, z_a = kernel.flow(Chips(), z_p), kernel.flow(EachRows(), z_a)
    g_down.second(kernel)
    g_gate = kernel.job(products_left, [h2_pre, dgate], [(wide, units)])
    first = kernel.flow(First(1), g_gate) if m == 4 else None
    g_up = kernel.job(products_left, [h2_pre, dup], [(wide, units)])
    got = kernel.call("in_grads")
    g_gate, g_up = summing(got[g_gate], 1), got[g_up]
    g_gate.take(got[first] if m == 4 else None)
    g_down = g_down.total(got)
    out_pre = (x2_pre + summed(z_p[0], got[z_p_parts])).astype(BF)
    out_act = (x2_act + jnp.sum(got[z_a].astype(F32), axis=0)).astype(BF)

    kernel = Kernel(7)
    first = kernel.flow(First(1), g_up) if m == 4 else None
    grad_down = kernel.flow(Columns(), g_down)
    out_act = kernel.flow(Line(), out_act)
    dh2_p = kernel.job(products_right, [dgate, w_gate, dup, w_up], [(items, wide)])
    dh2_p_core = kernel.flow(Core(), dh2_p)
    for k in range(1, half):
        kernel.relay(out_act, k)
    got = kernel.call("row_grads")
    out_act = got[out_act].reshape(n * aq, narrow)
    g_up = summing(g_up, 1)
    g_up.take(got[first] if m == 4 else None)
    grad_down = got[grad_down].astype(F32)
    dh2_p = pair_sum(got[dh2_p], got[dh2_p_core])

    kernel = Kernel(8)
    dh2_p_parts, dh2_a = kernel.flow(Chips(), dh2_p), kernel.flow(EachRows(), dh2_a)
    g_gate.second(kernel)
    g_up.second(kernel)
    act_parts = [kernel.flow(Swaps(), a) for a in act_back]
    got = kernel.call("sum_rows")
    g_gate, g_up = g_gate.total(got), g_up.total(got)
    act_sum = [summed(a[0], got[b]).astype(BF) for a, b in zip(act_back, act_parts)]
    if not even:
        act_sum = jnp.concatenate(act_sum, axis=0).reshape(3, n, d_act, few)
        act_sum = [act_sum.transpose(1, 0, 2, 3).reshape(n, 3 * d_act, few)]
    gx2n_pre, g_gain_pf = norm_backward(x2_pre, gain_pf, summed(dh2_p[0], got[dh2_p_parts]))
    gx2n_act, g_gain_af = norm_backward(x2_act, gain_af, jnp.sum(got[dh2_a].astype(F32), axis=0))
    gx2_pre = gz_pre.astype(F32) + gx2n_pre
    gx2_act = gz_act.astype(F32) + gx2n_act

    def both_rows(inputs, outputs):
        products_right(inputs[:2], [outputs[0].at[pl.ds(0, rows)]])
        products_right(inputs[2:], [outputs[0].at[pl.ds(rows, acts)]])

    def input_grads(first, count, inputs, outputs):
        w_in, operands = inputs[-1], []
        for h in range(heads):
            operands += [inputs[h].at[pl.ds(first, count)], w_in.at[:, pl.ds(h * HD, HD)]]
        operands += [inputs[heads].at[pl.ds(first, count)], w_in.at[:, pl.ds(split, 2 * HD)]]
        products_right(operands, outputs)

    def weight_grads(first, count, cut, inputs, outputs):
        inputs = [a if a.shape[0] == count else a.at[pl.ds(first, count)] for a in inputs]
        products_left(inputs, [outputs[0].at[cut]])

    kernel = Kernel(9)
    gy_pre = kernel.flow(Whole(), gx2_pre.astype(BF))
    gy_act = kernel.flow(Whole(), gx2_act.astype(BF))
    grad_gate = kernel.flow(Rows(), g_gate)
    kernel.ready(gy_pre)
    kernel.ready(gy_act)
    grad_up = kernel.flow(Rows(), g_up)
    gmix = kernel.job(both_rows, [gy_pre, w_out_pre, gy_act, w_out_act], [(total_rows, split)])
    *gq, gkv, shares = kernel.job(
        functools.partial(attend_backward, heads),
        probs + query + [keys, values, gmix],
        [(total_rows, HD)] * heads + [(total_rows, 2 * HD), (m, total_rows, kvw)],
    )
    share_parts = kernel.flow(Parts(), shares)
    gh1_pre = kernel.job(
        functools.partial(input_grads, 0, rows), gq + [gkv, w_in_pre], [(rows, wide)]
    )
    gh1_pre_parts = kernel.flow(Parts(), gh1_pre)
    gh1_act = kernel.job(
        functools.partial(input_grads, rows, acts), gq + [gkv, w_in_act], [(acts, narrow)]
    )
    gh1_act_parts = kernel.flow(Parts(), gh1_act)
    if even:
        both = [kernel.flow(Rows(), act_sum[0][k * narrow : (k + 1) * narrow]) for k in (0, 1)]
        act_sum = both + [kernel.flow(Columns(), act_sum[1])]
    else:
        act_sum = [kernel.flow(Each(), act_sum[0])]
    out_act = kernel.flow(Whole(), out_act)
    g_out_pre = g_out_act = g_q_pre = g_q_act = None
    for h in range(heads):
        heads_columns = (slice(None), pl.ds(h * HD, HD))
        of_pre = functools.partial(weight_grads, 0, rows)
        of_act = functools.partial(weight_grads, rows, acts)

        def grads(body, cut, pair, shape, into):
            return [kernel.job(functools.partial(body, cut), pair, [shape], into=into)]

        g_out_pre = grads(of_pre, heads_columns, [gy_pre, mixed[h]], (wide, split), g_out_pre)
        g_q_pre = grads(of_pre, heads_columns, [h1_pre, gq[h]], (wide, split), g_q_pre)
        g_out_act = grads(of_act, heads_columns, [gy_act, mixed[h]], (narrow, split), g_out_act)
        g_q_act = grads(of_act, heads_columns, [h1_act, gq[h]], (narrow, split), g_q_act)
    core_grads = [g[0] for g in (g_out_pre, g_q_pre, g_out_act, g_q_act)]
    from_core = [kernel.flow(CoreRows(), g) for g in core_grads]
    got = kernel.call("heads")
    grad_gate, grad_up = got[grad_gate].astype(F32), got[grad_up].astype(F32)
    here = lax.rem(me, 2)

    def of_core(array, core):
        size = array.shape[0] // n
        blocks = array.reshape(half, 2, size, array.shape[1])
        blocks = lax.dynamic_index_in_dim(blocks, core, 1, False)
        return blocks.reshape(half * size, array.shape[1])

    chip_grads = [add(of_core(got[g], here), got[f]) for g, f in zip(core_grads, from_core)]
    shares, gh1_pre, gh1_act, out_act = got[shares], got[gh1_pre], got[gh1_act], got[out_act]
    gkv_sum = summed(lax.dynamic_index_in_dim(shares, col, 0, False), got[share_parts])
    gh1_pre = summed(own(gh1_pre, rq), got[gh1_pre_parts])
    gh1_act = summed(own(gh1_act, aq), got[gh1_act_parts])
    act_sum = [got[a].astype(F32) for a in act_sum]
    gkv_sum = gkv_sum.astype(BF)
    g_kv_pre = dot_left(h1_pre, gkv_sum[:rows]).astype(BF)
    g_kv_act = dot_left(h1_act, gkv_sum[rows:]).astype(BF)
    gxn_pre, g_gain_pa = norm_backward(own(x_pre, rq), gain_pa, gh1_pre)
    gxn_act, g_gain_aa = norm_backward(own(x_act, aq), gain_aa, gh1_act)
    grad_pre = (gx2_pre + gxn_pre).astype(BF)
    gxa = (gx2_act + gxn_act).astype(BF)
    g_embed = dot_left(own(act_in, aq), gxa)
    act_grad = dot_right(gxa, embed).reshape(aq * dims_count // lanes, lanes)

    swap = [(i, i ^ 1) for i in range(n)]
    chip_grads += [
        add(of_core(g, here), lax.ppermute(of_core(g, 1 - here), "dp", swap))
        for g in (g_kv_pre, g_kv_act)
    ]
    def by_index(vector):
        return vector.reshape(n, -1, narrow // n).transpose(1, 0, 2).reshape(-1, narrow)

    tiny = [by_index(g) for g in (g_gain_pa, g_gain_pf, g_gain_aa, g_gain_af)] + [g_embed]
    tiny = jnp.concatenate(tiny, axis=0)
    tiny_rows = tiny.shape[0]
    tiny = columns_first(pad_rows(tiny, round_up(tiny_rows, 16)).astype(BF))

    kernel = Kernel(11)
    chip_parts = [kernel.flow(ChipRows(), g) for g in chip_grads]
    prefix_grad = kernel.flow(Whole(), grad_pre)
    prefix_output = kernel.flow(Whole(), out_pre)
    act_grad = kernel.flow(World(), act_grad)
    tiny = kernel.flow(Spread(), tiny)
    got = kernel.call("finish")

    def chip_sum(own_parts, parts):
        size = own_parts.shape[0] // half
        return summed(lax.dynamic_slice_in_dim(own_parts, me // 2 * size, size, 0), got[parts])

    grad_out, grad_query, grad_out_a, grad_query_a, *both = [
        chip_sum(g, f) for g, f in zip(chip_grads, chip_parts)
    ]
    grad_out, grad_out_a = grad_out.T, grad_out_a.T
    both = jnp.concatenate(both, axis=0).astype(BF)
    both = lax.all_gather(both, "mp", axis=1, tiled=True).astype(F32)
    prefix_grad = got[prefix_grad][:length].astype(F32)
    prefix_output = got[prefix_output][:length]
    act_grad = got[act_grad].reshape(n, acts, dims_count)[:, :steps]
    tiny = jnp.sum(got[tiny].astype(F32), axis=(0, 1))
    mine_items = (slot_item[:, None] == lax.broadcasted_iota(jnp.int32, (1, n), 1)).astype(F32)
    mine_turns = (slot_item[:, None] == jnp.stack(turns)[None, :]).astype(F32)
    out_act = out_act.reshape(1, m, n, aq, narrow).astype(F32)
    action_output = jnp.sum(mine_turns[:, None, :, None, None] * out_act, axis=2)
    action_output = action_output.reshape(slot_count, acts, narrow)[:, :steps].astype(BF)
    own_mask = lax.broadcasted_iota(jnp.int32, (slot_count, dims_count), 1) < valid_dims[:, None]
    action_grad = jnp.sum(
        mine_items[:, :, None, None] * act_grad[None], axis=1
    ) * own_mask.astype(F32)[:, None, :]
    grad_gain_pa = tiny[:twice].reshape(-1)
    grad_gain_pf = tiny[twice : 2 * twice].reshape(-1)
    rest = tiny[2 * twice : tiny_rows]

    if even:
        grad_gate_a, grad_up_a, grad_down_a = act_sum
    else:
        act_sum = act_sum[0]
        grad_gate_a = act_sum[:, :d_act].transpose(1, 0, 2).reshape(d_act, n * few)
        grad_up_a = act_sum[:, d_act : 2 * d_act].transpose(1, 0, 2).reshape(d_act, n * few)
        grad_down_a = act_sum[:, 2 * d_act :].transpose(0, 2, 1).reshape(n * few, d_act)
    return (
        prefix_output,
        action_output,
        prefix_grad,
        action_grad,
        grad_gain_pa,
        grad_query,
        both[:d_pre, :HD],
        both[:d_pre, HD:],
        grad_out,
        grad_gain_pf,
        grad_gate,
        grad_up,
        grad_down,
        rest[2:],
        rest[0],
        grad_query_a,
        both[d_pre:, :HD],
        both[d_pre:, HD:],
        grad_out_a,
        rest[1],
        grad_gate_a,
        grad_up_a,
        grad_down_a,
    )


def solution(mesh):
    return jax.shard_map(
        local,
        mesh=mesh,
        in_specs=(
            P("dp", None),
            P("dp", None, None),
            P("dp"),
            P("dp"),
            P("dp", None),
            P("dp"),
            P("dp", "mp"),
            P("dp", None),
            P("dp", None),
            P("mp", "dp"),
            P("dp"),
            P("dp", "mp"),
            P("dp", "mp"),
            P("mp", "dp"),
            P(None, "dp"),
            P("dp"),
            P("dp", "mp"),
            P("dp", None),
            P("dp", None),
            P("mp", "dp"),
            P("dp"),
            P("dp", "mp"),
            P("dp", "mp"),
            P("mp", "dp"),
            P("dp", None),
            P("dp", None, None),
        ),
        out_specs=(
            P("dp", None),
            P("dp", None, None),
            P("dp", None),
            P("dp", None, None),
            P("dp"),
            P("dp", "mp"),
            P("dp", None),
            P("dp", None),
            P("mp", "dp"),
            P("dp"),
            P("dp", "mp"),
            P("dp", "mp"),
            P("mp", "dp"),
            P(None, "dp"),
            P("dp"),
            P("dp", "mp"),
            P("dp", None),
            P("dp", None),
            P("mp", "dp"),
            P("dp"),
            P("dp", "mp"),
            P("dp", "mp"),
            P("mp", "dp"),
        ),
        check_vma=False,
    )
```

```python
import functools

import jax
import jax.numpy as jnp
from jax import lax
from jax.experimental import pallas as pl
from jax.experimental.pallas import tpu as pltpu
from jax.sharding import PartitionSpec as P

HD = 256
EPS = 1e-06
BF = jnp.bfloat16
F32 = jnp.float32
MESH = pl.DeviceIdType.MESH
HBM = pl.BlockSpec(memory_space=pl.ANY)


def rms_gain(values, gain):
    return values * lax.rsqrt(jnp.mean(values * values, axis=-1, keepdims=True) + EPS) * gain


def norm_backward(values, gain, grad_out):
    unused, pull = jax.vjp(rms_gain, values, gain)
    return pull(grad_out)


def glu_value(gate, upward):
    return jax.nn.gelu(gate, approximate=True) * upward


def glu_backward(gate, upward, grad):
    unused, pull = jax.vjp(glu_value, gate, upward)
    return pull(grad)


def dot_plain(left, right):
    return jnp.dot(left, right, preferred_element_type=F32)


def dot_left(left, right):
    return lax.dot_general(left, right, (((0,), (0,)), ((), ())), preferred_element_type=F32)


def dot_right(left, right):
    return lax.dot_general(left, right, (((1,), (1,)), ((), ())), preferred_element_type=F32)


def round_up(value, step):
    return -(-value // step) * step


def add(left, right):
    return (left.astype(F32) + right.astype(F32)).astype(BF)


def greet(devices):
    barrier = pltpu.get_barrier_semaphore()
    for device in devices:
        pl.semaphore_signal(barrier, inc=1, device_id=device, device_id_type=MESH)
    pl.semaphore_wait(barrier, len(devices))


def at(start, size):
    return pl.ds(pl.multiple_of(start * size, size), size)


class Place:
    def __init__(self, n, m, sent, arrived, first):
        self.n, self.m = n, m
        self.me, self.col = lax.axis_index("dp"), lax.axis_index("mp")
        self.sent, self.arrived, self.first = sent, arrived, first

    def remote(self, src, dst, slot, device):
        return pltpu.make_async_remote_copy(
            src_ref=src,
            dst_ref=dst,
            send_sem=self.sent.at[self.first + slot],
            recv_sem=self.arrived.at[self.first + slot],
            device_id=device,
            device_id_type=MESH,
        )

    def keep(self, src, dst):
        def scoped(buffer):
            pltpu.sync_copy(src, buffer)
            pltpu.sync_copy(buffer, dst)

        pl.run_scoped(scoped, pltpu.VMEM(src.shape, src.dtype))

    def over_dp(self, s):
        return (lax.rem(self.me + s, self.n), self.col)

    def over_mp(self, k):
        return (self.me, self.col ^ k)


def loop(first, last, body):
    lax.fori_loop(first, last, lambda s, carry: (body(s), carry)[1], 0)


class Flow:
    reach = "dp"
    kept = False

    def slots(self, n, m):
        return max(n, m, 4)

    def result(self, shape, n, m):
        return shape

    def each(self, p, src, dst, do):
        pass

    def own(self, p, src, dst):
        return None

    def start(self, p, src, dst):
        self.each(p, src, dst, lambda c: c.start())
        if self.kept:
            p.keep(*self.own(p, src, dst))

    def relay(self, p, src, dst, k):
        return None

    def wait(self, p, src, dst):
        self.each(p, src, dst, lambda c: c.wait())


class Rows(Flow):
    kept = True

    def result(self, shape, n, m):
        return (shape[0] // n, shape[1] * n)

    def own(self, p, src, dst):
        return src.at[at(p.me, src.shape[0] // p.n)], dst.at[:, at(p.me, dst.shape[1] // p.n)]

    def each(self, p, src, dst, do):
        def body(s):
            target = p.over_dp(s)
            block = src.at[at(target[0], src.shape[0] // p.n)]
            do(p.remote(block, dst.at[:, at(p.me, dst.shape[1] // p.n)], s, target))

        loop(1, p.n, body)


class Columns(Flow):
    kept = True

    def result(self, shape, n, m):
        return (shape[0] * n, shape[1] // n)

    def own(self, p, src, dst):
        return src.at[:, at(p.me, src.shape[1] // p.n)], dst.at[at(p.me, dst.shape[0] // p.n)]

    def each(self, p, src, dst, do):
        def body(s):
            target = p.over_dp(s)
            block = src.at[:, at(target[0], src.shape[1] // p.n)]
            do(p.remote(block, dst.at[at(p.me, dst.shape[0] // p.n)], s, target))

        loop(1, p.n, body)


class Each(Flow):
    kept = True

    def own(self, p, src, dst):
        return src.at[p.me], dst.at[p.me]

    def each(self, p, src, dst, do):
        def body(s):
            target = p.over_dp(s)
            do(p.remote(src.at[target[0]], dst.at[p.me], s, target))

        loop(1, p.n, body)


class EachRows(Each):
    def result(self, shape, n, m):
        return (n, shape[0] // n, shape[1])

    def own(self, p, src, dst):
        return src.at[at(p.me, dst.shape[1])], dst.at[p.me]

    def each(self, p, src, dst, do):
        def body(s):
            target = p.over_dp(s)
            do(p.remote(src.at[at(target[0], dst.shape[1])], dst.at[p.me], s, target))

        loop(1, p.n, body)


class Chips(Flow):
    def each(self, p, src, dst, do):
        loop(1, p.n // 2, lambda s: do(p.remote(src.at[s], dst.at[s], s, p.over_dp(2 * s))))


class Core(Flow):
    def result(self, shape, n, m):
        return (shape[0] // 2, shape[1])

    def each(self, p, src, dst, do):
        half = src.shape[0] // 2
        do(p.remote(src.at[pl.ds(half, half)], dst, 0, (p.me ^ 1, p.col)))


class CoreRows(Flow):
    def result(self, shape, n, m):
        return (shape[0] // 2, shape[1])

    def cut(self, ref, i, count):
        return ref.at[at(i, ref.shape[0] // count)]

    def each(self, p, src, dst, do):
        def body(c):
            block = self.cut(src, 2 * c + lax.rem(p.me + 1, 2), p.n)
            do(p.remote(block, self.cut(dst, c, p.n // 2), c, (p.me ^ 1, p.col)))

        loop(0, p.n // 2, body)


class ChipRows(CoreRows):
    def result(self, shape, n, m):
        return (n // 2, shape[0] // (n // 2), shape[1])

    def each(self, p, src, dst, do):
        def body(s):
            target = p.over_dp(2 * s)
            do(p.remote(self.cut(src, target[0] // 2, p.n // 2), dst.at[s], s, target))

        loop(1, p.n // 2, body)


class Line(Flow):
    def __init__(self, place=None, result=None, share=False):
        self.place = place or Line.in_turn
        self.shape = result
        self.share = share
        self.reach = "both" if share else "dp"

    def slots(self, n, m):
        return 2 * n + (n * m if self.share else 0)

    def in_turn(ref, i, j):
        chips = lax.axis_size("dp") // 2
        chip = lax.rem(i // 2 - j // 2 + chips, chips)
        return ref.at[chip + chips * lax.rem(i + j, 2)]

    def result(self, shape, n, m):
        return self.shape or (n,) + shape

    def origin(self, p, first, way, k):
        return lax.rem(first - (2, -2)[way] * k + 2 * p.n, p.n)

    def along(self, p, src, dst, way, k):
        i = self.origin(p, p.me, way, k - 1)
        target = lax.rem(p.me + (2, -2)[way] + p.n, p.n)
        source = src if k == 1 else self.place(dst, i, p.me)
        slot = way * p.n // 2 + k
        return p.remote(source, self.place(dst, i, target), slot, (target, p.col))

    def across(self, p, src, dst, way, k):
        i = self.origin(p, p.me, way, k)
        source = src if k == 0 else self.place(dst, i, p.me)
        slot = (2 + way) * p.n // 2 + k
        return p.remote(source, self.place(dst, i, p.me ^ 1), slot, (p.me ^ 1, p.col))

    def passed(self, p, dst, i, k, source=None):
        block = self.place(dst, i, p.me)
        source = block if source is None else source
        return p.remote(source, block, 2 * p.n + i * p.m + k, p.over_mp(k))

    def receives(self, p, way, k):
        chip = p.me // 2
        if k == 0:
            return chip >= 0
        return chip >= k if way == 0 else chip < p.n // 2 - k

    def sends(self, p, way, k):
        chip = p.me // 2
        beyond = chip < p.n // 2 - 1 if way == 0 else chip > 0
        return beyond & self.receives(p, way, k - 1)

    def start(self, p, src, dst):
        for way in (0, 1):
            pl.when(self.sends(p, way, 1))(self.along(p, src, dst, way, 1).start)
        self.across(p, src, dst, 0, 0).start()
        self.hand(p, dst, p.me, src)
        p.keep(src, self.place(dst, p.me, p.me))

    def hand(self, p, dst, i, source=None):
        if self.share:
            for k in range(1, p.m):
                self.passed(p, dst, i, k, source).start()

    def crossed(self, p, src, dst, way, k):
        self.across(p, src, dst, way, k).wait_recv()
        self.hand(p, dst, self.origin(p, p.me ^ 1, way, k))

    def relay(self, p, src, dst, k):
        if k == 1:
            self.crossed(p, src, dst, 0, 0)
        for way in (0, 1):

            @pl.when(self.receives(p, way, k))
            def _(way=way):
                self.along(p, src, dst, way, k).wait_recv()
                self.across(p, src, dst, way, k).start()
                self.hand(p, dst, self.origin(p, p.me, way, k))

            if k < p.n // 2 - 1:
                pl.when(self.sends(p, way, k + 1))(self.along(p, src, dst, way, k + 1).start)
            if k > 1:
                before = functools.partial(self.crossed, p, src, dst, way, k - 1)
                pl.when(self.receives(p, way, k - 1))(before)

    def wait(self, p, src, dst):
        last = p.n // 2 - 1
        for way in (0, 1):
            end = functools.partial(self.crossed, p, src, dst, way, last)
            pl.when(self.receives(p, way, last))(end)
        self.across(p, src, dst, 0, 0).wait_send()
        for way in (0, 1):
            for k in range(1, last + 1):
                pl.when(self.sends(p, way, k))(self.along(p, src, dst, way, k).wait_send)
                pl.when(self.receives(p, way, k))(self.across(p, src, dst, way, k).wait_send)
        if self.share:
            for k in range(1, p.m):
                loop(0, p.n, lambda i, k=k: self.passed(p, dst, i, k).wait())


class Pass(Flow):
    reach = "mp"
    kept = True
    parts = 8

    def __init__(self, axis):
        self.axis = axis

    def slots(self, n, m):
        return max(4, m) * self.parts

    def result(self, shape, n, m):
        return (shape[0], m * shape[1]) if self.axis else (m * shape[0], shape[1])

    def spot(self, p, src, dst, k, c=None):
        rows, width = src.shape
        first, count = (0, rows) if c is None else (c * (rows // self.parts), rows // self.parts)
        if self.axis:
            return dst.at[pl.ds(first, count), pl.ds(k * width, width)]
        return dst.at[pl.ds(k * rows + first, count)]

    def own(self, p, src, dst):
        return src, self.spot(p, src, dst, 0)

    def direct(self, p, src, dst, k, c):
        few = src.shape[0] // self.parts
        block = src.at[pl.ds(c * few, few)]
        slot = k * self.parts + c
        return p.remote(block, self.spot(p, src, dst, k, c), slot, p.over_mp(k))

    def turned(self, p, src, dst, c):
        via = 1 + c % 2
        source = self.spot(p, src, dst, via, c)
        slot = 3 * self.parts + c
        return p.remote(source, self.spot(p, src, dst, 3, c), slot, p.over_mp(3 - via))

    def each(self, p, src, dst, do):
        for c in range(self.parts):
            for k in range(1, 3 if p.m == 4 else p.m):
                do(self.direct(p, src, dst, k, c))

    def start(self, p, src, dst):
        self.each(p, src, dst, lambda c: c.start())

    def relay(self, p, src, dst, k):
        if p.m == 4:
            for c in range((k - 1) * self.parts // 2, k * self.parts // 2):
                self.direct(p, src, dst, 1 + c % 2, c).wait_recv()
                self.turned(p, src, dst, c).start()

    def wait(self, p, src, dst):
        p.keep(*self.own(p, src, dst))
        for c in range(self.parts):
            for k in range(1, 3 if p.m == 4 else p.m):
                copy = self.direct(p, src, dst, k, c)
                (copy.wait_send if p.m == 4 and k == 1 + c % 2 else copy.wait)()
            if p.m == 4:
                self.turned(p, src, dst, c).wait()


def by_way(rows, m):
    return round_up(rows // 2, 16) if m == 4 and rows >= 64 else 0


class Parts(Flow):
    reach = "mp"

    def result(self, shape, n, m):
        rows = shape[-2] if len(shape) == 3 else shape[0] // m
        return (m + 1, rows, shape[-1])

    def block(self, p, src, k):
        i = self.index(p, k)
        return src.at[i] if len(src.shape) == 3 else src.at[at(i, src.shape[0] // p.m)]

    def index(self, p, k):
        return p.col ^ k

    def halves(self, p, dst):
        first = by_way(dst.shape[1], p.m)
        return [(1, pl.ds(0, first)), (2, pl.ds(first, dst.shape[1] - first))] if first else []

    def each(self, p, src, dst, do):
        halves = self.halves(p, dst)
        for k in range(1, 3 if halves else p.m):
            do(p.remote(self.block(p, src, k), dst.at[k], k, p.over_mp(k)))

    def sideways(self, p, src, dst, via, cut):
        block = self.block(p, src, 3).at[cut]
        return p.remote(block, dst.at[p.m, cut], p.m + via, p.over_mp(via))

    def onward(self, p, dst, via, cut):
        return p.remote(dst.at[p.m, cut], dst.at[3, cut], p.m + 2 + via, p.over_mp(3 - via))

    def slots(self, n, m):
        return m + 5

    def start(self, p, src, dst):
        for via, cut in self.halves(p, dst):
            self.sideways(p, src, dst, via, cut).start()
        self.each(p, src, dst, lambda c: c.start())

    def relay(self, p, src, dst, k):
        for via, cut in self.halves(p, dst):
            self.sideways(p, src, dst, via, cut).wait_recv()
            self.onward(p, dst, via, cut).start()

    def wait(self, p, src, dst):
        self.each(p, src, dst, lambda c: c.wait())
        for via, cut in self.halves(p, dst):
            self.sideways(p, src, dst, via, cut).wait_send()
            self.onward(p, dst, via, cut).wait()


class Swaps(Parts):
    def __init__(self, axis=0):
        self.axis = axis

    def result(self, shape, n, m):
        if len(shape) == 3:
            return (m + 1,) + shape[1:]
        return (m + 1, shape[0], shape[1] // m) if self.axis else (m + 1, shape[0] // m, shape[1])

    def block(self, p, src, k):
        if len(src.shape) == 3:
            return src.at[k]
        size = src.shape[self.axis] // p.m
        cut = pl.ds(k * size, size)
        return src.at[:, cut] if self.axis else src.at[cut]


class Whole(Flow):
    reach = "mp"

    def result(self, shape, n, m):
        return (m * shape[0], shape[1])

    def slots(self, n, m):
        return m + 3

    def spot(self, src, dst, i, cut=None):
        rows = src.shape[0]
        if cut is None:
            return dst.at[at(i, rows)]
        return dst.at[pl.ds(pl.multiple_of(i * rows + cut[0], 16), cut[1])]

    def halves(self, p, src):
        first = by_way(src.shape[0], p.m)
        return [(1, (0, first)), (2, (first, src.shape[0] - first))] if first else []

    def direct(self, p, src, dst, k):
        return p.remote(src, self.spot(src, dst, p.col), k, p.over_mp(k))

    def onward(self, p, src, dst, via, cut):
        block = self.spot(src, dst, p.col ^ via, cut)
        return p.remote(block, block, p.m + via, p.over_mp(3 - via))

    def start(self, p, src, dst):
        for k in range(1, 3 if self.halves(p, src) else p.m):
            self.direct(p, src, dst, k).start()
        p.keep(src, self.spot(src, dst, p.col))

    def relay(self, p, src, dst, k):
        for via, cut in self.halves(p, src):
            self.direct(p, src, dst, via).wait_recv()
            self.onward(p, src, dst, via, cut).start()

    def wait(self, p, src, dst):
        halves = self.halves(p, src)
        for k in range(1, 3 if halves else p.m):
            copy = self.direct(p, src, dst, k)
            (copy.wait_send if halves else copy.wait)()
        for via, cut in halves:
            self.onward(p, src, dst, via, cut).wait()


class Swap(Flow):
    reach = "mp"

    def __init__(self, k):
        self.k = k

    def each(self, p, src, dst, do):
        do(p.remote(src, dst, 0, p.over_mp(self.k)))


class First(Flow):
    reach = "mp"

    def __init__(self, axis):
        self.axis = axis

    def result(self, shape, n, m):
        if self.axis:
            return (4, shape[0] // 2, shape[1] // m)
        return (4, shape[0] // m, shape[1] // 2)

    def each(self, p, src, dst, do):
        width, deep = src.shape[self.axis] // p.m, src.shape[1 - self.axis] // 2
        for k, part in enumerate((1, 3, 2, 3)):
            block, half = pl.ds(part * width, width), pl.ds(k // 2 * deep, deep)
            source = src.at[half, block] if self.axis else src.at[block, half]
            do(p.remote(source, dst.at[k], k, p.over_mp(1 + k // 2)))


class World(Flow):
    reach = "world"
    kept = True

    def slots(self, n, m):
        return n * m

    def result(self, shape, n, m):
        return (n, m) + shape

    def block(self, src, i):
        return src

    def own(self, p, src, dst):
        return self.block(src, p.me), dst.at[p.me, p.col]

    def each(self, p, src, dst, do):
        for k in range(p.m):

            def body(s, k=k):
                target = (lax.rem(p.me + s, p.n), p.col ^ k)
                copy = p.remote(
                    self.block(src, target[0]), dst.at[p.me, p.col], s * p.m + k, target
                )
                do(copy)

            loop(0 if k else 1, p.n, body)


class Spread(World):
    def result(self, shape, n, m):
        return (n, m) + shape[1:]

    def block(self, src, i):
        return src.at[i]


class Kernel:
    def __init__(self, collective_id):
        self.collective_id = collective_id
        self.inputs, self.outputs, self.flows, self.steps = [], [], [], []

    def operand(self, source):
        if isinstance(source, int):
            return ("out", source)
        self.inputs.append(source)
        return ("in", len(self.inputs) - 1)

    def shape_of(self, source):
        return self.outputs[source] if isinstance(source, int) else source

    def new_output(self, shape, dtype):
        self.outputs.append(jax.ShapeDtypeStruct(shape, dtype))
        return len(self.outputs) - 1

    def flow(self, kind, source, now=True, into=None):
        n, m = lax.axis_size("dp"), lax.axis_size("mp")
        like = self.shape_of(source)
        out = into
        if into is None:
            out = self.new_output(kind.result(like.shape, n, m), like.dtype)
        name = out if into is None else -1 - len(self.flows)
        self.flows.append((kind, self.operand(source), out, name))
        if now:
            self.go(name)
        return name

    def go(self, name):
        self.steps.append(("start", name))

    def relay(self, name, k):
        self.steps.append(("relay", name, k))

    def ready(self, name):
        self.steps.append(("wait", name))

    def job(self, body, sources, shapes, dtype=BF, into=None):
        outs = into or [self.new_output(s, dtype) for s in shapes]
        self.steps.append(("job", body, [self.operand(s) for s in sources], outs))
        return outs if len(outs) > 1 else outs[0]

    def call(self, name):
        n, m = lax.axis_size("dp"), lax.axis_size("mp")
        takes, gives = len(self.inputs), len(self.outputs)
        flows, steps = self.flows, self.steps
        rows = {flow[3]: row for row, flow in enumerate(flows)}
        reach = {flow[0].reach for flow in flows}
        firsts = [0]
        for flow in flows:
            firsts.append(firsts[-1] + flow[0].slots(n, m))

        def kernel(*refs):
            ins, outs = refs[:takes], refs[takes : takes + gives]
            sent, arrived = refs[takes + gives :]
            me, col = lax.axis_index("dp"), lax.axis_index("mp")
            if "world" in reach:
                greet([(lax.rem(me + s, n), col ^ k) for s in range(n) for k in range(m) if s or k])
            else:
                column = [(lax.rem(me + s, n), col) for s in range(1, n)]
                row = [(me, col ^ k) for k in range(1, m)]
                greet(
                    (column if reach & {"dp", "both"} else [])
                    + (row if reach & {"mp", "both"} else [])
                )

            def ref(operand):
                return (ins if operand[0] == "in" else outs)[operand[1]]

            def act(what, name, *rest):
                kind, source, out, unused = flows[rows[name]]
                place = Place(n, m, sent, arrived, firsts[rows[name]])
                getattr(kind, what)(place, ref(source), outs[out], *rest)

            ended = set()
            for step in steps:
                if step[0] == "job":
                    step[1]([ref(s) for s in step[2]], [outs[o] for o in step[3]])
                else:
                    act(*step)
                    if step[0] == "wait":
                        ended.add(step[1])
            for flow in flows:
                if flow[3] not in ended:
                    act("wait", flow[3])

        return pl.pallas_call(
            kernel,
            out_shape=self.outputs,
            in_specs=[HBM] * takes,
            out_specs=[HBM] * gives,
            scratch_shapes=[
                pltpu.SemaphoreType.DMA((firsts[-1],)),
                pltpu.SemaphoreType.DMA((firsts[-1],)),
            ],
            compiler_params=pltpu.CompilerParams(
                collective_id=self.collective_id,
                has_side_effects=True,
                vmem_limit_bytes=56 << 20,
            ),
            name=name,
        )(*self.inputs)


def tile(size, most):
    return max(t for t in range(16, most + 1, 16) if size % t == 0)


def products_plain(inputs, outputs):
    a, b = inputs
    (rows, depth), width = a.shape, b.shape[1]
    bm, bn = tile(rows, 832), tile(width, 512)

    def body(a_ref, b_ref, o_ref):
        o_ref[...] = dot_plain(a_ref[...], b_ref[...]).astype(BF)

    pltpu.emit_pipeline(
        body,
        grid=(width // bn, rows // bm),
        in_specs=[
            pl.BlockSpec((bm, depth), lambda j, i: (i, 0)),
            pl.BlockSpec((depth, bn), lambda j, i: (0, j)),
        ],
        out_specs=[pl.BlockSpec((bm, bn), lambda j, i: (i, j))],
    )(a, b, outputs[0])


def products_right(inputs, outputs):
    pairs = len(inputs) // 2
    rows, width = inputs[0].shape[0], inputs[1].shape[0]
    bm, bn = tile(rows, 832), tile(width, 512)

    def body(*refs):
        total = dot_right(refs[0][...], refs[1][...])
        for p in range(1, pairs):
            total = total + dot_right(refs[2 * p][...], refs[2 * p + 1][...])
        refs[-1][...] = total.astype(BF)

    specs = []
    for p in range(pairs):
        depth = inputs[2 * p].shape[1]
        specs.append(pl.BlockSpec((bm, depth), lambda i, j: (i, 0)))
        specs.append(pl.BlockSpec((bn, depth), lambda i, j: (j, 0)))
    pltpu.emit_pipeline(
        body,
        grid=(rows // bm, width // bn),
        in_specs=specs,
        out_specs=[pl.BlockSpec((bm, bn), lambda i, j: (i, j))],
    )(*inputs, outputs[0])


def products_left(inputs, outputs):
    a, rest = inputs[0], inputs[1:]
    (depth, rows), width = a.shape, rest[0].shape[1]
    bm, bn = tile(rows, 1024), tile(width, 512)
    count = len(rest)

    def body(a_ref, *refs):
        for p in range(count):
            refs[count + p][...] = dot_left(a_ref[...], refs[p][...]).astype(BF)

    pltpu.emit_pipeline(
        body,
        grid=(rows // bm, width // bn),
        in_specs=[pl.BlockSpec((depth, bm), lambda i, j: (0, i))]
        + [pl.BlockSpec((depth, bn), lambda i, j: (0, j))] * count,
        out_specs=[pl.BlockSpec((bm, bn), lambda i, j: (i, j))] * count,
    )(a, *rest, *outputs)


def hidden_forward(part, parts, inputs, outputs):
    h, w_gate, w_up = inputs
    (rows, depth), width = h.shape, w_gate.shape[1] // parts
    cut = pl.ds(part * width, width)
    w_gate, w_up = w_gate.at[:, cut], w_up.at[:, cut]
    outputs = [o.at[:, cut] for o in outputs]
    bm, bn = tile(rows, 832), tile(width, 512)

    def body(h_ref, gate_w, up_w, gate_ref, up_ref, hidden_ref):
        gate = dot_plain(h_ref[...], gate_w[...])
        upward = dot_plain(h_ref[...], up_w[...])
        gate_ref[...] = gate.astype(BF)
        up_ref[...] = upward.astype(BF)
        hidden_ref[...] = glu_value(gate, upward).astype(BF)

    block = pl.BlockSpec((bm, bn), lambda j, i: (i, j))
    pltpu.emit_pipeline(
        body,
        grid=(width // bn, rows // bm),
        in_specs=[pl.BlockSpec((bm, depth), lambda j, i: (i, 0))]
        + [pl.BlockSpec((depth, bn), lambda j, i: (0, j))] * 2,
        out_specs=[block] * 3,
    )(h, w_gate, w_up, *outputs)


def hidden_backward(inputs, outputs):
    gz, w_down, gate, upward = inputs
    (rows, depth), width = gz.shape, w_down.shape[0]
    bm, bn = tile(rows, 832), tile(width, 512)

    def body(gz_ref, down_w, gate_ref, up_ref, dgate_ref, dup_ref):
        grad = dot_right(gz_ref[...], down_w[...])
        dgate, dup = glu_backward(gate_ref[...].astype(F32), up_ref[...].astype(F32), grad)
        dgate_ref[...] = dgate.astype(BF)
        dup_ref[...] = dup.astype(BF)

    block = pl.BlockSpec((bm, bn), lambda j, i: (i, j))
    pltpu.emit_pipeline(
        body,
        grid=(width // bn, rows // bm),
        in_specs=[
            pl.BlockSpec((bm, depth), lambda j, i: (i, 0)),
            pl.BlockSpec((bn, depth), lambda j, i: (j, 0)),
            block,
            block,
        ],
        out_specs=[block] * 2,
    )(gz, w_down, gate, upward, *outputs)


def act_feed_forward(inputs, outputs):
    def body(h_ref, gz_ref, gate_w, up_w, down_w, z, dh2, g_gate, g_up, g_down):
        h, gz = h_ref[...], gz_ref[...]
        gate, upward = dot_plain(h, gate_w[...]), dot_plain(h, up_w[...])
        hidden = glu_value(gate, upward).astype(BF)
        z[...] = dot_plain(hidden, down_w[...]).astype(BF)
        g_down[...] = dot_left(hidden, gz).astype(BF)
        dgate, dup = glu_backward(gate, upward, dot_right(gz, down_w[...]))
        dgate, dup = dgate.astype(BF), dup.astype(BF)
        dh2[...] = (dot_right(dgate, gate_w[...]) + dot_right(dup, up_w[...])).astype(BF)
        g_gate[...] = dot_left(h, dgate).astype(BF)
        g_up[...] = dot_left(h, dup).astype(BF)

    def whole(ref):
        return pl.BlockSpec(ref.shape, lambda i: (0, 0))

    pltpu.emit_pipeline(
        body,
        grid=(1,),
        in_specs=[whole(r) for r in inputs],
        out_specs=[whole(r) for r in outputs],
    )(*inputs, *outputs)


def attend_forward(inputs, outputs):
    query, keys, values, seg_q, seg_k = inputs
    probs, mixed = outputs
    total = query.shape[0]
    rows = tile(total, 448)

    def body(q_ref, k_ref, v_ref, sq_ref, sk_ref, p_ref, o_ref):
        allowed = sq_ref[:, :1] >= sk_ref[:1]
        scores = dot_right(q_ref[...], k_ref[...]) * HD ** (-0.5)
        scores = jnp.where(allowed, scores, -1e30)
        raised = jnp.exp(scores - jnp.max(scores, axis=-1, keepdims=True))
        p = (raised / jnp.sum(raised, axis=-1, keepdims=True)).astype(BF)
        p_ref[...] = p
        o_ref[...] = dot_plain(p, v_ref[...]).astype(BF)

    def rest(shape):
        return pl.BlockSpec(shape, lambda i: (0, 0))

    pltpu.emit_pipeline(
        body,
        grid=(total // rows,),
        in_specs=[
            pl.BlockSpec((rows, HD), lambda i: (i, 0)),
            rest(keys.shape),
            rest(values.shape),
            pl.BlockSpec((rows, seg_q.shape[1]), lambda i: (i, 0)),
            rest(seg_k.shape),
        ],
        out_specs=[
            pl.BlockSpec((rows, total), lambda i: (i, 0)),
            pl.BlockSpec((rows, HD), lambda i: (i, 0)),
        ],
    )(query, keys, values, seg_q, seg_k, probs, mixed)


def attend_backward(heads, inputs, outputs):
    probs, query = inputs[:heads], inputs[heads : 2 * heads]
    keys, values, grad = inputs[2 * heads :]
    grad_query, (both, shares) = outputs[:heads], outputs[heads:]
    total, scale = keys.shape[0], HD ** (-0.5)
    rows = tile(total, 448)
    width = shares.shape[2]

    def scoped(sums, rounded, parted):
        sums[...] = jnp.zeros_like(sums)

        def body(*refs):
            k_ref, v_ref, g_ref = refs[2 * heads : 2 * heads + 3]
            for h in range(heads):
                g = g_ref[:, h * HD : (h + 1) * HD]
                p, q = refs[h][...], refs[heads + h][...]
                wide_p = p.astype(F32)
                dp = dot_right(g, v_ref[...])
                ds = wide_p * (dp - jnp.sum(wide_p * dp, axis=-1, keepdims=True))
                ds = ds.astype(BF)
                refs[2 * heads + 3 + h][...] = (dot_plain(ds, k_ref[...]) * scale).astype(BF)
                sums[:, :HD] += dot_left(ds, q) * scale
                sums[:, HD:] += dot_left(p, g)

        def rest(ref):
            return pl.BlockSpec(ref.shape, lambda i: (0, 0))

        block = pl.BlockSpec((rows, HD), lambda i: (i, 0))
        pltpu.emit_pipeline(
            body,
            grid=(total // rows,),
            in_specs=[pl.BlockSpec((rows, total), lambda i: (i, 0))] * heads
            + [block] * heads
            + [rest(keys), rest(values), pl.BlockSpec((rows, heads * HD), lambda i: (i, 0))],
            out_specs=[block] * heads,
        )(*probs, *query, keys, values, grad, *grad_query)
        rounded[...] = sums[...].astype(BF)
        for k in range(shares.shape[0]):
            parted[k] = sums[:, k * width : (k + 1) * width].astype(BF)
        pltpu.sync_copy(rounded, both)
        pltpu.sync_copy(parted, shares)

    pl.run_scoped(
        scoped,
        pltpu.VMEM((total, 2 * HD), F32),
        pltpu.VMEM((total, 2 * HD), BF),
        pltpu.VMEM(shares.shape, BF),
    )


def rows_from(first, count, body):
    return lambda inputs, outputs: body([inputs[0].at[pl.ds(first, count)]] + inputs[1:], outputs)


def add_pairs(pairs, outputs):
    (rows, width), count = outputs[0].shape, len(outputs)

    def body(*refs):
        for k in range(count):
            refs[2 * count + k][...] = add(refs[2 * k][...], refs[2 * k + 1][...])

    block = pl.BlockSpec((tile(rows, 256), width), lambda i: (i, 0))
    pltpu.emit_pipeline(
        body,
        grid=(rows // tile(rows, 256),),
        in_specs=[block] * (2 * count),
        out_specs=[block] * count,
    )(*[ref for pair in pairs for ref in pair], *outputs)


class Halves:
    def __init__(self, axis):
        self.axis = axis

    def settle(self, got):
        for name, value in vars(self).items():
            if name != "axis" and isinstance(value, int):
                setattr(self, name, got[value])

    def first(self, kernel, whole):
        self.whole = whole
        self.parts = kernel.flow(First(self.axis), whole)

    def second(self, kernel):
        axis = self.axis

        def take(inputs, outputs):
            whole, parts = inputs
            width, deep = whole.shape[axis] // 4, whole.shape[1 - axis] // 2

            def part(half, k):
                block, deeps = pl.ds(k * width, width), pl.ds(half * deep, deep)
                return whole.at[deeps, block] if axis else whole.at[block, deeps]

            own = [part(0, 0), part(0, 2), part(1, 0), part(1, 1)]
            add_pairs([(own[k], parts.at[k]) for k in range(4)], outputs)

        like = kernel.shape_of(self.parts).shape[1:]
        self.top, next_y, self.low, next_x = kernel.job(take, [self.whole, self.parts], [like] * 4)
        self.from_y = kernel.flow(Swap(2), next_y)
        self.from_x = kernel.flow(Swap(1), next_x)

    def total(self, kernel):
        axis = self.axis
        rows, width = kernel.shape_of(self.top).shape

        def join(inputs, outputs):
            top, low, from_y, from_x = inputs
            halves = [(top, from_y), (low, from_x)]
            for k, pair in enumerate(halves):
                spot = pl.ds(k * rows, rows) if axis else (slice(None), pl.ds(k * width, width))
                add_pairs([pair], [outputs[0].at[spot]])

        shape = (2 * rows, width) if axis else (rows, 2 * width)
        return kernel.job(join, [self.top, self.low, self.from_y, self.from_x], [shape])


class Direct:
    def __init__(self, axis):
        self.axis = axis

    def settle(self, got):
        if isinstance(self.whole, int):
            self.whole = got[self.whole]

    def first(self, kernel, whole):
        self.whole = whole

    def second(self, kernel):
        return None

    def total(self, kernel):
        parts = jnp.split(self.whole, lax.axis_size("mp"), axis=self.axis)
        total = parts[0].astype(F32)
        for k in range(1, len(parts)):
            pairs = [(i, i ^ k) for i in range(len(parts))]
            total = total + lax.ppermute(parts[k], "mp", pairs).astype(F32)
        return total.astype(BF)


def project_rows(first, heads, inputs, outputs):
    x, gain, w_in = inputs
    rows, depth = x.shape
    block = tile(rows, 416)

    def body(x_ref, gain_ref, w_ref, normed_ref, *refs):
        normed = rms_gain(x_ref[...].astype(F32), gain_ref[:1]).astype(BF)
        normed_ref[...] = normed
        for k in range(heads + 2):
            refs[k][...] = dot_plain(normed, w_ref[:, k * HD : (k + 1) * HD]).astype(BF)

    spots = [o.at[pl.ds(first, rows)] for o in outputs[1:]]
    pltpu.emit_pipeline(
        body,
        grid=(rows // block,),
        in_specs=[
            pl.BlockSpec((block, depth), lambda i: (i, 0)),
            pl.BlockSpec(gain.shape, lambda i: (0, 0)),
            pl.BlockSpec(w_in.shape, lambda i: (0, 0)),
        ],
        out_specs=[pl.BlockSpec((block, depth), lambda i: (i, 0))]
        + [pl.BlockSpec((block, HD), lambda i: (i, 0))] * (heads + 2),
    )(x, gain, w_in, outputs[0], *spots)


def local(
    prefix_input,
    action_input,
    valid_dims,
    slot_item,
    segments,
    pre_gain_attn,
    pre_query,
    pre_key,
    pre_value,
    pre_output,
    pre_gain_ffn,
    pre_gate,
    pre_up,
    pre_down,
    act_embed,
    act_gain_attn,
    act_query,
    act_key,
    act_value,
    act_output,
    act_gain_ffn,
    act_gate,
    act_up,
    act_down,
    prefix_cotangent,
    action_cotangent,
):
    n, m = lax.axis_size("dp"), lax.axis_size("mp")
    me, col = lax.axis_index("dp"), lax.axis_index("mp")
    length, wide = prefix_input.shape
    slot_count, steps, dims_count = action_input.shape
    narrow = action_cotangent.shape[2]
    rq = round_up(-(-length // m), 16)
    aq = round_up(-(-steps // m), 16)
    rows, acts = m * rq, m * aq
    total_rows = rows + acts
    half = n // 2
    heads = pre_query.shape[1] // HD
    split = heads * HD
    scale = HD ** (-0.5)
    kvw = 2 * HD // m
    d_pre, d_act = pre_query.shape[0], act_query.shape[0]
    few = act_gate.shape[1] // n
    lanes = 128
    twice = wide // narrow
    turns = [lax.rem(me + 2 * k, n) for k in range(half)]
    turns = turns + [t ^ 1 for t in turns]

    def own(array, count):
        return lax.dynamic_slice_in_dim(array, col * count, count, 0)

    def pad_rows(array, count):
        return jnp.pad(array, ((0, count - array.shape[0]), (0, 0)))

    def lane_rows(array):
        flat = array.reshape(-1)
        count = round_up(-(-flat.shape[0] // lanes), 16)
        return jnp.pad(flat, (0, count * lanes - flat.shape[0])).reshape(count, lanes)

    def columns_first(array):
        return array.reshape(array.shape[0], n, -1).transpose(1, 0, 2)

    even = few % lanes == 0 and d_act % lanes == 0

    smalls = [pre_gain_attn, pre_gain_ffn, act_gain_attn, act_gain_ffn, act_embed, action_input]
    small = jnp.concatenate([lane_rows(a) for a in smalls], axis=0)
    ints = jnp.pad(jnp.stack([slot_item, valid_dims]), ((0, 6), (0, lanes - slot_count)))
    cot_rows = lax.dynamic_slice_in_dim(
        jnp.pad(action_cotangent, ((0, 0), (0, acts - steps), (0, 0))), col * aq, aq, 1
    ).reshape(slot_count * aq, narrow)

    def share_of(key, value):
        return own(jnp.concatenate([key, value], axis=1).T, kvw).T

    def by_rows(size):
        return lambda ref, i, j: ref.at[at(i, size)]

    def by_columns(size):
        return lambda ref, i, j: ref.at[:, at(i, size)]

    def by_share(size):
        return lambda ref, i, j: ref.at[lax.axis_index("mp"), at(i, size)]

    def by_lead(ref, i, j):
        return ref.at[i]

    kernel = Kernel(1)
    aligned = kvw % lanes == 0
    in_pre, in_act = (wide, split + 2 * HD), (narrow, split + 2 * HD)
    kv_pre, kv_act = share_of(pre_key, pre_value), share_of(act_key, act_value)

    def in_columns(size, share):
        def place(ref, i, j):
            start = split + lax.axis_index("mp") * kvw if share else 0
            columns = pl.ds(pl.multiple_of(start, lanes), kvw if share else split)
            return ref.at[at(i, size), columns]

        return place

    if aligned:
        w_in_pre = kernel.flow(Line(in_columns(d_pre, True), in_pre, True), kv_pre)
        w_in_act = kernel.flow(Line(in_columns(d_act, True), in_act, True), kv_act)
        lines = [w_in_pre, w_in_act]
    else:
        w_kv_pre = kernel.flow(Line(by_share(d_pre), (m, wide, kvw), True), kv_pre)
        w_kv_act = kernel.flow(Line(by_share(d_act), (m, narrow, kvw), True), kv_act)
        lines = [w_kv_pre, w_kv_act]
    small = kernel.flow(Line(by_lead, (n,) + small.shape), small)
    ints = kernel.flow(Line(by_lead, (n, 8, lanes)), ints)
    if aligned:
        w_q_pre = kernel.flow(Line(in_columns(d_pre, False)), pre_query, into=w_in_pre)
        w_q_act = kernel.flow(Line(in_columns(d_act, False)), act_query, into=w_in_act)
    else:
        w_q_pre = kernel.flow(Line(by_rows(d_pre), (wide, split)), pre_query)
        w_q_act = kernel.flow(Line(by_rows(d_act), (narrow, split)), act_query)
    w_out_pre = kernel.flow(Line(by_columns(d_pre), (split, wide)), pre_output)
    if even:
        w_out_act = kernel.flow(Line(by_columns(d_act), (split, narrow)), act_output)
    else:
        w_out_act = kernel.flow(Line(by_lead, (n, split, d_act)), act_output)
    cot_all = kernel.flow(Line(by_lead, (n, slot_count * aq, narrow)), cot_rows)
    lines += [small, ints, w_q_pre, w_q_act, w_out_pre, w_out_act, cot_all]
    for k in range(1, half):
        for out in lines:
            kernel.relay(out, k)
    got = kernel.call("gather")
    small, ints, cot_all = got[small], got[ints], got[cot_all]
    w_out_pre, w_out_act = got[w_out_pre], got[w_out_act]
    if aligned:
        w_in_pre, w_in_act = got[w_in_pre], got[w_in_act]
    else:
        w_in_pre = jnp.concatenate([got[w_q_pre]] + [got[w_kv_pre][k] for k in range(m)], axis=1)
        w_in_act = jnp.concatenate([got[w_q_act]] + [got[w_kv_act][k] for k in range(m)], axis=1)
    smalls_all, begin = [], 0
    for a in smalls:
        count = round_up(-(-a.size // lanes), 16)
        flat = small[:, begin : begin + count].reshape(n, -1)[:, : a.size]
        smalls_all.append(flat.reshape((n,) + a.shape))
        begin += count
    gain_pa, gain_pf, gain_aa, gain_af = [g.reshape(-1).astype(F32) for g in smalls_all[:4]]
    embed = smalls_all[4].transpose(1, 0, 2).reshape(dims_count, narrow)
    act_all = smalls_all[5].reshape(n * slot_count, steps, dims_count)
    slot_all = ints[:, 0, :slot_count].reshape(-1)
    valid_all = ints[:, 1, :slot_count].reshape(-1)
    if not even:
        w_out_act = w_out_act.transpose(1, 0, 2).reshape(split, narrow)

    mine = (slot_all == me).astype(F32)
    valid = jnp.sum(mine * valid_all.astype(F32))
    dims_mask = (lax.broadcasted_iota(jnp.int32, (1, dims_count), 1).astype(F32) < valid).astype(BF)
    act_in = jnp.sum(mine[:, None, None] * act_all.astype(F32), axis=0).astype(BF) * dims_mask
    act_in = pad_rows(act_in, acts)

    x_pre = pad_rows(prefix_input, rows)
    x_act = dot_plain(act_in, embed)
    last, never = 1 << 10, 1 << 20
    seg = jnp.pad(segments[0], (0, rows - length), constant_values=never)
    seg_q = jnp.concatenate([jnp.minimum(seg, last), jnp.full((acts,), last, jnp.int32)])
    own_keys = jnp.where(jnp.arange(acts, dtype=jnp.int32) < steps, last, never)
    seg_k = jnp.concatenate([seg, own_keys])
    seg_q = jnp.broadcast_to(seg_q[:, None], (total_rows, lanes))
    seg_k = jnp.broadcast_to(seg_k[None, :], (8, total_rows))

    gz_pre = own(pad_rows(prefix_cotangent, rows), rq)
    if not even:
        act_weights = jnp.concatenate(
            [
                columns_first(act_gate),
                columns_first(act_up),
                act_down.reshape(n, few, d_act).transpose(0, 2, 1),
            ],
            axis=1,
        )

    def project(first, count):
        def body(inputs, outputs):
            pairs = len(inputs) - 1
            w_out = inputs[-1]
            width = w_out.shape[1]
            bm, bn = tile(count, 416), tile(width, 1024)

            def step(*refs):
                value = dot_plain(refs[0][...], refs[1][...])
                for h in range(1, pairs):
                    value = value + dot_plain(refs[2 * h][...], refs[2 * h + 1][...])
                refs[-1][...] = value.astype(BF)

            operands, specs = [], []
            for h in range(pairs):
                operands += [inputs[h].at[pl.ds(first, count)], w_out.at[pl.ds(h * HD, HD)]]
                specs += [
                    pl.BlockSpec((bm, HD), lambda j, i: (i, 0)),
                    pl.BlockSpec((HD, bn), lambda j, i: (0, j)),
                ]
            pltpu.emit_pipeline(
                step,
                grid=(width // bn, count // bm),
                in_specs=specs,
                out_specs=[pl.BlockSpec((bm, bn), lambda j, i: (i, j))],
            )(*operands, outputs[0])

        return body

    kernel = Kernel(2)
    gate_own = kernel.flow(Columns(), pre_gate)
    up_own = kernel.flow(Columns(), pre_up, now=False)
    h1_pre, *into = kernel.job(
        functools.partial(project_rows, 0, heads),
        [x_pre, jnp.broadcast_to(gain_pa, (8, wide)), w_in_pre],
        [(rows, wide)] + [(total_rows, HD)] * (heads + 2),
    )
    h1_act = kernel.new_output((acts, narrow), BF)
    kernel.job(
        functools.partial(project_rows, rows, heads),
        [x_act, jnp.broadcast_to(gain_aa, (8, narrow)), w_in_act],
        [],
        into=[h1_act] + into,
    )
    query, keys, values = into[:heads], into[heads], into[heads + 1]
    probs, mixed = [], []
    for h in range(heads):
        p, o = kernel.job(
            attend_forward,
            [query[h], keys, values, seg_q, seg_k],
            [(total_rows, total_rows), (total_rows, HD)],
        )
        probs.append(p)
        mixed.append(o)
    y_pre = kernel.job(project(0, rows), mixed + [w_out_pre], [(rows, wide)])
    y_act = kernel.job(project(rows, acts), mixed + [w_out_act], [(acts, narrow)])
    y_pre_parts = kernel.flow(Parts(), y_pre)
    y_act_parts = kernel.flow(Parts(), y_act)
    kernel.ready(gate_own)
    kernel.go(up_own)
    w_gate = kernel.flow(Pass(1), gate_own)
    kernel.relay(y_pre_parts, 1)
    kernel.relay(y_act_parts, 1)
    kernel.relay(w_gate, 1)
    down_own = kernel.flow(Rows(), pre_down)
    kernel.relay(w_gate, 2)
    got = kernel.call("attend")
    probs, mixed = [got[p] for p in probs], [got[o] for o in mixed]
    query, keys, values = [got[q] for q in query], got[keys], got[values]
    h1_pre, h1_act = got[h1_pre], got[h1_act]
    up_own, down_own, w_gate = got[up_own], got[down_own], got[w_gate]

    def summed(first, parts, count=None):
        value = first.astype(F32)
        for k in range(1, count or parts.shape[0]):
            value = value + parts[k].astype(F32)
        return value

    x2_pre = own(x_pre, rq).astype(F32) + summed(own(got[y_pre], rq), got[y_pre_parts], m)
    x2_act = own(x_act, aq) + summed(own(got[y_act], aq), got[y_act_parts], m)
    h2_pre = rms_gain(x2_pre, gain_pf).astype(BF)
    h2_act = rms_gain(x2_act, gain_af).astype(BF)

    kernel = Kernel(3)
    h2_pre = kernel.flow(Line(), h2_pre)
    h2_act = kernel.flow(Line(by_lead, (n, aq, narrow)), h2_act)
    w_up = kernel.flow(Pass(1), up_own)
    if even:
        act_own = [kernel.flow(Columns(), act_gate), kernel.flow(Columns(), act_up)]
        act_own.append(kernel.flow(Rows(), act_down))
    else:
        act_own = [kernel.flow(Each(), act_weights)]
    for k in range(1, half):
        kernel.relay(h2_pre, k)
        kernel.relay(h2_act, k)
        if k < 3:
            kernel.relay(w_up, k)
    got = kernel.call("spread")
    act_own = [got[a] for a in act_own]
    h2_pre, h2_act = got[h2_pre].reshape(n * rq, wide), got[h2_act].reshape(n * aq, narrow)
    w_up = got[w_up]
    items, units = h2_pre.shape[0], w_gate.shape[1]
    summing = Halves if m == 4 else Direct

    kernel = Kernel(4)
    gz_all = kernel.flow(Line(), gz_pre)
    w_down = kernel.flow(Pass(0), down_own)
    into = None
    for piece in range(2):
        into = kernel.job(
            functools.partial(hidden_forward, piece, 2),
            [h2_pre, w_gate, w_up],
            [(items, units)] * 3,
            into=into,
        )
        kernel.relay(gz_all, piece + 1)
    kernel.relay(w_down, 1)
    kernel.relay(w_down, 2)
    for k in range(3, half):
        kernel.relay(gz_all, k)
    got = kernel.call("hidden")
    gate, upward, hidden = [got[o] for o in into]
    w_down, gz_pre_all = got[w_down], got[gz_all].reshape(n * rq, wide)

    kernel = Kernel(5)
    if even:
        act_all_w = [kernel.flow(Pass(axis), a) for axis, a in zip((1, 1, 0), act_own)]
    else:
        act_all_w = [kernel.flow(Pass(0), act_own[0].reshape(n * 3 * d_act, few))]
    g_down = kernel.job(products_left, [hidden, gz_pre_all], [(units, wide)])
    down_sum, gate_sum, up_sum = summing(0), summing(1), summing(1)
    down_sum.first(kernel, g_down)
    z_p = kernel.job(products_plain, [hidden, w_down], [(items, wide)])
    z_p_core = kernel.flow(Core(), z_p)
    for k in (1, 2):
        for a in act_all_w:
            kernel.relay(a, k)
    dgate, dup = kernel.job(
        hidden_backward, [gz_pre_all, w_down, gate, upward], [(items, units)] * 2
    )
    got = kernel.call("hidden_grads")
    dgate, dup = got[dgate], got[dup]
    down_sum.settle(got)

    def pair_sum(parts, other):
        return add(parts[: other.shape[0]], other).reshape(half, -1, other.shape[1])

    z_p = pair_sum(got[z_p], got[z_p_core])
    if even:
        act_gate_w, act_up_w, act_down_w = [got[a] for a in act_all_w]
    else:
        act_all_w = got[act_all_w[0]].reshape(m, n, 3, d_act, few).transpose(2, 1, 3, 0, 4)
        act_gate_w, act_up_w, act_down_w = act_all_w.reshape(3, narrow, m * few)
        act_down_w = act_down_w.T

    match = (lax.broadcasted_iota(jnp.int32, (n, 1), 0) == slot_all[None, :]).astype(BF)
    cot_all = cot_all.reshape(n * slot_count, aq * narrow)
    gz_act_all = dot_plain(match, cot_all).astype(BF).reshape(n * aq, narrow)
    gz_act = lax.dynamic_slice_in_dim(gz_act_all, me * aq, aq, 0)
    kernel = Kernel(6)
    z_p_parts = kernel.flow(Chips(), z_p)
    down_sum.second(kernel)
    g_gate = kernel.job(products_left, [h2_pre, dgate], [(wide, units)])
    gate_sum.first(kernel, g_gate)
    z_a, dh2_a, g_gate_a, g_up_a, g_down_a = kernel.job(
        act_feed_forward,
        [h2_act, gz_act_all, act_gate_w, act_up_w, act_down_w],
        [(n * aq, narrow)] * 2 + [(narrow, m * few)] * 2 + [(m * few, narrow)],
    )
    z_a = kernel.flow(EachRows(), z_a)
    g_up = kernel.job(products_left, [h2_pre, dup], [(wide, units)])
    got = kernel.call("in_grads")
    dh2_a, g_gate_a, g_up_a, g_down_a = [got[o] for o in (dh2_a, g_gate_a, g_up_a, g_down_a)]
    act_back = [g_gate_a, g_up_a, g_down_a]
    if not even:
        act_back = jnp.concatenate([g_gate_a, g_up_a, g_down_a.T], axis=0)
        act_back = [jnp.stack(jnp.split(act_back, m, axis=1))]
    down_sum.settle(got)
    gate_sum.settle(got)
    g_up = got[g_up]
    out_pre = (x2_pre + summed(z_p[0], got[z_p_parts])).astype(BF)
    out_act = (x2_act + jnp.sum(got[z_a].astype(F32), axis=0)).astype(BF)

    kernel = Kernel(7)
    up_sum.first(kernel, g_up)
    grad_down = kernel.flow(Columns(), down_sum.total(kernel))
    out_act = kernel.flow(Line(), out_act)
    dh2_p = kernel.job(products_right, [dgate, w_gate, dup, w_up], [(items, wide)])
    dh2_p_core = kernel.flow(Core(), dh2_p)
    for k in range(1, half):
        kernel.relay(out_act, k)
    got = kernel.call("row_grads")
    out_act = got[out_act].reshape(n * aq, narrow)
    up_sum.settle(got)
    grad_down = got[grad_down].astype(F32)
    dh2_p = pair_sum(got[dh2_p], got[dh2_p_core])

    kernel = Kernel(8)
    dh2_p_parts, dh2_a = kernel.flow(Chips(), dh2_p), kernel.flow(EachRows(), dh2_a)
    act_parts = [kernel.flow(Swaps(axis), a) for axis, a in zip((1, 1, 0), act_back)]
    gate_sum.second(kernel)
    up_sum.second(kernel)
    for flow in act_parts:
        kernel.relay(flow, 1)
    got = kernel.call("sum_rows")
    gate_sum.settle(got)
    up_sum.settle(got)
    if even:
        act_back = [g_gate_a[:, :few], g_up_a[:, :few], g_down_a[:few]]
    else:
        act_back = [act_back[0][0]]
    act_sum = [summed(a, got[b], m).astype(BF) for a, b in zip(act_back, act_parts)]
    if not even:
        act_sum = jnp.concatenate(act_sum, axis=0).reshape(3, n, d_act, few)
        act_sum = [act_sum.transpose(1, 0, 2, 3).reshape(n, 3 * d_act, few)]
    gx2n_pre, g_gain_pf = norm_backward(x2_pre, gain_pf, summed(dh2_p[0], got[dh2_p_parts]))
    gx2n_act, g_gain_af = norm_backward(x2_act, gain_af, jnp.sum(got[dh2_a].astype(F32), axis=0))
    gx2_pre = gz_pre.astype(F32) + gx2n_pre
    gx2_act = gz_act.astype(F32) + gx2n_act

    def both_rows(inputs, outputs):
        products_right(inputs[:2], [outputs[0].at[pl.ds(0, rows)]])
        products_right(inputs[2:], [outputs[0].at[pl.ds(rows, acts)]])

    def input_grads(first, count, inputs, outputs):
        w_in, operands = inputs[-1], []
        for h in range(heads):
            operands += [inputs[h].at[pl.ds(first, count)], w_in.at[:, pl.ds(h * HD, HD)]]
        operands += [inputs[heads].at[pl.ds(first, count)], w_in.at[:, pl.ds(split, 2 * HD)]]
        products_right(operands, outputs)

    def weight_grads(first, count, cut, inputs, outputs):
        inputs = [a if a.shape[0] == count else a.at[pl.ds(first, count)] for a in inputs]
        products_left(inputs, [outputs[0].at[cut]])

    kernel = Kernel(9)
    gy_pre = kernel.flow(Whole(), gx2_pre.astype(BF))
    gy_act = kernel.flow(Whole(), gx2_act.astype(BF))
    grad_gate = kernel.flow(Rows(), gate_sum.total(kernel))
    kernel.relay(gy_pre, 1)
    kernel.relay(gy_act, 1)
    kernel.ready(gy_pre)
    kernel.ready(gy_act)
    grad_up = kernel.flow(Rows(), up_sum.total(kernel))
    gmix = kernel.job(both_rows, [gy_pre, w_out_pre, gy_act, w_out_act], [(total_rows, split)])
    *gq, gkv, shares = kernel.job(
        functools.partial(attend_backward, heads),
        probs + query + [keys, values, gmix],
        [(total_rows, HD)] * heads + [(total_rows, 2 * HD), (m, total_rows, kvw)],
    )
    share_parts = kernel.flow(Parts(), shares)
    gh1_pre = kernel.job(
        functools.partial(input_grads, 0, rows), gq + [gkv, w_in_pre], [(rows, wide)]
    )
    gh1_pre_parts = kernel.flow(Parts(), gh1_pre)
    gh1_act = kernel.job(
        functools.partial(input_grads, rows, acts), gq + [gkv, w_in_act], [(acts, narrow)]
    )
    gh1_act_parts = kernel.flow(Parts(), gh1_act)
    if even:
        act_sum = [kernel.flow(k(), a) for k, a in zip((Rows, Rows, Columns), act_sum)]
    else:
        act_sum = [kernel.flow(Each(), act_sum[0])]
    late = [share_parts, gh1_pre_parts, gh1_act_parts]
    g_out_pre = g_out_act = g_q_pre = g_q_act = None
    for h in range(heads):
        heads_columns = (slice(None), pl.ds(h * HD, HD))
        of_pre = functools.partial(weight_grads, 0, rows)
        of_act = functools.partial(weight_grads, rows, acts)

        def grads(body, cut, pair, shape, into):
            return [kernel.job(functools.partial(body, cut), pair, [shape], into=into)]

        g_out_pre = grads(of_pre, heads_columns, [gy_pre, mixed[h]], (wide, split), g_out_pre)
        g_q_pre = grads(of_pre, heads_columns, [h1_pre, gq[h]], (wide, split), g_q_pre)
        g_out_act = grads(of_act, heads_columns, [gy_act, mixed[h]], (narrow, split), g_out_act)
        g_q_act = grads(of_act, heads_columns, [h1_act, gq[h]], (narrow, split), g_q_act)
        if h == 0:
            for flow in late:
                kernel.relay(flow, 1)
    core_grads = [g[0] for g in (g_out_pre, g_q_pre, g_out_act, g_q_act)]
    from_core = [kernel.flow(CoreRows(), g) for g in core_grads]
    got = kernel.call("heads")
    grad_gate, grad_up = got[grad_gate].astype(F32), got[grad_up].astype(F32)
    here = lax.rem(me, 2)

    def of_core(array, core):
        size = array.shape[0] // n
        blocks = array.reshape(half, 2, size, array.shape[1])
        blocks = lax.dynamic_index_in_dim(blocks, core, 1, False)
        return blocks.reshape(half * size, array.shape[1])

    chip_grads = [add(of_core(got[g], here), got[f]) for g, f in zip(core_grads, from_core)]
    shares, gh1_pre, gh1_act = got[shares], got[gh1_pre], got[gh1_act]
    gkv_sum = summed(lax.dynamic_index_in_dim(shares, col, 0, False), got[share_parts], m)
    gh1_pre = summed(own(gh1_pre, rq), got[gh1_pre_parts], m)
    gh1_act = summed(own(gh1_act, aq), got[gh1_act_parts], m)
    act_sum = [got[a].astype(F32) for a in act_sum]
    gkv_sum = gkv_sum.astype(BF)
    g_kv_pre = dot_left(h1_pre, gkv_sum[:rows]).astype(BF)
    g_kv_act = dot_left(h1_act, gkv_sum[rows:]).astype(BF)
    gxn_pre, g_gain_pa = norm_backward(own(x_pre, rq).astype(F32), gain_pa, gh1_pre)
    gxn_act, g_gain_aa = norm_backward(own(x_act, aq), gain_aa, gh1_act)
    grad_pre = (gx2_pre + gxn_pre).astype(BF)
    gxa = (gx2_act + gxn_act).astype(BF)
    g_embed = dot_left(own(act_in, aq), gxa)
    act_grad = dot_right(gxa, embed).reshape(aq * dims_count // lanes, lanes)

    swap = [(i, i ^ 1) for i in range(n)]
    chip_grads += [
        add(of_core(g, here), lax.ppermute(of_core(g, 1 - here), "dp", swap))
        for g in (g_kv_pre, g_kv_act)
    ]
    def by_index(vector):
        return vector.reshape(n, -1, narrow // n).transpose(1, 0, 2).reshape(-1, narrow)

    tiny = [by_index(g) for g in (g_gain_pa, g_gain_pf, g_gain_aa, g_gain_af)] + [g_embed]
    tiny = jnp.concatenate(tiny, axis=0)
    tiny_rows = tiny.shape[0]
    tiny = columns_first(pad_rows(tiny, round_up(tiny_rows, 16)).astype(BF))

    kernel = Kernel(11)
    chip_parts = [kernel.flow(ChipRows(), g) for g in chip_grads]
    prefix_grad = kernel.flow(Whole(), grad_pre)
    prefix_output = kernel.flow(Whole(), out_pre)
    out_act = kernel.flow(Whole(), out_act)
    act_grad = kernel.flow(World(), act_grad)
    tiny = kernel.flow(Spread(), tiny)
    kernel.relay(prefix_grad, 1)
    kernel.relay(prefix_output, 1)
    kernel.relay(out_act, 1)
    got = kernel.call("finish")
    out_act = got[out_act]

    def chip_sum(own_parts, parts):
        size = own_parts.shape[0] // half
        return summed(lax.dynamic_slice_in_dim(own_parts, me // 2 * size, size, 0), got[parts])

    grad_out, grad_query, grad_out_a, grad_query_a, *both = [
        chip_sum(g, f) for g, f in zip(chip_grads, chip_parts)
    ]
    grad_out, grad_out_a = grad_out.T, grad_out_a.T
    both = jnp.concatenate(both, axis=0).astype(BF)
    both = lax.all_gather(both, "mp", axis=1, tiled=True).astype(F32)
    prefix_grad = got[prefix_grad][:length].astype(F32)
    prefix_output = got[prefix_output][:length]
    act_grad = got[act_grad].reshape(n, acts, dims_count)[:, :steps]
    tiny = jnp.sum(got[tiny].astype(F32), axis=(0, 1))
    mine_items = (slot_item[:, None] == lax.broadcasted_iota(jnp.int32, (1, n), 1)).astype(F32)
    mine_turns = (slot_item[:, None] == jnp.stack(turns)[None, :]).astype(F32)
    out_act = out_act.reshape(1, m, n, aq, narrow).astype(F32)
    action_output = jnp.sum(mine_turns[:, None, :, None, None] * out_act, axis=2)
    action_output = action_output.reshape(slot_count, acts, narrow)[:, :steps].astype(BF)
    own_mask = lax.broadcasted_iota(jnp.int32, (slot_count, dims_count), 1) < valid_dims[:, None]
    action_grad = jnp.sum(
        mine_items[:, :, None, None] * act_grad[None], axis=1
    ) * own_mask.astype(F32)[:, None, :]
    grad_gain_pa = tiny[:twice].reshape(-1)
    grad_gain_pf = tiny[twice : 2 * twice].reshape(-1)
    rest = tiny[2 * twice : tiny_rows]

    if even:
        grad_gate_a, grad_up_a, grad_down_a = act_sum
    else:
        act_sum = act_sum[0]
        grad_gate_a = act_sum[:, :d_act].transpose(1, 0, 2).reshape(d_act, n * few)
        grad_up_a = act_sum[:, d_act : 2 * d_act].transpose(1, 0, 2).reshape(d_act, n * few)
        grad_down_a = act_sum[:, 2 * d_act :].transpose(0, 2, 1).reshape(n * few, d_act)
    return (
        prefix_output,
        action_output,
        prefix_grad,
        action_grad,
        grad_gain_pa,
        grad_query,
        both[:d_pre, :HD],
        both[:d_pre, HD:],
        grad_out,
        grad_gain_pf,
        grad_gate,
        grad_up,
        grad_down,
        rest[2:],
        rest[0],
        grad_query_a,
        both[d_pre:, :HD],
        both[d_pre:, HD:],
        grad_out_a,
        rest[1],
        grad_gate_a,
        grad_up_a,
        grad_down_a,
    )


def solution(mesh):
    return jax.shard_map(
        local,
        mesh=mesh,
        in_specs=(
            P("dp", None),
            P("dp", None, None),
            P("dp"),
            P("dp"),
            P("dp", None),
            P("dp"),
            P("dp", "mp"),
            P("dp", None),
            P("dp", None),
            P("mp", "dp"),
            P("dp"),
            P("dp", "mp"),
            P("dp", "mp"),
            P("mp", "dp"),
            P(None, "dp"),
            P("dp"),
            P("dp", "mp"),
            P("dp", None),
            P("dp", None),
            P("mp", "dp"),
            P("dp"),
            P("dp", "mp"),
            P("dp", "mp"),
            P("mp", "dp"),
            P("dp", None),
            P("dp", None, None),
        ),
        out_specs=(
            P("dp", None),
            P("dp", None, None),
            P("dp", None),
            P("dp", None, None),
            P("dp"),
            P("dp", "mp"),
            P("dp", None),
            P("dp", None),
            P("mp", "dp"),
            P("dp"),
            P("dp", "mp"),
            P("dp", "mp"),
            P("mp", "dp"),
            P(None, "dp"),
            P("dp"),
            P("dp", "mp"),
            P("dp", None),
            P("dp", None),
            P("mp", "dp"),
            P("dp"),
            P("dp", "mp"),
            P("dp", "mp"),
            P("mp", "dp"),
        ),
        check_vma=False,
    )
```

```python
import functools

import jax
import jax.numpy as jnp
from jax import lax
from jax.experimental import pallas as pl
from jax.experimental.pallas import tpu as pltpu
from jax.sharding import PartitionSpec as P

HD = 256
EPS = 1e-06
BF = jnp.bfloat16
F32 = jnp.float32
MESH = pl.DeviceIdType.MESH
HBM = pl.BlockSpec(memory_space=pl.ANY)


def rms_gain(values, gain):
    return values * lax.rsqrt(jnp.mean(values * values, axis=-1, keepdims=True) + EPS) * gain


def norm_backward(values, gain, grad_out):
    unused, pull = jax.vjp(rms_gain, values, gain)
    return pull(grad_out)


def glu_value(gate, upward):
    return jax.nn.gelu(gate, approximate=True) * upward


def glu_backward(gate, upward, grad):
    unused, pull = jax.vjp(glu_value, gate, upward)
    return pull(grad)


def dot_plain(left, right):
    return jnp.dot(left, right, preferred_element_type=F32)


def dot_left(left, right):
    return lax.dot_general(left, right, (((0,), (0,)), ((), ())), preferred_element_type=F32)


def dot_right(left, right):
    return lax.dot_general(left, right, (((1,), (1,)), ((), ())), preferred_element_type=F32)


def round_up(value, step):
    return -(-value // step) * step


def add(left, right):
    return (left.astype(F32) + right.astype(F32)).astype(BF)


def greet(devices):
    barrier = pltpu.get_barrier_semaphore()
    for device in devices:
        pl.semaphore_signal(barrier, inc=1, device_id=device, device_id_type=MESH)
    pl.semaphore_wait(barrier, len(devices))


def at(start, size):
    return pl.ds(pl.multiple_of(start * size, size), size)


class Place:
    def __init__(self, n, m, sent, arrived, first):
        self.n, self.m = n, m
        self.me, self.col = lax.axis_index("dp"), lax.axis_index("mp")
        self.sent, self.arrived, self.first = sent, arrived, first

    def remote(self, src, dst, slot, device):
        return pltpu.make_async_remote_copy(
            src_ref=src,
            dst_ref=dst,
            send_sem=self.sent.at[self.first + slot],
            recv_sem=self.arrived.at[self.first + slot],
            device_id=device,
            device_id_type=MESH,
        )

    def keep(self, src, dst):
        def scoped(buffer):
            pltpu.sync_copy(src, buffer)
            pltpu.sync_copy(buffer, dst)

        pl.run_scoped(scoped, pltpu.VMEM(src.shape, src.dtype))

    def over_dp(self, s):
        return (lax.rem(self.me + s, self.n), self.col)

    def over_mp(self, k):
        return (self.me, self.col ^ k)


def loop(first, last, body):
    lax.fori_loop(first, last, lambda s, carry: (body(s), carry)[1], 0)


class Flow:
    reach = "dp"
    kept = False

    def slots(self, n, m):
        return max(n, m, 4)

    def result(self, shape, n, m):
        return shape

    def each(self, p, src, dst, do):
        pass

    def own(self, p, src, dst):
        return None

    def start(self, p, src, dst):
        self.each(p, src, dst, lambda c: c.start())
        if self.kept:
            p.keep(*self.own(p, src, dst))

    def relay(self, p, src, dst, k):
        return None

    def wait(self, p, src, dst):
        self.each(p, src, dst, lambda c: c.wait())


class Rows(Flow):
    kept = True

    def result(self, shape, n, m):
        return (shape[0] // n, shape[1] * n)

    def own(self, p, src, dst):
        return src.at[at(p.me, src.shape[0] // p.n)], dst.at[:, at(p.me, dst.shape[1] // p.n)]

    def each(self, p, src, dst, do):
        def body(s):
            target = p.over_dp(s)
            block = src.at[at(target[0], src.shape[0] // p.n)]
            do(p.remote(block, dst.at[:, at(p.me, dst.shape[1] // p.n)], s, target))

        loop(1, p.n, body)


class Columns(Flow):
    kept = True

    def result(self, shape, n, m):
        return (shape[0] * n, shape[1] // n)

    def own(self, p, src, dst):
        return src.at[:, at(p.me, src.shape[1] // p.n)], dst.at[at(p.me, dst.shape[0] // p.n)]

    def each(self, p, src, dst, do):
        def body(s):
            target = p.over_dp(s)
            block = src.at[:, at(target[0], src.shape[1] // p.n)]
            do(p.remote(block, dst.at[at(p.me, dst.shape[0] // p.n)], s, target))

        loop(1, p.n, body)


class Each(Flow):
    kept = True

    def own(self, p, src, dst):
        return src.at[p.me], dst.at[p.me]

    def each(self, p, src, dst, do):
        def body(s):
            target = p.over_dp(s)
            do(p.remote(src.at[target[0]], dst.at[p.me], s, target))

        loop(1, p.n, body)


class EachRows(Each):
    def result(self, shape, n, m):
        return (n, shape[0] // n, shape[1])

    def own(self, p, src, dst):
        return src.at[at(p.me, dst.shape[1])], dst.at[p.me]

    def each(self, p, src, dst, do):
        def body(s):
            target = p.over_dp(s)
            do(p.remote(src.at[at(target[0], dst.shape[1])], dst.at[p.me], s, target))

        loop(1, p.n, body)


class Chips(Flow):
    def each(self, p, src, dst, do):
        loop(1, p.n // 2, lambda s: do(p.remote(src.at[s], dst.at[s], s, p.over_dp(2 * s))))


class Core(Flow):
    def result(self, shape, n, m):
        return (shape[0] // 2, shape[1])

    def each(self, p, src, dst, do):
        half = src.shape[0] // 2
        do(p.remote(src.at[pl.ds(half, half)], dst, 0, (p.me ^ 1, p.col)))


class CoreRows(Flow):
    def result(self, shape, n, m):
        return (shape[0] // 2, shape[1])

    def cut(self, ref, i, count):
        return ref.at[at(i, ref.shape[0] // count)]

    def each(self, p, src, dst, do):
        def body(c):
            block = self.cut(src, 2 * c + lax.rem(p.me + 1, 2), p.n)
            do(p.remote(block, self.cut(dst, c, p.n // 2), c, (p.me ^ 1, p.col)))

        loop(0, p.n // 2, body)


class ChipRows(CoreRows):
    def result(self, shape, n, m):
        return (n // 2, shape[0] // (n // 2), shape[1])

    def each(self, p, src, dst, do):
        def body(s):
            target = p.over_dp(2 * s)
            do(p.remote(self.cut(src, target[0] // 2, p.n // 2), dst.at[s], s, target))

        loop(1, p.n // 2, body)


class Line(Flow):
    def __init__(self, place=None, result=None, share=False):
        self.place = place or Line.in_turn
        self.shape = result
        self.share = share
        self.reach = "both" if share else "dp"

    def slots(self, n, m):
        return 2 * n + (n * m if self.share else 0)

    def in_turn(ref, i, j):
        chips = lax.axis_size("dp") // 2
        chip = lax.rem(i // 2 - j // 2 + chips, chips)
        return ref.at[chip + chips * lax.rem(i + j, 2)]

    def result(self, shape, n, m):
        return self.shape or (n,) + shape

    def origin(self, p, first, way, k):
        return lax.rem(first - (2, -2)[way] * k + 2 * p.n, p.n)

    def along(self, p, src, dst, way, k):
        i = self.origin(p, p.me, way, k - 1)
        target = lax.rem(p.me + (2, -2)[way] + p.n, p.n)
        source = src if k == 1 else self.place(dst, i, p.me)
        slot = way * p.n // 2 + k
        return p.remote(source, self.place(dst, i, target), slot, (target, p.col))

    def across(self, p, src, dst, way, k):
        i = self.origin(p, p.me, way, k)
        source = src if k == 0 else self.place(dst, i, p.me)
        slot = (2 + way) * p.n // 2 + k
        return p.remote(source, self.place(dst, i, p.me ^ 1), slot, (p.me ^ 1, p.col))

    def passed(self, p, dst, i, k, source=None):
        block = self.place(dst, i, p.me)
        source = block if source is None else source
        return p.remote(source, block, 2 * p.n + i * p.m + k, p.over_mp(k))

    def receives(self, p, way, k):
        chip = p.me // 2
        if k == 0:
            return chip >= 0
        return chip >= k if way == 0 else chip < p.n // 2 - k

    def sends(self, p, way, k):
        chip = p.me // 2
        beyond = chip < p.n // 2 - 1 if way == 0 else chip > 0
        return beyond & self.receives(p, way, k - 1)

    def start(self, p, src, dst):
        for way in (0, 1):
            pl.when(self.sends(p, way, 1))(self.along(p, src, dst, way, 1).start)
        self.across(p, src, dst, 0, 0).start()
        self.hand(p, dst, p.me, src)
        p.keep(src, self.place(dst, p.me, p.me))

    def hand(self, p, dst, i, source=None):
        if self.share:
            for k in range(1, p.m):
                self.passed(p, dst, i, k, source).start()

    def crossed(self, p, src, dst, way, k):
        self.across(p, src, dst, way, k).wait_recv()
        self.hand(p, dst, self.origin(p, p.me ^ 1, way, k))

    def relay(self, p, src, dst, k):
        if k == 1:
            self.crossed(p, src, dst, 0, 0)
        for way in (0, 1):

            @pl.when(self.receives(p, way, k))
            def _(way=way):
                self.along(p, src, dst, way, k).wait_recv()
                self.across(p, src, dst, way, k).start()
                self.hand(p, dst, self.origin(p, p.me, way, k))

            if k < p.n // 2 - 1:
                pl.when(self.sends(p, way, k + 1))(self.along(p, src, dst, way, k + 1).start)
            if k > 1:
                before = functools.partial(self.crossed, p, src, dst, way, k - 1)
                pl.when(self.receives(p, way, k - 1))(before)

    def wait(self, p, src, dst):
        last = p.n // 2 - 1
        for way in (0, 1):
            end = functools.partial(self.crossed, p, src, dst, way, last)
            pl.when(self.receives(p, way, last))(end)
        self.across(p, src, dst, 0, 0).wait_send()
        for way in (0, 1):
            for k in range(1, last + 1):
                pl.when(self.sends(p, way, k))(self.along(p, src, dst, way, k).wait_send)
                pl.when(self.receives(p, way, k))(self.across(p, src, dst, way, k).wait_send)
        if self.share:
            for k in range(1, p.m):
                loop(0, p.n, lambda i, k=k: self.passed(p, dst, i, k).wait())


class Pass(Flow):
    reach = "mp"
    kept = True
    parts = 8

    def __init__(self, axis):
        self.axis = axis

    def slots(self, n, m):
        return max(4, m) * self.parts

    def result(self, shape, n, m):
        return (shape[0], m * shape[1]) if self.axis else (m * shape[0], shape[1])

    def spot(self, p, src, dst, k, c=None):
        rows, width = src.shape
        first, count = (0, rows) if c is None else (c * (rows // self.parts), rows // self.parts)
        if self.axis:
            return dst.at[pl.ds(first, count), pl.ds(k * width, width)]
        return dst.at[pl.ds(k * rows + first, count)]

    def own(self, p, src, dst):
        return src, self.spot(p, src, dst, 0)

    def direct(self, p, src, dst, k, c):
        few = src.shape[0] // self.parts
        block = src.at[pl.ds(c * few, few)]
        slot = k * self.parts + c
        return p.remote(block, self.spot(p, src, dst, k, c), slot, p.over_mp(k))

    def turned(self, p, src, dst, c):
        via = 1 + c % 2
        source = self.spot(p, src, dst, via, c)
        slot = 3 * self.parts + c
        return p.remote(source, self.spot(p, src, dst, 3, c), slot, p.over_mp(3 - via))

    def each(self, p, src, dst, do):
        for c in range(self.parts):
            for k in range(1, 3 if p.m == 4 else p.m):
                do(self.direct(p, src, dst, k, c))

    def start(self, p, src, dst):
        self.each(p, src, dst, lambda c: c.start())

    def relay(self, p, src, dst, k):
        if p.m == 4:
            for c in range((k - 1) * self.parts // 2, k * self.parts // 2):
                self.direct(p, src, dst, 1 + c % 2, c).wait_recv()
                self.turned(p, src, dst, c).start()

    def wait(self, p, src, dst):
        p.keep(*self.own(p, src, dst))
        for c in range(self.parts):
            for k in range(1, 3 if p.m == 4 else p.m):
                copy = self.direct(p, src, dst, k, c)
                (copy.wait_send if p.m == 4 and k == 1 + c % 2 else copy.wait)()
            if p.m == 4:
                self.turned(p, src, dst, c).wait()


def by_way(rows, m):
    return round_up(rows // 2, 16) if m == 4 and rows >= 64 else 0


class Parts(Flow):
    reach = "mp"

    def result(self, shape, n, m):
        rows = shape[-2] if len(shape) == 3 else shape[0] // m
        return (m + 1, rows, shape[-1])

    def block(self, p, src, k):
        i = self.index(p, k)
        return src.at[i] if len(src.shape) == 3 else src.at[at(i, src.shape[0] // p.m)]

    def index(self, p, k):
        return p.col ^ k

    def halves(self, p, dst):
        first = by_way(dst.shape[1], p.m)
        return [(1, pl.ds(0, first)), (2, pl.ds(first, dst.shape[1] - first))] if first else []

    def each(self, p, src, dst, do):
        halves = self.halves(p, dst)
        for k in range(1, 3 if halves else p.m):
            do(p.remote(self.block(p, src, k), dst.at[k], k, p.over_mp(k)))

    def sideways(self, p, src, dst, via, cut):
        block = self.block(p, src, 3).at[cut]
        return p.remote(block, dst.at[p.m, cut], p.m + via, p.over_mp(via))

    def onward(self, p, dst, via, cut):
        return p.remote(dst.at[p.m, cut], dst.at[3, cut], p.m + 2 + via, p.over_mp(3 - via))

    def slots(self, n, m):
        return m + 5

    def start(self, p, src, dst):
        for via, cut in self.halves(p, dst):
            self.sideways(p, src, dst, via, cut).start()
        self.each(p, src, dst, lambda c: c.start())

    def relay(self, p, src, dst, k):
        for via, cut in self.halves(p, dst):
            self.sideways(p, src, dst, via, cut).wait_recv()
            self.onward(p, dst, via, cut).start()

    def wait(self, p, src, dst):
        self.each(p, src, dst, lambda c: c.wait())
        for via, cut in self.halves(p, dst):
            self.sideways(p, src, dst, via, cut).wait_send()
            self.onward(p, dst, via, cut).wait()


class Swaps(Parts):
    def __init__(self, axis=0):
        self.axis = axis

    def result(self, shape, n, m):
        if len(shape) == 3:
            return (m + 1,) + shape[1:]
        return (m + 1, shape[0], shape[1] // m) if self.axis else (m + 1, shape[0] // m, shape[1])

    def block(self, p, src, k):
        if len(src.shape) == 3:
            return src.at[k]
        size = src.shape[self.axis] // p.m
        cut = pl.ds(k * size, size)
        return src.at[:, cut] if self.axis else src.at[cut]


class Whole(Flow):
    reach = "mp"

    def result(self, shape, n, m):
        return (m * shape[0], shape[1])

    def slots(self, n, m):
        return m + 3

    def spot(self, src, dst, i, cut=None):
        rows = src.shape[0]
        if cut is None:
            return dst.at[at(i, rows)]
        return dst.at[pl.ds(pl.multiple_of(i * rows + cut[0], 16), cut[1])]

    def halves(self, p, src):
        first = by_way(src.shape[0], p.m)
        return [(1, (0, first)), (2, (first, src.shape[0] - first))] if first else []

    def direct(self, p, src, dst, k):
        return p.remote(src, self.spot(src, dst, p.col), k, p.over_mp(k))

    def onward(self, p, src, dst, via, cut):
        block = self.spot(src, dst, p.col ^ via, cut)
        return p.remote(block, block, p.m + via, p.over_mp(3 - via))

    def start(self, p, src, dst):
        for k in range(1, 3 if self.halves(p, src) else p.m):
            self.direct(p, src, dst, k).start()
        p.keep(src, self.spot(src, dst, p.col))

    def relay(self, p, src, dst, k):
        for via, cut in self.halves(p, src):
            self.direct(p, src, dst, via).wait_recv()
            self.onward(p, src, dst, via, cut).start()

    def wait(self, p, src, dst):
        halves = self.halves(p, src)
        for k in range(1, 3 if halves else p.m):
            copy = self.direct(p, src, dst, k)
            (copy.wait_send if halves else copy.wait)()
        for via, cut in halves:
            self.onward(p, src, dst, via, cut).wait()


class Swap(Flow):
    reach = "mp"

    def __init__(self, k):
        self.k = k

    def each(self, p, src, dst, do):
        do(p.remote(src, dst, 0, p.over_mp(self.k)))


class First(Flow):
    reach = "mp"

    def __init__(self, axis):
        self.axis = axis

    def result(self, shape, n, m):
        if self.axis:
            return (4, shape[0] // 2, shape[1] // m)
        return (4, shape[0] // m, shape[1] // 2)

    def each(self, p, src, dst, do):
        width, deep = src.shape[self.axis] // p.m, src.shape[1 - self.axis] // 2
        for k, part in enumerate((1, 3, 2, 3)):
            block, half = pl.ds(part * width, width), pl.ds(k // 2 * deep, deep)
            source = src.at[half, block] if self.axis else src.at[block, half]
            do(p.remote(source, dst.at[k], k, p.over_mp(1 + k // 2)))


class World(Flow):
    reach = "world"
    kept = True

    def slots(self, n, m):
        return n * m

    def result(self, shape, n, m):
        return (n, m) + shape

    def block(self, src, i):
        return src

    def own(self, p, src, dst):
        return self.block(src, p.me), dst.at[p.me, p.col]

    def each(self, p, src, dst, do):
        for k in range(p.m):

            def body(s, k=k):
                target = (lax.rem(p.me + s, p.n), p.col ^ k)
                copy = p.remote(
                    self.block(src, target[0]), dst.at[p.me, p.col], s * p.m + k, target
                )
                do(copy)

            loop(0 if k else 1, p.n, body)


class Spread(World):
    def result(self, shape, n, m):
        return (n, m) + shape[1:]

    def block(self, src, i):
        return src.at[i]


class Kernel:
    def __init__(self, collective_id):
        self.collective_id = collective_id
        self.inputs, self.outputs, self.flows, self.steps = [], [], [], []

    def operand(self, source):
        if isinstance(source, int):
            return ("out", source)
        self.inputs.append(source)
        return ("in", len(self.inputs) - 1)

    def shape_of(self, source):
        return self.outputs[source] if isinstance(source, int) else source

    def new_output(self, shape, dtype):
        self.outputs.append(jax.ShapeDtypeStruct(shape, dtype))
        return len(self.outputs) - 1

    def flow(self, kind, source, now=True, into=None):
        n, m = lax.axis_size("dp"), lax.axis_size("mp")
        like = self.shape_of(source)
        out = into
        if into is None:
            out = self.new_output(kind.result(like.shape, n, m), like.dtype)
        name = out if into is None else -1 - len(self.flows)
        self.flows.append((kind, self.operand(source), out, name))
        if now:
            self.go(name)
        return name

    def go(self, name):
        self.steps.append(("start", name))

    def relay(self, name, k):
        self.steps.append(("relay", name, k))

    def ready(self, name):
        self.steps.append(("wait", name))

    def job(self, body, sources, shapes, dtype=BF, into=None):
        outs = into or [self.new_output(s, dtype) for s in shapes]
        self.steps.append(("job", body, [self.operand(s) for s in sources], outs))
        return outs if len(outs) > 1 else outs[0]

    def call(self, name):
        n, m = lax.axis_size("dp"), lax.axis_size("mp")
        takes, gives = len(self.inputs), len(self.outputs)
        flows, steps = self.flows, self.steps
        rows = {flow[3]: row for row, flow in enumerate(flows)}
        reach = {flow[0].reach for flow in flows}
        firsts = [0]
        for flow in flows:
            firsts.append(firsts[-1] + flow[0].slots(n, m))

        def kernel(*refs):
            ins, outs = refs[:takes], refs[takes : takes + gives]
            sent, arrived = refs[takes + gives :]
            me, col = lax.axis_index("dp"), lax.axis_index("mp")
            if "world" in reach:
                greet([(lax.rem(me + s, n), col ^ k) for s in range(n) for k in range(m) if s or k])
            else:
                column = [(lax.rem(me + s, n), col) for s in range(1, n)]
                row = [(me, col ^ k) for k in range(1, m)]
                greet(
                    (column if reach & {"dp", "both"} else [])
                    + (row if reach & {"mp", "both"} else [])
                )

            def ref(operand):
                return (ins if operand[0] == "in" else outs)[operand[1]]

            def act(what, name, *rest):
                kind, source, out, unused = flows[rows[name]]
                place = Place(n, m, sent, arrived, firsts[rows[name]])
                getattr(kind, what)(place, ref(source), outs[out], *rest)

            ended = set()
            for step in steps:
                if step[0] == "job":
                    step[1]([ref(s) for s in step[2]], [outs[o] for o in step[3]])
                else:
                    act(*step)
                    if step[0] == "wait":
                        ended.add(step[1])
            for flow in flows:
                if flow[3] not in ended:
                    act("wait", flow[3])

        return pl.pallas_call(
            kernel,
            out_shape=self.outputs,
            in_specs=[HBM] * takes,
            out_specs=[HBM] * gives,
            scratch_shapes=[
                pltpu.SemaphoreType.DMA((firsts[-1],)),
                pltpu.SemaphoreType.DMA((firsts[-1],)),
            ],
            compiler_params=pltpu.CompilerParams(
                collective_id=self.collective_id,
                has_side_effects=True,
                vmem_limit_bytes=56 << 20,
            ),
            name=name,
        )(*self.inputs)


def tile(size, most):
    return max(t for t in range(16, most + 1, 16) if size % t == 0)


def products_plain(inputs, outputs):
    a, b = inputs
    (rows, depth), width = a.shape, b.shape[1]
    bm, bn = tile(rows, 832), tile(width, 512)

    def body(a_ref, b_ref, o_ref):
        o_ref[...] = dot_plain(a_ref[...], b_ref[...]).astype(BF)

    pltpu.emit_pipeline(
        body,
        grid=(width // bn, rows // bm),
        in_specs=[
            pl.BlockSpec((bm, depth), lambda j, i: (i, 0)),
            pl.BlockSpec((depth, bn), lambda j, i: (0, j)),
        ],
        out_specs=[pl.BlockSpec((bm, bn), lambda j, i: (i, j))],
    )(a, b, outputs[0])


def products_right(inputs, outputs):
    pairs = len(inputs) // 2
    rows, width = inputs[0].shape[0], inputs[1].shape[0]
    bm, bn = tile(rows, 832), tile(width, 512)

    def body(*refs):
        total = dot_right(refs[0][...], refs[1][...])
        for p in range(1, pairs):
            total = total + dot_right(refs[2 * p][...], refs[2 * p + 1][...])
        refs[-1][...] = total.astype(BF)

    specs = []
    for p in range(pairs):
        depth = inputs[2 * p].shape[1]
        specs.append(pl.BlockSpec((bm, depth), lambda i, j: (i, 0)))
        specs.append(pl.BlockSpec((bn, depth), lambda i, j: (j, 0)))
    pltpu.emit_pipeline(
        body,
        grid=(rows // bm, width // bn),
        in_specs=specs,
        out_specs=[pl.BlockSpec((bm, bn), lambda i, j: (i, j))],
    )(*inputs, outputs[0])


def products_left(inputs, outputs):
    a, rest = inputs[0], inputs[1:]
    (depth, rows), width = a.shape, rest[0].shape[1]
    bm, bn = tile(rows, 1024), tile(width, 512)
    count = len(rest)

    def body(a_ref, *refs):
        for p in range(count):
            refs[count + p][...] = dot_left(a_ref[...], refs[p][...]).astype(BF)

    pltpu.emit_pipeline(
        body,
        grid=(rows // bm, width // bn),
        in_specs=[pl.BlockSpec((depth, bm), lambda i, j: (0, i))]
        + [pl.BlockSpec((depth, bn), lambda i, j: (0, j))] * count,
        out_specs=[pl.BlockSpec((bm, bn), lambda i, j: (i, j))] * count,
    )(a, *rest, *outputs)


def hidden_forward(part, parts, inputs, outputs):
    h, w_gate, w_up = inputs
    (rows, depth), width = h.shape, w_gate.shape[1] // parts
    cut = pl.ds(part * width, width)
    w_gate, w_up = w_gate.at[:, cut], w_up.at[:, cut]
    outputs = [o.at[:, cut] for o in outputs]
    bm, bn = tile(rows, 832), tile(width, 512)

    def body(h_ref, gate_w, up_w, gate_ref, up_ref, hidden_ref):
        gate = dot_plain(h_ref[...], gate_w[...])
        upward = dot_plain(h_ref[...], up_w[...])
        gate_ref[...] = gate.astype(BF)
        up_ref[...] = upward.astype(BF)
        hidden_ref[...] = glu_value(gate, upward).astype(BF)

    block = pl.BlockSpec((bm, bn), lambda j, i: (i, j))
    pltpu.emit_pipeline(
        body,
        grid=(width // bn, rows // bm),
        in_specs=[pl.BlockSpec((bm, depth), lambda j, i: (i, 0))]
        + [pl.BlockSpec((depth, bn), lambda j, i: (0, j))] * 2,
        out_specs=[block] * 3,
    )(h, w_gate, w_up, *outputs)


def hidden_backward(inputs, outputs):
    gz, w_down, gate, upward = inputs
    (rows, depth), width = gz.shape, w_down.shape[0]
    bm, bn = tile(rows, 832), tile(width, 512)

    def body(gz_ref, down_w, gate_ref, up_ref, dgate_ref, dup_ref):
        grad = dot_right(gz_ref[...], down_w[...])
        dgate, dup = glu_backward(gate_ref[...].astype(F32), up_ref[...].astype(F32), grad)
        dgate_ref[...] = dgate.astype(BF)
        dup_ref[...] = dup.astype(BF)

    block = pl.BlockSpec((bm, bn), lambda j, i: (i, j))
    pltpu.emit_pipeline(
        body,
        grid=(width // bn, rows // bm),
        in_specs=[
            pl.BlockSpec((bm, depth), lambda j, i: (i, 0)),
            pl.BlockSpec((bn, depth), lambda j, i: (j, 0)),
            block,
            block,
        ],
        out_specs=[block] * 2,
    )(gz, w_down, gate, upward, *outputs)


def act_feed_forward(inputs, outputs):
    def body(h_ref, gz_ref, gate_w, up_w, down_w, z, dh2, g_gate, g_up, g_down):
        h, gz = h_ref[...], gz_ref[...]
        gate, upward = dot_plain(h, gate_w[...]), dot_plain(h, up_w[...])
        hidden = glu_value(gate, upward).astype(BF)
        z[...] = dot_plain(hidden, down_w[...]).astype(BF)
        g_down[...] = dot_left(hidden, gz).astype(BF)
        dgate, dup = glu_backward(gate, upward, dot_right(gz, down_w[...]))
        dgate, dup = dgate.astype(BF), dup.astype(BF)
        dh2[...] = (dot_right(dgate, gate_w[...]) + dot_right(dup, up_w[...])).astype(BF)
        g_gate[...] = dot_left(h, dgate).astype(BF)
        g_up[...] = dot_left(h, dup).astype(BF)

    def whole(ref):
        return pl.BlockSpec(ref.shape, lambda i: (0, 0))

    pltpu.emit_pipeline(
        body,
        grid=(1,),
        in_specs=[whole(r) for r in inputs],
        out_specs=[whole(r) for r in outputs],
    )(*inputs, *outputs)


def attend_forward(inputs, outputs):
    query, keys, values, seg_q, seg_k = inputs
    probs, mixed = outputs
    total = query.shape[0]
    rows = tile(total, 448)

    def body(q_ref, k_ref, v_ref, sq_ref, sk_ref, p_ref, o_ref):
        allowed = sq_ref[:, :1] >= sk_ref[:1]
        scores = dot_right(q_ref[...], k_ref[...]) * HD ** (-0.5)
        scores = jnp.where(allowed, scores, -1e30)
        raised = jnp.exp(scores - jnp.max(scores, axis=-1, keepdims=True))
        p = (raised / jnp.sum(raised, axis=-1, keepdims=True)).astype(BF)
        p_ref[...] = p
        o_ref[...] = dot_plain(p, v_ref[...]).astype(BF)

    def rest(shape):
        return pl.BlockSpec(shape, lambda i: (0, 0))

    pltpu.emit_pipeline(
        body,
        grid=(total // rows,),
        in_specs=[
            pl.BlockSpec((rows, HD), lambda i: (i, 0)),
            rest(keys.shape),
            rest(values.shape),
            pl.BlockSpec((rows, seg_q.shape[1]), lambda i: (i, 0)),
            rest(seg_k.shape),
        ],
        out_specs=[
            pl.BlockSpec((rows, total), lambda i: (i, 0)),
            pl.BlockSpec((rows, HD), lambda i: (i, 0)),
        ],
    )(query, keys, values, seg_q, seg_k, probs, mixed)


def attend_backward(heads, inputs, outputs):
    probs, query = inputs[:heads], inputs[heads : 2 * heads]
    keys, values, grad = inputs[2 * heads :]
    grad_query, (both, shares) = outputs[:heads], outputs[heads:]
    total, scale = keys.shape[0], HD ** (-0.5)
    rows = tile(total, 448)
    width = shares.shape[2]

    def scoped(sums, rounded, parted):
        sums[...] = jnp.zeros_like(sums)

        def body(*refs):
            k_ref, v_ref, g_ref = refs[2 * heads : 2 * heads + 3]
            for h in range(heads):
                g = g_ref[:, h * HD : (h + 1) * HD]
                p, q = refs[h][...], refs[heads + h][...]
                wide_p = p.astype(F32)
                dp = dot_right(g, v_ref[...])
                ds = wide_p * (dp - jnp.sum(wide_p * dp, axis=-1, keepdims=True))
                ds = ds.astype(BF)
                refs[2 * heads + 3 + h][...] = (dot_plain(ds, k_ref[...]) * scale).astype(BF)
                sums[:, :HD] += dot_left(ds, q) * scale
                sums[:, HD:] += dot_left(p, g)

        def rest(ref):
            return pl.BlockSpec(ref.shape, lambda i: (0, 0))

        block = pl.BlockSpec((rows, HD), lambda i: (i, 0))
        pltpu.emit_pipeline(
            body,
            grid=(total // rows,),
            in_specs=[pl.BlockSpec((rows, total), lambda i: (i, 0))] * heads
            + [block] * heads
            + [rest(keys), rest(values), pl.BlockSpec((rows, heads * HD), lambda i: (i, 0))],
            out_specs=[block] * heads,
        )(*probs, *query, keys, values, grad, *grad_query)
        rounded[...] = sums[...].astype(BF)
        for k in range(shares.shape[0]):
            parted[k] = sums[:, k * width : (k + 1) * width].astype(BF)
        pltpu.sync_copy(rounded, both)
        pltpu.sync_copy(parted, shares)

    pl.run_scoped(
        scoped,
        pltpu.VMEM((total, 2 * HD), F32),
        pltpu.VMEM((total, 2 * HD), BF),
        pltpu.VMEM(shares.shape, BF),
    )


def rows_from(first, count, body):
    return lambda inputs, outputs: body([inputs[0].at[pl.ds(first, count)]] + inputs[1:], outputs)


def add_pairs(pairs, outputs):
    (rows, width), count = outputs[0].shape, len(outputs)

    def body(*refs):
        for k in range(count):
            refs[2 * count + k][...] = add(refs[2 * k][...], refs[2 * k + 1][...])

    block = pl.BlockSpec((tile(rows, 256), width), lambda i: (i, 0))
    pltpu.emit_pipeline(
        body,
        grid=(rows // tile(rows, 256),),
        in_specs=[block] * (2 * count),
        out_specs=[block] * count,
    )(*[ref for pair in pairs for ref in pair], *outputs)


def second_norm(count, inputs, outputs):
    x, y, parts, gain = inputs
    m, width = parts.shape[0] - 1, parts.shape[2]
    rows = at(lax.axis_index("mp"), count)

    def body(x_ref, y_ref, parts_ref, gain_ref, sum_ref, normed_ref):
        total = x_ref[...].astype(F32) + y_ref[...].astype(F32)
        for k in range(m - 1):
            total = total + parts_ref[k].astype(F32)
        sum_ref[...] = total
        normed_ref[...] = rms_gain(total, gain_ref[:1]).astype(BF)

    block = pl.BlockSpec((count, width), lambda i: (0, 0))
    pltpu.emit_pipeline(
        body,
        grid=(1,),
        in_specs=[
            block,
            block,
            pl.BlockSpec((m - 1, count, width), lambda i: (0, 0, 0)),
            pl.BlockSpec(gain.shape, lambda i: (0, 0)),
        ],
        out_specs=[block, block],
    )(x.at[rows], y.at[rows], parts.at[pl.ds(1, m - 1)], gain, *outputs)


class Halves:
    def __init__(self, axis):
        self.axis = axis

    def settle(self, got):
        for name, value in vars(self).items():
            if name != "axis" and isinstance(value, int):
                setattr(self, name, got[value])

    def first(self, kernel, whole):
        self.whole = whole
        self.parts = kernel.flow(First(self.axis), whole)

    def second(self, kernel):
        axis = self.axis

        def take(inputs, outputs):
            whole, parts = inputs
            width, deep = whole.shape[axis] // 4, whole.shape[1 - axis] // 2

            def part(half, k):
                block, deeps = pl.ds(k * width, width), pl.ds(half * deep, deep)
                return whole.at[deeps, block] if axis else whole.at[block, deeps]

            own = [part(0, 0), part(0, 2), part(1, 0), part(1, 1)]
            add_pairs([(own[k], parts.at[k]) for k in range(4)], outputs)

        like = kernel.shape_of(self.parts).shape[1:]
        self.top, next_y, self.low, next_x = kernel.job(take, [self.whole, self.parts], [like] * 4)
        self.from_y = kernel.flow(Swap(2), next_y)
        self.from_x = kernel.flow(Swap(1), next_x)

    def total(self, kernel):
        axis = self.axis
        rows, width = kernel.shape_of(self.top).shape

        def join(inputs, outputs):
            top, low, from_y, from_x = inputs
            halves = [(top, from_y), (low, from_x)]
            for k, pair in enumerate(halves):
                spot = pl.ds(k * rows, rows) if axis else (slice(None), pl.ds(k * width, width))
                add_pairs([pair], [outputs[0].at[spot]])

        shape = (2 * rows, width) if axis else (rows, 2 * width)
        return kernel.job(join, [self.top, self.low, self.from_y, self.from_x], [shape])


class Direct:
    def __init__(self, axis):
        self.axis = axis

    def settle(self, got):
        if isinstance(self.whole, int):
            self.whole = got[self.whole]

    def first(self, kernel, whole):
        self.whole = whole

    def second(self, kernel):
        return None

    def total(self, kernel):
        parts = jnp.split(self.whole, lax.axis_size("mp"), axis=self.axis)
        total = parts[0].astype(F32)
        for k in range(1, len(parts)):
            pairs = [(i, i ^ k) for i in range(len(parts))]
            total = total + lax.ppermute(parts[k], "mp", pairs).astype(F32)
        return total.astype(BF)


def project_rows(first, heads, inputs, outputs):
    x, gain, w_in = inputs
    rows, depth = x.shape
    block = tile(rows, 416)

    def body(x_ref, gain_ref, w_ref, normed_ref, *refs):
        normed = rms_gain(x_ref[...].astype(F32), gain_ref[:1]).astype(BF)
        normed_ref[...] = normed
        for k in range(heads + 2):
            refs[k][...] = dot_plain(normed, w_ref[:, k * HD : (k + 1) * HD]).astype(BF)

    spots = [o.at[pl.ds(first, rows)] for o in outputs[1:]]
    pltpu.emit_pipeline(
        body,
        grid=(rows // block,),
        in_specs=[
            pl.BlockSpec((block, depth), lambda i: (i, 0)),
            pl.BlockSpec(gain.shape, lambda i: (0, 0)),
            pl.BlockSpec(w_in.shape, lambda i: (0, 0)),
        ],
        out_specs=[pl.BlockSpec((block, depth), lambda i: (i, 0))]
        + [pl.BlockSpec((block, HD), lambda i: (i, 0))] * (heads + 2),
    )(x, gain, w_in, outputs[0], *spots)


def local(
    prefix_input,
    action_input,
    valid_dims,
    slot_item,
    segments,
    pre_gain_attn,
    pre_query,
    pre_key,
    pre_value,
    pre_output,
    pre_gain_ffn,
    pre_gate,
    pre_up,
    pre_down,
    act_embed,
    act_gain_attn,
    act_query,
    act_key,
    act_value,
    act_output,
    act_gain_ffn,
    act_gate,
    act_up,
    act_down,
    prefix_cotangent,
    action_cotangent,
):
    n, m = lax.axis_size("dp"), lax.axis_size("mp")
    me, col = lax.axis_index("dp"), lax.axis_index("mp")
    length, wide = prefix_input.shape
    slot_count, steps, dims_count = action_input.shape
    narrow = action_cotangent.shape[2]
    rq = round_up(-(-length // m), 16)
    aq = round_up(-(-steps // m), 16)
    rows, acts = m * rq, m * aq
    total_rows = rows + acts
    half = n // 2
    heads = pre_query.shape[1] // HD
    split = heads * HD
    scale = HD ** (-0.5)
    kvw = 2 * HD // m
    d_pre, d_act = pre_query.shape[0], act_query.shape[0]
    few = act_gate.shape[1] // n
    lanes = 128
    twice = wide // narrow
    turns = [lax.rem(me + 2 * k, n) for k in range(half)]
    turns = turns + [t ^ 1 for t in turns]

    def own(array, count):
        return lax.dynamic_slice_in_dim(array, col * count, count, 0)

    def pad_rows(array, count):
        return jnp.pad(array, ((0, count - array.shape[0]), (0, 0)))

    def lane_rows(array):
        flat = array.reshape(-1)
        count = round_up(-(-flat.shape[0] // lanes), 16)
        return jnp.pad(flat, (0, count * lanes - flat.shape[0])).reshape(count, lanes)

    def columns_first(array):
        return array.reshape(array.shape[0], n, -1).transpose(1, 0, 2)

    even = few % lanes == 0 and d_act % lanes == 0

    smalls = [pre_gain_attn, pre_gain_ffn, act_gain_attn, act_gain_ffn, act_embed, action_input]
    small = jnp.concatenate([lane_rows(a) for a in smalls], axis=0)
    ints = jnp.pad(jnp.stack([slot_item, valid_dims]), ((0, 6), (0, lanes - slot_count)))
    cot_rows = lax.dynamic_slice_in_dim(
        jnp.pad(action_cotangent, ((0, 0), (0, acts - steps), (0, 0))), col * aq, aq, 1
    ).reshape(slot_count * aq, narrow)

    def share_of(key, value):
        return own(jnp.concatenate([key, value], axis=1).T, kvw).T

    def by_rows(size):
        return lambda ref, i, j: ref.at[at(i, size)]

    def by_columns(size):
        return lambda ref, i, j: ref.at[:, at(i, size)]

    def by_share(size):
        return lambda ref, i, j: ref.at[lax.axis_index("mp"), at(i, size)]

    def by_lead(ref, i, j):
        return ref.at[i]

    kernel = Kernel(1)
    aligned = kvw % lanes == 0
    in_pre, in_act = (wide, split + 2 * HD), (narrow, split + 2 * HD)
    kv_pre, kv_act = share_of(pre_key, pre_value), share_of(act_key, act_value)

    def in_columns(size, share):
        def place(ref, i, j):
            start = split + lax.axis_index("mp") * kvw if share else 0
            columns = pl.ds(pl.multiple_of(start, lanes), kvw if share else split)
            return ref.at[at(i, size), columns]

        return place

    if aligned:
        w_in_pre = kernel.flow(Line(in_columns(d_pre, True), in_pre, True), kv_pre)
        w_in_act = kernel.flow(Line(in_columns(d_act, True), in_act, True), kv_act)
        lines = [w_in_pre, w_in_act]
    else:
        w_kv_pre = kernel.flow(Line(by_share(d_pre), (m, wide, kvw), True), kv_pre)
        w_kv_act = kernel.flow(Line(by_share(d_act), (m, narrow, kvw), True), kv_act)
        lines = [w_kv_pre, w_kv_act]
    small = kernel.flow(Line(by_lead, (n,) + small.shape), small)
    ints = kernel.flow(Line(by_lead, (n, 8, lanes)), ints)
    if aligned:
        w_q_pre = kernel.flow(Line(in_columns(d_pre, False)), pre_query, into=w_in_pre)
        w_q_act = kernel.flow(Line(in_columns(d_act, False)), act_query, into=w_in_act)
    else:
        w_q_pre = kernel.flow(Line(by_rows(d_pre), (wide, split)), pre_query)
        w_q_act = kernel.flow(Line(by_rows(d_act), (narrow, split)), act_query)
    w_out_pre = kernel.flow(Line(by_columns(d_pre), (split, wide)), pre_output)
    if even:
        w_out_act = kernel.flow(Line(by_columns(d_act), (split, narrow)), act_output)
    else:
        w_out_act = kernel.flow(Line(by_lead, (n, split, d_act)), act_output)
    cot_all = kernel.flow(Line(by_lead, (n, slot_count * aq, narrow)), cot_rows)
    lines += [small, ints, w_q_pre, w_q_act, w_out_pre, w_out_act, cot_all]
    for k in range(1, half):
        for out in lines:
            kernel.relay(out, k)
    got = kernel.call("gather")
    small, ints, cot_all = got[small], got[ints], got[cot_all]
    w_out_pre, w_out_act = got[w_out_pre], got[w_out_act]
    if aligned:
        w_in_pre, w_in_act = got[w_in_pre], got[w_in_act]
    else:
        w_in_pre = jnp.concatenate([got[w_q_pre]] + [got[w_kv_pre][k] for k in range(m)], axis=1)
        w_in_act = jnp.concatenate([got[w_q_act]] + [got[w_kv_act][k] for k in range(m)], axis=1)
    smalls_all, begin = [], 0
    for a in smalls:
        count = round_up(-(-a.size // lanes), 16)
        flat = small[:, begin : begin + count].reshape(n, -1)[:, : a.size]
        smalls_all.append(flat.reshape((n,) + a.shape))
        begin += count
    gain_pa, gain_pf, gain_aa, gain_af = [g.reshape(-1).astype(F32) for g in smalls_all[:4]]
    embed = smalls_all[4].transpose(1, 0, 2).reshape(dims_count, narrow)
    act_all = smalls_all[5].reshape(n * slot_count, steps, dims_count)
    slot_all = ints[:, 0, :slot_count].reshape(-1)
    valid_all = ints[:, 1, :slot_count].reshape(-1)
    if not even:
        w_out_act = w_out_act.transpose(1, 0, 2).reshape(split, narrow)

    mine = (slot_all == me).astype(F32)
    valid = jnp.sum(mine * valid_all.astype(F32))
    dims_mask = (lax.broadcasted_iota(jnp.int32, (1, dims_count), 1).astype(F32) < valid).astype(BF)
    act_in = jnp.sum(mine[:, None, None] * act_all.astype(F32), axis=0).astype(BF) * dims_mask
    act_in = pad_rows(act_in, acts)

    x_pre = pad_rows(prefix_input, rows)
    x_act = dot_plain(act_in, embed)
    last, never = 1 << 10, 1 << 20
    seg = jnp.pad(segments[0], (0, rows - length), constant_values=never)
    seg_q = jnp.concatenate([jnp.minimum(seg, last), jnp.full((acts,), last, jnp.int32)])
    own_keys = jnp.where(jnp.arange(acts, dtype=jnp.int32) < steps, last, never)
    seg_k = jnp.concatenate([seg, own_keys])
    seg_q = jnp.broadcast_to(seg_q[:, None], (total_rows, lanes))
    seg_k = jnp.broadcast_to(seg_k[None, :], (8, total_rows))

    gz_pre = own(pad_rows(prefix_cotangent, rows), rq)
    if not even:
        act_weights = jnp.concatenate(
            [
                columns_first(act_gate),
                columns_first(act_up),
                act_down.reshape(n, few, d_act).transpose(0, 2, 1),
            ],
            axis=1,
        )

    def project(first, count):
        def body(inputs, outputs):
            pairs = len(inputs) - 1
            w_out = inputs[-1]
            width = w_out.shape[1]
            bm, bn = tile(count, 416), tile(width, 1024)

            def step(*refs):
                value = dot_plain(refs[0][...], refs[1][...])
                for h in range(1, pairs):
                    value = value + dot_plain(refs[2 * h][...], refs[2 * h + 1][...])
                refs[-1][...] = value.astype(BF)

            operands, specs = [], []
            for h in range(pairs):
                operands += [inputs[h].at[pl.ds(first, count)], w_out.at[pl.ds(h * HD, HD)]]
                specs += [
                    pl.BlockSpec((bm, HD), lambda j, i: (i, 0)),
                    pl.BlockSpec((HD, bn), lambda j, i: (0, j)),
                ]
            pltpu.emit_pipeline(
                step,
                grid=(width // bn, count // bm),
                in_specs=specs,
                out_specs=[pl.BlockSpec((bm, bn), lambda j, i: (i, j))],
            )(*operands, outputs[0])

        return body

    kernel = Kernel(2)
    gate_own = kernel.flow(Columns(), pre_gate)
    up_own = kernel.flow(Columns(), pre_up, now=False)
    h1_pre, *into = kernel.job(
        functools.partial(project_rows, 0, heads),
        [x_pre, jnp.broadcast_to(gain_pa, (8, wide)), w_in_pre],
        [(rows, wide)] + [(total_rows, HD)] * (heads + 2),
    )
    h1_act = kernel.new_output((acts, narrow), BF)
    kernel.job(
        functools.partial(project_rows, rows, heads),
        [x_act, jnp.broadcast_to(gain_aa, (8, narrow)), w_in_act],
        [],
        into=[h1_act] + into,
    )
    query, keys, values = into[:heads], into[heads], into[heads + 1]
    probs, mixed = [], []
    for h in range(heads):
        p, o = kernel.job(
            attend_forward,
            [query[h], keys, values, seg_q, seg_k],
            [(total_rows, total_rows), (total_rows, HD)],
        )
        probs.append(p)
        mixed.append(o)
    y_pre = kernel.job(project(0, rows), mixed + [w_out_pre], [(rows, wide)])
    y_act = kernel.job(project(rows, acts), mixed + [w_out_act], [(acts, narrow)])
    y_pre_parts = kernel.flow(Parts(), y_pre)
    y_act_parts = kernel.flow(Parts(), y_act)
    kernel.ready(gate_own)
    kernel.go(up_own)
    kernel.relay(y_pre_parts, 1)
    kernel.relay(y_act_parts, 1)
    w_gate = kernel.flow(Pass(1), gate_own)
    kernel.ready(y_pre_parts)
    kernel.ready(y_act_parts)
    x2_pre, h2_pre = kernel.new_output((rq, wide), F32), kernel.new_output((rq, wide), BF)
    x2_act, h2_act = kernel.new_output((aq, narrow), F32), kernel.new_output((aq, narrow), BF)
    kernel.job(
        functools.partial(second_norm, rq),
        [x_pre, y_pre, y_pre_parts, jnp.broadcast_to(gain_pf, (8, wide))],
        [],
        into=[x2_pre, h2_pre],
    )
    kernel.job(
        functools.partial(second_norm, aq),
        [x_act, y_act, y_act_parts, jnp.broadcast_to(gain_af, (8, narrow))],
        [],
        into=[x2_act, h2_act],
    )
    h2_pre = kernel.flow(Line(), h2_pre)
    h2_act = kernel.flow(Line(by_lead, (n, aq, narrow)), h2_act)
    kernel.relay(w_gate, 1)
    kernel.relay(h2_pre, 1)
    kernel.relay(h2_act, 1)
    kernel.relay(w_gate, 2)
    down_own = kernel.flow(Rows(), pre_down)
    if even:
        act_own = [kernel.flow(Columns(), act_gate), kernel.flow(Columns(), act_up)]
        act_own.append(kernel.flow(Rows(), act_down))
    else:
        act_own = [kernel.flow(Each(), act_weights)]
    kernel.ready(up_own)
    w_up = kernel.flow(Pass(1), up_own)
    for k in range(2, half):
        kernel.relay(h2_pre, k)
        kernel.relay(h2_act, k)
        if k < 4:
            kernel.relay(w_up, k - 1)
    got = kernel.call("attend")
    probs, mixed = [got[p] for p in probs], [got[o] for o in mixed]
    query, keys, values = [got[q] for q in query], got[keys], got[values]
    h1_pre, h1_act = got[h1_pre], got[h1_act]
    down_own, w_gate, w_up = got[down_own], got[w_gate], got[w_up]
    x2_pre, x2_act = got[x2_pre], got[x2_act]
    h2_pre, h2_act = got[h2_pre].reshape(n * rq, wide), got[h2_act].reshape(n * aq, narrow)

    def summed(first, parts, count=None):
        value = first.astype(F32)
        for k in range(1, count or parts.shape[0]):
            value = value + parts[k].astype(F32)
        return value

    act_own = [got[a] for a in act_own]
    items, units = h2_pre.shape[0], w_gate.shape[1]
    summing = Halves if m == 4 else Direct

    def in_turn_rows(ref, i, j):
        chip = lax.rem(i // 2 - j // 2 + half, half)
        return ref.at[at(chip + half * lax.rem(i + j, 2), rq)]

    kernel = Kernel(4)
    gz_all = kernel.flow(Line(in_turn_rows, (items, wide)), gz_pre)
    w_down = kernel.flow(Pass(0), down_own)
    into = None
    for piece in range(2):
        into = kernel.job(
            functools.partial(hidden_forward, piece, 2),
            [h2_pre, w_gate, w_up],
            [(items, units)] * 3,
            into=into,
        )
        kernel.relay(gz_all, piece + 1)
    gate, upward, hidden = into
    kernel.relay(w_down, 1)
    kernel.relay(w_down, 2)
    for k in range(3, half):
        kernel.relay(gz_all, k)
    if even:
        act_all_w = [kernel.flow(Pass(axis), a) for axis, a in zip((1, 1, 0), act_own)]
    else:
        act_all_w = [kernel.flow(Pass(0), act_own[0].reshape(n * 3 * d_act, few))]
    kernel.ready(gz_all)
    g_down = kernel.job(products_left, [hidden, gz_all], [(units, wide)])
    down_sum, gate_sum, up_sum = summing(0), summing(1), summing(1)
    down_sum.first(kernel, g_down)
    kernel.ready(w_down)
    z_p = kernel.job(products_plain, [hidden, w_down], [(items, wide)])
    z_p_core = kernel.flow(Core(), z_p)
    for k in (1, 2):
        for a in act_all_w:
            kernel.relay(a, k)
    dgate, dup = kernel.job(
        hidden_backward, [gz_all, w_down, gate, upward], [(items, units)] * 2
    )
    got = kernel.call("hidden")
    dgate, dup = got[dgate], got[dup]
    down_sum.settle(got)

    def pair_sum(parts, other):
        return add(parts[: other.shape[0]], other).reshape(half, -1, other.shape[1])

    z_p = pair_sum(got[z_p], got[z_p_core])
    if even:
        act_gate_w, act_up_w, act_down_w = [got[a] for a in act_all_w]
    else:
        act_all_w = got[act_all_w[0]].reshape(m, n, 3, d_act, few).transpose(2, 1, 3, 0, 4)
        act_gate_w, act_up_w, act_down_w = act_all_w.reshape(3, narrow, m * few)
        act_down_w = act_down_w.T

    match = (lax.broadcasted_iota(jnp.int32, (n, 1), 0) == slot_all[None, :]).astype(BF)
    cot_all = cot_all.reshape(n * slot_count, aq * narrow)
    gz_act_all = dot_plain(match, cot_all).astype(BF).reshape(n * aq, narrow)
    gz_act = lax.dynamic_slice_in_dim(gz_act_all, me * aq, aq, 0)
    kernel = Kernel(6)
    z_p_parts = kernel.flow(Chips(), z_p)
    down_sum.second(kernel)
    g_gate = kernel.job(products_left, [h2_pre, dgate], [(wide, units)])
    gate_sum.first(kernel, g_gate)
    z_a, dh2_a, g_gate_a, g_up_a, g_down_a = kernel.job(
        act_feed_forward,
        [h2_act, gz_act_all, act_gate_w, act_up_w, act_down_w],
        [(n * aq, narrow)] * 2 + [(narrow, m * few)] * 2 + [(m * few, narrow)],
    )
    z_a = kernel.flow(EachRows(), z_a)
    g_up = kernel.job(products_left, [h2_pre, dup], [(wide, units)])
    got = kernel.call("in_grads")
    dh2_a, g_gate_a, g_up_a, g_down_a = [got[o] for o in (dh2_a, g_gate_a, g_up_a, g_down_a)]
    act_back = [g_gate_a, g_up_a, g_down_a]
    if not even:
        act_back = jnp.concatenate([g_gate_a, g_up_a, g_down_a.T], axis=0)
        act_back = [jnp.stack(jnp.split(act_back, m, axis=1))]
    down_sum.settle(got)
    gate_sum.settle(got)
    g_up = got[g_up]
    out_pre = (x2_pre + summed(z_p[0], got[z_p_parts])).astype(BF)
    out_act = (x2_act + jnp.sum(got[z_a].astype(F32), axis=0)).astype(BF)

    kernel = Kernel(7)
    up_sum.first(kernel, g_up)
    grad_down = kernel.flow(Columns(), down_sum.total(kernel))
    out_act = kernel.flow(Line(), out_act)
    dh2_p = kernel.job(products_right, [dgate, w_gate, dup, w_up], [(items, wide)])
    dh2_p_core = kernel.flow(Core(), dh2_p)
    for k in range(1, half):
        kernel.relay(out_act, k)
    got = kernel.call("row_grads")
    out_act = got[out_act].reshape(n * aq, narrow)
    up_sum.settle(got)
    grad_down = got[grad_down].astype(F32)
    dh2_p = pair_sum(got[dh2_p], got[dh2_p_core])

    kernel = Kernel(8)
    dh2_p_parts, dh2_a = kernel.flow(Chips(), dh2_p), kernel.flow(EachRows(), dh2_a)
    act_parts = [kernel.flow(Swaps(axis), a) for axis, a in zip((1, 1, 0), act_back)]
    gate_sum.second(kernel)
    up_sum.second(kernel)
    for flow in act_parts:
        kernel.relay(flow, 1)
    got = kernel.call("sum_rows")
    gate_sum.settle(got)
    up_sum.settle(got)
    if even:
        act_back = [g_gate_a[:, :few], g_up_a[:, :few], g_down_a[:few]]
    else:
        act_back = [act_back[0][0]]
    act_sum = [summed(a, got[b], m).astype(BF) for a, b in zip(act_back, act_parts)]
    if not even:
        act_sum = jnp.concatenate(act_sum, axis=0).reshape(3, n, d_act, few)
        act_sum = [act_sum.transpose(1, 0, 2, 3).reshape(n, 3 * d_act, few)]
    gx2n_pre, g_gain_pf = norm_backward(x2_pre, gain_pf, summed(dh2_p[0], got[dh2_p_parts]))
    gx2n_act, g_gain_af = norm_backward(x2_act, gain_af, jnp.sum(got[dh2_a].astype(F32), axis=0))
    gx2_pre = gz_pre.astype(F32) + gx2n_pre
    gx2_act = gz_act.astype(F32) + gx2n_act

    def both_rows(inputs, outputs):
        products_right(inputs[:2], [outputs[0].at[pl.ds(0, rows)]])
        products_right(inputs[2:], [outputs[0].at[pl.ds(rows, acts)]])

    def input_grads(first, count, inputs, outputs):
        w_in, operands = inputs[-1], []
        for h in range(heads):
            operands += [inputs[h].at[pl.ds(first, count)], w_in.at[:, pl.ds(h * HD, HD)]]
        operands += [inputs[heads].at[pl.ds(first, count)], w_in.at[:, pl.ds(split, 2 * HD)]]
        products_right(operands, outputs)

    def weight_grads(first, count, cut, inputs, outputs):
        inputs = [a if a.shape[0] == count else a.at[pl.ds(first, count)] for a in inputs]
        products_left(inputs, [outputs[0].at[cut]])

    kernel = Kernel(9)
    gy_pre = kernel.flow(Whole(), gx2_pre.astype(BF))
    gy_act = kernel.flow(Whole(), gx2_act.astype(BF))
    grad_gate = kernel.flow(Rows(), gate_sum.total(kernel))
    kernel.relay(gy_pre, 1)
    kernel.relay(gy_act, 1)
    kernel.ready(gy_pre)
    kernel.ready(gy_act)
    grad_up = kernel.flow(Rows(), up_sum.total(kernel))
    gmix = kernel.job(both_rows, [gy_pre, w_out_pre, gy_act, w_out_act], [(total_rows, split)])
    *gq, gkv, shares = kernel.job(
        functools.partial(attend_backward, heads),
        probs + query + [keys, values, gmix],
        [(total_rows, HD)] * heads + [(total_rows, 2 * HD), (m, total_rows, kvw)],
    )
    share_parts = kernel.flow(Parts(), shares)
    gh1_pre = kernel.job(
        functools.partial(input_grads, 0, rows), gq + [gkv, w_in_pre], [(rows, wide)]
    )
    gh1_pre_parts = kernel.flow(Parts(), gh1_pre)
    gh1_act = kernel.job(
        functools.partial(input_grads, rows, acts), gq + [gkv, w_in_act], [(acts, narrow)]
    )
    gh1_act_parts = kernel.flow(Parts(), gh1_act)
    if even:
        act_sum = [kernel.flow(k(), a) for k, a in zip((Rows, Rows, Columns), act_sum)]
    else:
        act_sum = [kernel.flow(Each(), act_sum[0])]
    late = [share_parts, gh1_pre_parts, gh1_act_parts]
    g_out_pre = g_out_act = g_q_pre = g_q_act = None
    for h in range(heads):
        heads_columns = (slice(None), pl.ds(h * HD, HD))
        of_pre = functools.partial(weight_grads, 0, rows)
        of_act = functools.partial(weight_grads, rows, acts)

        def grads(body, cut, pair, shape, into):
            return [kernel.job(functools.partial(body, cut), pair, [shape], into=into)]

        g_out_pre = grads(of_pre, heads_columns, [gy_pre, mixed[h]], (wide, split), g_out_pre)
        g_q_pre = grads(of_pre, heads_columns, [h1_pre, gq[h]], (wide, split), g_q_pre)
        g_out_act = grads(of_act, heads_columns, [gy_act, mixed[h]], (narrow, split), g_out_act)
        g_q_act = grads(of_act, heads_columns, [h1_act, gq[h]], (narrow, split), g_q_act)
        if h == 0:
            for flow in late:
                kernel.relay(flow, 1)
    core_grads = [g[0] for g in (g_out_pre, g_q_pre, g_out_act, g_q_act)]
    from_core = [kernel.flow(CoreRows(), g) for g in core_grads]
    got = kernel.call("heads")
    grad_gate, grad_up = got[grad_gate].astype(F32), got[grad_up].astype(F32)
    here = lax.rem(me, 2)

    def of_core(array, core):
        size = array.shape[0] // n
        blocks = array.reshape(half, 2, size, array.shape[1])
        blocks = lax.dynamic_index_in_dim(blocks, core, 1, False)
        return blocks.reshape(half * size, array.shape[1])

    chip_grads = [add(of_core(got[g], here), got[f]) for g, f in zip(core_grads, from_core)]
    shares, gh1_pre, gh1_act = got[shares], got[gh1_pre], got[gh1_act]
    gkv_sum = summed(lax.dynamic_index_in_dim(shares, col, 0, False), got[share_parts], m)
    gh1_pre = summed(own(gh1_pre, rq), got[gh1_pre_parts], m)
    gh1_act = summed(own(gh1_act, aq), got[gh1_act_parts], m)
    act_sum = [got[a].astype(F32) for a in act_sum]
    gkv_sum = gkv_sum.astype(BF)
    g_kv_pre = dot_left(h1_pre, gkv_sum[:rows]).astype(BF)
    g_kv_act = dot_left(h1_act, gkv_sum[rows:]).astype(BF)
    gxn_pre, g_gain_pa = norm_backward(own(x_pre, rq).astype(F32), gain_pa, gh1_pre)
    gxn_act, g_gain_aa = norm_backward(own(x_act, aq), gain_aa, gh1_act)
    grad_pre = (gx2_pre + gxn_pre).astype(BF)
    gxa = (gx2_act + gxn_act).astype(BF)
    g_embed = dot_left(own(act_in, aq), gxa)
    act_grad = dot_right(gxa, embed).reshape(aq * dims_count // lanes, lanes)

    swap = [(i, i ^ 1) for i in range(n)]
    chip_grads += [
        add(of_core(g, here), lax.ppermute(of_core(g, 1 - here), "dp", swap))
        for g in (g_kv_pre, g_kv_act)
    ]
    def by_index(vector):
        return vector.reshape(n, -1, narrow // n).transpose(1, 0, 2).reshape(-1, narrow)

    tiny = [by_index(g) for g in (g_gain_pa, g_gain_pf, g_gain_aa, g_gain_af)] + [g_embed]
    tiny = jnp.concatenate(tiny, axis=0)
    tiny_rows = tiny.shape[0]
    tiny = columns_first(pad_rows(tiny, round_up(tiny_rows, 16)).astype(BF))

    kernel = Kernel(11)
    chip_parts = [kernel.flow(ChipRows(), g) for g in chip_grads]
    prefix_grad = kernel.flow(Whole(), grad_pre)
    prefix_output = kernel.flow(Whole(), out_pre)
    out_act = kernel.flow(Whole(), out_act)
    act_grad = kernel.flow(World(), act_grad)
    tiny = kernel.flow(Spread(), tiny)
    kernel.relay(prefix_grad, 1)
    kernel.relay(prefix_output, 1)
    kernel.relay(out_act, 1)
    got = kernel.call("finish")
    out_act = got[out_act]

    def chip_sum(own_parts, parts):
        size = own_parts.shape[0] // half
        return summed(lax.dynamic_slice_in_dim(own_parts, me // 2 * size, size, 0), got[parts])

    grad_out, grad_query, grad_out_a, grad_query_a, *both = [
        chip_sum(g, f) for g, f in zip(chip_grads, chip_parts)
    ]
    grad_out, grad_out_a = grad_out.T, grad_out_a.T
    both = jnp.concatenate(both, axis=0).astype(BF)
    both = lax.all_gather(both, "mp", axis=1, tiled=True).astype(F32)
    prefix_grad = got[prefix_grad][:length].astype(F32)
    prefix_output = got[prefix_output][:length]
    act_grad = got[act_grad].reshape(n, acts, dims_count)[:, :steps]
    tiny = jnp.sum(got[tiny].astype(F32), axis=(0, 1))
    mine_items = (slot_item[:, None] == lax.broadcasted_iota(jnp.int32, (1, n), 1)).astype(F32)
    mine_turns = (slot_item[:, None] == jnp.stack(turns)[None, :]).astype(F32)
    out_act = out_act.reshape(1, m, n, aq, narrow).astype(F32)
    action_output = jnp.sum(mine_turns[:, None, :, None, None] * out_act, axis=2)
    action_output = action_output.reshape(slot_count, acts, narrow)[:, :steps].astype(BF)
    own_mask = lax.broadcasted_iota(jnp.int32, (slot_count, dims_count), 1) < valid_dims[:, None]
    action_grad = jnp.sum(
        mine_items[:, :, None, None] * act_grad[None], axis=1
    ) * own_mask.astype(F32)[:, None, :]
    grad_gain_pa = tiny[:twice].reshape(-1)
    grad_gain_pf = tiny[twice : 2 * twice].reshape(-1)
    rest = tiny[2 * twice : tiny_rows]

    if even:
        grad_gate_a, grad_up_a, grad_down_a = act_sum
    else:
        act_sum = act_sum[0]
        grad_gate_a = act_sum[:, :d_act].transpose(1, 0, 2).reshape(d_act, n * few)
        grad_up_a = act_sum[:, d_act : 2 * d_act].transpose(1, 0, 2).reshape(d_act, n * few)
        grad_down_a = act_sum[:, 2 * d_act :].transpose(0, 2, 1).reshape(n * few, d_act)
    return (
        prefix_output,
        action_output,
        prefix_grad,
        action_grad,
        grad_gain_pa,
        grad_query,
        both[:d_pre, :HD],
        both[:d_pre, HD:],
        grad_out,
        grad_gain_pf,
        grad_gate,
        grad_up,
        grad_down,
        rest[2:],
        rest[0],
        grad_query_a,
        both[d_pre:, :HD],
        both[d_pre:, HD:],
        grad_out_a,
        rest[1],
        grad_gate_a,
        grad_up_a,
        grad_down_a,
    )


def solution(mesh):
    return jax.shard_map(
        local,
        mesh=mesh,
        in_specs=(
            P("dp", None),
            P("dp", None, None),
            P("dp"),
            P("dp"),
            P("dp", None),
            P("dp"),
            P("dp", "mp"),
            P("dp", None),
            P("dp", None),
            P("mp", "dp"),
            P("dp"),
            P("dp", "mp"),
            P("dp", "mp"),
            P("mp", "dp"),
            P(None, "dp"),
            P("dp"),
            P("dp", "mp"),
            P("dp", None),
            P("dp", None),
            P("mp", "dp"),
            P("dp"),
            P("dp", "mp"),
            P("dp", "mp"),
            P("mp", "dp"),
            P("dp", None),
            P("dp", None, None),
        ),
        out_specs=(
            P("dp", None),
            P("dp", None, None),
            P("dp", None),
            P("dp", None, None),
            P("dp"),
            P("dp", "mp"),
            P("dp", None),
            P("dp", None),
            P("mp", "dp"),
            P("dp"),
            P("dp", "mp"),
            P("dp", "mp"),
            P("mp", "dp"),
            P(None, "dp"),
            P("dp"),
            P("dp", "mp"),
            P("dp", None),
            P("dp", None),
            P("mp", "dp"),
            P("dp"),
            P("dp", "mp"),
            P("dp", "mp"),
            P("mp", "dp"),
        ),
        check_vma=False,
    )
```

```python
import functools

import jax
import jax.numpy as jnp
from jax import lax
from jax.experimental import pallas as pl
from jax.experimental.pallas import tpu as pltpu
from jax.sharding import PartitionSpec as P

HD = 256
EPS = 1e-06
BF = jnp.bfloat16
F32 = jnp.float32
MESH = pl.DeviceIdType.MESH
HBM = pl.BlockSpec(memory_space=pl.ANY)


def rms_gain(values, gain):
    return values * lax.rsqrt(jnp.mean(values * values, axis=-1, keepdims=True) + EPS) * gain


def norm_backward(values, gain, grad_out):
    unused, pull = jax.vjp(rms_gain, values, gain)
    return pull(grad_out)


def glu_value(gate, upward):
    return jax.nn.gelu(gate, approximate=True) * upward


def glu_backward(gate, upward, grad):
    unused, pull = jax.vjp(glu_value, gate, upward)
    return pull(grad)


def dot_plain(left, right):
    return jnp.dot(left, right, preferred_element_type=F32)


def dot_left(left, right):
    return lax.dot_general(left, right, (((0,), (0,)), ((), ())), preferred_element_type=F32)


def dot_right(left, right):
    return lax.dot_general(left, right, (((1,), (1,)), ((), ())), preferred_element_type=F32)


def round_up(value, step):
    return -(-value // step) * step


def add(left, right):
    return (left.astype(F32) + right.astype(F32)).astype(BF)


def greet(devices):
    barrier = pltpu.get_barrier_semaphore()
    for device in devices:
        pl.semaphore_signal(barrier, inc=1, device_id=device, device_id_type=MESH)
    pl.semaphore_wait(barrier, len(devices))


def at(start, size):
    return pl.ds(pl.multiple_of(start * size, size), size)


class Place:
    def __init__(self, n, m, sent, arrived, first):
        self.n, self.m = n, m
        self.me, self.col = lax.axis_index("dp"), lax.axis_index("mp")
        self.sent, self.arrived, self.first = sent, arrived, first

    def remote(self, src, dst, slot, device):
        return pltpu.make_async_remote_copy(
            src_ref=src,
            dst_ref=dst,
            send_sem=self.sent.at[self.first + slot],
            recv_sem=self.arrived.at[self.first + slot],
            device_id=device,
            device_id_type=MESH,
        )

    def keep(self, src, dst):
        def scoped(buffer):
            pltpu.sync_copy(src, buffer)
            pltpu.sync_copy(buffer, dst)

        pl.run_scoped(scoped, pltpu.VMEM(src.shape, src.dtype))

    def over_dp(self, s):
        return (lax.rem(self.me + s, self.n), self.col)

    def over_mp(self, k):
        return (self.me, self.col ^ k)


def loop(first, last, body):
    lax.fori_loop(first, last, lambda s, carry: (body(s), carry)[1], 0)


class Flow:
    reach = "dp"
    kept = False

    def slots(self, n, m):
        return max(n, m, 4)

    def result(self, shape, n, m):
        return shape

    def each(self, p, src, dst, do):
        pass

    def own(self, p, src, dst):
        return None

    def start(self, p, src, dst):
        self.each(p, src, dst, lambda c: c.start())
        if self.kept:
            p.keep(*self.own(p, src, dst))

    def relay(self, p, src, dst, k):
        return None

    def wait(self, p, src, dst):
        self.each(p, src, dst, lambda c: c.wait())


class Rows(Flow):
    kept = True

    def result(self, shape, n, m):
        return (shape[0] // n, shape[1] * n)

    def own(self, p, src, dst):
        return src.at[at(p.me, src.shape[0] // p.n)], dst.at[:, at(p.me, dst.shape[1] // p.n)]

    def each(self, p, src, dst, do):
        def body(s):
            target = p.over_dp(s)
            block = src.at[at(target[0], src.shape[0] // p.n)]
            do(p.remote(block, dst.at[:, at(p.me, dst.shape[1] // p.n)], s, target))

        loop(1, p.n, body)


class Columns(Flow):
    kept = True

    def result(self, shape, n, m):
        return (shape[0] * n, shape[1] // n)

    def own(self, p, src, dst):
        return src.at[:, at(p.me, src.shape[1] // p.n)], dst.at[at(p.me, dst.shape[0] // p.n)]

    def each(self, p, src, dst, do):
        def body(s):
            target = p.over_dp(s)
            block = src.at[:, at(target[0], src.shape[1] // p.n)]
            do(p.remote(block, dst.at[at(p.me, dst.shape[0] // p.n)], s, target))

        loop(1, p.n, body)


class Each(Flow):
    kept = True

    def own(self, p, src, dst):
        return src.at[p.me], dst.at[p.me]

    def each(self, p, src, dst, do):
        def body(s):
            target = p.over_dp(s)
            do(p.remote(src.at[target[0]], dst.at[p.me], s, target))

        loop(1, p.n, body)


class EachRows(Each):
    def result(self, shape, n, m):
        return (n, shape[0] // n, shape[1])

    def own(self, p, src, dst):
        return src.at[at(p.me, dst.shape[1])], dst.at[p.me]

    def each(self, p, src, dst, do):
        def body(s):
            target = p.over_dp(s)
            do(p.remote(src.at[at(target[0], dst.shape[1])], dst.at[p.me], s, target))

        loop(1, p.n, body)


class Chips(Flow):
    def each(self, p, src, dst, do):
        loop(1, p.n // 2, lambda s: do(p.remote(src.at[s], dst.at[s], s, p.over_dp(2 * s))))


class Core(Flow):
    def result(self, shape, n, m):
        return (shape[0] // 2, shape[1])

    def each(self, p, src, dst, do):
        half = src.shape[0] // 2
        do(p.remote(src.at[pl.ds(half, half)], dst, 0, (p.me ^ 1, p.col)))


class CoreRows(Flow):
    def result(self, shape, n, m):
        return (shape[0] // 2, shape[1])

    def cut(self, ref, i, count):
        return ref.at[at(i, ref.shape[0] // count)]

    def each(self, p, src, dst, do):
        def body(c):
            block = self.cut(src, 2 * c + lax.rem(p.me + 1, 2), p.n)
            do(p.remote(block, self.cut(dst, c, p.n // 2), c, (p.me ^ 1, p.col)))

        loop(0, p.n // 2, body)


class ChipRows(CoreRows):
    def result(self, shape, n, m):
        return (n // 2, shape[0] // (n // 2), shape[1])

    def each(self, p, src, dst, do):
        def body(s):
            target = p.over_dp(2 * s)
            do(p.remote(self.cut(src, target[0] // 2, p.n // 2), dst.at[s], s, target))

        loop(1, p.n // 2, body)


class Line(Flow):
    def __init__(self, place=None, result=None, share=False):
        self.place = place or Line.in_turn
        self.shape = result
        self.share = share
        self.reach = "both" if share else "dp"

    def slots(self, n, m):
        return 2 * n + (n * m if self.share else 0)

    def in_turn(ref, i, j):
        chips = lax.axis_size("dp") // 2
        chip = lax.rem(i // 2 - j // 2 + chips, chips)
        return ref.at[chip + chips * lax.rem(i + j, 2)]

    def result(self, shape, n, m):
        return self.shape or (n,) + shape

    def origin(self, p, first, way, k):
        return lax.rem(first - (2, -2)[way] * k + 2 * p.n, p.n)

    def along(self, p, src, dst, way, k):
        i = self.origin(p, p.me, way, k - 1)
        target = lax.rem(p.me + (2, -2)[way] + p.n, p.n)
        source = src if k == 1 else self.place(dst, i, p.me)
        slot = way * p.n // 2 + k
        return p.remote(source, self.place(dst, i, target), slot, (target, p.col))

    def across(self, p, src, dst, way, k):
        i = self.origin(p, p.me, way, k)
        source = src if k == 0 else self.place(dst, i, p.me)
        slot = (2 + way) * p.n // 2 + k
        return p.remote(source, self.place(dst, i, p.me ^ 1), slot, (p.me ^ 1, p.col))

    def passed(self, p, dst, i, k, source=None):
        block = self.place(dst, i, p.me)
        source = block if source is None else source
        return p.remote(source, block, 2 * p.n + i * p.m + k, p.over_mp(k))

    def receives(self, p, way, k):
        chip = p.me // 2
        if k == 0:
            return chip >= 0
        return chip >= k if way == 0 else chip < p.n // 2 - k

    def sends(self, p, way, k):
        chip = p.me // 2
        beyond = chip < p.n // 2 - 1 if way == 0 else chip > 0
        return beyond & self.receives(p, way, k - 1)

    def start(self, p, src, dst):
        for way in (0, 1):
            pl.when(self.sends(p, way, 1))(self.along(p, src, dst, way, 1).start)
        self.across(p, src, dst, 0, 0).start()
        self.hand(p, dst, p.me, src)
        p.keep(src, self.place(dst, p.me, p.me))

    def hand(self, p, dst, i, source=None):
        if self.share:
            for k in range(1, p.m):
                self.passed(p, dst, i, k, source).start()

    def crossed(self, p, src, dst, way, k):
        self.across(p, src, dst, way, k).wait_recv()
        self.hand(p, dst, self.origin(p, p.me ^ 1, way, k))

    def relay(self, p, src, dst, k):
        if k == 1:
            self.crossed(p, src, dst, 0, 0)
        for way in (0, 1):

            @pl.when(self.receives(p, way, k))
            def _(way=way):
                self.along(p, src, dst, way, k).wait_recv()
                self.across(p, src, dst, way, k).start()
                self.hand(p, dst, self.origin(p, p.me, way, k))

            if k < p.n // 2 - 1:
                pl.when(self.sends(p, way, k + 1))(self.along(p, src, dst, way, k + 1).start)
            if k > 1:
                before = functools.partial(self.crossed, p, src, dst, way, k - 1)
                pl.when(self.receives(p, way, k - 1))(before)

    def wait(self, p, src, dst):
        last = p.n // 2 - 1
        for way in (0, 1):
            end = functools.partial(self.crossed, p, src, dst, way, last)
            pl.when(self.receives(p, way, last))(end)
        self.across(p, src, dst, 0, 0).wait_send()
        for way in (0, 1):
            for k in range(1, last + 1):
                pl.when(self.sends(p, way, k))(self.along(p, src, dst, way, k).wait_send)
                pl.when(self.receives(p, way, k))(self.across(p, src, dst, way, k).wait_send)
        if self.share:
            for k in range(1, p.m):
                loop(0, p.n, lambda i, k=k: self.passed(p, dst, i, k).wait())


class Pass(Flow):
    reach = "mp"
    kept = True
    parts = 8

    def __init__(self, axis):
        self.axis = axis

    def slots(self, n, m):
        return max(4, m) * self.parts

    def result(self, shape, n, m):
        return (shape[0], m * shape[1]) if self.axis else (m * shape[0], shape[1])

    def spot(self, p, src, dst, k, c=None):
        rows, width = src.shape
        first, count = (0, rows) if c is None else (c * (rows // self.parts), rows // self.parts)
        if self.axis:
            return dst.at[pl.ds(first, count), pl.ds(k * width, width)]
        return dst.at[pl.ds(k * rows + first, count)]

    def own(self, p, src, dst):
        return src, self.spot(p, src, dst, 0)

    def direct(self, p, src, dst, k, c):
        few = src.shape[0] // self.parts
        block = src.at[pl.ds(c * few, few)]
        slot = k * self.parts + c
        return p.remote(block, self.spot(p, src, dst, k, c), slot, p.over_mp(k))

    def turned(self, p, src, dst, c):
        via = 1 + c % 2
        source = self.spot(p, src, dst, via, c)
        slot = 3 * self.parts + c
        return p.remote(source, self.spot(p, src, dst, 3, c), slot, p.over_mp(3 - via))

    def each(self, p, src, dst, do):
        for c in range(self.parts):
            for k in range(1, 3 if p.m == 4 else p.m):
                do(self.direct(p, src, dst, k, c))

    def start(self, p, src, dst):
        self.each(p, src, dst, lambda c: c.start())

    def relay(self, p, src, dst, k):
        if p.m == 4:
            for c in range((k - 1) * self.parts // 2, k * self.parts // 2):
                self.direct(p, src, dst, 1 + c % 2, c).wait_recv()
                self.turned(p, src, dst, c).start()

    def wait(self, p, src, dst):
        p.keep(*self.own(p, src, dst))
        for c in range(self.parts):
            for k in range(1, 3 if p.m == 4 else p.m):
                copy = self.direct(p, src, dst, k, c)
                (copy.wait_send if p.m == 4 and k == 1 + c % 2 else copy.wait)()
            if p.m == 4:
                self.turned(p, src, dst, c).wait()


def by_way(rows, m):
    return round_up(rows // 2, 16) if m == 4 and rows >= 64 else 0


class Parts(Flow):
    reach = "mp"

    def result(self, shape, n, m):
        rows = shape[-2] if len(shape) == 3 else shape[0] // m
        return (m + 1, rows, shape[-1])

    def block(self, p, src, k):
        i = self.index(p, k)
        return src.at[i] if len(src.shape) == 3 else src.at[at(i, src.shape[0] // p.m)]

    def index(self, p, k):
        return p.col ^ k

    def halves(self, p, dst):
        first = by_way(dst.shape[1], p.m)
        return [(1, pl.ds(0, first)), (2, pl.ds(first, dst.shape[1] - first))] if first else []

    def each(self, p, src, dst, do):
        halves = self.halves(p, dst)
        for k in range(1, 3 if halves else p.m):
            do(p.remote(self.block(p, src, k), dst.at[k], k, p.over_mp(k)))

    def sideways(self, p, src, dst, via, cut):
        block = self.block(p, src, 3).at[cut]
        return p.remote(block, dst.at[p.m, cut], p.m + via, p.over_mp(via))

    def onward(self, p, dst, via, cut):
        return p.remote(dst.at[p.m, cut], dst.at[3, cut], p.m + 2 + via, p.over_mp(3 - via))

    def slots(self, n, m):
        return m + 5

    def start(self, p, src, dst):
        for via, cut in self.halves(p, dst):
            self.sideways(p, src, dst, via, cut).start()
        self.each(p, src, dst, lambda c: c.start())

    def relay(self, p, src, dst, k):
        for via, cut in self.halves(p, dst):
            self.sideways(p, src, dst, via, cut).wait_recv()
            self.onward(p, dst, via, cut).start()

    def wait(self, p, src, dst):
        self.each(p, src, dst, lambda c: c.wait())
        for via, cut in self.halves(p, dst):
            self.sideways(p, src, dst, via, cut).wait_send()
            self.onward(p, dst, via, cut).wait()


class Swaps(Parts):
    def __init__(self, axis=0):
        self.axis = axis

    def result(self, shape, n, m):
        if len(shape) == 3:
            return (m + 1,) + shape[1:]
        return (m + 1, shape[0], shape[1] // m) if self.axis else (m + 1, shape[0] // m, shape[1])

    def block(self, p, src, k):
        if len(src.shape) == 3:
            return src.at[k]
        size = src.shape[self.axis] // p.m
        cut = pl.ds(k * size, size)
        return src.at[:, cut] if self.axis else src.at[cut]


class Whole(Flow):
    reach = "mp"

    def result(self, shape, n, m):
        return (m * shape[0], shape[1])

    def slots(self, n, m):
        return m + 3

    def spot(self, src, dst, i, cut=None):
        rows = src.shape[0]
        if cut is None:
            return dst.at[at(i, rows)]
        return dst.at[pl.ds(pl.multiple_of(i * rows + cut[0], 16), cut[1])]

    def halves(self, p, src):
        first = by_way(src.shape[0], p.m)
        return [(1, (0, first)), (2, (first, src.shape[0] - first))] if first else []

    def direct(self, p, src, dst, k):
        return p.remote(src, self.spot(src, dst, p.col), k, p.over_mp(k))

    def onward(self, p, src, dst, via, cut):
        block = self.spot(src, dst, p.col ^ via, cut)
        return p.remote(block, block, p.m + via, p.over_mp(3 - via))

    def start(self, p, src, dst):
        for k in range(1, 3 if self.halves(p, src) else p.m):
            self.direct(p, src, dst, k).start()
        p.keep(src, self.spot(src, dst, p.col))

    def relay(self, p, src, dst, k):
        for via, cut in self.halves(p, src):
            self.direct(p, src, dst, via).wait_recv()
            self.onward(p, src, dst, via, cut).start()

    def wait(self, p, src, dst):
        halves = self.halves(p, src)
        for k in range(1, 3 if halves else p.m):
            copy = self.direct(p, src, dst, k)
            (copy.wait_send if halves else copy.wait)()
        for via, cut in halves:
            self.onward(p, src, dst, via, cut).wait()


class Swap(Flow):
    reach = "mp"

    def __init__(self, k):
        self.k = k

    def each(self, p, src, dst, do):
        do(p.remote(src, dst, 0, p.over_mp(self.k)))


class First(Flow):
    reach = "mp"

    def __init__(self, axis):
        self.axis = axis

    def result(self, shape, n, m):
        if self.axis:
            return (4, shape[0] // 2, shape[1] // m)
        return (4, shape[0] // m, shape[1] // 2)

    def each(self, p, src, dst, do):
        width, deep = src.shape[self.axis] // p.m, src.shape[1 - self.axis] // 2
        for k, part in enumerate((1, 3, 2, 3)):
            block, half = pl.ds(part * width, width), pl.ds(k // 2 * deep, deep)
            source = src.at[half, block] if self.axis else src.at[block, half]
            do(p.remote(source, dst.at[k], k, p.over_mp(1 + k // 2)))


class World(Flow):
    reach = "world"
    kept = True

    def slots(self, n, m):
        return n * m

    def result(self, shape, n, m):
        return (n, m) + shape

    def block(self, src, i):
        return src

    def own(self, p, src, dst):
        return self.block(src, p.me), dst.at[p.me, p.col]

    def each(self, p, src, dst, do):
        for k in range(p.m):

            def body(s, k=k):
                target = (lax.rem(p.me + s, p.n), p.col ^ k)
                copy = p.remote(
                    self.block(src, target[0]), dst.at[p.me, p.col], s * p.m + k, target
                )
                do(copy)

            loop(0 if k else 1, p.n, body)


class Spread(World):
    def result(self, shape, n, m):
        return (n, m) + shape[1:]

    def block(self, src, i):
        return src.at[i]


class Kernel:
    def __init__(self, collective_id):
        self.collective_id = collective_id
        self.inputs, self.outputs, self.flows, self.steps = [], [], [], []

    def operand(self, source):
        if isinstance(source, int):
            return ("out", source)
        self.inputs.append(source)
        return ("in", len(self.inputs) - 1)

    def shape_of(self, source):
        return self.outputs[source] if isinstance(source, int) else source

    def new_output(self, shape, dtype):
        self.outputs.append(jax.ShapeDtypeStruct(shape, dtype))
        return len(self.outputs) - 1

    def flow(self, kind, source, now=True, into=None):
        n, m = lax.axis_size("dp"), lax.axis_size("mp")
        like = self.shape_of(source)
        out = into
        if into is None:
            out = self.new_output(kind.result(like.shape, n, m), like.dtype)
        name = out if into is None else -1 - len(self.flows)
        self.flows.append((kind, self.operand(source), out, name))
        if now:
            self.go(name)
        return name

    def go(self, name):
        self.steps.append(("start", name))

    def relay(self, name, k):
        self.steps.append(("relay", name, k))

    def ready(self, name):
        self.steps.append(("wait", name))

    def job(self, body, sources, shapes, dtype=BF, into=None):
        outs = into or [self.new_output(s, dtype) for s in shapes]
        self.steps.append(("job", body, [self.operand(s) for s in sources], outs))
        return outs if len(outs) > 1 else outs[0]

    def call(self, name):
        n, m = lax.axis_size("dp"), lax.axis_size("mp")
        takes, gives = len(self.inputs), len(self.outputs)
        flows, steps = self.flows, self.steps
        rows = {flow[3]: row for row, flow in enumerate(flows)}
        reach = {flow[0].reach for flow in flows}
        firsts = [0]
        for flow in flows:
            firsts.append(firsts[-1] + flow[0].slots(n, m))

        def kernel(*refs):
            ins, outs = refs[:takes], refs[takes : takes + gives]
            sent, arrived = refs[takes + gives :]
            me, col = lax.axis_index("dp"), lax.axis_index("mp")
            if "world" in reach:
                greet([(lax.rem(me + s, n), col ^ k) for s in range(n) for k in range(m) if s or k])
            else:
                column = [(lax.rem(me + s, n), col) for s in range(1, n)]
                row = [(me, col ^ k) for k in range(1, m)]
                greet(
                    (column if reach & {"dp", "both"} else [])
                    + (row if reach & {"mp", "both"} else [])
                )

            def ref(operand):
                return (ins if operand[0] == "in" else outs)[operand[1]]

            def act(what, name, *rest):
                kind, source, out, unused = flows[rows[name]]
                place = Place(n, m, sent, arrived, firsts[rows[name]])
                getattr(kind, what)(place, ref(source), outs[out], *rest)

            ended = set()
            for step in steps:
                if step[0] == "job":
                    step[1]([ref(s) for s in step[2]], [outs[o] for o in step[3]])
                else:
                    act(*step)
                    if step[0] == "wait":
                        ended.add(step[1])
            for flow in flows:
                if flow[3] not in ended:
                    act("wait", flow[3])

        return pl.pallas_call(
            kernel,
            out_shape=self.outputs,
            in_specs=[HBM] * takes,
            out_specs=[HBM] * gives,
            scratch_shapes=[
                pltpu.SemaphoreType.DMA((firsts[-1],)),
                pltpu.SemaphoreType.DMA((firsts[-1],)),
            ],
            compiler_params=pltpu.CompilerParams(
                collective_id=self.collective_id,
                has_side_effects=True,
                vmem_limit_bytes=56 << 20,
            ),
            name=name,
        )(*self.inputs)


def tile(size, most):
    return max(t for t in range(16, most + 1, 16) if size % t == 0)


def products_plain(inputs, outputs):
    a, b = inputs
    (rows, depth), width = a.shape, b.shape[1]
    bm, bn = tile(rows, 832), tile(width, 512)

    def body(a_ref, b_ref, o_ref):
        o_ref[...] = dot_plain(a_ref[...], b_ref[...]).astype(BF)

    pltpu.emit_pipeline(
        body,
        grid=(width // bn, rows // bm),
        in_specs=[
            pl.BlockSpec((bm, depth), lambda j, i: (i, 0)),
            pl.BlockSpec((depth, bn), lambda j, i: (0, j)),
        ],
        out_specs=[pl.BlockSpec((bm, bn), lambda j, i: (i, j))],
    )(a, b, outputs[0])


def products_right(inputs, outputs):
    pairs = len(inputs) // 2
    rows, width = inputs[0].shape[0], inputs[1].shape[0]
    bm, bn = tile(rows, 832), tile(width, 512)

    def body(*refs):
        total = dot_right(refs[0][...], refs[1][...])
        for p in range(1, pairs):
            total = total + dot_right(refs[2 * p][...], refs[2 * p + 1][...])
        refs[-1][...] = total.astype(BF)

    specs = []
    for p in range(pairs):
        depth = inputs[2 * p].shape[1]
        specs.append(pl.BlockSpec((bm, depth), lambda i, j: (i, 0)))
        specs.append(pl.BlockSpec((bn, depth), lambda i, j: (j, 0)))
    pltpu.emit_pipeline(
        body,
        grid=(rows // bm, width // bn),
        in_specs=specs,
        out_specs=[pl.BlockSpec((bm, bn), lambda i, j: (i, j))],
    )(*inputs, outputs[0])


def products_left(inputs, outputs):
    a, rest = inputs[0], inputs[1:]
    (depth, rows), width = a.shape, rest[0].shape[1]
    bm, bn = tile(rows, 1024), tile(width, 512)
    count = len(rest)

    def body(a_ref, *refs):
        for p in range(count):
            refs[count + p][...] = dot_left(a_ref[...], refs[p][...]).astype(BF)

    pltpu.emit_pipeline(
        body,
        grid=(rows // bm, width // bn),
        in_specs=[pl.BlockSpec((depth, bm), lambda i, j: (0, i))]
        + [pl.BlockSpec((depth, bn), lambda i, j: (0, j))] * count,
        out_specs=[pl.BlockSpec((bm, bn), lambda i, j: (i, j))] * count,
    )(a, *rest, *outputs)


def hidden_forward(part, parts, inputs, outputs):
    h, w_gate, w_up = inputs
    (rows, depth), width = h.shape, w_gate.shape[1] // parts
    cut = pl.ds(part * width, width)
    w_gate, w_up = w_gate.at[:, cut], w_up.at[:, cut]
    outputs = [o.at[:, cut] for o in outputs]
    bm, bn = tile(rows, 832), tile(width, 512)

    def body(h_ref, gate_w, up_w, gate_ref, up_ref, hidden_ref):
        gate = dot_plain(h_ref[...], gate_w[...])
        upward = dot_plain(h_ref[...], up_w[...])
        gate_ref[...] = gate.astype(BF)
        up_ref[...] = upward.astype(BF)
        hidden_ref[...] = glu_value(gate, upward).astype(BF)

    block = pl.BlockSpec((bm, bn), lambda j, i: (i, j))
    pltpu.emit_pipeline(
        body,
        grid=(width // bn, rows // bm),
        in_specs=[pl.BlockSpec((bm, depth), lambda j, i: (i, 0))]
        + [pl.BlockSpec((depth, bn), lambda j, i: (0, j))] * 2,
        out_specs=[block] * 3,
    )(h, w_gate, w_up, *outputs)


def hidden_backward(inputs, outputs):
    gz, w_down, gate, upward = inputs
    (rows, depth), width = gz.shape, w_down.shape[0]
    bm, bn = tile(rows, 832), tile(width, 512)

    def body(gz_ref, down_w, gate_ref, up_ref, dgate_ref, dup_ref):
        grad = dot_right(gz_ref[...], down_w[...])
        dgate, dup = glu_backward(gate_ref[...].astype(F32), up_ref[...].astype(F32), grad)
        dgate_ref[...] = dgate.astype(BF)
        dup_ref[...] = dup.astype(BF)

    block = pl.BlockSpec((bm, bn), lambda j, i: (i, j))
    pltpu.emit_pipeline(
        body,
        grid=(width // bn, rows // bm),
        in_specs=[
            pl.BlockSpec((bm, depth), lambda j, i: (i, 0)),
            pl.BlockSpec((bn, depth), lambda j, i: (j, 0)),
            block,
            block,
        ],
        out_specs=[block] * 2,
    )(gz, w_down, gate, upward, *outputs)


def act_feed_forward(inputs, outputs):
    def body(h_ref, gz_ref, gate_w, up_w, down_w, z, dh2, g_gate, g_up, g_down):
        h, gz = h_ref[...], gz_ref[...]
        gate, upward = dot_plain(h, gate_w[...]), dot_plain(h, up_w[...])
        hidden = glu_value(gate, upward).astype(BF)
        z[...] = dot_plain(hidden, down_w[...]).astype(BF)
        g_down[...] = dot_left(hidden, gz).astype(BF)
        dgate, dup = glu_backward(gate, upward, dot_right(gz, down_w[...]))
        dgate, dup = dgate.astype(BF), dup.astype(BF)
        dh2[...] = (dot_right(dgate, gate_w[...]) + dot_right(dup, up_w[...])).astype(BF)
        g_gate[...] = dot_left(h, dgate).astype(BF)
        g_up[...] = dot_left(h, dup).astype(BF)

    def whole(ref):
        return pl.BlockSpec(ref.shape, lambda i: (0, 0))

    pltpu.emit_pipeline(
        body,
        grid=(1,),
        in_specs=[whole(r) for r in inputs],
        out_specs=[whole(r) for r in outputs],
    )(*inputs, *outputs)


def attend_forward(inputs, outputs):
    query, keys, values, seg_q, seg_k = inputs
    probs, mixed = outputs
    total = query.shape[0]
    rows = tile(total, 448)

    def body(q_ref, k_ref, v_ref, sq_ref, sk_ref, p_ref, o_ref):
        allowed = sq_ref[:, :1] >= sk_ref[:1]
        scores = dot_right(q_ref[...], k_ref[...]) * HD ** (-0.5)
        scores = jnp.where(allowed, scores, -1e30)
        raised = jnp.exp(scores - jnp.max(scores, axis=-1, keepdims=True))
        p = (raised / jnp.sum(raised, axis=-1, keepdims=True)).astype(BF)
        p_ref[...] = p
        o_ref[...] = dot_plain(p, v_ref[...]).astype(BF)

    def rest(shape):
        return pl.BlockSpec(shape, lambda i: (0, 0))

    pltpu.emit_pipeline(
        body,
        grid=(total // rows,),
        in_specs=[
            pl.BlockSpec((rows, HD), lambda i: (i, 0)),
            rest(keys.shape),
            rest(values.shape),
            pl.BlockSpec((rows, seg_q.shape[1]), lambda i: (i, 0)),
            rest(seg_k.shape),
        ],
        out_specs=[
            pl.BlockSpec((rows, total), lambda i: (i, 0)),
            pl.BlockSpec((rows, HD), lambda i: (i, 0)),
        ],
    )(query, keys, values, seg_q, seg_k, probs, mixed)


def attend_backward(heads, inputs, outputs):
    probs, query = inputs[:heads], inputs[heads : 2 * heads]
    keys, values, grad = inputs[2 * heads :]
    grad_query, (both, shares) = outputs[:heads], outputs[heads:]
    total, scale = keys.shape[0], HD ** (-0.5)
    rows = tile(total, 448)
    width = shares.shape[2]

    def scoped(sums, rounded, parted):
        sums[...] = jnp.zeros_like(sums)

        def body(*refs):
            k_ref, v_ref, g_ref = refs[2 * heads : 2 * heads + 3]
            for h in range(heads):
                g = g_ref[:, h * HD : (h + 1) * HD]
                p, q = refs[h][...], refs[heads + h][...]
                wide_p = p.astype(F32)
                dp = dot_right(g, v_ref[...])
                ds = wide_p * (dp - jnp.sum(wide_p * dp, axis=-1, keepdims=True))
                ds = ds.astype(BF)
                refs[2 * heads + 3 + h][...] = (dot_plain(ds, k_ref[...]) * scale).astype(BF)
                sums[:, :HD] += dot_left(ds, q) * scale
                sums[:, HD:] += dot_left(p, g)

        def rest(ref):
            return pl.BlockSpec(ref.shape, lambda i: (0, 0))

        block = pl.BlockSpec((rows, HD), lambda i: (i, 0))
        pltpu.emit_pipeline(
            body,
            grid=(total // rows,),
            in_specs=[pl.BlockSpec((rows, total), lambda i: (i, 0))] * heads
            + [block] * heads
            + [rest(keys), rest(values), pl.BlockSpec((rows, heads * HD), lambda i: (i, 0))],
            out_specs=[block] * heads,
        )(*probs, *query, keys, values, grad, *grad_query)
        rounded[...] = sums[...].astype(BF)
        for k in range(shares.shape[0]):
            parted[k] = sums[:, k * width : (k + 1) * width].astype(BF)
        pltpu.sync_copy(rounded, both)
        pltpu.sync_copy(parted, shares)

    pl.run_scoped(
        scoped,
        pltpu.VMEM((total, 2 * HD), F32),
        pltpu.VMEM((total, 2 * HD), BF),
        pltpu.VMEM(shares.shape, BF),
    )


def rows_from(first, count, body):
    return lambda inputs, outputs: body([inputs[0].at[pl.ds(first, count)]] + inputs[1:], outputs)


def add_pairs(pairs, outputs):
    (rows, width), count = outputs[0].shape, len(outputs)

    def body(*refs):
        for k in range(count):
            refs[2 * count + k][...] = add(refs[2 * k][...], refs[2 * k + 1][...])

    block = pl.BlockSpec((tile(rows, 256), width), lambda i: (i, 0))
    pltpu.emit_pipeline(
        body,
        grid=(rows // tile(rows, 256),),
        in_specs=[block] * (2 * count),
        out_specs=[block] * count,
    )(*[ref for pair in pairs for ref in pair], *outputs)


def second_norm(count, inputs, outputs):
    x, y, parts, gain = inputs
    m, width = parts.shape[0] - 1, parts.shape[2]
    rows = at(lax.axis_index("mp"), count)

    def body(x_ref, y_ref, parts_ref, gain_ref, sum_ref, normed_ref):
        total = x_ref[...].astype(F32) + y_ref[...].astype(F32)
        for k in range(m - 1):
            total = total + parts_ref[k].astype(F32)
        sum_ref[...] = total
        normed_ref[...] = rms_gain(total, gain_ref[:1]).astype(BF)

    block = pl.BlockSpec((count, width), lambda i: (0, 0))
    pltpu.emit_pipeline(
        body,
        grid=(1,),
        in_specs=[
            block,
            block,
            pl.BlockSpec((m - 1, count, width), lambda i: (0, 0, 0)),
            pl.BlockSpec(gain.shape, lambda i: (0, 0)),
        ],
        out_specs=[block, block],
    )(x.at[rows], y.at[rows], parts.at[pl.ds(1, m - 1)], gain, *outputs)


class Halves:
    def __init__(self, axis):
        self.axis = axis

    def settle(self, got):
        for name, value in vars(self).items():
            if name != "axis" and isinstance(value, int):
                setattr(self, name, got[value])

    def first(self, kernel, whole):
        self.whole = whole
        self.parts = kernel.flow(First(self.axis), whole)

    def second(self, kernel):
        axis = self.axis

        def take(inputs, outputs):
            whole, parts = inputs
            width, deep = whole.shape[axis] // 4, whole.shape[1 - axis] // 2

            def part(half, k):
                block, deeps = pl.ds(k * width, width), pl.ds(half * deep, deep)
                return whole.at[deeps, block] if axis else whole.at[block, deeps]

            own = [part(0, 0), part(0, 2), part(1, 0), part(1, 1)]
            add_pairs([(own[k], parts.at[k]) for k in range(4)], outputs)

        like = kernel.shape_of(self.parts).shape[1:]
        self.top, next_y, self.low, next_x = kernel.job(take, [self.whole, self.parts], [like] * 4)
        self.from_y = kernel.flow(Swap(2), next_y)
        self.from_x = kernel.flow(Swap(1), next_x)

    def total(self, kernel):
        axis = self.axis
        rows, width = kernel.shape_of(self.top).shape

        def join(inputs, outputs):
            top, low, from_y, from_x = inputs
            halves = [(top, from_y), (low, from_x)]
            for k, pair in enumerate(halves):
                spot = pl.ds(k * rows, rows) if axis else (slice(None), pl.ds(k * width, width))
                add_pairs([pair], [outputs[0].at[spot]])

        shape = (2 * rows, width) if axis else (rows, 2 * width)
        return kernel.job(join, [self.top, self.low, self.from_y, self.from_x], [shape])


class Direct:
    def __init__(self, axis):
        self.axis = axis

    def settle(self, got):
        if isinstance(self.whole, int):
            self.whole = got[self.whole]

    def first(self, kernel, whole):
        self.whole = whole

    def second(self, kernel):
        return None

    def total(self, kernel):
        parts = jnp.split(self.whole, lax.axis_size("mp"), axis=self.axis)
        total = parts[0].astype(F32)
        for k in range(1, len(parts)):
            pairs = [(i, i ^ k) for i in range(len(parts))]
            total = total + lax.ppermute(parts[k], "mp", pairs).astype(F32)
        return total.astype(BF)


def project_rows(first, heads, inputs, outputs):
    x, gain, w_in = inputs
    rows, depth = x.shape
    block = tile(rows, 416)

    def body(x_ref, gain_ref, w_ref, normed_ref, *refs):
        normed = rms_gain(x_ref[...].astype(F32), gain_ref[:1]).astype(BF)
        normed_ref[...] = normed
        for k in range(heads + 2):
            refs[k][...] = dot_plain(normed, w_ref[:, k * HD : (k + 1) * HD]).astype(BF)

    spots = [o.at[pl.ds(first, rows)] for o in outputs[1:]]
    pltpu.emit_pipeline(
        body,
        grid=(rows // block,),
        in_specs=[
            pl.BlockSpec((block, depth), lambda i: (i, 0)),
            pl.BlockSpec(gain.shape, lambda i: (0, 0)),
            pl.BlockSpec(w_in.shape, lambda i: (0, 0)),
        ],
        out_specs=[pl.BlockSpec((block, depth), lambda i: (i, 0))]
        + [pl.BlockSpec((block, HD), lambda i: (i, 0))] * (heads + 2),
    )(x, gain, w_in, outputs[0], *spots)


def local(
    prefix_input,
    action_input,
    valid_dims,
    slot_item,
    segments,
    pre_gain_attn,
    pre_query,
    pre_key,
    pre_value,
    pre_output,
    pre_gain_ffn,
    pre_gate,
    pre_up,
    pre_down,
    act_embed,
    act_gain_attn,
    act_query,
    act_key,
    act_value,
    act_output,
    act_gain_ffn,
    act_gate,
    act_up,
    act_down,
    prefix_cotangent,
    action_cotangent,
):
    n, m = lax.axis_size("dp"), lax.axis_size("mp")
    me, col = lax.axis_index("dp"), lax.axis_index("mp")
    length, wide = prefix_input.shape
    slot_count, steps, dims_count = action_input.shape
    narrow = action_cotangent.shape[2]
    rq = round_up(-(-length // m), 16)
    aq = round_up(-(-steps // m), 16)
    rows, acts = m * rq, m * aq
    total_rows = rows + acts
    half = n // 2
    heads = pre_query.shape[1] // HD
    split = heads * HD
    scale = HD ** (-0.5)
    kvw = 2 * HD // m
    d_pre, d_act = pre_query.shape[0], act_query.shape[0]
    few = act_gate.shape[1] // n
    lanes = 128
    twice = wide // narrow
    turns = [lax.rem(me + 2 * k, n) for k in range(half)]
    turns = turns + [t ^ 1 for t in turns]

    def own(array, count):
        return lax.dynamic_slice_in_dim(array, col * count, count, 0)

    def pad_rows(array, count):
        return jnp.pad(array, ((0, count - array.shape[0]), (0, 0)))

    def lane_rows(array):
        flat = array.reshape(-1)
        count = round_up(-(-flat.shape[0] // lanes), 16)
        return jnp.pad(flat, (0, count * lanes - flat.shape[0])).reshape(count, lanes)

    def columns_first(array):
        return array.reshape(array.shape[0], n, -1).transpose(1, 0, 2)

    even = few % lanes == 0 and d_act % lanes == 0

    smalls = [pre_gain_attn, pre_gain_ffn, act_gain_attn, act_gain_ffn, act_embed, action_input]
    small = jnp.concatenate([lane_rows(a) for a in smalls], axis=0)
    ints = jnp.pad(jnp.stack([slot_item, valid_dims]), ((0, 6), (0, lanes - slot_count)))
    cot_rows = lax.dynamic_slice_in_dim(
        jnp.pad(action_cotangent, ((0, 0), (0, acts - steps), (0, 0))), col * aq, aq, 1
    ).reshape(slot_count * aq, narrow)

    def share_of(key, value):
        return own(jnp.concatenate([key, value], axis=1).T, kvw).T

    def by_rows(size):
        return lambda ref, i, j: ref.at[at(i, size)]

    def by_columns(size):
        return lambda ref, i, j: ref.at[:, at(i, size)]

    def by_share(size):
        return lambda ref, i, j: ref.at[lax.axis_index("mp"), at(i, size)]

    def by_lead(ref, i, j):
        return ref.at[i]

    kernel = Kernel(1)
    aligned = kvw % lanes == 0
    in_pre, in_act = (wide, split + 2 * HD), (narrow, split + 2 * HD)
    kv_pre, kv_act = share_of(pre_key, pre_value), share_of(act_key, act_value)

    def in_columns(size, share):
        def place(ref, i, j):
            start = split + lax.axis_index("mp") * kvw if share else 0
            columns = pl.ds(pl.multiple_of(start, lanes), kvw if share else split)
            return ref.at[at(i, size), columns]

        return place

    if aligned:
        w_in_pre = kernel.flow(Line(in_columns(d_pre, True), in_pre, True), kv_pre)
        w_in_act = kernel.flow(Line(in_columns(d_act, True), in_act, True), kv_act)
        lines = [w_in_pre, w_in_act]
    else:
        w_kv_pre = kernel.flow(Line(by_share(d_pre), (m, wide, kvw), True), kv_pre)
        w_kv_act = kernel.flow(Line(by_share(d_act), (m, narrow, kvw), True), kv_act)
        lines = [w_kv_pre, w_kv_act]
    small = kernel.flow(Line(by_lead, (n,) + small.shape), small)
    ints = kernel.flow(Line(by_lead, (n, 8, lanes)), ints)
    if aligned:
        w_q_pre = kernel.flow(Line(in_columns(d_pre, False)), pre_query, into=w_in_pre)
        w_q_act = kernel.flow(Line(in_columns(d_act, False)), act_query, into=w_in_act)
    else:
        w_q_pre = kernel.flow(Line(by_rows(d_pre), (wide, split)), pre_query)
        w_q_act = kernel.flow(Line(by_rows(d_act), (narrow, split)), act_query)
    w_out_pre = kernel.flow(Line(by_columns(d_pre), (split, wide)), pre_output)
    if even:
        w_out_act = kernel.flow(Line(by_columns(d_act), (split, narrow)), act_output)
    else:
        w_out_act = kernel.flow(Line(by_lead, (n, split, d_act)), act_output)
    cot_all = kernel.flow(Line(by_lead, (n, slot_count * aq, narrow)), cot_rows)
    lines += [small, ints, w_q_pre, w_q_act, w_out_pre, w_out_act, cot_all]
    for k in range(1, half):
        for out in lines:
            kernel.relay(out, k)
    got = kernel.call("gather")
    small, ints, cot_all = got[small], got[ints], got[cot_all]
    w_out_pre, w_out_act = got[w_out_pre], got[w_out_act]
    if aligned:
        w_in_pre, w_in_act = got[w_in_pre], got[w_in_act]
    else:
        w_in_pre = jnp.concatenate([got[w_q_pre]] + [got[w_kv_pre][k] for k in range(m)], axis=1)
        w_in_act = jnp.concatenate([got[w_q_act]] + [got[w_kv_act][k] for k in range(m)], axis=1)
    smalls_all, begin = [], 0
    for a in smalls:
        count = round_up(-(-a.size // lanes), 16)
        flat = small[:, begin : begin + count].reshape(n, -1)[:, : a.size]
        smalls_all.append(flat.reshape((n,) + a.shape))
        begin += count
    gain_pa, gain_pf, gain_aa, gain_af = [g.reshape(-1).astype(F32) for g in smalls_all[:4]]
    embed = smalls_all[4].transpose(1, 0, 2).reshape(dims_count, narrow)
    act_all = smalls_all[5].reshape(n * slot_count, steps, dims_count)
    slot_all = ints[:, 0, :slot_count].reshape(-1)
    valid_all = ints[:, 1, :slot_count].reshape(-1)
    if not even:
        w_out_act = w_out_act.transpose(1, 0, 2).reshape(split, narrow)

    mine = (slot_all == me).astype(F32)
    valid = jnp.sum(mine * valid_all.astype(F32))
    dims_mask = (lax.broadcasted_iota(jnp.int32, (1, dims_count), 1).astype(F32) < valid).astype(BF)
    act_in = jnp.sum(mine[:, None, None] * act_all.astype(F32), axis=0).astype(BF) * dims_mask
    act_in = pad_rows(act_in, acts)

    x_pre = pad_rows(prefix_input, rows)
    x_act = dot_plain(act_in, embed)
    last, never = 1 << 10, 1 << 20
    seg = jnp.pad(segments[0], (0, rows - length), constant_values=never)
    seg_q = jnp.concatenate([jnp.minimum(seg, last), jnp.full((acts,), last, jnp.int32)])
    own_keys = jnp.where(jnp.arange(acts, dtype=jnp.int32) < steps, last, never)
    seg_k = jnp.concatenate([seg, own_keys])
    seg_q = jnp.broadcast_to(seg_q[:, None], (total_rows, lanes))
    seg_k = jnp.broadcast_to(seg_k[None, :], (8, total_rows))

    gz_pre = own(pad_rows(prefix_cotangent, rows), rq)
    if not even:
        act_weights = jnp.concatenate(
            [
                columns_first(act_gate),
                columns_first(act_up),
                act_down.reshape(n, few, d_act).transpose(0, 2, 1),
            ],
            axis=1,
        )

    def project(first, count):
        def body(inputs, outputs):
            pairs = len(inputs) - 1
            w_out = inputs[-1]
            width = w_out.shape[1]
            bm, bn = tile(count, 416), tile(width, 1024)

            def step(*refs):
                value = dot_plain(refs[0][...], refs[1][...])
                for h in range(1, pairs):
                    value = value + dot_plain(refs[2 * h][...], refs[2 * h + 1][...])
                refs[-1][...] = value.astype(BF)

            operands, specs = [], []
            for h in range(pairs):
                operands += [inputs[h].at[pl.ds(first, count)], w_out.at[pl.ds(h * HD, HD)]]
                specs += [
                    pl.BlockSpec((bm, HD), lambda j, i: (i, 0)),
                    pl.BlockSpec((HD, bn), lambda j, i: (0, j)),
                ]
            pltpu.emit_pipeline(
                step,
                grid=(width // bn, count // bm),
                in_specs=specs,
                out_specs=[pl.BlockSpec((bm, bn), lambda j, i: (i, j))],
            )(*operands, outputs[0])

        return body

    kernel = Kernel(2)
    gate_own = kernel.flow(Columns(), pre_gate)
    up_own = kernel.flow(Columns(), pre_up, now=False)
    h1_pre, *into = kernel.job(
        functools.partial(project_rows, 0, heads),
        [x_pre, jnp.broadcast_to(gain_pa, (8, wide)), w_in_pre],
        [(rows, wide)] + [(total_rows, HD)] * (heads + 2),
    )
    h1_act = kernel.new_output((acts, narrow), BF)
    kernel.job(
        functools.partial(project_rows, rows, heads),
        [x_act, jnp.broadcast_to(gain_aa, (8, narrow)), w_in_act],
        [],
        into=[h1_act] + into,
    )
    query, keys, values = into[:heads], into[heads], into[heads + 1]
    probs, mixed = [], []
    for h in range(heads):
        p, o = kernel.job(
            attend_forward,
            [query[h], keys, values, seg_q, seg_k],
            [(total_rows, total_rows), (total_rows, HD)],
        )
        probs.append(p)
        mixed.append(o)
    y_pre = kernel.job(project(0, rows), mixed + [w_out_pre], [(rows, wide)])
    y_act = kernel.job(project(rows, acts), mixed + [w_out_act], [(acts, narrow)])
    y_pre_parts = kernel.flow(Parts(), y_pre)
    y_act_parts = kernel.flow(Parts(), y_act)
    kernel.ready(gate_own)
    kernel.go(up_own)
    kernel.relay(y_pre_parts, 1)
    kernel.relay(y_act_parts, 1)
    w_gate = kernel.flow(Pass(1), gate_own)
    kernel.ready(y_pre_parts)
    kernel.ready(y_act_parts)
    x2_pre, h2_pre = kernel.new_output((rq, wide), F32), kernel.new_output((rq, wide), BF)
    x2_act, h2_act = kernel.new_output((aq, narrow), F32), kernel.new_output((aq, narrow), BF)
    kernel.job(
        functools.partial(second_norm, rq),
        [x_pre, y_pre, y_pre_parts, jnp.broadcast_to(gain_pf, (8, wide))],
        [],
        into=[x2_pre, h2_pre],
    )
    kernel.job(
        functools.partial(second_norm, aq),
        [x_act, y_act, y_act_parts, jnp.broadcast_to(gain_af, (8, narrow))],
        [],
        into=[x2_act, h2_act],
    )
    h2_pre = kernel.flow(Line(), h2_pre)
    h2_act = kernel.flow(Line(by_lead, (n, aq, narrow)), h2_act)
    kernel.relay(w_gate, 1)
    kernel.relay(h2_pre, 1)
    kernel.relay(h2_act, 1)
    kernel.relay(w_gate, 2)
    down_own = kernel.flow(Rows(), pre_down)
    if even:
        act_own = [kernel.flow(Columns(), act_gate), kernel.flow(Columns(), act_up)]
        act_own.append(kernel.flow(Rows(), act_down))
    else:
        act_own = [kernel.flow(Each(), act_weights)]
    kernel.ready(up_own)
    w_up = kernel.flow(Pass(1), up_own)
    for k in range(2, half):
        kernel.relay(h2_pre, k)
        kernel.relay(h2_act, k)
        if k < 4:
            kernel.relay(w_up, k - 1)
    got = kernel.call("attend")
    probs, mixed = [got[p] for p in probs], [got[o] for o in mixed]
    query, keys, values = [got[q] for q in query], got[keys], got[values]
    h1_pre, h1_act = got[h1_pre], got[h1_act]
    down_own, w_gate, w_up = got[down_own], got[w_gate], got[w_up]
    x2_pre, x2_act = got[x2_pre], got[x2_act]
    h2_pre, h2_act = got[h2_pre].reshape(n * rq, wide), got[h2_act].reshape(n * aq, narrow)

    def summed(first, parts, count=None):
        value = first.astype(F32)
        for k in range(1, count or parts.shape[0]):
            value = value + parts[k].astype(F32)
        return value

    act_own = [got[a] for a in act_own]
    items, units = h2_pre.shape[0], w_gate.shape[1]
    summing = Halves if m == 4 else Direct

    def in_turn_rows(ref, i, j):
        chip = lax.rem(i // 2 - j // 2 + half, half)
        return ref.at[at(chip + half * lax.rem(i + j, 2), rq)]

    kernel = Kernel(4)
    gz_all = kernel.flow(Line(in_turn_rows, (items, wide)), gz_pre)
    w_down = kernel.flow(Pass(0), down_own)
    into = None
    for piece in range(2):
        into = kernel.job(
            functools.partial(hidden_forward, piece, 2),
            [h2_pre, w_gate, w_up],
            [(items, units)] * 3,
            into=into,
        )
        kernel.relay(gz_all, piece + 1)
    gate, upward, hidden = into
    kernel.relay(w_down, 1)
    kernel.relay(w_down, 2)
    for k in range(3, half):
        kernel.relay(gz_all, k)
    if even:
        act_all_w = [kernel.flow(Pass(axis), a) for axis, a in zip((1, 1, 0), act_own)]
    else:
        act_all_w = [kernel.flow(Pass(0), act_own[0].reshape(n * 3 * d_act, few))]
    kernel.ready(gz_all)
    g_down = kernel.job(products_left, [hidden, gz_all], [(units, wide)])
    down_sum, gate_sum, up_sum = summing(0), summing(1), summing(1)
    down_sum.first(kernel, g_down)
    kernel.ready(w_down)
    z_p = kernel.job(products_plain, [hidden, w_down], [(items, wide)])
    z_p_core = kernel.flow(Core(), z_p)
    for k in (1, 2):
        for a in act_all_w:
            kernel.relay(a, k)
    dgate, dup = kernel.job(
        hidden_backward, [gz_all, w_down, gate, upward], [(items, units)] * 2
    )

    def pair_sum(inputs, outputs):
        parts, other = inputs
        add_pairs([(parts.at[pl.ds(0, other.shape[0])], other)], outputs)

    kernel.ready(z_p_core)
    z_p = kernel.job(pair_sum, [z_p, z_p_core], [(items // 2, wide)])
    got = kernel.call("hidden")
    dgate, dup = got[dgate], got[dup]
    down_sum.settle(got)

    z_p = got[z_p].reshape(half, rq, wide)
    if even:
        act_gate_w, act_up_w, act_down_w = [got[a] for a in act_all_w]
    else:
        act_all_w = got[act_all_w[0]].reshape(m, n, 3, d_act, few).transpose(2, 1, 3, 0, 4)
        act_gate_w, act_up_w, act_down_w = act_all_w.reshape(3, narrow, m * few)
        act_down_w = act_down_w.T

    to_rows = lax.broadcasted_iota(jnp.int32, (n * aq, 1), 0)
    from_rows = lax.broadcasted_iota(jnp.int32, (1, n * slot_count * aq), 1)
    match = (to_rows // aq == jnp.repeat(slot_all, aq)[None, :]) & (to_rows % aq == from_rows % aq)
    cot_all = cot_all.reshape(n * slot_count * aq, narrow)
    gz_act_all = dot_plain(match.astype(BF), cot_all).astype(BF)
    gz_act = lax.dynamic_slice_in_dim(gz_act_all, me * aq, aq, 0)
    kernel = Kernel(6)
    z_p_parts = kernel.flow(Chips(), z_p)
    down_sum.second(kernel)
    g_gate = kernel.job(products_left, [h2_pre, dgate], [(wide, units)])
    gate_sum.first(kernel, g_gate)
    z_a, dh2_a, g_gate_a, g_up_a, g_down_a = kernel.job(
        act_feed_forward,
        [h2_act, gz_act_all, act_gate_w, act_up_w, act_down_w],
        [(n * aq, narrow)] * 2 + [(narrow, m * few)] * 2 + [(m * few, narrow)],
    )
    z_a = kernel.flow(EachRows(), z_a)
    g_up = kernel.job(products_left, [h2_pre, dup], [(wide, units)])
    got = kernel.call("in_grads")
    dh2_a, g_gate_a, g_up_a, g_down_a = [got[o] for o in (dh2_a, g_gate_a, g_up_a, g_down_a)]
    act_back = [g_gate_a, g_up_a, g_down_a]
    if not even:
        act_back = jnp.concatenate([g_gate_a, g_up_a, g_down_a.T], axis=0)
        act_back = [jnp.stack(jnp.split(act_back, m, axis=1))]
    down_sum.settle(got)
    gate_sum.settle(got)
    g_up = got[g_up]
    out_pre = (x2_pre + summed(z_p[0], got[z_p_parts])).astype(BF)
    out_act = (x2_act + jnp.sum(got[z_a].astype(F32), axis=0)).astype(BF)

    kernel = Kernel(7)
    up_sum.first(kernel, g_up)
    grad_down = kernel.flow(Columns(), down_sum.total(kernel))
    out_act = kernel.flow(Line(), out_act)
    dh2_p = kernel.job(products_right, [dgate, w_gate, dup, w_up], [(items, wide)])
    dh2_p_core = kernel.flow(Core(), dh2_p)
    for k in range(1, half):
        kernel.relay(out_act, k)
    kernel.ready(dh2_p_core)
    dh2_p = kernel.job(pair_sum, [dh2_p, dh2_p_core], [(items // 2, wide)])
    got = kernel.call("row_grads")
    out_act = got[out_act].reshape(n * aq, narrow)
    up_sum.settle(got)
    grad_down = got[grad_down].astype(F32)
    dh2_p = got[dh2_p].reshape(half, rq, wide)

    kernel = Kernel(8)
    dh2_p_parts, dh2_a = kernel.flow(Chips(), dh2_p), kernel.flow(EachRows(), dh2_a)
    act_parts = [kernel.flow(Swaps(axis), a) for axis, a in zip((1, 1, 0), act_back)]
    gate_sum.second(kernel)
    up_sum.second(kernel)
    for flow in act_parts:
        kernel.relay(flow, 1)
    got = kernel.call("sum_rows")
    gate_sum.settle(got)
    up_sum.settle(got)
    if even:
        act_back = [g_gate_a[:, :few], g_up_a[:, :few], g_down_a[:few]]
    else:
        act_back = [act_back[0][0]]
    act_sum = [summed(a, got[b], m).astype(BF) for a, b in zip(act_back, act_parts)]
    if not even:
        act_sum = jnp.concatenate(act_sum, axis=0).reshape(3, n, d_act, few)
        act_sum = [act_sum.transpose(1, 0, 2, 3).reshape(n, 3 * d_act, few)]
    gx2n_pre, g_gain_pf = norm_backward(x2_pre, gain_pf, summed(dh2_p[0], got[dh2_p_parts]))
    gx2n_act, g_gain_af = norm_backward(x2_act, gain_af, jnp.sum(got[dh2_a].astype(F32), axis=0))
    gx2_pre = gz_pre.astype(F32) + gx2n_pre
    gx2_act = gz_act.astype(F32) + gx2n_act

    def both_rows(inputs, outputs):
        products_right(inputs[:2], [outputs[0].at[pl.ds(0, rows)]])
        products_right(inputs[2:], [outputs[0].at[pl.ds(rows, acts)]])

    def input_grads(first, count, inputs, outputs):
        w_in, operands = inputs[-1], []
        for h in range(heads):
            operands += [inputs[h].at[pl.ds(first, count)], w_in.at[:, pl.ds(h * HD, HD)]]
        operands += [inputs[heads].at[pl.ds(first, count)], w_in.at[:, pl.ds(split, 2 * HD)]]
        products_right(operands, outputs)

    def weight_grads(first, count, cut, inputs, outputs):
        inputs = [a if a.shape[0] == count else a.at[pl.ds(first, count)] for a in inputs]
        products_left(inputs, [outputs[0].at[cut]])

    kernel = Kernel(9)
    gy_pre = kernel.flow(Whole(), gx2_pre.astype(BF))
    gy_act = kernel.flow(Whole(), gx2_act.astype(BF))
    grad_gate = kernel.flow(Rows(), gate_sum.total(kernel))
    kernel.relay(gy_pre, 1)
    kernel.relay(gy_act, 1)
    kernel.ready(gy_pre)
    kernel.ready(gy_act)
    grad_up = kernel.flow(Rows(), up_sum.total(kernel))
    gmix = kernel.job(both_rows, [gy_pre, w_out_pre, gy_act, w_out_act], [(total_rows, split)])
    *gq, gkv, shares = kernel.job(
        functools.partial(attend_backward, heads),
        probs + query + [keys, values, gmix],
        [(total_rows, HD)] * heads + [(total_rows, 2 * HD), (m, total_rows, kvw)],
    )
    share_parts = kernel.flow(Parts(), shares)
    gh1_pre = kernel.job(
        functools.partial(input_grads, 0, rows), gq + [gkv, w_in_pre], [(rows, wide)]
    )
    gh1_pre_parts = kernel.flow(Parts(), gh1_pre)
    gh1_act = kernel.job(
        functools.partial(input_grads, rows, acts), gq + [gkv, w_in_act], [(acts, narrow)]
    )
    gh1_act_parts = kernel.flow(Parts(), gh1_act)
    if even:
        act_sum = [kernel.flow(k(), a) for k, a in zip((Rows, Rows, Columns), act_sum)]
    else:
        act_sum = [kernel.flow(Each(), act_sum[0])]
    late = [share_parts, gh1_pre_parts, gh1_act_parts]
    g_out_pre = g_out_act = g_q_pre = g_q_act = None
    for h in range(heads):
        heads_columns = (slice(None), pl.ds(h * HD, HD))
        of_pre = functools.partial(weight_grads, 0, rows)
        of_act = functools.partial(weight_grads, rows, acts)

        def grads(body, cut, pair, shape, into):
            return [kernel.job(functools.partial(body, cut), pair, [shape], into=into)]

        g_out_pre = grads(of_pre, heads_columns, [gy_pre, mixed[h]], (wide, split), g_out_pre)
        g_q_pre = grads(of_pre, heads_columns, [h1_pre, gq[h]], (wide, split), g_q_pre)
        g_out_act = grads(of_act, heads_columns, [gy_act, mixed[h]], (narrow, split), g_out_act)
        g_q_act = grads(of_act, heads_columns, [h1_act, gq[h]], (narrow, split), g_q_act)
        if h == 0:
            for flow in late:
                kernel.relay(flow, 1)
    core_grads = [g[0] for g in (g_out_pre, g_q_pre, g_out_act, g_q_act)]
    from_core = [kernel.flow(CoreRows(), g) for g in core_grads]
    got = kernel.call("heads")
    grad_gate, grad_up = got[grad_gate].astype(F32), got[grad_up].astype(F32)
    here = lax.rem(me, 2)

    def of_core(array, core):
        size = array.shape[0] // n
        blocks = array.reshape(half, 2, size, array.shape[1])
        blocks = lax.dynamic_index_in_dim(blocks, core, 1, False)
        return blocks.reshape(half * size, array.shape[1])

    chip_grads = [add(of_core(got[g], here), got[f]) for g, f in zip(core_grads, from_core)]
    shares, gh1_pre, gh1_act = got[shares], got[gh1_pre], got[gh1_act]
    gkv_sum = summed(lax.dynamic_index_in_dim(shares, col, 0, False), got[share_parts], m)
    gh1_pre = summed(own(gh1_pre, rq), got[gh1_pre_parts], m)
    gh1_act = summed(own(gh1_act, aq), got[gh1_act_parts], m)
    act_sum = [got[a].astype(F32) for a in act_sum]
    gkv_sum = gkv_sum.astype(BF)
    g_kv_pre = dot_left(h1_pre, gkv_sum[:rows]).astype(BF)
    g_kv_act = dot_left(h1_act, gkv_sum[rows:]).astype(BF)
    gxn_pre, g_gain_pa = norm_backward(own(x_pre, rq).astype(F32), gain_pa, gh1_pre)
    gxn_act, g_gain_aa = norm_backward(own(x_act, aq), gain_aa, gh1_act)
    grad_pre = (gx2_pre + gxn_pre).astype(BF)
    gxa = (gx2_act + gxn_act).astype(BF)
    g_embed = dot_left(own(act_in, aq), gxa)
    act_grad = dot_right(gxa, embed).reshape(aq * dims_count // lanes, lanes)

    swap = [(i, i ^ 1) for i in range(n)]
    chip_grads += [
        add(of_core(g, here), lax.ppermute(of_core(g, 1 - here), "dp", swap))
        for g in (g_kv_pre, g_kv_act)
    ]
    def by_index(vector):
        return vector.reshape(n, -1, narrow // n).transpose(1, 0, 2).reshape(-1, narrow)

    tiny = [by_index(g) for g in (g_gain_pa, g_gain_pf, g_gain_aa, g_gain_af)] + [g_embed]
    tiny = jnp.concatenate(tiny, axis=0)
    tiny_rows = tiny.shape[0]
    tiny = columns_first(pad_rows(tiny, round_up(tiny_rows, 16)).astype(BF))

    kernel = Kernel(11)
    chip_parts = [kernel.flow(ChipRows(), g) for g in chip_grads]
    prefix_grad = kernel.flow(Whole(), grad_pre)
    prefix_output = kernel.flow(Whole(), out_pre)
    out_act = kernel.flow(Whole(), out_act)
    act_grad = kernel.flow(World(), act_grad)
    tiny = kernel.flow(Spread(), tiny)
    kernel.relay(prefix_grad, 1)
    kernel.relay(prefix_output, 1)
    kernel.relay(out_act, 1)
    got = kernel.call("finish")
    out_act = got[out_act]

    def chip_sum(own_parts, parts):
        size = own_parts.shape[0] // half
        return summed(lax.dynamic_slice_in_dim(own_parts, me // 2 * size, size, 0), got[parts])

    grad_out, grad_query, grad_out_a, grad_query_a, *both = [
        chip_sum(g, f) for g, f in zip(chip_grads, chip_parts)
    ]
    grad_out, grad_out_a = grad_out.T, grad_out_a.T
    both = jnp.concatenate(both, axis=0).astype(BF)
    both = lax.all_gather(both, "mp", axis=1, tiled=True).astype(F32)
    prefix_grad = got[prefix_grad][:length].astype(F32)
    prefix_output = got[prefix_output][:length]
    act_grad = got[act_grad].reshape(n, acts, dims_count)[:, :steps]
    tiny = jnp.sum(got[tiny].astype(F32), axis=(0, 1))
    mine_items = (slot_item[:, None] == lax.broadcasted_iota(jnp.int32, (1, n), 1)).astype(F32)
    mine_turns = (slot_item[:, None] == jnp.stack(turns)[None, :]).astype(F32)
    out_act = out_act.reshape(1, m, n, aq, narrow).astype(F32)
    action_output = jnp.sum(mine_turns[:, None, :, None, None] * out_act, axis=2)
    action_output = action_output.reshape(slot_count, acts, narrow)[:, :steps].astype(BF)
    own_mask = lax.broadcasted_iota(jnp.int32, (slot_count, dims_count), 1) < valid_dims[:, None]
    action_grad = jnp.sum(
        mine_items[:, :, None, None] * act_grad[None], axis=1
    ) * own_mask.astype(F32)[:, None, :]
    grad_gain_pa = tiny[:twice].reshape(-1)
    grad_gain_pf = tiny[twice : 2 * twice].reshape(-1)
    rest = tiny[2 * twice : tiny_rows]

    if even:
        grad_gate_a, grad_up_a, grad_down_a = act_sum
    else:
        act_sum = act_sum[0]
        grad_gate_a = act_sum[:, :d_act].transpose(1, 0, 2).reshape(d_act, n * few)
        grad_up_a = act_sum[:, d_act : 2 * d_act].transpose(1, 0, 2).reshape(d_act, n * few)
        grad_down_a = act_sum[:, 2 * d_act :].transpose(0, 2, 1).reshape(n * few, d_act)
    return (
        prefix_output,
        action_output,
        prefix_grad,
        action_grad,
        grad_gain_pa,
        grad_query,
        both[:d_pre, :HD],
        both[:d_pre, HD:],
        grad_out,
        grad_gain_pf,
        grad_gate,
        grad_up,
        grad_down,
        rest[2:],
        rest[0],
        grad_query_a,
        both[d_pre:, :HD],
        both[d_pre:, HD:],
        grad_out_a,
        rest[1],
        grad_gate_a,
        grad_up_a,
        grad_down_a,
    )


def solution(mesh):
    return jax.shard_map(
        local,
        mesh=mesh,
        in_specs=(
            P("dp", None),
            P("dp", None, None),
            P("dp"),
            P("dp"),
            P("dp", None),
            P("dp"),
            P("dp", "mp"),
            P("dp", None),
            P("dp", None),
            P("mp", "dp"),
            P("dp"),
            P("dp", "mp"),
            P("dp", "mp"),
            P("mp", "dp"),
            P(None, "dp"),
            P("dp"),
            P("dp", "mp"),
            P("dp", None),
            P("dp", None),
            P("mp", "dp"),
            P("dp"),
            P("dp", "mp"),
            P("dp", "mp"),
            P("mp", "dp"),
            P("dp", None),
            P("dp", None, None),
        ),
        out_specs=(
            P("dp", None),
            P("dp", None, None),
            P("dp", None),
            P("dp", None, None),
            P("dp"),
            P("dp", "mp"),
            P("dp", None),
            P("dp", None),
            P("mp", "dp"),
            P("dp"),
            P("dp", "mp"),
            P("dp", "mp"),
            P("mp", "dp"),
            P(None, "dp"),
            P("dp"),
            P("dp", "mp"),
            P("dp", None),
            P("dp", None),
            P("mp", "dp"),
            P("dp"),
            P("dp", "mp"),
            P("dp", "mp"),
            P("mp", "dp"),
        ),
        check_vma=False,
    )
```
